128 devices in a mesh: row: 8 (over y, x_hi), col: 16 (over x_lo, z, core).
Axes of the slice: x: 4 (x_hi: 2, x_lo: 2; x = x_hi * 2 + x_lo), y: 4, z: 4, core: 2. Of those that a mesh axis runs over, the one named last changes fastest.
Arguments:
- traces: bfloat16 [4, 64, 4, 64, 2048], P(None, None, None, 'row', 'col'), may hold values from -6 to 6
- cell_type: int32 [64, 2048], P('row', 'col'), may hold values from 0 to 7
- port_cell: int32 [4], replicated, may hold values from 0 to 131071
- port_profile: bfloat16 [4, 64, 4], replicated, may hold values from -6 to 6
- mode_shapes: float32 [8, 256, 256], P('row', None, 'col'), may hold values from -0.375 to 0.375
- mode_values: float32 [8, 256], P('row', 'col'), may hold values from 0.3 to 1.5
- mode_weights: float32 [8, 256, 256], P('row', 'col'), may hold values from -0.375 to 0.375
Outputs:
- traces_next: bfloat16 [4, 64, 4, 64, 2048], P(None, None, None, 'row', 'col')
The draws below stay inside these ranges and needn't reach their ends.
Inputs may be any that keep to these rules, and one draw needn't show every extreme that they name: `port_cell`: each port's cell as row * 2048 + column; two ports may share a cell.
All inputs are finite; a program needn't handle non-finite values.
Results may differ from the reference program's by a relative error of at most 0.0064.
Values may be sent and summed in bfloat16 or wider, within the bound.
No kernel may reach another device: no remote copies, remote signals or barrier semaphores. Data moves between devices by JAX's collectives and lax.ppermute only.
A program may use at most 64 MiB of HBM per device.

```python
import math
import jax
import jax.numpy as jnp
import numpy as np
from jax import lax

P_SIZE = 64
K = 256
TYPES = 8
S = 4
CELL_BLOCK = 64
SWEEPS = 2
NR = 64
NC = 2048


def touch_ends(values, rng, least, largest):
    longest = values.shape.index(max(values.shape))
    spots = []
    for shift in (0, 1):
        where = [jax.random.randint(jax.random.fold_in(rng, axis), (), 0, length) for axis, length in enumerate(values.shape)]
        where[longest] = (where[longest] + shift) % values.shape[longest]
        spots.append(tuple(where))
    return values.at[spots[0]].set(least).at[spots[1]].set(largest)


def levels(key, extent, split, smallest, top_value):
    def one(position, parts):
        heights = jax.random.uniform(jax.random.fold_in(jax.random.fold_in(key, 6), position), (parts,), jnp.float32, smallest / len(split), top_value / len(split))
        return jnp.repeat(jnp.exp(heights), extent[position] // parts).reshape((-1,) + (1,) * (len(extent) - position - 1))

    level = one(*split[0])
    for cut in split[1:]:
        level = level * one(*cut)
    return level


def cumulative_ranks(count, slope):
    loads = [(1 << 20) // math.isqrt(grade ** slope) + 1 for grade in range(1, count + 1)]
    scale = 1 + sum(loads) // (1 << 30)
    return np.cumsum(np.array([max(1, weight // scale) for weight in loads]))


def ranked_ids(stream_key, extent, amount, slope):
    grid = cumulative_ranks(amount, slope)
    ticket = jax.random.randint(jax.random.fold_in(stream_key, 1), extent, 0, int(grid[amount - 1]))
    grade = jnp.searchsorted(jnp.asarray(grid, jnp.int32), ticket, side="right")
    return jax.random.permutation(jax.random.fold_in(stream_key, 2), amount)[grade].astype(jnp.int32)


def normal_values(own_key, extent, width, reach, shards=(), held_as=jnp.bfloat16):
    gain = levels(own_key, extent, shards, -0.22, 0.18) if shards else 1.0
    drawn = jax.random.normal(own_key, extent, jnp.float32) * width * gain
    return jnp.minimum(jnp.maximum(drawn, -reach), reach).astype(held_as)


def setup_inputs(seed: int = 0) -> dict:
    key_of = jax.random.split(jax.random.key(seed), 8)
    return {
        "traces": normal_values(key_of[0], (4, P_SIZE, S, NR, NC), 1.0, 6.0, ((3, 8), (4, 16))),
        "cell_type": touch_ends(ranked_ids(key_of[1], (NR, NC), TYPES, 2), jax.random.fold_in(key_of[1], 3), 0, TYPES - 1).astype(jnp.int32),
        "port_cell": touch_ends(jax.random.randint(key_of[2], (S,), 0, NR * NC), jax.random.fold_in(key_of[2], 1), 0, (NR * NC) - 1).astype(jnp.int32),
        "port_profile": normal_values(key_of[3], (4, P_SIZE, S), 1.0, 6.0),
        "mode_shapes": normal_values(key_of[4], (TYPES, K, K), K ** -0.5, 0.375, ((0, 8), (2, 16)), jnp.float32),
        "mode_values": jnp.clip(jnp.exp(math.log(1.5) - 1.60943787 * jax.random.uniform(key_of[5], (TYPES, K), jnp.float32) ** levels(key_of[5], (TYPES, K), ((0, 8), (1, 16)), -0.2, 0.2)), 0.3, 1.5),
        "mode_weights": normal_values(key_of[6], (TYPES, K, K), K ** -0.5, 0.375, ((0, 8), (1, 16)), jnp.float32),
    }


def build_maps(mode_shapes, mode_values, mode_weights):
    scaled = mode_shapes * mode_values[:, None, :]
    summed = jnp.einsum('tkm,tmj->tkj', scaled, mode_weights, precision=lax.Precision.HIGHEST)
    return summed.astype(jnp.bfloat16)


def group_cells(types_flat):
    total = types_flat.shape[0]
    onehot = (types_flat[None, :] == jnp.arange(TYPES, dtype=jnp.int32)[:, None]).astype(jnp.int32)
    counts = jnp.sum(onehot, axis=1)
    blocks = (counts + CELL_BLOCK - 1) // CELL_BLOCK
    starts = jnp.cumsum(blocks) - blocks
    ranks = jnp.sum((jnp.cumsum(onehot, axis=1) - 1) * onehot, axis=0)
    slots = (jnp.sum(starts[:, None] * onehot, axis=0) * CELL_BLOCK + ranks).astype(jnp.int32)
    nblock = total // CELL_BLOCK + TYPES
    sources = jnp.zeros((nblock * CELL_BLOCK,), jnp.int32).at[slots].set(jnp.arange(total, dtype=jnp.int32))
    ends = starts + blocks
    block_type = jnp.sum((jnp.arange(nblock, dtype=jnp.int32)[:, None] >= ends[None, :]).astype(jnp.int32), axis=1)
    block_type = jnp.minimum(block_type, TYPES - 1).astype(jnp.int32)
    return slots, sources, block_type, nblock


def apply_types(incoming, cell_maps, slots, sources, block_type, nblock):
    total = incoming.shape[3] * incoming.shape[4]
    flat = incoming.reshape(K, S, total)

    def one_block(index):
        columns = lax.dynamic_slice_in_dim(sources, index * CELL_BLOCK, CELL_BLOCK)
        piece = jnp.take(flat, columns, axis=2).reshape(K, S * CELL_BLOCK)
        matrix = cell_maps[block_type[index]]
        result = jnp.dot(matrix, piece, preferred_element_type=jnp.float32)
        return result.astype(jnp.bfloat16).reshape(K, S, CELL_BLOCK)

    blocked = lax.map(one_block, jnp.arange(nblock, dtype=jnp.int32))
    spread = jnp.transpose(blocked, (1, 2, 0, 3)).reshape(K, S, nblock * CELL_BLOCK)
    return jnp.take(spread, slots, axis=2).reshape(incoming.shape)


def neighbours(outgoing):
    north = jnp.pad(outgoing[1], ((0, 0), (0, 0), (1, 0), (0, 0)))[:, :, :-1, :]
    south = jnp.pad(outgoing[0], ((0, 0), (0, 0), (0, 1), (0, 0)))[:, :, 1:, :]
    west = jnp.pad(outgoing[3], ((0, 0), (0, 0), (0, 0), (1, 0)))[:, :, :, :-1]
    east = jnp.pad(outgoing[2], ((0, 0), (0, 0), (0, 0), (0, 1)))[:, :, :, 1:]
    return jnp.stack([north, south, west, east])


def reference(traces, cell_type, port_cell, port_profile, mode_shapes, mode_values, mode_weights):
    cell_maps = build_maps(mode_shapes, mode_values, mode_weights)
    ncols = cell_type.shape[1]
    slots, sources, block_type, nblock = group_cells(cell_type.reshape(-1).astype(jnp.int32))
    port_rows = (port_cell // ncols).astype(jnp.int32)
    port_cols = (port_cell % ncols).astype(jnp.int32)
    port_index = jnp.arange(S, dtype=jnp.int32)
    incoming = traces
    for sweep_index in range(SWEEPS):
        outgoing = apply_types(incoming, cell_maps, slots, sources, block_type, nblock)
        received = neighbours(outgoing)
        current = received[:, :, port_index, port_rows, port_cols]
        updated = (current.astype(jnp.float32) + port_profile.astype(jnp.float32)).astype(jnp.bfloat16)
        incoming = received.at[:, :, port_index, port_rows, port_cols].set(updated)
    return incoming
```

```python
import functools

import jax
import jax.numpy as jnp
from jax import lax
from jax.experimental import pallas as pl
from jax.experimental.pallas import tpu as pltpu
from jax.sharding import PartitionSpec as P

BF = jnp.bfloat16
F32 = jnp.float32
LANES = 128


def gather_modes(mode_shapes, mode_values, mode_weights):
    scaled = (mode_shapes * mode_values[:, None, :])[0].T
    own = jnp.concatenate([scaled, mode_weights[0]], axis=0)
    count = lax.axis_size("col")
    spread = jnp.broadcast_to(own[None], (count,) + own.shape)
    every = lax.all_to_all(spread, "col", 0, 0, tiled=True)
    modes = scaled.shape[0]
    left = every[:, :modes].reshape(count * modes, -1)
    right = every[:, modes:].reshape(count * modes, -1)
    return left, right


def all_maps(mode_shapes, mode_values, mode_weights):
    left, right = gather_modes(mode_shapes, mode_values, mode_weights)
    own_map = lax.dot_general(
        left, right, (((0,), (0,)), ((), ())), precision=lax.Precision.HIGHEST
    ).astype(BF)
    count = lax.axis_size("row")
    maps = [own_map]
    for step in range(1, count):
        pairs = [(i, (i + step) % count) for i in range(count)]
        maps.append(lax.ppermute(own_map, "row", pairs))
    return maps


def patch(block, rows, width, port_ref, profile_ref, halo_refs):
    north, south, west, east = halo_refs
    quarter = block.shape[0] // 4
    port = pl.program_id(0)
    lane = lax.broadcasted_iota(jnp.int32, (quarter, LANES), 1)
    block[0:quarter, 0:LANES] = north[...]
    block[quarter : 2 * quarter, (rows - 1) * LANES : rows * LANES] = south[...]
    west_all = west[...].astype(F32)
    east_all = east[...].astype(F32)
    for row in range(rows):
        place = port * rows + row
        cols = slice(row * LANES, (row + 1) * LANES)
        from_west = pltpu.roll(west_all, (LANES - place) % LANES, 1)
        from_east = pltpu.roll(east_all, LANES - 1 - place, 1)
        west_part = block[2 * quarter : 3 * quarter, cols].astype(F32)
        east_part = block[3 * quarter : 4 * quarter, cols].astype(F32)
        block[2 * quarter : 3 * quarter, cols] = jnp.where(lane == 0, from_west, west_part).astype(BF)
        block[3 * quarter : 4 * quarter, cols] = jnp.where(
            lane == LANES - 1, from_east, east_part
        ).astype(BF)
    all_cols = width * lax.axis_size("col")
    cell = port_ref[port]
    row = cell // all_cols - lax.axis_index("row") * rows
    col = cell % all_cols - lax.axis_index("col") * width

    @pl.when((row >= 0) & (row < rows) & (col >= 0) & (col < width))
    def _():
        cols = pl.ds(pl.multiple_of(row * LANES, LANES), LANES)
        here = lax.broadcasted_iota(jnp.int32, (4 * quarter, LANES), 1) == col
        current = block[:, cols].astype(F32)
        added = current + profile_ref[0].astype(F32)
        block[:, cols] = jnp.where(here, added, current).astype(BF)


def apply_maps(x, types_ref, map_refs, next_ref, rim_refs, rows):
    north_out, south_out, west_out, east_out = rim_refs
    order = x.shape[0]
    quarter = order // 4
    kinds = len(map_refs)
    port = pl.program_id(0)
    mine = lax.axis_index("row")
    types = jnp.broadcast_to(types_ref[...].astype(F32).astype(BF), x.shape)
    total = None
    for step in range(kinds):
        kind = lax.rem(mine - step + kinds, kinds).astype(F32).astype(BF)
        masked = jnp.where(types == kind, x, jnp.zeros((), BF))
        product = jnp.dot(map_refs[step][...], masked, preferred_element_type=F32)
        total = product if total is None else total + product
    last = (rows - 1) * LANES
    north = total[0:quarter].astype(BF)
    south = total[quarter : 2 * quarter].astype(BF)
    north_out[...] = north[:, 0:LANES]
    south_out[...] = south[:, last:]
    next_ref[0:quarter, LANES:] = south[:, :last]
    next_ref[0:quarter, 0:LANES] = jnp.zeros((quarter, LANES), BF)
    next_ref[quarter : 2 * quarter, :last] = north[:, LANES:]
    next_ref[quarter : 2 * quarter, last:] = jnp.zeros((quarter, LANES), BF)
    lane = lax.broadcasted_iota(jnp.int32, (quarter, LANES), 1)
    west_rim = jnp.where(port == 0, 0.0, west_out[...].astype(F32))
    east_rim = jnp.where(port == 0, 0.0, east_out[...].astype(F32))
    for row in range(rows):
        place = port * rows + row
        cols = slice(row * LANES, (row + 1) * LANES)
        west = total[2 * quarter : 3 * quarter, cols]
        east = total[3 * quarter : 4 * quarter, cols]
        next_ref[2 * quarter : 3 * quarter, cols] = pltpu.roll(east, 1, 1).astype(BF)
        next_ref[3 * quarter : 4 * quarter, cols] = pltpu.roll(west, LANES - 1, 1).astype(BF)
        west_rim = jnp.where(lane == place, pltpu.roll(west, place, 1), west_rim)
        east_rim = jnp.where(lane == place, pltpu.roll(east, place + 1, 1), east_rim)
    west_out[...] = west_rim.astype(BF)
    east_out[...] = east_rim.astype(BF)


def first_kernel(rows, x_ref, types_ref, *refs):
    apply_maps(x_ref[...], types_ref, refs[:-5], refs[-5], refs[-4:], rows)


def second_kernel(rows, width, port_ref, x_ref, types_ref, profile_ref, *refs):
    halo_refs, refs = refs[:4], refs[4:]
    block = refs[-1]
    block[...] = x_ref[...]
    patch(block, rows, width, port_ref, profile_ref, halo_refs)
    apply_maps(block[...], types_ref, refs[:-6], refs[-6], refs[-5:-1], rows)


def last_kernel(rows, width, port_ref, x_ref, profile_ref, *refs):
    out_ref = refs[-1]
    out_ref[...] = x_ref[...]
    patch(out_ref, rows, width, port_ref, profile_ref, refs[:4])


def exchange(rims):
    north, south, west, east = rims

    def send(value, axis, step):
        count = lax.axis_size(axis)
        pairs = [(i, i + step) for i in range(count) if 0 <= i + step < count]
        return lax.ppermute(value, axis, pairs)

    return (
        send(south, "row", 1),
        send(north, "row", -1),
        send(east, "col", 1),
        send(west, "col", -1),
    )


def body(traces, cell_type, port_cell, port_profile, mode_shapes, mode_values, mode_weights):
    edges, samples, ports, rows, width = traces.shape
    order = edges * samples
    quarter = samples
    tile = rows * width
    maps = all_maps(mode_shapes, mode_values, mode_weights)
    x = traces.reshape(order, ports * tile)
    types = cell_type.reshape(1, tile)
    profile = jnp.broadcast_to(
        jnp.transpose(port_profile.reshape(order, ports))[:, :, None], (ports, order, LANES)
    )
    block = pl.BlockSpec((order, tile), lambda i: (0, i))
    types_spec = pl.BlockSpec((1, tile), lambda i: (0, 0))
    map_specs = [pl.BlockSpec((order, order), lambda i: (0, 0))] * len(maps)
    long_rim = pl.BlockSpec((quarter, LANES), lambda i: (0, i))
    short_rim = pl.BlockSpec((quarter, LANES), lambda i: (0, 0))
    rims = [long_rim, long_rim, short_rim, short_rim]
    ports_spec = pl.BlockSpec(memory_space=pltpu.SMEM)
    profile_spec = pl.BlockSpec((1, order, LANES), lambda i: (i, 0, 0))
    next_shape = jax.ShapeDtypeStruct((order, ports * tile), BF)
    rim_shapes = [jax.ShapeDtypeStruct((quarter, ports * LANES), BF)] * 2 + [
        jax.ShapeDtypeStruct((quarter, LANES), BF)
    ] * 2
    params = pltpu.CompilerParams(vmem_limit_bytes=40 * 2**20)
    x, *sent = pl.pallas_call(
        functools.partial(first_kernel, rows),
        grid=(ports,),
        in_specs=[block, types_spec] + map_specs,
        out_specs=[block] + rims,
        out_shape=[next_shape] + rim_shapes,
        compiler_params=params,
    )(x, types, *maps)
    halos = exchange(sent)
    x, *sent = pl.pallas_call(
        functools.partial(second_kernel, rows, width),
        grid=(ports,),
        in_specs=[ports_spec, block, types_spec, profile_spec] + rims + map_specs,
        out_specs=[block] + rims,
        out_shape=[next_shape] + rim_shapes,
        scratch_shapes=[pltpu.VMEM((order, tile), BF)],
        compiler_params=params,
    )(port_cell, x, types, profile, *halos, *maps)
    halos = exchange(sent)
    x = pl.pallas_call(
        functools.partial(last_kernel, rows, width),
        grid=(ports,),
        in_specs=[ports_spec, block, profile_spec] + rims,
        out_specs=block,
        out_shape=next_shape,
        compiler_params=params,
    )(port_cell, x, profile, *halos)
    return x.reshape(traces.shape)


def solution(mesh):
    return jax.shard_map(
        body,
        mesh=mesh,
        in_specs=(
            P(None, None, None, "row", "col"),
            P("row", "col"),
            P(),
            P(),
            P("row", None, "col"),
            P("row", "col"),
            P("row", "col", None),
        ),
        out_specs=P(None, None, None, "row", "col"),
        check_vma=False,
    )
```

```python
import functools

import jax
import jax.numpy as jnp
from jax import lax
from jax.experimental import pallas as pl
from jax.experimental.pallas import tpu as pltpu
from jax.sharding import PartitionSpec as P

BF = jnp.bfloat16
F32 = jnp.float32
LANES = 128


def gather_modes(mode_shapes, mode_values, mode_weights):
    scaled = (mode_shapes * mode_values[:, None, :])[0].T
    own = jnp.concatenate([scaled, mode_weights[0]], axis=0)
    count = lax.axis_size("col")
    spread = jnp.broadcast_to(own[None], (count,) + own.shape)
    every = lax.all_to_all(spread, "col", 0, 0, tiled=True)
    modes = scaled.shape[0]
    left = every[:, :modes].reshape(count * modes, -1)
    right = every[:, modes:].reshape(count * modes, -1)
    return left, right


def all_maps(mode_shapes, mode_values, mode_weights):
    left, right = gather_modes(mode_shapes, mode_values, mode_weights)
    own_map = lax.dot_general(
        left, right, (((0,), (0,)), ((), ())), precision=lax.Precision.HIGHEST
    ).astype(BF)
    count = lax.axis_size("row")
    maps = [own_map]
    for step in range(1, count):
        pairs = [(i, (i + step) % count) for i in range(count)]
        maps.append(lax.ppermute(own_map, "row", pairs))
    return maps


def patch(block, rows, width, port_ref, profile_ref, halo_refs):
    north, south, west, east = halo_refs
    quarter = block.shape[0] // 4
    port = pl.program_id(0)
    lane = lax.broadcasted_iota(jnp.int32, (quarter, LANES), 1)
    mine, count = lax.axis_index("row"), lax.axis_size("row")
    mine_col, count_col = lax.axis_index("col"), lax.axis_size("col")
    zero = jnp.zeros((), BF)
    block[0:quarter, 0:LANES] = jnp.where(mine > 0, north[...], zero)
    block[quarter : 2 * quarter, (rows - 1) * LANES : rows * LANES] = jnp.where(
        mine < count - 1, south[...], zero
    )
    west_all = jnp.where(mine_col > 0, west[...].astype(F32), 0.0)
    east_all = jnp.where(mine_col < count_col - 1, east[...].astype(F32), 0.0)
    for row in range(rows):
        place = port * rows + row
        cols = slice(row * LANES, (row + 1) * LANES)
        from_west = pltpu.roll(west_all, (LANES - place) % LANES, 1)
        from_east = pltpu.roll(east_all, LANES - 1 - place, 1)
        west_part = block[2 * quarter : 3 * quarter, cols].astype(F32)
        east_part = block[3 * quarter : 4 * quarter, cols].astype(F32)
        block[2 * quarter : 3 * quarter, cols] = jnp.where(lane == 0, from_west, west_part).astype(BF)
        block[3 * quarter : 4 * quarter, cols] = jnp.where(
            lane == LANES - 1, from_east, east_part
        ).astype(BF)
    cell = port_ref[port]
    row = cell // (width * count_col) - mine * rows
    col = cell % (width * count_col) - mine_col * width

    @pl.when((row >= 0) & (row < rows) & (col >= 0) & (col < width))
    def _():
        cols = pl.ds(pl.multiple_of(row * LANES, LANES), LANES)
        here = lax.broadcasted_iota(jnp.int32, (4 * quarter, LANES), 1) == col
        current = block[:, cols].astype(F32)
        added = current + profile_ref[0].astype(F32)
        block[:, cols] = jnp.where(here, added, current).astype(BF)


def apply_maps(x, types_ref, map_refs, next_ref, rim_refs, rows):
    north_out, south_out, west_out, east_out = rim_refs
    order = x.shape[0]
    quarter = order // 4
    kinds = len(map_refs)
    port = pl.program_id(0)
    mine = lax.axis_index("row")
    types = jnp.broadcast_to(types_ref[...].astype(F32).astype(BF), x.shape)
    total = None
    for step in range(kinds):
        kind = lax.rem(mine - step + kinds, kinds).astype(F32).astype(BF)
        masked = jnp.where(types == kind, x, jnp.zeros((), BF))
        product = jnp.dot(map_refs[step][...], masked, preferred_element_type=F32)
        total = product if total is None else total + product
    last = (rows - 1) * LANES
    north = total[0:quarter].astype(BF)
    south = total[quarter : 2 * quarter].astype(BF)
    north_out[...] = north[:, 0:LANES]
    south_out[...] = south[:, last:]
    next_ref[0:quarter, LANES:] = south[:, :last]
    next_ref[0:quarter, 0:LANES] = jnp.zeros((quarter, LANES), BF)
    next_ref[quarter : 2 * quarter, :last] = north[:, LANES:]
    next_ref[quarter : 2 * quarter, last:] = jnp.zeros((quarter, LANES), BF)
    lane = lax.broadcasted_iota(jnp.int32, (quarter, LANES), 1)
    west_rim = jnp.where(port == 0, 0.0, west_out[...].astype(F32))
    east_rim = jnp.where(port == 0, 0.0, east_out[...].astype(F32))
    for row in range(rows):
        place = port * rows + row
        cols = slice(row * LANES, (row + 1) * LANES)
        west = total[2 * quarter : 3 * quarter, cols]
        east = total[3 * quarter : 4 * quarter, cols]
        next_ref[2 * quarter : 3 * quarter, cols] = pltpu.roll(east, 1, 1).astype(BF)
        next_ref[3 * quarter : 4 * quarter, cols] = pltpu.roll(west, LANES - 1, 1).astype(BF)
        west_rim = jnp.where(lane == place, pltpu.roll(west, place, 1), west_rim)
        east_rim = jnp.where(lane == place, pltpu.roll(east, place + 1, 1), east_rim)
    west_out[...] = west_rim.astype(BF)
    east_out[...] = east_rim.astype(BF)


def first_kernel(rows, x_ref, types_ref, *refs):
    apply_maps(x_ref[...], types_ref, refs[:-5], refs[-5], refs[-4:], rows)


def second_kernel(rows, width, port_ref, x_ref, types_ref, profile_ref, *refs):
    halo_refs, refs = refs[:4], refs[4:]
    block = refs[-1]
    block[...] = x_ref[...]
    patch(block, rows, width, port_ref, profile_ref, halo_refs)
    apply_maps(block[...], types_ref, refs[:-6], refs[-6], refs[-5:-1], rows)


def last_kernel(rows, width, port_ref, x_ref, profile_ref, *refs):
    out_ref = refs[-1]
    out_ref[...] = x_ref[...]
    patch(out_ref, rows, width, port_ref, profile_ref, refs[:4])


def exchange(rims):
    north, south, west, east = rims

    def send(value, axis, step):
        count = lax.axis_size(axis)
        return lax.ppermute(value, axis, [(i, (i + step) % count) for i in range(count)])

    return (
        send(south, "row", 1),
        send(north, "row", -1),
        send(east, "col", 1),
        send(west, "col", -1),
    )


def body(traces, cell_type, port_cell, port_profile, mode_shapes, mode_values, mode_weights):
    edges, samples, ports, rows, width = traces.shape
    order = edges * samples
    quarter = samples
    tile = rows * width
    maps = all_maps(mode_shapes, mode_values, mode_weights)
    x = traces.reshape(order, ports * tile)
    types = cell_type.reshape(1, tile)
    profile = jnp.broadcast_to(
        jnp.transpose(port_profile.reshape(order, ports))[:, :, None], (ports, order, LANES)
    )
    block = pl.BlockSpec((order, tile), lambda i: (0, i))
    types_spec = pl.BlockSpec((1, tile), lambda i: (0, 0))
    map_specs = [pl.BlockSpec((order, order), lambda i: (0, 0))] * len(maps)
    long_rim = pl.BlockSpec((quarter, LANES), lambda i: (0, i))
    short_rim = pl.BlockSpec((quarter, LANES), lambda i: (0, 0))
    rims = [long_rim, long_rim, short_rim, short_rim]
    ports_spec = pl.BlockSpec(memory_space=pltpu.SMEM)
    profile_spec = pl.BlockSpec((1, order, LANES), lambda i: (i, 0, 0))
    next_shape = jax.ShapeDtypeStruct((order, ports * tile), BF)
    rim_shapes = [jax.ShapeDtypeStruct((quarter, ports * LANES), BF)] * 2 + [
        jax.ShapeDtypeStruct((quarter, LANES), BF)
    ] * 2
    params = pltpu.CompilerParams(vmem_limit_bytes=20 * 2**20)
    x, *sent = pl.pallas_call(
        functools.partial(first_kernel, rows),
        grid=(ports,),
        in_specs=[block, types_spec] + map_specs,
        out_specs=[block] + rims,
        out_shape=[next_shape] + rim_shapes,
        compiler_params=params,
    )(x, types, *maps)
    halos = exchange(sent)
    x, *sent = pl.pallas_call(
        functools.partial(second_kernel, rows, width),
        grid=(ports,),
        in_specs=[ports_spec, block, types_spec, profile_spec] + rims + map_specs,
        out_specs=[block] + rims,
        out_shape=[next_shape] + rim_shapes,
        scratch_shapes=[pltpu.VMEM((order, tile), BF)],
        compiler_params=params,
    )(port_cell, x, types, profile, *halos, *maps)
    halos = exchange(sent)
    x = pl.pallas_call(
        functools.partial(last_kernel, rows, width),
        grid=(ports,),
        in_specs=[ports_spec, block, profile_spec] + rims,
        out_specs=block,
        out_shape=next_shape,
        compiler_params=params,
    )(port_cell, x, profile, *halos)
    return x.reshape(traces.shape)


def solution(mesh):
    return jax.shard_map(
        body,
        mesh=mesh,
        in_specs=(
            P(None, None, None, "row", "col"),
            P("row", "col"),
            P(),
            P(),
            P("row", None, "col"),
            P("row", "col"),
            P("row", "col", None),
        ),
        out_specs=P(None, None, None, "row", "col"),
        check_vma=False,
    )
```

```python
import functools

import jax
import jax.numpy as jnp
from jax import lax
from jax.experimental import pallas as pl
from jax.experimental.pallas import tpu as pltpu
from jax.sharding import PartitionSpec as P

BF = jnp.bfloat16
F32 = jnp.float32
LANES = 128


def gather_modes(mode_shapes, mode_values, mode_weights):
    scaled = (mode_shapes * mode_values[:, None, :])[0].T
    own = jnp.concatenate([scaled, mode_weights[0]], axis=0)
    count = lax.axis_size("col")
    spread = jnp.broadcast_to(own[None], (count,) + own.shape)
    every = lax.all_to_all(spread, "col", 0, 0, tiled=True)
    modes = scaled.shape[0]
    left = every[:, :modes].reshape(count * modes, -1)
    right = every[:, modes:].reshape(count * modes, -1)
    return left, right


def all_maps(mode_shapes, mode_values, mode_weights):
    left, right = gather_modes(mode_shapes, mode_values, mode_weights)
    own_map = lax.dot_general(
        left, right, (((0,), (0,)), ((), ())), precision=lax.Precision.HIGHEST
    ).astype(BF)
    count = lax.axis_size("row")
    return [own_map] + [
        lax.ppermute(own_map, "row", [(i, i ^ step) for i in range(count)])
        for step in range(1, count)
    ]


def patch(block, rows, width, east_lane, port_ref, profile_ref, halo_refs):
    north, south, west, east = halo_refs
    quarter = block.shape[0] // 4
    port = pl.program_id(0)
    lane = lax.broadcasted_iota(jnp.int32, (quarter, LANES), 1)
    mine, count = lax.axis_index("row"), lax.axis_size("row")
    mine_col, count_col = lax.axis_index("col"), lax.axis_size("col")
    zero = jnp.zeros((), BF)
    block[0:quarter, 0:LANES] = jnp.where(mine > 0, north[...], zero)
    block[quarter : 2 * quarter, (rows - 1) * LANES : rows * LANES] = jnp.where(
        mine < count - 1, south[...], zero
    )
    west_all = jnp.where(mine_col > 0, west[...].astype(F32), 0.0)
    east_all = jnp.where(mine_col < count_col - 1, east[...].astype(F32), 0.0)
    for row in range(rows):
        place = port * rows + row
        cols = slice(row * LANES, (row + 1) * LANES)
        from_west = pltpu.roll(west_all, lax.rem(2 * LANES - east_lane - place, LANES), 1)
        from_east = pltpu.roll(east_all, LANES - 1 - place, 1)
        west_part = block[2 * quarter : 3 * quarter, cols].astype(F32)
        east_part = block[3 * quarter : 4 * quarter, cols].astype(F32)
        block[2 * quarter : 3 * quarter, cols] = jnp.where(lane == 0, from_west, west_part).astype(BF)
        block[3 * quarter : 4 * quarter, cols] = jnp.where(
            lane == LANES - 1, from_east, east_part
        ).astype(BF)
    cell = port_ref[port]
    row = cell // (width * count_col) - mine * rows
    col = cell % (width * count_col) - mine_col * width

    @pl.when((row >= 0) & (row < rows) & (col >= 0) & (col < width))
    def _():
        cols = pl.ds(pl.multiple_of(row * LANES, LANES), LANES)
        here = lax.broadcasted_iota(jnp.int32, (4 * quarter, LANES), 1) == col
        current = block[:, cols].astype(F32)
        added = current + profile_ref[0].astype(F32)
        block[:, cols] = jnp.where(here, added, current).astype(BF)


def products(x, types, map_refs, first, last):
    mine = lax.axis_index("row")
    types = jnp.broadcast_to(types, x.shape)
    total = None
    for step, map_ref in enumerate(map_refs):
        kind = (mine ^ step).astype(F32).astype(BF)
        masked = jnp.where(types == kind, x, jnp.zeros((), BF))
        product = jnp.dot(map_ref[first:last, :], masked, preferred_element_type=F32)
        total = product if total is None else total + product
    return total


def shifted(total, next_ref, rows):
    quarter = total.shape[0] // 4
    last = (rows - 1) * LANES
    north = total[0:quarter].astype(BF)
    south = total[quarter : 2 * quarter].astype(BF)
    next_ref[0:quarter, LANES:] = south[:, :last]
    next_ref[0:quarter, 0:LANES] = jnp.zeros((quarter, LANES), BF)
    next_ref[quarter : 2 * quarter, :last] = north[:, LANES:]
    next_ref[quarter : 2 * quarter, last:] = jnp.zeros((quarter, LANES), BF)
    for row in range(rows):
        cols = slice(row * LANES, (row + 1) * LANES)
        west = total[2 * quarter : 3 * quarter, cols]
        east = total[3 * quarter : 4 * quarter, cols]
        next_ref[2 * quarter : 3 * quarter, cols] = pltpu.roll(east, 1, 1).astype(BF)
        next_ref[3 * quarter : 4 * quarter, cols] = pltpu.roll(west, LANES - 1, 1).astype(BF)
    return north, south


def rim_kernel(rows, ports, x_ref, types_ref, *refs):
    map_refs = refs[:-4]
    north_out, south_out, west_out, east_out = refs[-4:]
    order = x_ref.shape[0]
    quarter = order // 4
    tile = rows * LANES
    types = types_ref[...].astype(F32)
    starts = [port * tile for port in range(ports)]
    for edge, out, offset in ((0, north_out, 0), (1, south_out, tile - LANES)):
        cells = jnp.concatenate(
            [x_ref[:, start + offset : start + offset + LANES] for start in starts], axis=1
        )
        kinds = jnp.concatenate([types[:, offset : offset + LANES]] * ports, axis=1).astype(BF)
        out[...] = products(cells, kinds, map_refs, edge * quarter, (edge + 1) * quarter).astype(BF)
    wide = 2 * LANES
    spread = jnp.broadcast_to(types, (16, tile)).astype(BF)
    place = lax.broadcasted_iota(jnp.int32, (wide, LANES), 0)
    lane = lax.broadcasted_iota(jnp.int32, (wide, LANES), 1)
    wanted = jnp.where(lane < 64, lane * LANES, (lane - 64) * LANES + LANES - 1)
    picked = None
    for start in range(0, ports * tile, wide):
        pick = jnp.where(place + start == wanted, 1.0, 0.0).astype(BF)
        inside = start % tile
        both = jnp.concatenate(
            [x_ref[:, start : start + wide], spread[:, inside : inside + wide]], axis=0
        )
        part = jnp.dot(both, pick, preferred_element_type=F32)
        picked = part if picked is None else picked + part
    cells = picked[0:order].astype(BF)
    kinds = picked[order : order + 1].astype(BF)
    sides = products(cells, kinds, map_refs, 2 * quarter, 4 * quarter).astype(BF)
    west_out[...] = sides[0:quarter]
    east_out[...] = sides[quarter : 2 * quarter]


def first_kernel(rows, x_ref, types_ref, *refs):
    x = x_ref[...]
    types = types_ref[...].astype(F32).astype(BF)
    shifted(products(x, types, refs[:-1], 0, x.shape[0]), refs[-1], rows)


def second_kernel(rows, width, port_ref, x_ref, types_ref, profile_ref, *refs):
    halo_refs, map_refs, next_ref = refs[:4], refs[4:-6], refs[-6]
    north_out, south_out, west_out, east_out, block = refs[-5:]
    block[...] = x_ref[...]
    patch(block, rows, width, 64, port_ref, profile_ref, halo_refs)
    order = block.shape[0]
    quarter = order // 4
    types = types_ref[...].astype(F32).astype(BF)
    total = products(block[...], types, map_refs, 0, order)
    north, south = shifted(total, next_ref, rows)
    north_out[...] = north[:, 0:LANES]
    south_out[...] = south[:, (rows - 1) * LANES :]
    port = pl.program_id(0)
    lane = lax.broadcasted_iota(jnp.int32, (quarter, LANES), 1)
    west_rim = jnp.where(port == 0, 0.0, west_out[...].astype(F32))
    east_rim = jnp.where(port == 0, 0.0, east_out[...].astype(F32))
    for row in range(rows):
        place = port * rows + row
        cols = slice(row * LANES, (row + 1) * LANES)
        west = total[2 * quarter : 3 * quarter, cols]
        east = total[3 * quarter : 4 * quarter, cols]
        west_rim = jnp.where(lane == place, pltpu.roll(west, place, 1), west_rim)
        east_rim = jnp.where(lane == place, pltpu.roll(east, place + 1, 1), east_rim)
    west_out[...] = west_rim.astype(BF)
    east_out[...] = east_rim.astype(BF)


def last_kernel(rows, width, port_ref, x_ref, profile_ref, *refs):
    out_ref, block = refs[-2:]
    block[...] = x_ref[...]
    patch(block, rows, width, 0, port_ref, profile_ref, refs[:4])
    out_ref[...] = block[...].astype(F32).reshape(out_ref.shape).astype(BF)


def exchange(rims):
    north, south, west, east = rims

    def send(value, axis, step):
        count = lax.axis_size(axis)
        return lax.ppermute(value, axis, [(i, (i + step) % count) for i in range(count)])

    return (
        send(south, "row", 1),
        send(north, "row", -1),
        send(east, "col", 1),
        send(west, "col", -1),
    )


def body(traces, cell_type, port_cell, port_profile, mode_shapes, mode_values, mode_weights):
    edges, samples, ports, rows, width = traces.shape
    order = edges * samples
    quarter = samples
    tile = rows * width
    maps = all_maps(mode_shapes, mode_values, mode_weights)
    x = traces.reshape(order, ports * tile)
    types = cell_type.reshape(1, tile)
    profile = jnp.broadcast_to(
        jnp.transpose(port_profile.reshape(order, ports))[:, :, None], (ports, order, LANES)
    )
    block = pl.BlockSpec((order, tile), lambda i: (0, i))
    types_spec = pl.BlockSpec((1, tile), lambda i: (0, 0))
    map_specs = [pl.BlockSpec((order, order), lambda i: (0, 0))] * len(maps)
    long_rim = pl.BlockSpec((quarter, LANES), lambda i: (0, i))
    short_rim = pl.BlockSpec((quarter, LANES), lambda i: (0, 0))
    rims = [long_rim, long_rim, short_rim, short_rim]
    ports_spec = pl.BlockSpec(memory_space=pltpu.SMEM)
    profile_spec = pl.BlockSpec((1, order, LANES), lambda i: (i, 0, 0))
    next_shape = jax.ShapeDtypeStruct((order, ports * tile), BF)
    rim_shapes = [jax.ShapeDtypeStruct((quarter, ports * LANES), BF)] * 2 + [
        jax.ShapeDtypeStruct((quarter, LANES), BF)
    ] * 2
    params = pltpu.CompilerParams(vmem_limit_bytes=20 * 2**20)
    whole = pl.BlockSpec(memory_space=pltpu.VMEM)
    work = 2 * order * order * len(maps) * ports * tile
    sent = pl.pallas_call(
        functools.partial(rim_kernel, rows, ports),
        in_specs=[whole] * (2 + len(maps)),
        out_specs=[whole] * 4,
        out_shape=rim_shapes,
        compiler_params=params,
        cost_estimate=pl.CostEstimate(flops=work // 8, bytes_accessed=0, transcendentals=0),
    )(x, types, *maps)
    halos = exchange(sent)
    x = pl.pallas_call(
        functools.partial(first_kernel, rows),
        grid=(ports,),
        in_specs=[block, types_spec] + map_specs,
        out_specs=block,
        out_shape=next_shape,
        compiler_params=params,
        cost_estimate=pl.CostEstimate(flops=work, bytes_accessed=0, transcendentals=0),
    )(x, types, *maps)
    x, *sent = pl.pallas_call(
        functools.partial(second_kernel, rows, width),
        grid=(ports,),
        in_specs=[ports_spec, block, types_spec, profile_spec] + rims + map_specs,
        out_specs=[block] + rims,
        out_shape=[next_shape] + rim_shapes,
        scratch_shapes=[pltpu.VMEM((order, tile), BF)],
        compiler_params=params,
        cost_estimate=pl.CostEstimate(flops=work, bytes_accessed=0, transcendentals=0),
    )(port_cell, x, types, profile, *halos, *maps)
    halos = exchange(sent)
    out = pl.pallas_call(
        functools.partial(last_kernel, rows, width),
        grid=(ports,),
        in_specs=[ports_spec, block, profile_spec] + rims,
        out_specs=pl.BlockSpec((order, 1, rows, LANES), lambda i: (0, i, 0, 0)),
        out_shape=jax.ShapeDtypeStruct((order, ports, rows, width), BF),
        scratch_shapes=[pltpu.VMEM((order, tile), BF)],
        compiler_params=params,
    )(port_cell, x, profile, *halos)
    return out.reshape(traces.shape)


def solution(mesh):
    return jax.shard_map(
        body,
        mesh=mesh,
        in_specs=(
            P(None, None, None, "row", "col"),
            P("row", "col"),
            P(),
            P(),
            P("row", None, "col"),
            P("row", "col"),
            P("row", "col", None),
        ),
        out_specs=P(None, None, None, "row", "col"),
        check_vma=False,
    )
```

```python
import functools

import jax
import jax.numpy as jnp
from jax import lax
from jax.experimental import pallas as pl
from jax.experimental.pallas import tpu as pltpu
from jax.sharding import PartitionSpec as P

BF = jnp.bfloat16
F32 = jnp.float32
LANES = 128


def swap(value, axis, first, second=None):
    second = first if second is None else second
    rows, cols = lax.axis_size("row"), lax.axis_size("col")
    pairs = []
    for row in range(rows):
        for col in range(cols):
            step = second if col % 2 else first
            other = (row ^ step, col) if axis == "row" else (row, col ^ step)
            pairs.append((row * cols + col, other[0] * cols + other[1]))
    return lax.ppermute(value, ("row", "col"), pairs)


def own_type_map(mode_shapes, mode_values, mode_weights, x):
    scaled = (mode_shapes * mode_values[:, None, :])[0].T
    own = jnp.concatenate([scaled, mode_weights[0]], axis=0)
    far = swap(own, "col", 4)
    pair = jnp.concatenate([own, swap(own, "col", 1)], axis=0)
    got = [swap(pair, "col", 8, 10), swap(pair, "col", 2, 14), swap(pair, "col", 6, 12)]
    *got, x = lax.optimization_barrier((*got, x))
    every = jnp.concatenate([own, far] + got, axis=0).reshape((-1, 2) + scaled.shape)
    left = every[:, 0].reshape(-1, scaled.shape[1])
    right = every[:, 1].reshape(-1, scaled.shape[1])
    partial = lax.dot_general(
        left, right, (((0,), (0,)), ((), ())), precision=lax.Precision.HIGHEST
    )
    partial = lax.optimization_barrier(partial)
    return (partial + swap(partial, "col", 1)).astype(BF), x


MAP_STEPS = ((0, 0), (1, 3), (2, 7), (6, 5), (3, 1), (7, 2), (5, 6), (4, 4))


def all_maps(own_map):
    core = lax.rem(lax.axis_index("col"), 2)
    half = own_map.shape[0] // 2
    mine = swap(lax.dynamic_slice_in_dim(own_map, core * half, half), "row", 4)
    got = [swap(own_map, "row", first, second) for first, second in MAP_STEPS[1:4]]
    return [own_map] + got + [swap(value, "col", 1) for value in got + [mine]] + [mine]


def patch(block, rows, width, east_lane, port_ref, profile_ref, halo_refs):
    north, south, west, east = halo_refs
    quarter = block.shape[0] // 4
    port = pl.program_id(0)
    lane = lax.broadcasted_iota(jnp.int32, (quarter, LANES), 1)
    mine, count = lax.axis_index("row"), lax.axis_size("row")
    mine_col, count_col = lax.axis_index("col"), lax.axis_size("col")
    zero = jnp.zeros((), BF)
    block[0:quarter, 0:LANES] = jnp.where(mine > 0, north[...], zero)
    block[quarter : 2 * quarter, (rows - 1) * LANES : rows * LANES] = jnp.where(
        mine < count - 1, south[...], zero
    )
    west_all = jnp.where(mine_col > 0, west[...].astype(F32), 0.0)
    east_all = jnp.where(mine_col < count_col - 1, east[...].astype(F32), 0.0)
    for row in range(rows):
        place = port * rows + row
        cols = slice(row * LANES, (row + 1) * LANES)
        from_west = pltpu.roll(west_all, lax.rem(2 * LANES - east_lane - place, LANES), 1)
        from_east = pltpu.roll(east_all, LANES - 1 - place, 1)
        west_part = block[2 * quarter : 3 * quarter, cols].astype(F32)
        east_part = block[3 * quarter : 4 * quarter, cols].astype(F32)
        block[2 * quarter : 3 * quarter, cols] = jnp.where(lane == 0, from_west, west_part).astype(BF)
        block[3 * quarter : 4 * quarter, cols] = jnp.where(
            lane == LANES - 1, from_east, east_part
        ).astype(BF)
    cell = port_ref[port]
    row = cell // (width * count_col) - mine * rows
    col = cell % (width * count_col) - mine_col * width

    @pl.when((row >= 0) & (row < rows) & (col >= 0) & (col < width))
    def _():
        cols = pl.ds(pl.multiple_of(row * LANES, LANES), LANES)
        here = lax.broadcasted_iota(jnp.int32, (4 * quarter, LANES), 1) == col
        current = block[:, cols].astype(F32)
        added = current + profile_ref[0].astype(F32)
        block[:, cols] = jnp.where(here, added, current).astype(BF)


def products(x, types, map_refs, first, last):
    mine = lax.axis_index("row")
    types = jnp.broadcast_to(types, x.shape)
    total = None
    core = lax.rem(lax.axis_index("col"), 2)
    for number, (even, odd) in enumerate(MAP_STEPS):
        kind = (mine ^ jnp.where(core == 0, even, odd)).astype(F32).astype(BF)
        masked = jnp.where(types == kind, x, jnp.zeros((), BF))
        if number + 1 < len(MAP_STEPS):
            part = map_refs[number][first:last, :]
        else:
            swapped, own = map_refs[number][...], map_refs[number + 1][...]
            low, high = jnp.where(core == 0, own, swapped), jnp.where(core == 0, swapped, own)
            part = jnp.concatenate([low, high], axis=0)[first:last]
        product = jnp.dot(part, masked, preferred_element_type=F32)
        total = product if total is None else total + product
    return total


def shifted(total, next_ref, rows):
    quarter = total.shape[0] // 4
    last = (rows - 1) * LANES
    north = total[0:quarter].astype(BF)
    south = total[quarter : 2 * quarter].astype(BF)
    next_ref[0:quarter, LANES:] = south[:, :last]
    next_ref[0:quarter, 0:LANES] = jnp.zeros((quarter, LANES), BF)
    next_ref[quarter : 2 * quarter, :last] = north[:, LANES:]
    next_ref[quarter : 2 * quarter, last:] = jnp.zeros((quarter, LANES), BF)
    for row in range(rows):
        cols = slice(row * LANES, (row + 1) * LANES)
        west = total[2 * quarter : 3 * quarter, cols]
        east = total[3 * quarter : 4 * quarter, cols]
        next_ref[2 * quarter : 3 * quarter, cols] = pltpu.roll(east, 1, 1).astype(BF)
        next_ref[3 * quarter : 4 * quarter, cols] = pltpu.roll(west, LANES - 1, 1).astype(BF)
    return north, south


def rim_kernel(rows, ports, x_ref, types_ref, *refs):
    map_refs = refs[:-4]
    north_out, south_out, west_out, east_out = refs[-4:]
    order = x_ref.shape[0]
    quarter = order // 4
    tile = rows * LANES
    types = types_ref[...].astype(F32)
    starts = [port * tile for port in range(ports)]
    for edge, out, offset in ((0, north_out, 0), (1, south_out, tile - LANES)):
        cells = jnp.concatenate(
            [x_ref[:, start + offset : start + offset + LANES] for start in starts], axis=1
        )
        kinds = jnp.concatenate([types[:, offset : offset + LANES]] * ports, axis=1).astype(BF)
        out[...] = products(cells, kinds, map_refs, edge * quarter, (edge + 1) * quarter).astype(BF)
    wide = 2 * LANES
    spread = jnp.broadcast_to(types, (16, tile)).astype(BF)
    place = lax.broadcasted_iota(jnp.int32, (wide, LANES), 0)
    lane = lax.broadcasted_iota(jnp.int32, (wide, LANES), 1)
    wanted = jnp.where(lane < 64, lane * LANES, (lane - 64) * LANES + LANES - 1)
    picked = None
    for start in range(0, ports * tile, wide):
        pick = jnp.where(place + start == wanted, 1.0, 0.0).astype(BF)
        inside = start % tile
        both = jnp.concatenate(
            [x_ref[:, start : start + wide], spread[:, inside : inside + wide]], axis=0
        )
        part = jnp.dot(both, pick, preferred_element_type=F32)
        picked = part if picked is None else picked + part
    cells = picked[0:order].astype(BF)
    kinds = picked[order : order + 1].astype(BF)
    sides = products(cells, kinds, map_refs, 2 * quarter, 4 * quarter).astype(BF)
    west_out[...] = sides[0:quarter]
    east_out[...] = sides[quarter : 2 * quarter]


def first_kernel(rows, x_ref, types_ref, *refs):
    x = x_ref[...]
    types = types_ref[...].astype(F32).astype(BF)
    shifted(products(x, types, refs[:-1], 0, x.shape[0]), refs[-1], rows)


def second_kernel(rows, width, port_ref, x_ref, types_ref, profile_ref, *refs):
    halo_refs, map_refs, next_ref = refs[:4], refs[4:-6], refs[-6]
    north_out, south_out, west_out, east_out, block = refs[-5:]
    block[...] = x_ref[...]
    patch(block, rows, width, 64, port_ref, profile_ref, halo_refs)
    order = block.shape[0]
    quarter = order // 4
    types = types_ref[...].astype(F32).astype(BF)
    total = products(block[...], types, map_refs, 0, order)
    north, south = shifted(total, next_ref, rows)
    north_out[...] = north[:, 0:LANES]
    south_out[...] = south[:, (rows - 1) * LANES :]
    port = pl.program_id(0)
    lane = lax.broadcasted_iota(jnp.int32, (quarter, LANES), 1)
    west_rim = jnp.where(port == 0, 0.0, west_out[...].astype(F32))
    east_rim = jnp.where(port == 0, 0.0, east_out[...].astype(F32))
    for row in range(rows):
        place = port * rows + row
        cols = slice(row * LANES, (row + 1) * LANES)
        west = total[2 * quarter : 3 * quarter, cols]
        east = total[3 * quarter : 4 * quarter, cols]
        west_rim = jnp.where(lane == place, pltpu.roll(west, place, 1), west_rim)
        east_rim = jnp.where(lane == place, pltpu.roll(east, place + 1, 1), east_rim)
    west_out[...] = west_rim.astype(BF)
    east_out[...] = east_rim.astype(BF)


def last_kernel(rows, width, port_ref, x_ref, profile_ref, *refs):
    out_ref, block = refs[-2:]
    block[...] = x_ref[...]
    patch(block, rows, width, 0, port_ref, profile_ref, refs[:4])
    out_ref[...] = block[...].astype(F32).reshape(out_ref.shape).astype(BF)


def exchange(rims):
    north, south, west, east = rims

    def send(value, axis, step):
        count = lax.axis_size(axis)
        return lax.ppermute(value, axis, [(i, (i + step) % count) for i in range(count)])

    return (
        send(south, "row", 1),
        send(north, "row", -1),
        send(east, "col", 1),
        send(west, "col", -1),
    )


def body(traces, cell_type, port_cell, port_profile, mode_shapes, mode_values, mode_weights):
    edges, samples, ports, rows, width = traces.shape
    order = edges * samples
    quarter = samples
    tile = rows * width
    x = traces.reshape(order, ports * tile)
    own_map, x = own_type_map(mode_shapes, mode_values, mode_weights, x)
    maps = all_maps(own_map)
    types = cell_type.reshape(1, tile)
    profile = jnp.broadcast_to(
        jnp.transpose(port_profile.reshape(order, ports))[:, :, None], (ports, order, LANES)
    )
    block = pl.BlockSpec((order, tile), lambda i: (0, i))
    types_spec = pl.BlockSpec((1, tile), lambda i: (0, 0))
    map_specs = [pl.BlockSpec(value.shape, lambda i: (0, 0)) for value in maps]
    long_rim = pl.BlockSpec((quarter, LANES), lambda i: (0, i))
    short_rim = pl.BlockSpec((quarter, LANES), lambda i: (0, 0))
    rims = [long_rim, long_rim, short_rim, short_rim]
    ports_spec = pl.BlockSpec(memory_space=pltpu.SMEM)
    profile_spec = pl.BlockSpec((1, order, LANES), lambda i: (i, 0, 0))
    next_shape = jax.ShapeDtypeStruct((order, ports * tile), BF)
    rim_shapes = [jax.ShapeDtypeStruct((quarter, ports * LANES), BF)] * 2 + [
        jax.ShapeDtypeStruct((quarter, LANES), BF)
    ] * 2
    params = pltpu.CompilerParams(vmem_limit_bytes=20 * 2**20)
    whole = pl.BlockSpec(memory_space=pltpu.VMEM)
    work = 2 * order * order * len(MAP_STEPS) * ports * tile
    sent = pl.pallas_call(
        functools.partial(rim_kernel, rows, ports),
        in_specs=[whole] * (2 + len(maps)),
        out_specs=[whole] * 4,
        out_shape=rim_shapes,
        compiler_params=params,
        cost_estimate=pl.CostEstimate(flops=work // 8, bytes_accessed=0, transcendentals=0),
    )(x, types, *maps)
    halos = exchange(sent)
    x = pl.pallas_call(
        functools.partial(first_kernel, rows),
        grid=(ports,),
        in_specs=[block, types_spec] + map_specs,
        out_specs=block,
        out_shape=next_shape,
        compiler_params=params,
        cost_estimate=pl.CostEstimate(flops=work, bytes_accessed=0, transcendentals=0),
    )(x, types, *maps)
    x, *sent = pl.pallas_call(
        functools.partial(second_kernel, rows, width),
        grid=(ports,),
        in_specs=[ports_spec, block, types_spec, profile_spec] + rims + map_specs,
        out_specs=[block] + rims,
        out_shape=[next_shape] + rim_shapes,
        scratch_shapes=[pltpu.VMEM((order, tile), BF)],
        compiler_params=params,
        cost_estimate=pl.CostEstimate(flops=work, bytes_accessed=0, transcendentals=0),
    )(port_cell, x, types, profile, *halos, *maps)
    halos = exchange(sent)
    out = pl.pallas_call(
        functools.partial(last_kernel, rows, width),
        grid=(ports,),
        in_specs=[ports_spec, block, profile_spec] + rims,
        out_specs=pl.BlockSpec((order, 1, rows, LANES), lambda i: (0, i, 0, 0)),
        out_shape=jax.ShapeDtypeStruct((order, ports, rows, width), BF),
        scratch_shapes=[pltpu.VMEM((order, tile), BF)],
        compiler_params=params,
    )(port_cell, x, profile, *halos)
    return out.reshape(traces.shape)


def solution(mesh):
    return jax.shard_map(
        body,
        mesh=mesh,
        in_specs=(
            P(None, None, None, "row", "col"),
            P("row", "col"),
            P(),
            P(),
            P("row", None, "col"),
            P("row", "col"),
            P("row", "col", None),
        ),
        out_specs=P(None, None, None, "row", "col"),
        check_vma=False,
    )
```

```python
import functools

import jax
import jax.numpy as jnp
from jax import lax
from jax.experimental import pallas as pl
from jax.experimental.pallas import tpu as pltpu
from jax.sharding import PartitionSpec as P

BF = jnp.bfloat16
F32 = jnp.float32
LANES = 128
PARAMS = pltpu.CompilerParams(vmem_limit_bytes=20 * 2**20)


def swap(value, axis, first, second=None):
    second = first if second is None else second
    rows, cols = lax.axis_size("row"), lax.axis_size("col")
    pairs = []
    for row in range(rows):
        for col in range(cols):
            step = second if col % 2 else first
            other = (row ^ step, col) if axis == "row" else (row, col ^ step)
            pairs.append((row * cols + col, other[0] * cols + other[1]))
    return lax.ppermute(value, ("row", "col"), pairs)


def pack_kernel(shapes_ref, values_ref, weights_ref, out_ref):
    modes = shapes_ref.shape[0]
    row = lax.broadcasted_iota(jnp.int32, (modes, modes), 0)
    col = lax.broadcasted_iota(jnp.int32, (modes, modes), 1)
    values = jnp.broadcast_to(values_ref[...], (modes, modes))
    column = jnp.sum(jnp.where(row == col, values, 0.0), axis=1, keepdims=True)
    out_ref[0:modes] = shapes_ref[...] * column
    out_ref[modes:] = weights_ref[...]


def partial_kernel(modes, *refs):
    left, right = [], []
    for ref in refs[:-1]:
        for start in range(0, ref.shape[0], 2 * modes):
            left.append(ref[start : start + modes])
            right.append(ref[start + modes : start + 2 * modes])
    refs[-1][...] = lax.dot_general(
        jnp.concatenate(left, axis=0),
        jnp.concatenate(right, axis=0),
        (((0,), (0,)), ((), ())),
        precision=lax.Precision.HIGHEST,
        preferred_element_type=F32,
    )


WHOLE = pl.BlockSpec(memory_space=pltpu.VMEM)


def whole_call(kernel, shapes, *operands, flops=0):
    return pl.pallas_call(
        kernel,
        in_specs=[WHOLE] * len(operands),
        out_specs=[WHOLE] * len(shapes),
        out_shape=shapes,
        compiler_params=PARAMS,
        cost_estimate=pl.CostEstimate(flops=flops, bytes_accessed=0, transcendentals=0),
    )(*operands)


def own_type_map(mode_shapes, mode_values, mode_weights, traces):
    modes, order = mode_weights.shape[1:]
    (own,) = whole_call(
        pack_kernel,
        [jax.ShapeDtypeStruct((2 * modes, order), F32)],
        mode_shapes[0].T,
        mode_values,
        mode_weights[0],
    )
    far = swap(own, "col", 4)
    pair = jnp.concatenate([own, swap(own, "col", 1)], axis=0)
    pair, traces = lax.optimization_barrier((pair, traces))
    got = [swap(pair, "col", 8, 10), swap(pair, "col", 2, 14), swap(pair, "col", 6, 12)]
    x = traces.reshape(order, -1)
    *got, x = lax.optimization_barrier((*got, x))
    (partial,) = whole_call(
        functools.partial(partial_kernel, modes),
        [jax.ShapeDtypeStruct((order, order), F32)],
        own,
        far,
        *got,
    )
    return (partial + swap(partial, "col", 1)).astype(BF), x


MAP_STEPS = ((0, 0), (1, 3), (2, 7), (6, 5), (3, 1), (7, 2), (5, 6), (4, 4))


def patch(block, rows, width, east_lane, port_ref, profile_ref, halo_refs):
    north, south, west, east = halo_refs
    quarter = block.shape[0] // 4
    port = pl.program_id(0)
    lane = lax.broadcasted_iota(jnp.int32, (quarter, LANES), 1)
    mine, count = lax.axis_index("row"), lax.axis_size("row")
    mine_col, count_col = lax.axis_index("col"), lax.axis_size("col")
    zero = jnp.zeros((), BF)
    block[0:quarter, 0:LANES] = jnp.where(mine > 0, north[...], zero)
    block[quarter : 2 * quarter, (rows - 1) * LANES : rows * LANES] = jnp.where(
        mine < count - 1, south[...], zero
    )
    west_all = jnp.where(mine_col > 0, west[...].astype(F32), 0.0)
    east_all = jnp.where(mine_col < count_col - 1, east[...].astype(F32), 0.0)
    for row in range(rows):
        place = port * rows + row
        cols = slice(row * LANES, (row + 1) * LANES)
        from_west = pltpu.roll(west_all, lax.rem(2 * LANES - east_lane - place, LANES), 1)
        from_east = pltpu.roll(east_all, LANES - 1 - place, 1)
        west_part = block[2 * quarter : 3 * quarter, cols].astype(F32)
        east_part = block[3 * quarter : 4 * quarter, cols].astype(F32)
        block[2 * quarter : 3 * quarter, cols] = jnp.where(lane == 0, from_west, west_part).astype(BF)
        block[3 * quarter : 4 * quarter, cols] = jnp.where(
            lane == LANES - 1, from_east, east_part
        ).astype(BF)
    cell = port_ref[port]
    row = cell // (width * count_col) - mine * rows
    col = cell % (width * count_col) - mine_col * width

    @pl.when((row >= 0) & (row < rows) & (col >= 0) & (col < width))
    def _():
        cols = pl.ds(pl.multiple_of(row * LANES, LANES), LANES)
        here = lax.broadcasted_iota(jnp.int32, (4 * quarter, LANES), 1) == col
        current = block[:, cols].astype(F32)
        added = current + profile_ref[0].astype(F32)
        block[:, cols] = jnp.where(here, added, current).astype(BF)


def map_rows(map_refs, first, last):
    if len(map_refs) == 1:
        return map_refs[0][first:last, :]
    core = lax.rem(lax.axis_index("col"), 2)
    swapped, own = map_refs[0][...], map_refs[1][...]
    low, high = jnp.where(core == 0, own, swapped), jnp.where(core == 0, swapped, own)
    return jnp.concatenate([low, high], axis=0)[first:last]


def products(x, types, maps, first, last, total=None):
    mine = lax.axis_index("row")
    core = lax.rem(lax.axis_index("col"), 2)
    types = jnp.broadcast_to(types, x.shape)
    for (even, odd), map_refs in maps:
        kind = (mine ^ jnp.where(core == 0, even, odd)).astype(F32).astype(BF)
        masked = jnp.where(types == kind, x, jnp.zeros((), BF))
        part = map_rows(map_refs, first, last)
        product = jnp.dot(part, masked, preferred_element_type=F32)
        total = product if total is None else total + product
    return total


def with_steps(map_refs, first, last):
    refs = [(ref,) for ref in map_refs]
    if last == len(MAP_STEPS):
        refs[-2:] = [refs[-2] + refs[-1]]
    return list(zip(MAP_STEPS[first:last], refs, strict=True))


def shifted(total, next_ref, rows):
    quarter = total.shape[0] // 4
    last = (rows - 1) * LANES
    north = total[0:quarter].astype(BF)
    south = total[quarter : 2 * quarter].astype(BF)
    next_ref[0:quarter, LANES:] = south[:, :last]
    next_ref[0:quarter, 0:LANES] = jnp.zeros((quarter, LANES), BF)
    next_ref[quarter : 2 * quarter, :last] = north[:, LANES:]
    next_ref[quarter : 2 * quarter, last:] = jnp.zeros((quarter, LANES), BF)
    for row in range(rows):
        cols = slice(row * LANES, (row + 1) * LANES)
        west = total[2 * quarter : 3 * quarter, cols]
        east = total[3 * quarter : 4 * quarter, cols]
        next_ref[2 * quarter : 3 * quarter, cols] = pltpu.roll(east, 1, 1).astype(BF)
        next_ref[3 * quarter : 4 * quarter, cols] = pltpu.roll(west, LANES - 1, 1).astype(BF)
    return north, south


def rim_columns(x_ref, types, ports, offset):
    tile = types.shape[1]
    starts = [port * tile + offset for port in range(ports)]
    cells = jnp.concatenate([x_ref[:, start : start + LANES] for start in starts], axis=1)
    return cells, jnp.concatenate([types[:, offset : offset + LANES]] * ports, axis=1).astype(BF)


def side_columns(x_ref, types, ports):
    order, tile = x_ref.shape[0], types.shape[1]
    wide = 2 * LANES
    spread = jnp.broadcast_to(types, (16, tile)).astype(BF)
    place = lax.broadcasted_iota(jnp.int32, (wide, LANES), 0)
    lane = lax.broadcasted_iota(jnp.int32, (wide, LANES), 1)
    wanted = jnp.where(lane < 64, lane * LANES, (lane - 64) * LANES + LANES - 1)
    picked = None
    for start in range(0, ports * tile, wide):
        pick = jnp.where(place + start == wanted, 1.0, 0.0).astype(BF)
        inside = start % tile
        both = jnp.concatenate(
            [x_ref[:, start : start + wide], spread[:, inside : inside + wide]], axis=0
        )
        part = jnp.dot(both, pick, preferred_element_type=F32)
        picked = part if picked is None else picked + part
    return picked[0:order].astype(BF), picked[order:].astype(BF)


def rims(x_ref, types, ports, sides, kinds, maps, so_far):
    order, tile = x_ref.shape[0], types.shape[1]
    quarter = order // 4
    before = [None if ref is None else ref[...].astype(F32) for ref in so_far]
    cells, cell_kinds = rim_columns(x_ref, types, ports, 0)
    north = products(cells, cell_kinds, maps, 0, quarter, before[0])
    cells, cell_kinds = rim_columns(x_ref, types, ports, tile - LANES)
    south = products(cells, cell_kinds, maps, quarter, 2 * quarter, before[1])
    side = products(sides, kinds, maps, 2 * quarter, order, before[2])
    return north.astype(BF), south.astype(BF), side.astype(BF)


def early_kernel(ports, first, last, x_ref, types_ref, *refs):
    maps = with_steps(refs[: last - first], first, last)
    refs = refs[last - first :]
    types = types_ref[...].astype(F32)
    tile = types.shape[1]
    if first == 0:
        done_ref, so_far = None, [None] * 3
        sides, kinds = side_columns(x_ref, types, ports)
        refs[4][...] = sides
        refs[5][...] = kinds
    else:
        done_ref, so_far = refs[0], refs[1:4]
        sides, kinds = refs[4][...], refs[5][...]
        refs = refs[6:]
    outs = rims(x_ref, types, ports, sides, kinds[0:1], maps, so_far)
    for ref, value in zip(refs[1:4], outs):
        ref[...] = value
    for port in range(ports):
        cols = slice(port * tile, (port + 1) * tile)
        before = None if done_ref is None else done_ref[:, cols].astype(F32)
        total = products(x_ref[:, cols], types.astype(BF), maps, 0, x_ref.shape[0], before)
        refs[0][:, cols] = total.astype(BF)


def rim_kernel(ports, first, x_ref, types_ref, *refs):
    maps = with_steps(refs[:-9], first, len(MAP_STEPS))
    so_far, (sides, kinds) = refs[-9:-6], refs[-6:-4]
    outs = rims(
        x_ref, types_ref[...].astype(F32), ports, sides[...], kinds[0:1, :], maps, so_far
    )
    quarter = x_ref.shape[0] // 4
    refs[-4][...] = outs[0]
    refs[-3][...] = outs[1]
    refs[-2][...] = outs[2][0:quarter]
    refs[-1][...] = outs[2][quarter:]


def first_kernel(rows, first, x_ref, types_ref, done_ref, *refs):
    maps = with_steps(refs[:-1], first, len(MAP_STEPS))
    types = types_ref[...].astype(F32).astype(BF)
    before = done_ref[...].astype(F32)
    total = products(x_ref[...], types, maps, 0, x_ref.shape[0], before)
    shifted(total, refs[-1], rows)


def second_kernel(rows, width, port_ref, x_ref, types_ref, profile_ref, *refs):
    halo_refs, map_refs, next_ref = refs[:4], refs[4:-6], refs[-6]
    north_out, south_out, west_out, east_out, block = refs[-5:]
    block[...] = x_ref[...]
    patch(block, rows, width, 64, port_ref, profile_ref, halo_refs)
    order = block.shape[0]
    quarter = order // 4
    types = types_ref[...].astype(F32).astype(BF)
    maps = with_steps(map_refs, 0, len(MAP_STEPS))
    total = products(block[...], types, maps, 0, order)
    north, south = shifted(total, next_ref, rows)
    north_out[...] = north[:, 0:LANES]
    south_out[...] = south[:, (rows - 1) * LANES :]
    port = pl.program_id(0)
    lane = lax.broadcasted_iota(jnp.int32, (quarter, LANES), 1)
    west_rim = jnp.where(port == 0, 0.0, west_out[...].astype(F32))
    east_rim = jnp.where(port == 0, 0.0, east_out[...].astype(F32))
    for row in range(rows):
        place = port * rows + row
        cols = slice(row * LANES, (row + 1) * LANES)
        west = total[2 * quarter : 3 * quarter, cols]
        east = total[3 * quarter : 4 * quarter, cols]
        west_rim = jnp.where(lane == place, pltpu.roll(west, place, 1), west_rim)
        east_rim = jnp.where(lane == place, pltpu.roll(east, place + 1, 1), east_rim)
    west_out[...] = west_rim.astype(BF)
    east_out[...] = east_rim.astype(BF)


def last_kernel(rows, width, port_ref, x_ref, profile_ref, *refs):
    out_ref, block = refs[-2:]
    block[...] = x_ref[...]
    patch(block, rows, width, 0, port_ref, profile_ref, refs[:4])
    out_ref[...] = block[...].astype(F32).reshape(out_ref.shape).astype(BF)


def exchange(rims):
    north, south, west, east = rims

    def send(value, axis, step):
        count = lax.axis_size(axis)
        return lax.ppermute(value, axis, [(i, (i + step) % count) for i in range(count)])

    return (
        send(south, "row", 1),
        send(north, "row", -1),
        send(east, "col", 1),
        send(west, "col", -1),
    )


def body(traces, cell_type, port_cell, port_profile, mode_shapes, mode_values, mode_weights):
    edges, samples, ports, rows, width = traces.shape
    order = edges * samples
    quarter = samples
    tile = rows * width
    own_map, x = own_type_map(mode_shapes, mode_values, mode_weights, traces)
    core = lax.rem(lax.axis_index("col"), 2)
    half = lax.dynamic_slice_in_dim(own_map, core * (order // 2), order // 2)
    fetched = [swap(own_map, "row", *steps) for steps in MAP_STEPS[1:4]]
    half = swap(half, "row", 4)
    swapped = [swap(fetched[0], "col", 1)]
    types = cell_type.reshape(1, tile)
    profile = jnp.broadcast_to(
        jnp.transpose(port_profile.reshape(order, ports))[:, :, None], (ports, order, LANES)
    )
    block = pl.BlockSpec((order, tile), lambda i: (0, i))
    types_spec = pl.BlockSpec((1, tile), lambda i: (0, 0))
    long_rim = pl.BlockSpec((quarter, LANES), lambda i: (0, i))
    short_rim = pl.BlockSpec((quarter, LANES), lambda i: (0, 0))
    rims = [long_rim, long_rim, short_rim, short_rim]
    ports_spec = pl.BlockSpec(memory_space=pltpu.SMEM)
    profile_spec = pl.BlockSpec((1, order, LANES), lambda i: (i, 0, 0))
    next_shape = jax.ShapeDtypeStruct((order, ports * tile), BF)
    rim_shapes = [jax.ShapeDtypeStruct((quarter, ports * LANES), BF)] * 2 + [
        jax.ShapeDtypeStruct((quarter, LANES), BF)
    ] * 2
    work = 2 * order * order * len(MAP_STEPS) * ports * tile
    early = (0, 2, 4)
    side_shapes = [
        jax.ShapeDtypeStruct((order, LANES), BF),
        jax.ShapeDtypeStruct((16, LANES), BF),
    ]
    part_shapes = [next_shape] + rim_shapes[:2] + [jax.ShapeDtypeStruct((2 * quarter, LANES), BF)]
    *parts, sides, kinds = whole_call(
        functools.partial(early_kernel, ports, early[0], early[1]),
        part_shapes + side_shapes,
        x,
        types,
        own_map,
        fetched[0],
        flops=work // 3,
    )
    parts, rest, half = lax.optimization_barrier((parts, fetched[1:], half))
    swapped += [swap(value, "col", 1) for value in rest + [half]]
    parts = whole_call(
        functools.partial(early_kernel, ports, early[1], early[2]),
        part_shapes,
        x,
        types,
        *rest,
        *parts,
        sides,
        kinds,
        flops=work // 3,
    )
    done, *parts = parts
    late = swapped + [half]
    maps = [own_map, fetched[0]] + rest + late
    map_specs = [pl.BlockSpec(value.shape, lambda i: (0, 0)) for value in maps]
    sent = whole_call(
        functools.partial(rim_kernel, ports, early[2]),
        rim_shapes,
        x,
        types,
        *late,
        *parts,
        sides,
        kinds,
        flops=work // 8,
    )
    halos = exchange(sent)
    x = pl.pallas_call(
        functools.partial(first_kernel, rows, early[2]),
        grid=(ports,),
        in_specs=[block, types_spec, block] + map_specs[early[2] :],
        out_specs=block,
        out_shape=next_shape,
        compiler_params=PARAMS,
        cost_estimate=pl.CostEstimate(flops=work // 2, bytes_accessed=0, transcendentals=0),
    )(x, types, done, *late)
    x, *sent = pl.pallas_call(
        functools.partial(second_kernel, rows, width),
        grid=(ports,),
        in_specs=[ports_spec, block, types_spec, profile_spec] + rims + map_specs,
        out_specs=[block] + rims,
        out_shape=[next_shape] + rim_shapes,
        scratch_shapes=[pltpu.VMEM((order, tile), BF)],
        compiler_params=PARAMS,
        cost_estimate=pl.CostEstimate(flops=work, bytes_accessed=0, transcendentals=0),
    )(port_cell, x, types, profile, *halos, *maps)
    halos = exchange(sent)
    out = pl.pallas_call(
        functools.partial(last_kernel, rows, width),
        grid=(ports,),
        in_specs=[ports_spec, block, profile_spec] + rims,
        out_specs=pl.BlockSpec((order, 1, rows, LANES), lambda i: (0, i, 0, 0)),
        out_shape=jax.ShapeDtypeStruct((order, ports, rows, width), BF),
        scratch_shapes=[pltpu.VMEM((order, tile), BF)],
        compiler_params=PARAMS,
    )(port_cell, x, profile, *halos)
    return out.reshape(traces.shape)


def solution(mesh):
    return jax.shard_map(
        body,
        mesh=mesh,
        in_specs=(
            P(None, None, None, "row", "col"),
            P("row", "col"),
            P(),
            P(),
            P("row", None, "col"),
            P("row", "col"),
            P("row", "col", None),
        ),
        out_specs=P(None, None, None, "row", "col"),
        check_vma=False,
    )
```

```python
import functools
import math

import jax
import jax.numpy as jnp
from jax import lax
from jax.experimental import pallas as pl
from jax.experimental.pallas import tpu as pltpu
from jax.sharding import PartitionSpec as P

BF = jnp.bfloat16
F32 = jnp.float32
LANES = 128
PARAMS = pltpu.CompilerParams(vmem_limit_bytes=20 * 2**20)
WIDE_PARAMS = pltpu.CompilerParams(vmem_limit_bytes=50 * 2**20)


def swap(value, axis, first, second=None):
    second = first if second is None else second
    rows, cols = lax.axis_size("row"), lax.axis_size("col")
    pairs = []
    for row in range(rows):
        for col in range(cols):
            step = second if col % 2 else first
            other = (row ^ step, col) if axis == "row" else (row, col ^ step)
            pairs.append((row * cols + col, other[0] * cols + other[1]))
    return lax.ppermute(value, ("row", "col"), pairs)


def flat_kernel(x_hbm, out_ref, x_ref, sems):
    order, ports, rows, width = x_ref.shape
    quarter, tile = order // 4, rows * width
    edges = [slice(edge * quarter, (edge + 1) * quarter) for edge in range(4)]
    copies = [
        pltpu.make_async_copy(x_hbm.at[lines], x_ref.at[lines], sems.at[edge])
        for edge, lines in enumerate(edges)
    ]
    for copy in copies:
        copy.start()
    for copy, lines in zip(copies, edges):
        copy.wait()
        for port in range(ports):
            value = x_ref[lines, port].astype(F32).reshape(quarter, tile)
            out_ref[lines, port * tile : (port + 1) * tile] = value.astype(BF)


def partial_kernel(modes, *refs):
    left, right = [], []
    for ref in refs[:-1]:
        for start in range(0, ref.shape[0], 2 * modes):
            left.append(ref[start : start + modes])
            right.append(ref[start + modes : start + 2 * modes])
    refs[-1][...] = lax.dot_general(
        jnp.concatenate(left, axis=0),
        jnp.concatenate(right, axis=0),
        (((0,), (0,)), ((), ())),
        precision=lax.Precision.HIGHEST,
        preferred_element_type=F32,
    )


WHOLE = pl.BlockSpec(memory_space=pltpu.VMEM)


def whole_call(kernel, shapes, *operands, flops=0):
    return pl.pallas_call(
        kernel,
        in_specs=[WHOLE] * len(operands),
        out_specs=[WHOLE] * len(shapes),
        out_shape=shapes,
        compiler_params=PARAMS,
        cost_estimate=pl.CostEstimate(flops=flops, bytes_accessed=0, transcendentals=0),
    )(*operands)


def own_type_map(mode_shapes, mode_values, mode_weights, traces):
    modes, order = mode_weights.shape[1:]
    own = jnp.concatenate([mode_shapes[0].T, mode_weights[0]], axis=0)
    own = own * jnp.concatenate([mode_values[0], jnp.ones((modes,), F32)])[:, None]
    far = swap(own, "col", 4)
    pair = jnp.concatenate([own, swap(own, "col", 1)], axis=0)
    pair, traces = lax.optimization_barrier((pair, traces))
    got = [swap(pair, "col", 8, 10), swap(pair, "col", 2, 14), swap(pair, "col", 6, 12)]
    shape = (order,) + traces.shape[2:]
    x = pl.pallas_call(
        flat_kernel,
        in_specs=[pl.BlockSpec(memory_space=pltpu.HBM)],
        out_specs=WHOLE,
        out_shape=jax.ShapeDtypeStruct((order, math.prod(shape[1:])), BF),
        scratch_shapes=[pltpu.VMEM(shape, BF), pltpu.SemaphoreType.DMA((4,))],
        compiler_params=WIDE_PARAMS,
        cost_estimate=pl.CostEstimate(flops=2**30, bytes_accessed=0, transcendentals=0),
    )(traces.reshape(shape))
    *got, x = lax.optimization_barrier((*got, x))
    (partial,) = whole_call(
        functools.partial(partial_kernel, modes),
        [jax.ShapeDtypeStruct((order, order), F32)],
        own,
        far,
        *got,
    )
    return (partial + swap(partial, "col", 1)).astype(BF), x


MAP_STEPS = ((0, 0), (1, 3), (2, 7), (6, 5), (3, 1), (7, 2), (5, 6), (4, 4))


def halos_inside(halo_refs):
    north, south, west, east = (ref[...].astype(F32) for ref in halo_refs)
    row, rows = lax.axis_index("row"), lax.axis_size("row")
    col, cols = lax.axis_index("col"), lax.axis_size("col")
    return (
        jnp.where(row > 0, north, 0.0),
        jnp.where(row < rows - 1, south, 0.0),
        jnp.where(col > 0, west, 0.0),
        jnp.where(col < cols - 1, east, 0.0),
    )


def lane_of(value, lane):
    return jnp.broadcast_to(value[:, lane : lane + 1], (value.shape[0], LANES))


def port_place(port_ref, port, rows, width):
    all_cols = width * lax.axis_size("col")
    cell = port_ref[port]
    row = cell // all_cols - lax.axis_index("row") * rows
    col = cell % all_cols - lax.axis_index("col") * width
    return row, col, (row >= 0) & (row < rows) & (col >= 0) & (col < width)


def map_rows(map_refs, first, last):
    if len(map_refs) == 1:
        return map_refs[0][first:last, :]
    core = lax.rem(lax.axis_index("col"), 2)
    swapped, own = map_refs[0][...], map_refs[1][...]
    low, high = jnp.where(core == 0, own, swapped), jnp.where(core == 0, swapped, own)
    return jnp.concatenate([low, high], axis=0)[first:last]


def products(x, types, maps, first, last, total=None):
    mine = lax.axis_index("row")
    core = lax.rem(lax.axis_index("col"), 2)
    types = jnp.broadcast_to(types, x.shape)
    for (even, odd), map_refs in maps:
        kind = (mine ^ jnp.where(core == 0, even, odd)).astype(F32).astype(BF)
        masked = jnp.where(types == kind, x, jnp.zeros((), BF))
        part = map_rows(map_refs, first, last)
        product = jnp.dot(part, masked, preferred_element_type=F32)
        total = product if total is None else total + product
    return total


def with_steps(map_refs, first, last):
    refs = [(ref,) for ref in map_refs]
    if last == len(MAP_STEPS):
        refs[-2:] = [refs[-2] + refs[-1]]
    return list(zip(MAP_STEPS[first:last], refs, strict=True))


def shifted(total, next_ref, rows):
    quarter = total.shape[0] // 4
    last = (rows - 1) * LANES
    north = total[0:quarter].astype(BF)
    south = total[quarter : 2 * quarter].astype(BF)
    next_ref[0:quarter, LANES:] = south[:, :last]
    next_ref[0:quarter, 0:LANES] = jnp.zeros((quarter, LANES), BF)
    next_ref[quarter : 2 * quarter, :last] = north[:, LANES:]
    next_ref[quarter : 2 * quarter, last:] = jnp.zeros((quarter, LANES), BF)
    for row in range(rows):
        cols = slice(row * LANES, (row + 1) * LANES)
        west = total[2 * quarter : 3 * quarter, cols]
        east = total[3 * quarter : 4 * quarter, cols]
        next_ref[2 * quarter : 3 * quarter, cols] = pltpu.roll(east, 1, 1).astype(BF)
        next_ref[3 * quarter : 4 * quarter, cols] = pltpu.roll(west, LANES - 1, 1).astype(BF)
    return north, south


def rim_columns(x_ref, types, ports, offset):
    tile = types.shape[1]
    starts = [port * tile + offset for port in range(ports)]
    cells = jnp.concatenate([x_ref[:, start : start + LANES] for start in starts], axis=1)
    return cells, jnp.concatenate([types[:, offset : offset + LANES]] * ports, axis=1).astype(BF)


def side_columns(x_ref, types, ports):
    order, tile = x_ref.shape[0], types.shape[1]
    rows = tile // LANES

    def pick(block_of, lines):
        lane = lax.broadcasted_iota(jnp.int32, (lines, LANES), 1)
        first = last = jnp.zeros((lines, LANES), F32)
        for place in range(ports * rows):
            turned = pltpu.roll(block_of(place), place + 1, 1)
            first = jnp.where(lane == place + 1, turned, first)
            last = jnp.where(lane == place, turned, last)
        first = pltpu.roll(first, LANES - 1, 1)
        return jnp.where(lane < 64, first, pltpu.roll(last, 64, 1)).astype(BF)

    def types_of(place):
        start = place % rows * LANES
        return jnp.broadcast_to(types[:, start : start + LANES], (16, LANES))

    quarter = order // 4
    sides = [
        pick(
            lambda place: x_ref[edge * quarter : (edge + 1) * quarter,
                                place * LANES : (place + 1) * LANES].astype(F32),
            quarter,
        )
        for edge in range(4)
    ]
    return jnp.concatenate(sides, axis=0), pick(types_of, 16)


def rims(x_ref, types, ports, sides, kinds, maps, so_far):
    order, tile = x_ref.shape[0], types.shape[1]
    quarter = order // 4
    before = [None if ref is None else ref[...].astype(F32) for ref in so_far]
    cells, cell_kinds = rim_columns(x_ref, types, ports, 0)
    north = products(cells, cell_kinds, maps, 0, quarter, before[0])
    cells, cell_kinds = rim_columns(x_ref, types, ports, tile - LANES)
    south = products(cells, cell_kinds, maps, quarter, 2 * quarter, before[1])
    side = products(sides, kinds, maps, 2 * quarter, order, before[2])
    return north.astype(BF), south.astype(BF), side.astype(BF)


def early_kernel(ports, first, last, x_ref, types_ref, *refs):
    maps = with_steps(refs[: last - first], first, last)
    refs = refs[last - first :]
    types = types_ref[...].astype(F32)
    tile = types.shape[1]
    if first == 0:
        done_ref, so_far = None, [None] * 3
        sides, kinds = side_columns(x_ref, types, ports)
        refs[4][...] = sides
        refs[5][...] = kinds
    else:
        done_ref, so_far = refs[0], refs[1:4]
        sides, kinds = refs[4][...], refs[5][...]
        refs = refs[6:]
    outs = rims(x_ref, types, ports, sides, kinds[0:1], maps, so_far)
    for ref, value in zip(refs[1:4], outs):
        ref[...] = value
    for port in range(ports):
        cols = slice(port * tile, (port + 1) * tile)
        before = None if done_ref is None else done_ref[:, cols].astype(F32)
        total = products(x_ref[:, cols], types.astype(BF), maps, 0, x_ref.shape[0], before)
        refs[0][:, cols] = total.astype(BF)


def rim_kernel(ports, first, x_ref, types_ref, *refs):
    maps = with_steps(refs[:-9], first, len(MAP_STEPS))
    so_far, (sides, kinds) = refs[-9:-6], refs[-6:-4]
    outs = rims(
        x_ref, types_ref[...].astype(F32), ports, sides[...], kinds[0:1, :], maps, so_far
    )
    quarter = x_ref.shape[0] // 4
    refs[-4][...] = outs[0]
    refs[-3][...] = outs[1]
    refs[-2][...] = outs[2][0:quarter]
    refs[-1][...] = outs[2][quarter:]


def first_kernel(rows, ports, first, x_ref, types_ref, done_ref, *refs):
    maps = with_steps(refs[:-1], first, len(MAP_STEPS))
    types = types_ref[...].astype(F32).astype(BF)
    tile = types.shape[1]
    for port in range(ports):
        cols = slice(port * tile, (port + 1) * tile)
        before = done_ref[:, cols].astype(F32)
        total = products(x_ref[:, cols], types, maps, 0, x_ref.shape[0], before)
        shifted(total, refs[-1].at[:, cols], rows)


def second_kernel(rows, width, port_ref, x_ref, types_ref, profile_ref, *refs):
    halo_refs, map_refs, next_ref = refs[:4], refs[4:-6], refs[-6]
    north_out, south_out, west_out, east_out, blocks = refs[-5:]
    types = types_ref[...].astype(F32).astype(BF)
    tile = types.shape[1]
    order = x_ref.shape[0]
    quarter = order // 4
    maps = with_steps(map_refs, 0, len(MAP_STEPS))
    north_in, south_in, west_in, east_in = halos_inside(halo_refs)
    lane = lax.broadcasted_iota(jnp.int32, (quarter, LANES), 1)
    west_rim = east_rim = jnp.zeros((quarter, LANES), F32)
    for port in range(x_ref.shape[1] // tile):
        own = slice(port * tile, (port + 1) * tile)
        rim = slice(port * LANES, (port + 1) * LANES)
        block = blocks.at[port % 2]
        block[...] = x_ref[:, own]
        block[0:quarter, 0:LANES] = north_in[:, rim].astype(BF)
        block[quarter : 2 * quarter, tile - LANES :] = south_in[:, rim].astype(BF)
        for row in range(rows):
            place = port * rows + row
            cols = slice(row * LANES, (row + 1) * LANES)
            west = block[2 * quarter : 3 * quarter, cols].astype(F32)
            east = block[3 * quarter :, cols].astype(F32)
            west = jnp.where(lane == 0, lane_of(west_in, 64 + place), west)
            east = jnp.where(lane == LANES - 1, lane_of(east_in, place), east)
            block[2 * quarter : 3 * quarter, cols] = west.astype(BF)
            block[3 * quarter :, cols] = east.astype(BF)
        row, col, inside = port_place(port_ref, port, rows, width)

        @pl.when(inside)
        def _():
            cols = pl.ds(pl.multiple_of(row * LANES, LANES), LANES)
            here = lax.broadcasted_iota(jnp.int32, (order, LANES), 1) == col
            current = block[:, cols].astype(F32)
            added = current + profile_ref[port].astype(F32)
            block[:, cols] = jnp.where(here, added, current).astype(BF)

        total = products(block[...], types, maps, 0, order)
        north, south = shifted(total, next_ref.at[:, own], rows)
        north_out[:, rim] = north[:, 0:LANES]
        south_out[:, rim] = south[:, tile - LANES :]
        for row in range(rows):
            place = port * rows + row
            west = lane_of(total[2 * quarter : 3 * quarter], row * LANES)
            east = lane_of(total[3 * quarter :], (row + 1) * LANES - 1)
            west_rim = jnp.where(lane == place, west, west_rim)
            east_rim = jnp.where(lane == place, east, east_rim)
    west_out[...] = west_rim.astype(BF)
    east_out[...] = east_rim.astype(BF)


def last_kernel(rows, width, port_ref, x_ref, profile_ref, *refs):
    out_ref, buffer, sems = refs[4:]
    order, ports = buffer.shape[:2]
    quarter, tile = order // 4, rows * width
    north_in, south_in, west_in, east_in = halos_inside(refs[:4])
    lane = lax.broadcasted_iota(jnp.int32, (quarter, LANES), 1)
    copies = []
    for edge in (2, 3, 0, 1):
        lines = slice(edge * quarter, (edge + 1) * quarter)
        for port in range(ports):
            rim = slice(port * LANES, (port + 1) * LANES)
            starts = [port * tile + row * LANES for row in range(rows)]
            parts = [x_ref[lines, start : start + LANES].astype(F32) for start in starts]
            places = range(port * rows, (port + 1) * rows)
            if edge == 0:
                parts[0] = north_in[:, rim]
            elif edge == 1:
                parts[-1] = south_in[:, rim]
            elif edge == 2:
                parts = [
                    jnp.where(lane == 0, lane_of(west_in, place), part)
                    for place, part in zip(places, parts)
                ]
            else:
                parts = [
                    jnp.where(lane == LANES - 1, lane_of(east_in, place), part)
                    for place, part in zip(places, parts)
                ]
            value = jnp.concatenate(parts, axis=1).reshape(quarter, rows, LANES)
            buffer[lines, port] = value.astype(BF)
        for port in range(ports):
            row, col, inside = port_place(port_ref, port, rows, width)

            @pl.when(inside)
            def _():
                current = buffer[lines, port].astype(F32)
                here = (lax.broadcasted_iota(jnp.int32, current.shape, 1) == row) & (
                    lax.broadcasted_iota(jnp.int32, current.shape, 2) == col
                )
                profile = profile_ref[port, lines, :].astype(F32).reshape(quarter, 1, LANES)
                added = current + jnp.broadcast_to(profile, current.shape)
                buffer[lines, port] = jnp.where(here, added, current).astype(BF)

        copy = pltpu.make_async_copy(buffer.at[lines], out_ref.at[lines], sems.at[edge])
        copy.start()
        copies.append(copy)
    for copy in copies:
        copy.wait()


def exchange(rims):
    north, south, west, east = rims

    def send(value, axis, step):
        count = lax.axis_size(axis)
        return lax.ppermute(value, axis, [(i, (i + step) % count) for i in range(count)])

    return (
        send(south, "row", 1),
        send(north, "row", -1),
        send(east, "col", 1),
        send(west, "col", -1),
    )


def body(traces, cell_type, port_cell, port_profile, mode_shapes, mode_values, mode_weights):
    edges, samples, ports, rows, width = traces.shape
    order = edges * samples
    quarter = samples
    tile = rows * width
    own_map, x = own_type_map(mode_shapes, mode_values, mode_weights, traces)
    core = lax.rem(lax.axis_index("col"), 2)
    half = lax.dynamic_slice_in_dim(own_map, core * (order // 2), order // 2)
    fetched = [swap(own_map, "row", *steps) for steps in MAP_STEPS[1:4]]
    half = swap(half, "row", 4)
    swapped = [swap(fetched[0], "col", 1)]
    types = cell_type.reshape(1, tile)
    profile = jnp.broadcast_to(
        jnp.transpose(port_profile.reshape(order, ports))[:, :, None], (ports, order, LANES)
    )
    ports_spec = pl.BlockSpec(memory_space=pltpu.SMEM)
    next_shape = jax.ShapeDtypeStruct((order, ports * tile), BF)
    rim_shapes = [jax.ShapeDtypeStruct((quarter, ports * LANES), BF)] * 2 + [
        jax.ShapeDtypeStruct((quarter, LANES), BF)
    ] * 2
    work = 2 * order * order * len(MAP_STEPS) * ports * tile
    early = (0, 2, 4)
    side_shapes = [
        jax.ShapeDtypeStruct((order, LANES), BF),
        jax.ShapeDtypeStruct((16, LANES), BF),
    ]
    part_shapes = [next_shape] + rim_shapes[:2] + [jax.ShapeDtypeStruct((2 * quarter, LANES), BF)]
    *parts, sides, kinds = whole_call(
        functools.partial(early_kernel, ports, early[0], early[1]),
        part_shapes + side_shapes,
        x,
        types,
        own_map,
        fetched[0],
        flops=work // 3,
    )
    parts, rest, half = lax.optimization_barrier((parts, fetched[1:], half))
    swapped += [swap(value, "col", 1) for value in rest + [half]]
    parts = whole_call(
        functools.partial(early_kernel, ports, early[1], early[2]),
        part_shapes,
        x,
        types,
        *rest,
        *parts,
        sides,
        kinds,
        flops=work // 3,
    )
    done, *parts = parts
    late = swapped + [half]
    maps = [own_map, fetched[0]] + rest + late
    sent = whole_call(
        functools.partial(rim_kernel, ports, early[2]),
        rim_shapes,
        x,
        types,
        *late,
        *parts,
        sides,
        kinds,
        flops=work // 8,
    )
    halos = exchange(sent)
    (x,) = whole_call(
        functools.partial(first_kernel, rows, ports, early[2]),
        [next_shape],
        x,
        types,
        done,
        *late,
        flops=work // 2,
    )
    operands = [port_cell, x, types, profile, *halos, *maps]
    x, *sent = pl.pallas_call(
        functools.partial(second_kernel, rows, width),
        in_specs=[ports_spec] + [WHOLE] * (len(operands) - 1),
        out_specs=[WHOLE] * 5,
        out_shape=[next_shape] + rim_shapes,
        scratch_shapes=[pltpu.VMEM((2, order, tile), BF)],
        compiler_params=PARAMS,
        cost_estimate=pl.CostEstimate(flops=work, bytes_accessed=0, transcendentals=0),
    )(*operands)
    operands = [port_cell, x, profile, *exchange(sent)]
    out = pl.pallas_call(
        functools.partial(last_kernel, rows, width),
        in_specs=[ports_spec] + [WHOLE] * (len(operands) - 1),
        out_specs=pl.BlockSpec(memory_space=pl.ANY),
        out_shape=jax.ShapeDtypeStruct((order, ports, rows, width), BF),
        scratch_shapes=[
            pltpu.VMEM((order, ports, rows, width), BF),
            pltpu.SemaphoreType.DMA((4,)),
        ],
        compiler_params=PARAMS,
    )(*operands)
    return out.reshape(traces.shape)


def solution(mesh):
    return jax.shard_map(
        body,
        mesh=mesh,
        in_specs=(
            P(None, None, None, "row", "col"),
            P("row", "col"),
            P(),
            P(),
            P("row", None, "col"),
            P("row", "col"),
            P("row", "col", None),
        ),
        out_specs=P(None, None, None, "row", "col"),
        check_vma=False,
    )
```

```python
import functools
import math

import jax
import jax.numpy as jnp
from jax import lax
from jax.experimental import pallas as pl
from jax.experimental.pallas import tpu as pltpu
from jax.sharding import PartitionSpec as P

BF = jnp.bfloat16
F32 = jnp.float32
LANES = 128
PARAMS = pltpu.CompilerParams(vmem_limit_bytes=20 * 2**20)
WIDE_PARAMS = pltpu.CompilerParams(vmem_limit_bytes=50 * 2**20)


def swap(value, axis, first, second=None):
    second = first if second is None else second
    rows, cols = lax.axis_size("row"), lax.axis_size("col")
    pairs = []
    for row in range(rows):
        for col in range(cols):
            step = second if col % 2 else first
            other = (row ^ step, col) if axis == "row" else (row, col ^ step)
            pairs.append((row * cols + col, other[0] * cols + other[1]))
    return lax.ppermute(value, ("row", "col"), pairs)


def flat_kernel(x_hbm, out_ref, x_ref, sems):
    order, ports, rows, width = x_ref.shape
    quarter, tile = order // 4, rows * width
    edges = [slice(edge * quarter, (edge + 1) * quarter) for edge in range(4)]
    copies = [
        pltpu.make_async_copy(x_hbm.at[lines], x_ref.at[lines], sems.at[edge])
        for edge, lines in enumerate(edges)
    ]
    for copy in copies:
        copy.start()
    for copy, lines in zip(copies, edges):
        copy.wait()
        for port in range(ports):
            value = x_ref[lines, port].astype(F32).reshape(quarter, tile)
            out_ref[lines, port * tile : (port + 1) * tile] = value.astype(BF)


def partial_kernel(modes, *refs):
    left, right = [], []
    for ref in refs[:-1]:
        for start in range(0, ref.shape[0], 2 * modes):
            left.append(ref[start : start + modes])
            right.append(ref[start + modes : start + 2 * modes])
    refs[-1][...] = lax.dot_general(
        jnp.concatenate(left, axis=0),
        jnp.concatenate(right, axis=0),
        (((0,), (0,)), ((), ())),
        precision=lax.Precision.HIGHEST,
        preferred_element_type=F32,
    )


WHOLE = pl.BlockSpec(memory_space=pltpu.VMEM)


def whole_call(kernel, shapes, *operands, flops=0):
    return pl.pallas_call(
        kernel,
        in_specs=[WHOLE] * len(operands),
        out_specs=[WHOLE] * len(shapes),
        out_shape=shapes,
        compiler_params=PARAMS,
        cost_estimate=pl.CostEstimate(flops=flops, bytes_accessed=0, transcendentals=0),
    )(*operands)


def own_type_map(mode_shapes, mode_values, mode_weights, traces):
    modes, order = mode_weights.shape[1:]
    own = jnp.concatenate([mode_shapes[0].T, mode_weights[0]], axis=0)
    values = jnp.broadcast_to(mode_values[0][None, :, None], (2, modes, order)).reshape(own.shape)
    line = lax.broadcasted_iota(jnp.int32, own.shape, 0)
    own = jnp.where(line < modes, own * values, own)
    far = swap(own, "col", 4)
    pair = jnp.concatenate([own, swap(own, "col", 1)], axis=0)
    pair, traces = lax.optimization_barrier((pair, traces))
    got = [swap(pair, "col", 8, 10), swap(pair, "col", 2, 14), swap(pair, "col", 6, 12)]
    shape = (order,) + traces.shape[2:]
    x = pl.pallas_call(
        flat_kernel,
        in_specs=[pl.BlockSpec(memory_space=pltpu.HBM)],
        out_specs=WHOLE,
        out_shape=jax.ShapeDtypeStruct((order, math.prod(shape[1:])), BF),
        scratch_shapes=[pltpu.VMEM(shape, BF), pltpu.SemaphoreType.DMA((4,))],
        compiler_params=WIDE_PARAMS,
        cost_estimate=pl.CostEstimate(flops=2**30, bytes_accessed=0, transcendentals=0),
    )(traces.reshape(shape))
    *got, x = lax.optimization_barrier((*got, x))
    (partial,) = whole_call(
        functools.partial(partial_kernel, modes),
        [jax.ShapeDtypeStruct((order, order), F32)],
        own,
        far,
        *got,
    )
    return (partial + swap(partial, "col", 1)).astype(BF), x


MAP_STEPS = ((0, 0), (1, 3), (2, 7), (6, 5), (3, 1), (7, 2), (5, 6), (4, 4))


def even(axis):
    return lax.rem(lax.axis_index(axis), 2) == 0


def halos_inside(halo_refs):
    row_one, row_two, col_one, col_two = (ref[...].astype(F32) for ref in halo_refs)
    row, rows = lax.axis_index("row"), lax.axis_size("row")
    col, cols = lax.axis_index("col"), lax.axis_size("col")
    north = jnp.where(even("row"), row_two, row_one)
    south = jnp.where(even("row"), row_one, row_two)
    west = jnp.where(even("col"), col_two, col_one)
    east = jnp.where(even("col"), col_one, col_two)
    return (
        jnp.where(row > 0, north, 0.0),
        jnp.where(row < rows - 1, south, 0.0),
        jnp.where(col > 0, west, 0.0),
        jnp.where(col < cols - 1, east, 0.0),
    )


def store_rims(out_refs, north, south, west, east):
    first, second, third, fourth = out_refs
    first[...] = jnp.where(even("row"), south, north).astype(BF)
    second[...] = jnp.where(even("row"), north, south).astype(BF)
    third[...] = jnp.where(even("col"), east, west).astype(BF)
    fourth[...] = jnp.where(even("col"), west, east).astype(BF)


def lane_of(value, lane):
    return jnp.broadcast_to(value[:, lane : lane + 1], (value.shape[0], LANES))


def port_place(port_ref, port, rows, width):
    all_cols = width * lax.axis_size("col")
    cell = port_ref[port]
    row = cell // all_cols - lax.axis_index("row") * rows
    col = cell % all_cols - lax.axis_index("col") * width
    return row, col, (row >= 0) & (row < rows) & (col >= 0) & (col < width)


def map_rows(map_refs, first, last):
    if len(map_refs) == 1:
        return map_refs[0][first:last, :]
    core = lax.rem(lax.axis_index("col"), 2)
    swapped, own = map_refs[0][...], map_refs[1][...]
    low, high = jnp.where(core == 0, own, swapped), jnp.where(core == 0, swapped, own)
    return jnp.concatenate([low, high], axis=0)[first:last]


def products(x, types, maps, first, last, total=None):
    mine = lax.axis_index("row")
    core = lax.rem(lax.axis_index("col"), 2)
    types = jnp.broadcast_to(types, x.shape)
    for (even, odd), map_refs in maps:
        kind = (mine ^ jnp.where(core == 0, even, odd)).astype(F32).astype(BF)
        masked = jnp.where(types == kind, x, jnp.zeros((), BF))
        part = map_rows(map_refs, first, last)
        product = jnp.dot(part, masked, preferred_element_type=F32)
        total = product if total is None else total + product
    return total


def with_steps(map_refs, first, last):
    refs = [(ref,) for ref in map_refs]
    if last == len(MAP_STEPS):
        refs[-2:] = [refs[-2] + refs[-1]]
    return list(zip(MAP_STEPS[first:last], refs, strict=True))


def shifted(total, next_ref, rows):
    quarter = total.shape[0] // 4
    last = (rows - 1) * LANES
    north = total[0:quarter].astype(BF)
    south = total[quarter : 2 * quarter].astype(BF)
    next_ref[0:quarter, LANES:] = south[:, :last]
    next_ref[0:quarter, 0:LANES] = jnp.zeros((quarter, LANES), BF)
    next_ref[quarter : 2 * quarter, :last] = north[:, LANES:]
    next_ref[quarter : 2 * quarter, last:] = jnp.zeros((quarter, LANES), BF)
    for row in range(rows):
        cols = slice(row * LANES, (row + 1) * LANES)
        west = total[2 * quarter : 3 * quarter, cols]
        east = total[3 * quarter : 4 * quarter, cols]
        next_ref[2 * quarter : 3 * quarter, cols] = pltpu.roll(east, 1, 1).astype(BF)
        next_ref[3 * quarter : 4 * quarter, cols] = pltpu.roll(west, LANES - 1, 1).astype(BF)
    return north, south


def rim_columns(x_ref, types, ports, offset):
    tile = types.shape[1]
    starts = [port * tile + offset for port in range(ports)]
    cells = jnp.concatenate([x_ref[:, start : start + LANES] for start in starts], axis=1)
    return cells, jnp.concatenate([types[:, offset : offset + LANES]] * ports, axis=1).astype(BF)


def side_columns(x_ref, types, ports):
    order, tile = x_ref.shape[0], types.shape[1]
    rows = tile // LANES

    def pick(block_of, lines):
        lane = lax.broadcasted_iota(jnp.int32, (lines, LANES), 1)
        first = last = jnp.zeros((lines, LANES), F32)
        for place in range(ports * rows):
            turned = pltpu.roll(block_of(place), place + 1, 1)
            first = jnp.where(lane == place + 1, turned, first)
            last = jnp.where(lane == place, turned, last)
        first = pltpu.roll(first, LANES - 1, 1)
        return jnp.where(lane < 64, first, pltpu.roll(last, 64, 1)).astype(BF)

    def types_of(place):
        start = place % rows * LANES
        return jnp.broadcast_to(types[:, start : start + LANES], (16, LANES))

    quarter = order // 4
    sides = [
        pick(
            lambda place: x_ref[edge * quarter : (edge + 1) * quarter,
                                place * LANES : (place + 1) * LANES].astype(F32),
            quarter,
        )
        for edge in range(4)
    ]
    return jnp.concatenate(sides, axis=0), pick(types_of, 16)


def rims(x_ref, types, ports, sides, kinds, maps, so_far):
    order, tile = x_ref.shape[0], types.shape[1]
    quarter = order // 4
    before = [None if ref is None else ref[...].astype(F32) for ref in so_far]
    cells, cell_kinds = rim_columns(x_ref, types, ports, 0)
    north = products(cells, cell_kinds, maps, 0, quarter, before[0])
    cells, cell_kinds = rim_columns(x_ref, types, ports, tile - LANES)
    south = products(cells, cell_kinds, maps, quarter, 2 * quarter, before[1])
    side = products(sides, kinds, maps, 2 * quarter, order, before[2])
    return north.astype(BF), south.astype(BF), side.astype(BF)


def early_kernel(ports, first, last, x_ref, types_ref, *refs):
    maps = with_steps(refs[: last - first], first, last)
    refs = refs[last - first :]
    types = types_ref[...].astype(F32)
    tile = types.shape[1]
    if first == 0:
        done_ref, so_far = None, [None] * 3
        sides, kinds = side_columns(x_ref, types, ports)
        refs[4][...] = sides
        refs[5][...] = kinds
    else:
        done_ref, so_far = refs[0], refs[1:4]
        sides, kinds = refs[4][...], refs[5][...]
        refs = refs[6:]
    outs = rims(x_ref, types, ports, sides, kinds[0:1], maps, so_far)
    for ref, value in zip(refs[1:4], outs):
        ref[...] = value
    for port in range(ports):
        cols = slice(port * tile, (port + 1) * tile)
        before = None if done_ref is None else done_ref[:, cols].astype(F32)
        total = products(x_ref[:, cols], types.astype(BF), maps, 0, x_ref.shape[0], before)
        refs[0][:, cols] = total.astype(BF)


def rim_kernel(ports, first, x_ref, types_ref, *refs):
    maps = with_steps(refs[:-9], first, len(MAP_STEPS))
    so_far, (sides, kinds) = refs[-9:-6], refs[-6:-4]
    outs = rims(
        x_ref, types_ref[...].astype(F32), ports, sides[...], kinds[0:1, :], maps, so_far
    )
    quarter = x_ref.shape[0] // 4
    store_rims(refs[-4:], outs[0], outs[1], outs[2][0:quarter], outs[2][quarter:])


def first_kernel(rows, ports, first, x_ref, types_ref, done_ref, *refs):
    maps = with_steps(refs[:-1], first, len(MAP_STEPS))
    types = types_ref[...].astype(F32).astype(BF)
    tile = types.shape[1]
    for port in range(ports):
        cols = slice(port * tile, (port + 1) * tile)
        before = done_ref[:, cols].astype(F32)
        total = products(x_ref[:, cols], types, maps, 0, x_ref.shape[0], before)
        shifted(total, refs[-1].at[:, cols], rows)


def second_kernel(rows, width, port_ref, x_ref, types_ref, profile_ref, *refs):
    halo_refs, map_refs, next_ref = refs[:4], refs[4:-6], refs[-6]
    rim_refs, blocks = refs[-5:-1], refs[-1]
    types = types_ref[...].astype(F32).astype(BF)
    tile = types.shape[1]
    order = x_ref.shape[0]
    quarter = order // 4
    maps = with_steps(map_refs, 0, len(MAP_STEPS))
    north_in, south_in, west_in, east_in = halos_inside(halo_refs)
    lane = lax.broadcasted_iota(jnp.int32, (quarter, LANES), 1)
    west_rim = east_rim = jnp.zeros((quarter, LANES), F32)
    north_rim, south_rim = [], []
    for port in range(x_ref.shape[1] // tile):
        own = slice(port * tile, (port + 1) * tile)
        rim = slice(port * LANES, (port + 1) * LANES)
        block = blocks.at[port % 2]
        block[...] = x_ref[:, own]
        block[0:quarter, 0:LANES] = north_in[:, rim].astype(BF)
        block[quarter : 2 * quarter, tile - LANES :] = south_in[:, rim].astype(BF)
        for row in range(rows):
            place = port * rows + row
            cols = slice(row * LANES, (row + 1) * LANES)
            west = block[2 * quarter : 3 * quarter, cols].astype(F32)
            east = block[3 * quarter :, cols].astype(F32)
            west = jnp.where(lane == 0, lane_of(west_in, 64 + place), west)
            east = jnp.where(lane == LANES - 1, lane_of(east_in, place), east)
            block[2 * quarter : 3 * quarter, cols] = west.astype(BF)
            block[3 * quarter :, cols] = east.astype(BF)
        row, col, inside = port_place(port_ref, port, rows, width)

        @pl.when(inside)
        def _():
            cols = pl.ds(pl.multiple_of(row * LANES, LANES), LANES)
            here = lax.broadcasted_iota(jnp.int32, (order, LANES), 1) == col
            current = block[:, cols].astype(F32)
            added = current + profile_ref[port].astype(F32)
            block[:, cols] = jnp.where(here, added, current).astype(BF)

        total = products(block[...], types, maps, 0, order)
        north, south = shifted(total, next_ref.at[:, own], rows)
        north_rim.append(north[:, 0:LANES])
        south_rim.append(south[:, tile - LANES :])
        for row in range(rows):
            place = port * rows + row
            west = lane_of(total[2 * quarter : 3 * quarter], row * LANES)
            east = lane_of(total[3 * quarter :], (row + 1) * LANES - 1)
            west_rim = jnp.where(lane == place, west, west_rim)
            east_rim = jnp.where(lane == place, east, east_rim)
    north_rim, south_rim = (jnp.concatenate(value, axis=1) for value in (north_rim, south_rim))
    store_rims(rim_refs, north_rim, south_rim, west_rim, east_rim)


def last_kernel(rows, width, port_ref, x_ref, profile_ref, *refs):
    out_ref, buffer, sems = refs[4:]
    order, ports = buffer.shape[:2]
    quarter, tile = order // 4, rows * width
    north_in, south_in, west_in, east_in = halos_inside(refs[:4])
    lane = lax.broadcasted_iota(jnp.int32, (quarter, LANES), 1)
    copies = []
    for edge in (2, 3, 0, 1):
        lines = slice(edge * quarter, (edge + 1) * quarter)
        for port in range(ports):
            rim = slice(port * LANES, (port + 1) * LANES)
            starts = [port * tile + row * LANES for row in range(rows)]
            parts = [x_ref[lines, start : start + LANES].astype(F32) for start in starts]
            places = range(port * rows, (port + 1) * rows)
            if edge == 0:
                parts[0] = north_in[:, rim]
            elif edge == 1:
                parts[-1] = south_in[:, rim]
            elif edge == 2:
                parts = [
                    jnp.where(lane == 0, lane_of(west_in, place), part)
                    for place, part in zip(places, parts)
                ]
            else:
                parts = [
                    jnp.where(lane == LANES - 1, lane_of(east_in, place), part)
                    for place, part in zip(places, parts)
                ]
            value = jnp.concatenate(parts, axis=1).reshape(quarter, rows, LANES)
            buffer[lines, port] = value.astype(BF)
        for port in range(ports):
            row, col, inside = port_place(port_ref, port, rows, width)

            @pl.when(inside)
            def _():
                current = buffer[lines, port].astype(F32)
                here = (lax.broadcasted_iota(jnp.int32, current.shape, 1) == row) & (
                    lax.broadcasted_iota(jnp.int32, current.shape, 2) == col
                )
                profile = profile_ref[port, lines, :].astype(F32).reshape(quarter, 1, LANES)
                added = current + jnp.broadcast_to(profile, current.shape)
                buffer[lines, port] = jnp.where(here, added, current).astype(BF)

        copy = pltpu.make_async_copy(buffer.at[lines], out_ref.at[lines], sems.at[edge])
        copy.start()
        copies.append(copy)
    for copy in copies:
        copy.wait()


def exchange(rims):
    def pairs(axis, first):
        count = lax.axis_size(axis)
        near = [(i, (i + 1) % count) for i in range(first, count, 2)]
        return near + [(target, source) for source, target in near]

    axes = (("row", 0), ("row", 1), ("col", 0), ("col", 1))
    return [lax.ppermute(rim, axis, pairs(axis, first)) for rim, (axis, first) in zip(rims, axes)]


def body(traces, cell_type, port_cell, port_profile, mode_shapes, mode_values, mode_weights):
    edges, samples, ports, rows, width = traces.shape
    order = edges * samples
    quarter = samples
    tile = rows * width
    own_map, x = own_type_map(mode_shapes, mode_values, mode_weights, traces)
    core = lax.rem(lax.axis_index("col"), 2)
    half = lax.dynamic_slice_in_dim(own_map, core * (order // 2), order // 2)
    fetched = [swap(own_map, "row", *steps) for steps in MAP_STEPS[1:4]]
    half = swap(half, "row", 4)
    swapped = [swap(fetched[0], "col", 1)]
    types = cell_type.reshape(1, tile)
    profile = jnp.broadcast_to(
        jnp.transpose(port_profile.reshape(order, ports))[:, :, None], (ports, order, LANES)
    )
    ports_spec = pl.BlockSpec(memory_space=pltpu.SMEM)
    next_shape = jax.ShapeDtypeStruct((order, ports * tile), BF)
    rim_shapes = [jax.ShapeDtypeStruct((quarter, ports * LANES), BF)] * 2 + [
        jax.ShapeDtypeStruct((quarter, LANES), BF)
    ] * 2
    work = 2 * order * order * len(MAP_STEPS) * ports * tile
    early = (0, 2, 4)
    side_shapes = [
        jax.ShapeDtypeStruct((order, LANES), BF),
        jax.ShapeDtypeStruct((16, LANES), BF),
    ]
    part_shapes = [next_shape] + rim_shapes[:2] + [jax.ShapeDtypeStruct((2 * quarter, LANES), BF)]
    *parts, sides, kinds = whole_call(
        functools.partial(early_kernel, ports, early[0], early[1]),
        part_shapes + side_shapes,
        x,
        types,
        own_map,
        fetched[0],
        flops=work // 3,
    )
    parts, rest, half = lax.optimization_barrier((parts, fetched[1:], half))
    swapped += [swap(value, "col", 1) for value in rest + [half]]
    parts = whole_call(
        functools.partial(early_kernel, ports, early[1], early[2]),
        part_shapes,
        x,
        types,
        *rest,
        *parts,
        sides,
        kinds,
        flops=work // 3,
    )
    done, *parts = parts
    late = swapped + [half]
    maps = [own_map, fetched[0]] + rest + late
    sent = whole_call(
        functools.partial(rim_kernel, ports, early[2]),
        rim_shapes,
        x,
        types,
        *late,
        *parts,
        sides,
        kinds,
        flops=work // 8,
    )
    halos = exchange(sent)
    (x,) = whole_call(
        functools.partial(first_kernel, rows, ports, early[2]),
        [next_shape],
        x,
        types,
        done,
        *late,
        flops=work // 2,
    )
    operands = [port_cell, x, types, profile, *halos, *maps]
    x, *sent = pl.pallas_call(
        functools.partial(second_kernel, rows, width),
        in_specs=[ports_spec] + [WHOLE] * (len(operands) - 1),
        out_specs=[WHOLE] * 5,
        out_shape=[next_shape] + rim_shapes,
        scratch_shapes=[pltpu.VMEM((2, order, tile), BF)],
        compiler_params=PARAMS,
        cost_estimate=pl.CostEstimate(flops=work, bytes_accessed=0, transcendentals=0),
    )(*operands)
    operands = [port_cell, x, profile, *exchange(sent)]
    out = pl.pallas_call(
        functools.partial(last_kernel, rows, width),
        in_specs=[ports_spec] + [WHOLE] * (len(operands) - 1),
        out_specs=pl.BlockSpec(memory_space=pl.ANY),
        out_shape=jax.ShapeDtypeStruct((order, ports, rows, width), BF),
        scratch_shapes=[
            pltpu.VMEM((order, ports, rows, width), BF),
            pltpu.SemaphoreType.DMA((4,)),
        ],
        compiler_params=PARAMS,
    )(*operands)
    return out.reshape(traces.shape)


def solution(mesh):
    return jax.shard_map(
        body,
        mesh=mesh,
        in_specs=(
            P(None, None, None, "row", "col"),
            P("row", "col"),
            P(),
            P(),
            P("row", None, "col"),
            P("row", "col"),
            P("row", "col", None),
        ),
        out_specs=P(None, None, None, "row", "col"),
        check_vma=False,
    )
```

```python
import functools
import math

import jax
import jax.numpy as jnp
from jax import lax
from jax.experimental import pallas as pl
from jax.experimental.pallas import tpu as pltpu
from jax.sharding import PartitionSpec as P

BF = jnp.bfloat16
F32 = jnp.float32
LANES = 128
PARAMS = pltpu.CompilerParams(vmem_limit_bytes=20 * 2**20)
WIDE_PARAMS = pltpu.CompilerParams(vmem_limit_bytes=50 * 2**20)


def swap(value, axis, first, second=None):
    second = first if second is None else second
    rows, cols = lax.axis_size("row"), lax.axis_size("col")
    pairs = []
    for row in range(rows):
        for col in range(cols):
            step = second if col % 2 else first
            other = (row ^ step, col) if axis == "row" else (row, col ^ step)
            pairs.append((row * cols + col, other[0] * cols + other[1]))
    return lax.ppermute(value, ("row", "col"), pairs)


def flat_kernel(x_hbm, out_ref, x_ref, sems):
    order, ports, rows, width = x_ref.shape
    quarter, tile = order // 4, rows * width
    edges = [slice(edge * quarter, (edge + 1) * quarter) for edge in range(4)]
    copies = [
        pltpu.make_async_copy(x_hbm.at[lines], x_ref.at[lines], sems.at[edge])
        for edge, lines in enumerate(edges)
    ]
    for copy in copies:
        copy.start()
    for copy, lines in zip(copies, edges):
        copy.wait()
        for port in range(ports):
            value = x_ref[lines, port].astype(F32).reshape(quarter, tile)
            out_ref[lines, port * tile : (port + 1) * tile] = value.astype(BF)


def partial_kernel(modes, *refs):
    left, right = [], []
    for ref in refs[:-1]:
        for start in range(0, ref.shape[0], 2 * modes):
            left.append(ref[start : start + modes])
            right.append(ref[start + modes : start + 2 * modes])
    refs[-1][...] = lax.dot_general(
        jnp.concatenate(left, axis=0),
        jnp.concatenate(right, axis=0),
        (((0,), (0,)), ((), ())),
        precision=lax.Precision.HIGHEST,
        preferred_element_type=F32,
    )


WHOLE = pl.BlockSpec(memory_space=pltpu.VMEM)


def whole_call(kernel, shapes, *operands, flops=0):
    return pl.pallas_call(
        kernel,
        in_specs=[WHOLE] * len(operands),
        out_specs=[WHOLE] * len(shapes),
        out_shape=shapes,
        compiler_params=PARAMS,
        cost_estimate=pl.CostEstimate(flops=flops, bytes_accessed=0, transcendentals=0),
    )(*operands)


def own_type_map(mode_shapes, mode_values, mode_weights, traces, types):
    modes, order = mode_weights.shape[1:]
    scaled = mode_shapes[0].T * mode_values[0][:, None]
    part = lax.broadcasted_iota(jnp.int32, (2, modes, order), 0)
    own = jnp.where(part == 0, scaled[None], mode_weights).reshape(2 * modes, order)
    far = swap(own, "col", 4)
    pair = jnp.concatenate([own, swap(own, "col", 1)], axis=0)
    pair, traces = lax.optimization_barrier((pair, traces))
    got = [swap(pair, "col", 8, 10), swap(pair, "col", 2, 14), swap(pair, "col", 6, 12)]
    shape = (order,) + traces.shape[2:]
    x = pl.pallas_call(
        flat_kernel,
        in_specs=[pl.BlockSpec(memory_space=pltpu.HBM)],
        out_specs=WHOLE,
        out_shape=jax.ShapeDtypeStruct((order, math.prod(shape[1:])), BF),
        scratch_shapes=[pltpu.VMEM(shape, BF), pltpu.SemaphoreType.DMA((4,))],
        compiler_params=WIDE_PARAMS,
        cost_estimate=pl.CostEstimate(flops=2**30, bytes_accessed=0, transcendentals=0),
    )(traces.reshape(shape))
    *got, x = lax.optimization_barrier((*got, x))
    (partial,) = whole_call(
        functools.partial(partial_kernel, modes),
        [jax.ShapeDtypeStruct((order, order), F32)],
        own,
        far,
        *got,
    )
    partial, x = lax.optimization_barrier((partial, x))
    other = swap(partial, "col", 1)
    sides = whole_call(
        functools.partial(sides_kernel, traces.shape[2]),
        [jax.ShapeDtypeStruct((order, LANES), BF), jax.ShapeDtypeStruct((16, LANES), BF)],
        x,
        types,
        flops=2**30,
    )
    other, sides = lax.optimization_barrier((other, sides))
    return (partial + other).astype(BF), x, sides


MAP_STEPS = ((0, 0), (1, 3), (2, 7), (6, 5), (3, 1), (7, 2), (5, 6), (4, 4))


def even(axis):
    return lax.rem(lax.axis_index(axis), 2) == 0


def halos_inside(axis, one, two):
    one, two = one[...].astype(F32), two[...].astype(F32)
    index, count = lax.axis_index(axis), lax.axis_size(axis)
    low = jnp.where(even(axis), two, one)
    high = jnp.where(even(axis), one, two)
    return jnp.where(index > 0, low, 0.0), jnp.where(index < count - 1, high, 0.0)


def store_rims(out_refs, north, south, west, east):
    first, second, third, fourth = out_refs
    first[...] = jnp.where(even("row"), south, north).astype(BF)
    second[...] = jnp.where(even("row"), north, south).astype(BF)
    third[...] = jnp.where(even("col"), east, west).astype(BF)
    fourth[...] = jnp.where(even("col"), west, east).astype(BF)


def lane_of(value, lane):
    return jnp.broadcast_to(value[:, lane : lane + 1], (value.shape[0], LANES))


def port_place(port_ref, port, rows, width):
    all_cols = width * lax.axis_size("col")
    cell = port_ref[port]
    row = cell // all_cols - lax.axis_index("row") * rows
    col = cell % all_cols - lax.axis_index("col") * width
    return row, col, (row >= 0) & (row < rows) & (col >= 0) & (col < width)


def map_rows(map_refs, first, last):
    if len(map_refs) == 1:
        return map_refs[0][first:last, :]
    core = lax.rem(lax.axis_index("col"), 2)
    swapped, own = map_refs[0][...], map_refs[1][...]
    low, high = jnp.where(core == 0, own, swapped), jnp.where(core == 0, swapped, own)
    return jnp.concatenate([low, high], axis=0)[first:last]


def products(x, types, maps, first, last, total=None):
    mine = lax.axis_index("row")
    core = lax.rem(lax.axis_index("col"), 2)
    types = jnp.broadcast_to(types, x.shape)
    for (even, odd), map_refs in maps:
        kind = (mine ^ jnp.where(core == 0, even, odd)).astype(F32).astype(BF)
        masked = jnp.where(types == kind, x, jnp.zeros((), BF))
        part = map_rows(map_refs, first, last)
        product = jnp.dot(part, masked, preferred_element_type=F32)
        total = product if total is None else total + product
    return total


def with_steps(map_refs, first, last):
    refs = [(ref,) for ref in map_refs]
    if last == len(MAP_STEPS):
        refs[-2:] = [refs[-2] + refs[-1]]
    return list(zip(MAP_STEPS[first:last], refs, strict=True))


def shifted(total, next_ref, rows):
    quarter = total.shape[0] // 4
    last = (rows - 1) * LANES
    north = total[0:quarter].astype(BF)
    south = total[quarter : 2 * quarter].astype(BF)
    next_ref[0:quarter, LANES:] = south[:, :last]
    next_ref[0:quarter, 0:LANES] = jnp.zeros((quarter, LANES), BF)
    next_ref[quarter : 2 * quarter, :last] = north[:, LANES:]
    next_ref[quarter : 2 * quarter, last:] = jnp.zeros((quarter, LANES), BF)
    for row in range(rows):
        cols = slice(row * LANES, (row + 1) * LANES)
        west = total[2 * quarter : 3 * quarter, cols]
        east = total[3 * quarter : 4 * quarter, cols]
        next_ref[2 * quarter : 3 * quarter, cols] = pltpu.roll(east, 1, 1).astype(BF)
        next_ref[3 * quarter : 4 * quarter, cols] = pltpu.roll(west, LANES - 1, 1).astype(BF)
    return north, south


def rim_columns(x_ref, types, ports, offset):
    tile = types.shape[1]
    starts = [port * tile + offset for port in range(ports)]
    cells = jnp.concatenate([x_ref[:, start : start + LANES] for start in starts], axis=1)
    return cells, jnp.concatenate([types[:, offset : offset + LANES]] * ports, axis=1).astype(BF)


def side_columns(x_ref, types, ports):
    order, tile = x_ref.shape[0], types.shape[1]
    rows = tile // LANES

    def pick(block_of, lines):
        lane = lax.broadcasted_iota(jnp.int32, (lines, LANES), 1)
        first = last = jnp.zeros((lines, LANES), F32)
        for place in range(ports * rows):
            turned = pltpu.roll(block_of(place), place + 1, 1)
            first = jnp.where(lane == place + 1, turned, first)
            last = jnp.where(lane == place, turned, last)
        first = pltpu.roll(first, LANES - 1, 1)
        return jnp.where(lane < 64, first, pltpu.roll(last, 64, 1)).astype(BF)

    def types_of(place):
        start = place % rows * LANES
        return jnp.broadcast_to(types[:, start : start + LANES], (16, LANES))

    quarter = order // 4
    sides = [
        pick(
            lambda place: x_ref[edge * quarter : (edge + 1) * quarter,
                                place * LANES : (place + 1) * LANES].astype(F32),
            quarter,
        )
        for edge in range(4)
    ]
    return jnp.concatenate(sides, axis=0), pick(types_of, 16)


def rims(x_ref, types, ports, sides, kinds, maps, so_far):
    order, tile = x_ref.shape[0], types.shape[1]
    quarter = order // 4
    before = [None if ref is None else ref[...].astype(F32) for ref in so_far]
    cells, cell_kinds = rim_columns(x_ref, types, ports, 0)
    north = products(cells, cell_kinds, maps, 0, quarter, before[0])
    cells, cell_kinds = rim_columns(x_ref, types, ports, tile - LANES)
    south = products(cells, cell_kinds, maps, quarter, 2 * quarter, before[1])
    side = products(sides, kinds, maps, 2 * quarter, order, before[2])
    return north.astype(BF), south.astype(BF), side.astype(BF)


def sides_kernel(ports, x_ref, types_ref, sides_ref, kinds_ref):
    sides_ref[...], kinds_ref[...] = side_columns(x_ref, types_ref[...].astype(F32), ports)


def early_kernel(ports, first, last, x_ref, types_ref, sides_ref, kinds_ref, *refs):
    maps = with_steps(refs[: last - first], first, last)
    types = types_ref[...].astype(F32)
    tile = types.shape[1]
    so_far, outs = refs[last - first : -4], refs[-4:]
    done_ref, *so_far = so_far if first else [None] * 4
    values = rims(x_ref, types, ports, sides_ref[...], kinds_ref[0:1, :], maps, so_far)
    for ref, value in zip(outs[1:], values):
        ref[...] = value
    for port in range(ports):
        cols = slice(port * tile, (port + 1) * tile)
        before = None if done_ref is None else done_ref[:, cols].astype(F32)
        total = products(x_ref[:, cols], types.astype(BF), maps, 0, x_ref.shape[0], before)
        outs[0][:, cols] = total.astype(BF)


def rim_kernel(ports, first, x_ref, types_ref, sides_ref, kinds_ref, *refs):
    maps = with_steps(refs[:-7], first, len(MAP_STEPS))
    types = types_ref[...].astype(F32)
    quarter = x_ref.shape[0] // 4
    values = rims(x_ref, types, ports, sides_ref[...], kinds_ref[0:1, :], maps, refs[-7:-4])
    store_rims(refs[-4:], values[0], values[1], values[2][0:quarter], values[2][quarter:])


def first_kernel(rows, ports, first, x_ref, types_ref, done_ref, *refs):
    maps = with_steps(refs[:-1], first, len(MAP_STEPS))
    types = types_ref[...].astype(F32).astype(BF)
    tile = types.shape[1]
    for port in range(ports):
        cols = slice(port * tile, (port + 1) * tile)
        before = done_ref[:, cols].astype(F32)
        total = products(x_ref[:, cols], types, maps, 0, x_ref.shape[0], before)
        shifted(total, refs[-1].at[:, cols], rows)


def second_kernel(rows, width, port_ref, x_ref, types_ref, profile_ref, *refs):
    halo_refs, map_refs, next_ref = refs[:4], refs[4:-6], refs[-6]
    rim_refs, blocks = refs[-5:-1], refs[-1]
    types = types_ref[...].astype(F32).astype(BF)
    tile = types.shape[1]
    order = x_ref.shape[0]
    quarter = order // 4
    maps = with_steps(map_refs, 0, len(MAP_STEPS))
    north_in, south_in = halos_inside("row", *halo_refs[:2])
    west_in, east_in = halos_inside("col", *halo_refs[2:])
    lane = lax.broadcasted_iota(jnp.int32, (quarter, LANES), 1)
    west_rim = east_rim = jnp.zeros((quarter, LANES), F32)
    north_rim, south_rim = [], []
    for port in range(x_ref.shape[1] // tile):
        own = slice(port * tile, (port + 1) * tile)
        rim = slice(port * LANES, (port + 1) * LANES)
        block = blocks.at[port % 2]
        block[...] = x_ref[:, own]
        block[0:quarter, 0:LANES] = north_in[:, rim].astype(BF)
        block[quarter : 2 * quarter, tile - LANES :] = south_in[:, rim].astype(BF)
        for row in range(rows):
            place = port * rows + row
            cols = slice(row * LANES, (row + 1) * LANES)
            west = block[2 * quarter : 3 * quarter, cols].astype(F32)
            east = block[3 * quarter :, cols].astype(F32)
            west = jnp.where(lane == 0, lane_of(west_in, 64 + place), west)
            east = jnp.where(lane == LANES - 1, lane_of(east_in, place), east)
            block[2 * quarter : 3 * quarter, cols] = west.astype(BF)
            block[3 * quarter :, cols] = east.astype(BF)
        row, col, inside = port_place(port_ref, port, rows, width)

        @pl.when(inside)
        def _():
            cols = pl.ds(pl.multiple_of(row * LANES, LANES), LANES)
            here = lax.broadcasted_iota(jnp.int32, (order, LANES), 1) == col
            current = block[:, cols].astype(F32)
            added = current + profile_ref[port].astype(F32)
            block[:, cols] = jnp.where(here, added, current).astype(BF)

        total = products(block[...], types, maps, 0, order)
        north, south = shifted(total, next_ref.at[:, own], rows)
        north_rim.append(north[:, 0:LANES])
        south_rim.append(south[:, tile - LANES :])
        for row in range(rows):
            place = port * rows + row
            west = lane_of(total[2 * quarter : 3 * quarter], row * LANES)
            east = lane_of(total[3 * quarter :], (row + 1) * LANES - 1)
            west_rim = jnp.where(lane == place, west, west_rim)
            east_rim = jnp.where(lane == place, east, east_rim)
    north_rim, south_rim = (jnp.concatenate(value, axis=1) for value in (north_rim, south_rim))
    store_rims(rim_refs, north_rim, south_rim, west_rim, east_rim)


def last_kernel(rows, width, axis, port_ref, x_ref, profile_ref, one_ref, two_ref, *refs):
    out_ref, buffer, sems = refs[-3:]
    ports = buffer.shape[1]
    quarter, tile = x_ref.shape[0] // 4, rows * width
    low, high = halos_inside(axis, one_ref, two_ref)
    lane = lax.broadcasted_iota(jnp.int32, (quarter, LANES), 1)
    copies = []
    for edge in (0, 1) if axis == "row" else (2, 3):
        lines = slice(edge * quarter, (edge + 1) * quarter)
        local = slice(edge % 2 * quarter, (edge % 2 + 1) * quarter)
        for port in range(ports):
            rim = slice(port * LANES, (port + 1) * LANES)
            starts = [port * tile + row * LANES for row in range(rows)]
            parts = [x_ref[lines, start : start + LANES].astype(F32) for start in starts]
            places = range(port * rows, (port + 1) * rows)
            if edge == 0:
                parts[0] = low[:, rim]
            elif edge == 1:
                parts[-1] = high[:, rim]
            elif edge == 2:
                parts = [
                    jnp.where(lane == 0, lane_of(low, place), part)
                    for place, part in zip(places, parts)
                ]
            else:
                parts = [
                    jnp.where(lane == LANES - 1, lane_of(high, place), part)
                    for place, part in zip(places, parts)
                ]
            value = jnp.concatenate(parts, axis=1).reshape(quarter, rows, LANES)
            buffer[local, port] = value.astype(BF)
        for port in range(ports):
            row, col, inside = port_place(port_ref, port, rows, width)

            @pl.when(inside)
            def _():
                current = buffer[local, port].astype(F32)
                here = (lax.broadcasted_iota(jnp.int32, current.shape, 1) == row) & (
                    lax.broadcasted_iota(jnp.int32, current.shape, 2) == col
                )
                profile = profile_ref[port, lines, :].astype(F32).reshape(quarter, 1, LANES)
                added = current + jnp.broadcast_to(profile, current.shape)
                buffer[local, port] = jnp.where(here, added, current).astype(BF)

        copy = pltpu.make_async_copy(buffer.at[local], out_ref.at[lines], sems.at[edge % 2])
        copy.start()
        copies.append(copy)
    for copy in copies:
        copy.wait()


def exchange(rims):
    def pairs(axis, first):
        count = lax.axis_size(axis)
        near = [(i, (i + 1) % count) for i in range(first, count, 2)]
        return near + [(target, source) for source, target in near]

    axes = (("row", 0), ("row", 1), ("col", 0), ("col", 1))
    return [lax.ppermute(rim, axis, pairs(axis, first)) for rim, (axis, first) in zip(rims, axes)]


def body(traces, cell_type, port_cell, port_profile, mode_shapes, mode_values, mode_weights):
    edges, samples, ports, rows, width = traces.shape
    order = edges * samples
    quarter = samples
    tile = rows * width
    types = cell_type.reshape(1, tile)
    own_map, x, sides = own_type_map(mode_shapes, mode_values, mode_weights, traces, types)
    core = lax.rem(lax.axis_index("col"), 2)
    half = lax.dynamic_slice_in_dim(own_map, core * (order // 2), order // 2)
    fetched = [swap(own_map, "row", *steps) for steps in MAP_STEPS[1:4]]
    half = swap(half, "row", 4)
    swapped = [swap(fetched[0], "col", 1)]
    profile = jnp.broadcast_to(
        jnp.transpose(port_profile.reshape(order, ports))[:, :, None], (ports, order, LANES)
    )
    ports_spec = pl.BlockSpec(memory_space=pltpu.SMEM)
    next_shape = jax.ShapeDtypeStruct((order, ports * tile), BF)
    rim_shapes = [jax.ShapeDtypeStruct((quarter, ports * LANES), BF)] * 2 + [
        jax.ShapeDtypeStruct((quarter, LANES), BF)
    ] * 2
    work = 2 * order * order * len(MAP_STEPS) * ports * tile
    part_shapes = [next_shape] + rim_shapes[:2] + [jax.ShapeDtypeStruct((2 * quarter, LANES), BF)]

    def early(first, maps, parts=()):
        last = first + len(maps)
        kernel = functools.partial(early_kernel, ports, first, last)
        flops = work * len(maps) // 7
        return whole_call(kernel, part_shapes, x, types, *sides, *maps, *parts, flops=flops)

    parts = early(0, [own_map, fetched[0]])
    parts, rest = lax.optimization_barrier((parts, fetched[1:]))
    swapped += [swap(value, "col", 1) for value in rest]
    parts = early(2, rest, parts)
    parts, half = lax.optimization_barrier((parts, half))
    swapped += [swap(half, "col", 1)]
    parts = early(4, swapped[:1], parts)
    parts, swapped[3] = lax.optimization_barrier((parts, swapped[3]))
    done, *parts = parts
    maps = [own_map, fetched[0]] + rest + swapped + [half]
    late = maps[5:]
    sent = whole_call(
        functools.partial(rim_kernel, ports, 5),
        rim_shapes,
        x,
        types,
        *sides,
        *late,
        *parts,
        flops=work // 8,
    )
    halos = exchange(sent)
    (x,) = whole_call(
        functools.partial(first_kernel, rows, ports, 5),
        [next_shape],
        x,
        types,
        done,
        *late,
        flops=work // 2,
    )
    operands = [port_cell, x, types, profile, *halos, *maps]
    x, *sent = pl.pallas_call(
        functools.partial(second_kernel, rows, width),
        in_specs=[ports_spec] + [WHOLE] * (len(operands) - 1),
        out_specs=[WHOLE] * 5,
        out_shape=[next_shape] + rim_shapes,
        scratch_shapes=[pltpu.VMEM((2, order, tile), BF)],
        compiler_params=PARAMS,
        cost_estimate=pl.CostEstimate(flops=work, bytes_accessed=0, transcendentals=0),
    )(*operands)
    halos = exchange(sent)
    out = []
    for axis, pair in (("row", halos[:2]), ("col", halos[2:])):
        operands = [port_cell, x, profile, *pair, *out]
        out = [
            pl.pallas_call(
                functools.partial(last_kernel, rows, width, axis),
                in_specs=[ports_spec] + [WHOLE] * 4 + [pl.BlockSpec(memory_space=pl.ANY)] * len(out),
                out_specs=pl.BlockSpec(memory_space=pl.ANY),
                out_shape=jax.ShapeDtypeStruct((order, ports, rows, width), BF),
                scratch_shapes=[
                    pltpu.VMEM((order // 2, ports, rows, width), BF),
                    pltpu.SemaphoreType.DMA((2,)),
                ],
                input_output_aliases={5: 0} if out else {},
                compiler_params=PARAMS,
                cost_estimate=pl.CostEstimate(flops=2**30, bytes_accessed=0, transcendentals=0),
            )(*operands)
        ]
    return out[0].reshape(traces.shape)


def solution(mesh):
    return jax.shard_map(
        body,
        mesh=mesh,
        in_specs=(
            P(None, None, None, "row", "col"),
            P("row", "col"),
            P(),
            P(),
            P("row", None, "col"),
            P("row", "col"),
            P("row", "col", None),
        ),
        out_specs=P(None, None, None, "row", "col"),
        check_vma=False,
    )
```

```python
import functools
import math

import jax
import jax.numpy as jnp
from jax import lax
from jax.experimental import pallas as pl
from jax.experimental.pallas import tpu as pltpu
from jax.sharding import PartitionSpec as P

BF = jnp.bfloat16
F32 = jnp.float32
LANES = 128
PARAMS = pltpu.CompilerParams(vmem_limit_bytes=20 * 2**20)
WIDE_PARAMS = pltpu.CompilerParams(vmem_limit_bytes=50 * 2**20)


def swap(value, axis, first, second=None):
    second = first if second is None else second
    rows, cols = lax.axis_size("row"), lax.axis_size("col")
    pairs = []
    for row in range(rows):
        for col in range(cols):
            step = second if col % 2 else first
            other = (row ^ step, col) if axis == "row" else (row, col ^ step)
            pairs.append((row * cols + col, other[0] * cols + other[1]))
    return lax.ppermute(value, ("row", "col"), pairs)


def flat_kernel(x_hbm, out_ref, x_ref, sems):
    order, ports, rows, width = x_ref.shape
    quarter, tile = order // 4, rows * width
    edges = [slice(edge * quarter, (edge + 1) * quarter) for edge in range(4)]
    copies = [
        pltpu.make_async_copy(x_hbm.at[lines], x_ref.at[lines], sems.at[edge])
        for edge, lines in enumerate(edges)
    ]
    for copy in copies:
        copy.start()
    for copy, lines in zip(copies, edges):
        copy.wait()
        for port in range(ports):
            value = x_ref[lines, port].astype(F32).reshape(quarter, tile)
            out_ref[lines, port * tile : (port + 1) * tile] = value.astype(BF)


def partial_kernel(modes, *refs):
    left, right = [], []
    for ref in refs[:-1]:
        for start in range(0, ref.shape[0], 2 * modes):
            left.append(ref[start : start + modes])
            right.append(ref[start + modes : start + 2 * modes])
    refs[-1][...] = lax.dot_general(
        jnp.concatenate(left, axis=0),
        jnp.concatenate(right, axis=0),
        (((0,), (0,)), ((), ())),
        precision=lax.Precision.HIGHEST,
        preferred_element_type=F32,
    )


WHOLE = pl.BlockSpec(memory_space=pltpu.VMEM)


def whole_call(kernel, shapes, *operands, flops=0):
    return pl.pallas_call(
        kernel,
        in_specs=[WHOLE] * len(operands),
        out_specs=[WHOLE] * len(shapes),
        out_shape=shapes,
        compiler_params=PARAMS,
        cost_estimate=pl.CostEstimate(flops=flops, bytes_accessed=0, transcendentals=0),
    )(*operands)


def own_type_map(mode_shapes, mode_values, mode_weights, traces, types):
    modes, order = mode_weights.shape[1:]
    own = jnp.concatenate([mode_shapes[0].T, mode_weights[0]], axis=0).reshape(2, modes, order)
    part = lax.broadcasted_iota(jnp.int32, own.shape, 0)
    own = own * jnp.where(part == 0, mode_values[0][None, :, None], 1.0)
    own = own.reshape(2 * modes, order)
    far = swap(own, "col", 4)
    pair = jnp.concatenate([own, swap(own, "col", 1)], axis=0)
    pair, traces = lax.optimization_barrier((pair, traces))
    got = [swap(pair, "col", 8, 10), swap(pair, "col", 2, 14), swap(pair, "col", 6, 12)]
    shape = (order,) + traces.shape[2:]
    x = pl.pallas_call(
        flat_kernel,
        in_specs=[pl.BlockSpec(memory_space=pltpu.HBM)],
        out_specs=WHOLE,
        out_shape=jax.ShapeDtypeStruct((order, math.prod(shape[1:])), BF),
        scratch_shapes=[pltpu.VMEM(shape, BF), pltpu.SemaphoreType.DMA((4,))],
        compiler_params=WIDE_PARAMS,
        cost_estimate=pl.CostEstimate(flops=2**30, bytes_accessed=0, transcendentals=0),
    )(traces.reshape(shape))
    *got, x = lax.optimization_barrier((*got, x))
    (partial,) = whole_call(
        functools.partial(partial_kernel, modes),
        [jax.ShapeDtypeStruct((order, order), F32)],
        own,
        far,
        *got,
    )
    partial, x = lax.optimization_barrier((partial, x))
    other = swap(partial, "col", 1)
    sides = whole_call(
        functools.partial(sides_kernel, traces.shape[2]),
        [jax.ShapeDtypeStruct((order, LANES), BF), jax.ShapeDtypeStruct((16, LANES), BF)],
        x,
        types,
        flops=2**30,
    )
    other, sides = lax.optimization_barrier((other, sides))
    return (partial + other).astype(BF), x, sides


MAP_STEPS = ((0, 0), (1, 3), (2, 7), (6, 5), (3, 1), (7, 2), (5, 6), (4, 4))


def even(axis):
    return lax.rem(lax.axis_index(axis), 2) == 0


def halos_inside(axis, one, two):
    one, two = one[...].astype(F32), two[...].astype(F32)
    index, count = lax.axis_index(axis), lax.axis_size(axis)
    low = jnp.where(even(axis), two, one)
    high = jnp.where(even(axis), one, two)
    return jnp.where(index > 0, low, 0.0), jnp.where(index < count - 1, high, 0.0)


def store_rims(out_refs, north, south, west, east):
    first, second, third, fourth = out_refs
    first[...] = jnp.where(even("row"), south, north).astype(BF)
    second[...] = jnp.where(even("row"), north, south).astype(BF)
    third[...] = jnp.where(even("col"), east, west).astype(BF)
    fourth[...] = jnp.where(even("col"), west, east).astype(BF)


def lane_of(value, lane):
    return jnp.broadcast_to(value[:, lane : lane + 1], (value.shape[0], LANES))


def port_place(port_ref, port, rows, width):
    all_cols = width * lax.axis_size("col")
    cell = port_ref[port]
    row = cell // all_cols - lax.axis_index("row") * rows
    col = cell % all_cols - lax.axis_index("col") * width
    return row, col, (row >= 0) & (row < rows) & (col >= 0) & (col < width)


def map_rows(map_refs, first, last):
    if len(map_refs) == 1:
        return map_refs[0][first:last, :]
    core = lax.rem(lax.axis_index("col"), 2)
    swapped, own = map_refs[0][...], map_refs[1][...]
    low, high = jnp.where(core == 0, own, swapped), jnp.where(core == 0, swapped, own)
    return jnp.concatenate([low, high], axis=0)[first:last]


def products(x, types, maps, first, last, total=None):
    mine = lax.axis_index("row")
    core = lax.rem(lax.axis_index("col"), 2)
    types = jnp.broadcast_to(types, x.shape)
    for (even, odd), map_refs in maps:
        kind = (mine ^ jnp.where(core == 0, even, odd)).astype(F32).astype(BF)
        masked = jnp.where(types == kind, x, jnp.zeros((), BF))
        part = map_rows(map_refs, first, last)
        product = jnp.dot(part, masked, preferred_element_type=F32)
        total = product if total is None else total + product
    return total


def with_steps(map_refs, first, last):
    refs = [(ref,) for ref in map_refs]
    if last == len(MAP_STEPS):
        refs[-2:] = [refs[-2] + refs[-1]]
    return list(zip(MAP_STEPS[first:last], refs, strict=True))


def shifted(total, next_ref, rows):
    quarter = total.shape[0] // 4
    last = (rows - 1) * LANES
    north = total[0:quarter].astype(BF)
    south = total[quarter : 2 * quarter].astype(BF)
    next_ref[0:quarter, LANES:] = south[:, :last]
    next_ref[0:quarter, 0:LANES] = jnp.zeros((quarter, LANES), BF)
    next_ref[quarter : 2 * quarter, :last] = north[:, LANES:]
    next_ref[quarter : 2 * quarter, last:] = jnp.zeros((quarter, LANES), BF)
    for row in range(rows):
        cols = slice(row * LANES, (row + 1) * LANES)
        west = total[2 * quarter : 3 * quarter, cols]
        east = total[3 * quarter : 4 * quarter, cols]
        next_ref[2 * quarter : 3 * quarter, cols] = pltpu.roll(east, 1, 1).astype(BF)
        next_ref[3 * quarter : 4 * quarter, cols] = pltpu.roll(west, LANES - 1, 1).astype(BF)
    return north, south


def rim_columns(x_ref, types, ports, offset):
    tile = types.shape[1]
    starts = [port * tile + offset for port in range(ports)]
    cells = jnp.concatenate([x_ref[:, start : start + LANES] for start in starts], axis=1)
    return cells, jnp.concatenate([types[:, offset : offset + LANES]] * ports, axis=1).astype(BF)


def side_columns(x_ref, types, ports):
    order, tile = x_ref.shape[0], types.shape[1]
    rows = tile // LANES

    def pick(block_of, lines):
        lane = lax.broadcasted_iota(jnp.int32, (lines, LANES), 1)
        first = last = jnp.zeros((lines, LANES), F32)
        for place in range(ports * rows):
            turned = pltpu.roll(block_of(place), place + 1, 1)
            first = jnp.where(lane == place + 1, turned, first)
            last = jnp.where(lane == place, turned, last)
        first = pltpu.roll(first, LANES - 1, 1)
        return jnp.where(lane < 64, first, pltpu.roll(last, 64, 1)).astype(BF)

    def types_of(place):
        start = place % rows * LANES
        return jnp.broadcast_to(types[:, start : start + LANES], (16, LANES))

    quarter = order // 4
    sides = [
        pick(
            lambda place: x_ref[edge * quarter : (edge + 1) * quarter,
                                place * LANES : (place + 1) * LANES].astype(F32),
            quarter,
        )
        for edge in range(4)
    ]
    return jnp.concatenate(sides, axis=0), pick(types_of, 16)


def rims(x_ref, types, ports, sides, kinds, maps, so_far):
    order, tile = x_ref.shape[0], types.shape[1]
    quarter = order // 4
    before = [None if ref is None else ref[...].astype(F32) for ref in so_far]
    cells, cell_kinds = rim_columns(x_ref, types, ports, 0)
    north = products(cells, cell_kinds, maps, 0, quarter, before[0])
    cells, cell_kinds = rim_columns(x_ref, types, ports, tile - LANES)
    south = products(cells, cell_kinds, maps, quarter, 2 * quarter, before[1])
    side = products(sides, kinds, maps, 2 * quarter, order, before[2])
    return north.astype(BF), south.astype(BF), side.astype(BF)


def sides_kernel(ports, x_ref, types_ref, sides_ref, kinds_ref):
    sides_ref[...], kinds_ref[...] = side_columns(x_ref, types_ref[...].astype(F32), ports)


def early_kernel(ports, first, last, x_ref, types_ref, sides_ref, kinds_ref, *refs):
    maps = with_steps(refs[: last - first], first, last)
    types = types_ref[...].astype(F32)
    tile = types.shape[1]
    so_far, outs = refs[last - first : -4], refs[-4:]
    done_ref, *so_far = so_far if first else [None] * 4
    values = rims(x_ref, types, ports, sides_ref[...], kinds_ref[0:1, :], maps, so_far)
    for ref, value in zip(outs[1:], values):
        ref[...] = value
    for port in range(ports):
        cols = slice(port * tile, (port + 1) * tile)
        before = None if done_ref is None else done_ref[:, cols].astype(F32)
        total = products(x_ref[:, cols], types.astype(BF), maps, 0, x_ref.shape[0], before)
        outs[0][:, cols] = total.astype(BF)


def rim_kernel(ports, first, x_ref, types_ref, sides_ref, kinds_ref, *refs):
    maps = with_steps(refs[:-7], first, len(MAP_STEPS))
    types = types_ref[...].astype(F32)
    quarter = x_ref.shape[0] // 4
    values = rims(x_ref, types, ports, sides_ref[...], kinds_ref[0:1, :], maps, refs[-7:-4])
    store_rims(refs[-4:], values[0], values[1], values[2][0:quarter], values[2][quarter:])


def first_kernel(rows, ports, first, x_ref, types_ref, done_ref, *refs):
    maps = with_steps(refs[:-1], first, len(MAP_STEPS))
    types = types_ref[...].astype(F32).astype(BF)
    tile = types.shape[1]
    for port in range(ports):
        cols = slice(port * tile, (port + 1) * tile)
        before = done_ref[:, cols].astype(F32)
        total = products(x_ref[:, cols], types, maps, 0, x_ref.shape[0], before)
        shifted(total, refs[-1].at[:, cols], rows)


def second_kernel(rows, width, port_ref, x_ref, types_ref, profile_ref, *refs):
    halo_refs, map_refs, next_ref = refs[:4], refs[4:-6], refs[-6]
    rim_refs, blocks = refs[-5:-1], refs[-1]
    types = types_ref[...].astype(F32).astype(BF)
    tile = types.shape[1]
    order = x_ref.shape[0]
    quarter = order // 4
    maps = with_steps(map_refs, 0, len(MAP_STEPS))
    north_in, south_in = halos_inside("row", *halo_refs[:2])
    west_in, east_in = halos_inside("col", *halo_refs[2:])
    lane = lax.broadcasted_iota(jnp.int32, (quarter, LANES), 1)
    west_rim = east_rim = jnp.zeros((quarter, LANES), F32)
    north_rim, south_rim = [], []
    for port in range(x_ref.shape[1] // tile):
        own = slice(port * tile, (port + 1) * tile)
        rim = slice(port * LANES, (port + 1) * LANES)
        block = blocks.at[port % 2]
        block[...] = x_ref[:, own]
        block[0:quarter, 0:LANES] = north_in[:, rim].astype(BF)
        block[quarter : 2 * quarter, tile - LANES :] = south_in[:, rim].astype(BF)
        for row in range(rows):
            place = port * rows + row
            cols = slice(row * LANES, (row + 1) * LANES)
            west = block[2 * quarter : 3 * quarter, cols].astype(F32)
            east = block[3 * quarter :, cols].astype(F32)
            west = jnp.where(lane == 0, lane_of(west_in, 64 + place), west)
            east = jnp.where(lane == LANES - 1, lane_of(east_in, place), east)
            block[2 * quarter : 3 * quarter, cols] = west.astype(BF)
            block[3 * quarter :, cols] = east.astype(BF)
        row, col, inside = port_place(port_ref, port, rows, width)

        @pl.when(inside)
        def _():
            cols = pl.ds(pl.multiple_of(row * LANES, LANES), LANES)
            here = lax.broadcasted_iota(jnp.int32, (order, LANES), 1) == col
            current = block[:, cols].astype(F32)
            added = current + profile_ref[port].astype(F32)
            block[:, cols] = jnp.where(here, added, current).astype(BF)

        total = products(block[...], types, maps, 0, order)
        north, south = shifted(total, next_ref.at[:, own], rows)
        north_rim.append(north[:, 0:LANES])
        south_rim.append(south[:, tile - LANES :])
        for row in range(rows):
            place = port * rows + row
            west = lane_of(total[2 * quarter : 3 * quarter], row * LANES)
            east = lane_of(total[3 * quarter :], (row + 1) * LANES - 1)
            west_rim = jnp.where(lane == place, west, west_rim)
            east_rim = jnp.where(lane == place, east, east_rim)
    north_rim, south_rim = (jnp.concatenate(value, axis=1) for value in (north_rim, south_rim))
    store_rims(rim_refs, north_rim, south_rim, west_rim, east_rim)


def last_kernel(rows, width, port_ref, x_ref, profile_ref, *refs):
    out_ref, buffer, sems = refs[4:]
    order, ports = buffer.shape[:2]
    quarter, tile = order // 4, rows * width
    north_in, south_in = halos_inside("row", *refs[:2])
    west_in, east_in = halos_inside("col", *refs[2:4])
    lane = lax.broadcasted_iota(jnp.int32, (quarter, LANES), 1)
    copies = []
    for edge in (2, 3, 0, 1):
        lines = slice(edge * quarter, (edge + 1) * quarter)
        for port in range(ports):
            rim = slice(port * LANES, (port + 1) * LANES)
            starts = [port * tile + row * LANES for row in range(rows)]
            parts = [x_ref[lines, start : start + LANES].astype(F32) for start in starts]
            places = range(port * rows, (port + 1) * rows)
            if edge == 0:
                parts[0] = north_in[:, rim]
            elif edge == 1:
                parts[-1] = south_in[:, rim]
            elif edge == 2:
                parts = [
                    jnp.where(lane == 0, lane_of(west_in, place), part)
                    for place, part in zip(places, parts)
                ]
            else:
                parts = [
                    jnp.where(lane == LANES - 1, lane_of(east_in, place), part)
                    for place, part in zip(places, parts)
                ]
            value = jnp.concatenate(parts, axis=1).reshape(quarter, rows, LANES)
            buffer[lines, port] = value.astype(BF)
        for port in range(ports):
            row, col, inside = port_place(port_ref, port, rows, width)

            @pl.when(inside)
            def _():
                current = buffer[lines, port].astype(F32)
                here = (lax.broadcasted_iota(jnp.int32, current.shape, 1) == row) & (
                    lax.broadcasted_iota(jnp.int32, current.shape, 2) == col
                )
                profile = profile_ref[port, lines, :].astype(F32).reshape(quarter, 1, LANES)
                added = current + jnp.broadcast_to(profile, current.shape)
                buffer[lines, port] = jnp.where(here, added, current).astype(BF)

        copy = pltpu.make_async_copy(buffer.at[lines], out_ref.at[lines], sems.at[edge])
        copy.start()
        copies.append(copy)
    for copy in copies:
        copy.wait()


def exchange(rims):
    def pairs(axis, first):
        count = lax.axis_size(axis)
        near = [(i, (i + 1) % count) for i in range(first, count, 2)]
        return near + [(target, source) for source, target in near]

    axes = (("row", 0), ("row", 1), ("col", 0), ("col", 1))
    return [lax.ppermute(rim, axis, pairs(axis, first)) for rim, (axis, first) in zip(rims, axes)]


def body(traces, cell_type, port_cell, port_profile, mode_shapes, mode_values, mode_weights):
    edges, samples, ports, rows, width = traces.shape
    order = edges * samples
    quarter = samples
    tile = rows * width
    types = cell_type.reshape(1, tile)
    own_map, x, sides = own_type_map(mode_shapes, mode_values, mode_weights, traces, types)
    core = lax.rem(lax.axis_index("col"), 2)
    half = lax.dynamic_slice_in_dim(own_map, core * (order // 2), order // 2)
    fetched = [swap(own_map, "row", *steps) for steps in MAP_STEPS[1:4]]
    half = swap(half, "row", 4)
    profile = jnp.broadcast_to(
        jnp.transpose(port_profile.reshape(order, ports))[:, :, None], (ports, order, LANES)
    )
    ports_spec = pl.BlockSpec(memory_space=pltpu.SMEM)
    next_shape = jax.ShapeDtypeStruct((order, ports * tile), BF)
    rim_shapes = [jax.ShapeDtypeStruct((quarter, ports * LANES), BF)] * 2 + [
        jax.ShapeDtypeStruct((quarter, LANES), BF)
    ] * 2
    work = 2 * order * order * len(MAP_STEPS) * ports * tile
    part_shapes = [next_shape] + rim_shapes[:2] + [jax.ShapeDtypeStruct((2 * quarter, LANES), BF)]

    def early(first, maps, parts=()):
        last = first + len(maps)
        kernel = functools.partial(early_kernel, ports, first, last)
        flops = work * len(maps) // 7
        return whole_call(kernel, part_shapes, x, types, *sides, *maps, *parts, flops=flops)

    parts = early(0, [own_map, fetched[0]])
    parts, fetched = lax.optimization_barrier((parts, fetched))
    swapped = [swap(value, "col", 1) for value in fetched]
    parts = early(2, fetched[1:], parts)
    parts, half = lax.optimization_barrier((parts, half))
    swapped.append(swap(half, "col", 1))
    done, *parts = parts
    late = swapped + [half]
    maps = [own_map] + fetched + late
    sent = whole_call(
        functools.partial(rim_kernel, ports, 4),
        rim_shapes,
        x,
        types,
        *sides,
        *late,
        *parts,
        flops=work // 8,
    )
    halos = exchange(sent)
    (x,) = whole_call(
        functools.partial(first_kernel, rows, ports, 4),
        [next_shape],
        x,
        types,
        done,
        *late,
        flops=work // 2,
    )
    operands = [port_cell, x, types, profile, *halos, *maps]
    x, *sent = pl.pallas_call(
        functools.partial(second_kernel, rows, width),
        in_specs=[ports_spec] + [WHOLE] * (len(operands) - 1),
        out_specs=[WHOLE] * 5,
        out_shape=[next_shape] + rim_shapes,
        scratch_shapes=[pltpu.VMEM((2, order, tile), BF)],
        compiler_params=PARAMS,
        cost_estimate=pl.CostEstimate(flops=work, bytes_accessed=0, transcendentals=0),
    )(*operands)
    operands = [port_cell, x, profile, *exchange(sent)]
    out = pl.pallas_call(
        functools.partial(last_kernel, rows, width),
        in_specs=[ports_spec] + [WHOLE] * (len(operands) - 1),
        out_specs=pl.BlockSpec(memory_space=pl.ANY),
        out_shape=jax.ShapeDtypeStruct((order, ports, rows, width), BF),
        scratch_shapes=[
            pltpu.VMEM((order, ports, rows, width), BF),
            pltpu.SemaphoreType.DMA((4,)),
        ],
        compiler_params=PARAMS,
    )(*operands)
    return out.reshape(traces.shape)


def solution(mesh):
    return jax.shard_map(
        body,
        mesh=mesh,
        in_specs=(
            P(None, None, None, "row", "col"),
            P("row", "col"),
            P(),
            P(),
            P("row", None, "col"),
            P("row", "col"),
            P("row", "col", None),
        ),
        out_specs=P(None, None, None, "row", "col"),
        check_vma=False,
    )
```

```python
import functools
import math

import jax
import jax.numpy as jnp
from jax import lax
from jax.experimental import pallas as pl
from jax.experimental.pallas import tpu as pltpu
from jax.sharding import PartitionSpec as P

BF = jnp.bfloat16
F32 = jnp.float32
LANES = 128
PARAMS = pltpu.CompilerParams(vmem_limit_bytes=20 * 2**20)
WIDE_PARAMS = pltpu.CompilerParams(vmem_limit_bytes=50 * 2**20)


def swap(value, first, second=None):
    second = first if second is None else second
    rows, cols = lax.axis_size("row"), lax.axis_size("col")
    pairs = []
    for row in range(rows):
        for col in range(cols):
            down, along = second if col % 2 else first
            pairs.append((row * cols + col, (row ^ down) * cols + (col ^ along)))
    return lax.ppermute(value, ("row", "col"), pairs)


def swap_cores(value):
    return swap(value, (0, 1))


def flat_kernel(x_hbm, out_ref, x_ref, sems):
    order, ports, rows, width = x_ref.shape
    quarter, tile = order // 4, rows * width
    edges = [slice(edge * quarter, (edge + 1) * quarter) for edge in range(4)]
    copies = [
        pltpu.make_async_copy(x_hbm.at[lines], x_ref.at[lines], sems.at[edge])
        for edge, lines in enumerate(edges)
    ]
    for copy in copies:
        copy.start()
    for copy, lines in zip(copies, edges):
        copy.wait()
        for port in range(ports):
            value = x_ref[lines, port].astype(F32).reshape(quarter, tile)
            out_ref[lines, port * tile : (port + 1) * tile] = value.astype(BF)


def partial_kernel(modes, *refs):
    left, right = [], []
    for ref in refs[:-1]:
        for start in range(0, ref.shape[0], 2 * modes):
            left.append(ref[start : start + modes])
            right.append(ref[start + modes : start + 2 * modes])
    refs[-1][...] = lax.dot_general(
        jnp.concatenate(left, axis=0),
        jnp.concatenate(right, axis=0),
        (((0,), (0,)), ((), ())),
        precision=lax.Precision.HIGHEST,
        preferred_element_type=F32,
    )


WHOLE = pl.BlockSpec(memory_space=pltpu.VMEM)


def whole_call(kernel, shapes, *operands, flops=0):
    return pl.pallas_call(
        kernel,
        in_specs=[WHOLE] * len(operands),
        out_specs=[WHOLE] * len(shapes),
        out_shape=shapes,
        compiler_params=PARAMS,
        cost_estimate=pl.CostEstimate(flops=flops, bytes_accessed=0, transcendentals=0),
    )(*operands)


def own_type_map(mode_shapes, mode_values, mode_weights, traces, types):
    modes, order = mode_weights.shape[1:]
    own = jnp.concatenate([mode_shapes[0].T, mode_weights[0]], axis=0).reshape(2, modes, order)
    part = lax.broadcasted_iota(jnp.int32, own.shape, 0)
    own = own * jnp.where(part == 0, mode_values[0][None, :, None], 1.0)
    own = own.reshape(2 * modes, order)
    far = swap(own, (0, 4))
    pair = jnp.concatenate([own, swap_cores(own)], axis=0)
    pair, traces = lax.optimization_barrier((pair, traces))
    steps = (((0, 8), (0, 10)), ((0, 2), (0, 14)), ((0, 6), (0, 12)))
    got = [swap(pair, *step) for step in steps]
    shape = (order,) + traces.shape[2:]
    x = pl.pallas_call(
        flat_kernel,
        in_specs=[pl.BlockSpec(memory_space=pltpu.HBM)],
        out_specs=WHOLE,
        out_shape=jax.ShapeDtypeStruct((order, math.prod(shape[1:])), BF),
        scratch_shapes=[pltpu.VMEM(shape, BF), pltpu.SemaphoreType.DMA((4,))],
        compiler_params=WIDE_PARAMS,
        cost_estimate=pl.CostEstimate(flops=2**30, bytes_accessed=0, transcendentals=0),
    )(traces.reshape(shape))
    *got, x = lax.optimization_barrier((*got, x))
    (partial,) = whole_call(
        functools.partial(partial_kernel, modes),
        [jax.ShapeDtypeStruct((order, order), F32)],
        own,
        far,
        *got,
    )
    partial, x = lax.optimization_barrier((partial, x))
    other = swap_cores(partial)
    sides = whole_call(
        functools.partial(sides_kernel, traces.shape[2]),
        [jax.ShapeDtypeStruct((order, LANES), BF), jax.ShapeDtypeStruct((16, LANES), BF)],
        x,
        types,
        flops=2**30,
    )
    other, sides = lax.optimization_barrier((other, sides))
    return (partial + other).astype(BF), x, sides


MAP_STEPS = ((0, 0), (1, 3), (2, 7), (6, 5), (3, 1), (7, 2), (5, 6), (4, 4))


def even(axis):
    return lax.rem(lax.axis_index(axis), 2) == 0


def halos_inside(axis, one, two):
    one, two = one[...].astype(F32), two[...].astype(F32)
    index, count = lax.axis_index(axis), lax.axis_size(axis)
    low = jnp.where(even(axis), two, one)
    high = jnp.where(even(axis), one, two)
    return jnp.where(index > 0, low, 0.0), jnp.where(index < count - 1, high, 0.0)


def store_rims(out_refs, north, south, west, east):
    first, second, third, fourth = out_refs
    first[...] = jnp.where(even("row"), south, north).astype(BF)
    second[...] = jnp.where(even("row"), north, south).astype(BF)
    third[...] = jnp.where(even("col"), east, west).astype(BF)
    fourth[...] = jnp.where(even("col"), west, east).astype(BF)


def lane_of(value, lane):
    return jnp.broadcast_to(value[:, lane : lane + 1], (value.shape[0], LANES))


def port_place(port_ref, port, rows, width):
    all_cols = width * lax.axis_size("col")
    cell = port_ref[port]
    row = cell // all_cols - lax.axis_index("row") * rows
    col = cell % all_cols - lax.axis_index("col") * width
    return row, col, (row >= 0) & (row < rows) & (col >= 0) & (col < width)


def map_rows(map_refs, first, last):
    if len(map_refs) == 1:
        return map_refs[0][first:last, :]
    core = lax.rem(lax.axis_index("col"), 2)
    swapped, own = map_refs[0][...], map_refs[1][...]
    low, high = jnp.where(core == 0, own, swapped), jnp.where(core == 0, swapped, own)
    return jnp.concatenate([low, high], axis=0)[first:last]


def products(x, types, maps, first, last, total=None):
    mine = lax.axis_index("row")
    core = lax.rem(lax.axis_index("col"), 2)
    types = jnp.broadcast_to(types, x.shape)
    for (even, odd), map_refs in maps:
        kind = (mine ^ jnp.where(core == 0, even, odd)).astype(F32).astype(BF)
        masked = jnp.where(types == kind, x, jnp.zeros((), BF))
        part = map_rows(map_refs, first, last)
        product = jnp.dot(part, masked, preferred_element_type=F32)
        total = product if total is None else total + product
    return total


def with_steps(map_refs, first, last):
    refs = [(ref,) for ref in map_refs]
    if last == len(MAP_STEPS):
        refs[-2:] = [refs[-2] + refs[-1]]
    return list(zip(MAP_STEPS[first:last], refs, strict=True))


def shifted(total, next_ref, rows):
    quarter = total.shape[0] // 4
    last = (rows - 1) * LANES
    north = total[0:quarter].astype(BF)
    south = total[quarter : 2 * quarter].astype(BF)
    next_ref[0:quarter, LANES:] = south[:, :last]
    next_ref[0:quarter, 0:LANES] = jnp.zeros((quarter, LANES), BF)
    next_ref[quarter : 2 * quarter, :last] = north[:, LANES:]
    next_ref[quarter : 2 * quarter, last:] = jnp.zeros((quarter, LANES), BF)
    for row in range(rows):
        cols = slice(row * LANES, (row + 1) * LANES)
        west = total[2 * quarter : 3 * quarter, cols]
        east = total[3 * quarter : 4 * quarter, cols]
        next_ref[2 * quarter : 3 * quarter, cols] = pltpu.roll(east, 1, 1).astype(BF)
        next_ref[3 * quarter : 4 * quarter, cols] = pltpu.roll(west, LANES - 1, 1).astype(BF)
    return north, south


def rim_columns(x_ref, types, ports, offset):
    tile = types.shape[1]
    starts = [port * tile + offset for port in range(ports)]
    cells = jnp.concatenate([x_ref[:, start : start + LANES] for start in starts], axis=1)
    return cells, jnp.concatenate([types[:, offset : offset + LANES]] * ports, axis=1).astype(BF)


def side_columns(x_ref, types, ports):
    order, tile = x_ref.shape[0], types.shape[1]
    rows = tile // LANES

    def pick(block_of, lines):
        lane = lax.broadcasted_iota(jnp.int32, (lines, LANES), 1)
        first = last = jnp.zeros((lines, LANES), F32)
        for place in range(ports * rows):
            turned = pltpu.roll(block_of(place), place + 1, 1)
            first = jnp.where(lane == place + 1, turned, first)
            last = jnp.where(lane == place, turned, last)
        first = pltpu.roll(first, LANES - 1, 1)
        return jnp.where(lane < 64, first, pltpu.roll(last, 64, 1)).astype(BF)

    def types_of(place):
        start = place % rows * LANES
        return jnp.broadcast_to(types[:, start : start + LANES], (16, LANES))

    quarter = order // 4
    sides = [
        pick(
            lambda place: x_ref[edge * quarter : (edge + 1) * quarter,
                                place * LANES : (place + 1) * LANES].astype(F32),
            quarter,
        )
        for edge in range(4)
    ]
    return jnp.concatenate(sides, axis=0), pick(types_of, 16)


def rims(x_ref, types, ports, sides, kinds, maps, so_far):
    order, tile = x_ref.shape[0], types.shape[1]
    quarter = order // 4
    before = [None if ref is None else ref[...].astype(F32) for ref in so_far]
    cells, cell_kinds = rim_columns(x_ref, types, ports, 0)
    north = products(cells, cell_kinds, maps, 0, quarter, before[0])
    cells, cell_kinds = rim_columns(x_ref, types, ports, tile - LANES)
    south = products(cells, cell_kinds, maps, quarter, 2 * quarter, before[1])
    side = products(sides, kinds, maps, 2 * quarter, order, before[2])
    return north.astype(BF), south.astype(BF), side.astype(BF)


def sides_kernel(ports, x_ref, types_ref, sides_ref, kinds_ref):
    sides_ref[...], kinds_ref[...] = side_columns(x_ref, types_ref[...].astype(F32), ports)


def early_kernel(ports, first, last, x_ref, types_ref, sides_ref, kinds_ref, *refs):
    maps = with_steps(refs[: last - first], first, last)
    types = types_ref[...].astype(F32)
    tile = types.shape[1]
    so_far, outs = refs[last - first : -4], refs[-4:]
    done_ref, *so_far = so_far if first else [None] * 4
    values = rims(x_ref, types, ports, sides_ref[...], kinds_ref[0:1, :], maps, so_far)
    for ref, value in zip(outs[1:], values):
        ref[...] = value
    for port in range(ports):
        cols = slice(port * tile, (port + 1) * tile)
        before = None if done_ref is None else done_ref[:, cols].astype(F32)
        total = products(x_ref[:, cols], types.astype(BF), maps, 0, x_ref.shape[0], before)
        outs[0][:, cols] = total.astype(BF)


def rim_kernel(ports, first, x_ref, types_ref, sides_ref, kinds_ref, *refs):
    maps = with_steps(refs[:-7], first, len(MAP_STEPS))
    types = types_ref[...].astype(F32)
    quarter = x_ref.shape[0] // 4
    values = rims(x_ref, types, ports, sides_ref[...], kinds_ref[0:1, :], maps, refs[-7:-4])
    store_rims(refs[-4:], values[0], values[1], values[2][0:quarter], values[2][quarter:])


def first_kernel(rows, ports, first, x_ref, types_ref, done_ref, *refs):
    maps = with_steps(refs[:-1], first, len(MAP_STEPS))
    types = types_ref[...].astype(F32).astype(BF)
    tile = types.shape[1]
    for port in range(ports):
        cols = slice(port * tile, (port + 1) * tile)
        before = done_ref[:, cols].astype(F32)
        total = products(x_ref[:, cols], types, maps, 0, x_ref.shape[0], before)
        shifted(total, refs[-1].at[:, cols], rows)


def second_kernel(rows, width, port_ref, x_ref, types_ref, profile_ref, *refs):
    halo_refs, map_refs, next_ref = refs[:4], refs[4:-6], refs[-6]
    rim_refs, blocks = refs[-5:-1], refs[-1]
    types = types_ref[...].astype(F32).astype(BF)
    tile = types.shape[1]
    order = x_ref.shape[0]
    quarter = order // 4
    maps = with_steps(map_refs, 0, len(MAP_STEPS))
    north_in, south_in = halos_inside("row", *halo_refs[:2])
    west_in, east_in = halos_inside("col", *halo_refs[2:])
    lane = lax.broadcasted_iota(jnp.int32, (quarter, LANES), 1)
    west_rim = east_rim = jnp.zeros((quarter, LANES), F32)
    north_rim, south_rim = [], []
    for port in range(x_ref.shape[1] // tile):
        own = slice(port * tile, (port + 1) * tile)
        rim = slice(port * LANES, (port + 1) * LANES)
        block = blocks.at[port % 2]
        block[...] = x_ref[:, own]
        block[0:quarter, 0:LANES] = north_in[:, rim].astype(BF)
        block[quarter : 2 * quarter, tile - LANES :] = south_in[:, rim].astype(BF)
        for row in range(rows):
            place = port * rows + row
            cols = slice(row * LANES, (row + 1) * LANES)
            west = block[2 * quarter : 3 * quarter, cols].astype(F32)
            east = block[3 * quarter :, cols].astype(F32)
            west = jnp.where(lane == 0, lane_of(west_in, 64 + place), west)
            east = jnp.where(lane == LANES - 1, lane_of(east_in, place), east)
            block[2 * quarter : 3 * quarter, cols] = west.astype(BF)
            block[3 * quarter :, cols] = east.astype(BF)
        row, col, inside = port_place(port_ref, port, rows, width)

        @pl.when(inside)
        def _():
            cols = pl.ds(pl.multiple_of(row * LANES, LANES), LANES)
            here = lax.broadcasted_iota(jnp.int32, (order, LANES), 1) == col
            current = block[:, cols].astype(F32)
            added = current + profile_ref[port].astype(F32)
            block[:, cols] = jnp.where(here, added, current).astype(BF)

        total = products(block[...], types, maps, 0, order)
        north, south = shifted(total, next_ref.at[:, own], rows)
        north_rim.append(north[:, 0:LANES])
        south_rim.append(south[:, tile - LANES :])
        for row in range(rows):
            place = port * rows + row
            west = lane_of(total[2 * quarter : 3 * quarter], row * LANES)
            east = lane_of(total[3 * quarter :], (row + 1) * LANES - 1)
            west_rim = jnp.where(lane == place, west, west_rim)
            east_rim = jnp.where(lane == place, east, east_rim)
    north_rim, south_rim = (jnp.concatenate(value, axis=1) for value in (north_rim, south_rim))
    store_rims(rim_refs, north_rim, south_rim, west_rim, east_rim)


def last_kernel(rows, width, port_ref, x_ref, profile_ref, *refs):
    out_ref, buffer, sems = refs[4:]
    order, ports = buffer.shape[:2]
    quarter, tile = order // 4, rows * width
    north_in, south_in = halos_inside("row", *refs[:2])
    west_in, east_in = halos_inside("col", *refs[2:4])
    lane = lax.broadcasted_iota(jnp.int32, (quarter, LANES), 1)
    copies = []
    for edge in (2, 3, 0, 1):
        lines = slice(edge * quarter, (edge + 1) * quarter)
        for port in range(ports):
            rim = slice(port * LANES, (port + 1) * LANES)
            starts = [port * tile + row * LANES for row in range(rows)]
            parts = [x_ref[lines, start : start + LANES].astype(F32) for start in starts]
            places = range(port * rows, (port + 1) * rows)
            if edge == 0:
                parts[0] = north_in[:, rim]
            elif edge == 1:
                parts[-1] = south_in[:, rim]
            elif edge == 2:
                parts = [
                    jnp.where(lane == 0, lane_of(west_in, place), part)
                    for place, part in zip(places, parts)
                ]
            else:
                parts = [
                    jnp.where(lane == LANES - 1, lane_of(east_in, place), part)
                    for place, part in zip(places, parts)
                ]
            value = jnp.concatenate(parts, axis=1).reshape(quarter, rows, LANES)
            buffer[lines, port] = value.astype(BF)
        for port in range(ports):
            row, col, inside = port_place(port_ref, port, rows, width)

            @pl.when(inside)
            def _():
                current = buffer[lines, port].astype(F32)
                here = (lax.broadcasted_iota(jnp.int32, current.shape, 1) == row) & (
                    lax.broadcasted_iota(jnp.int32, current.shape, 2) == col
                )
                profile = profile_ref[port, lines, :].astype(F32).reshape(quarter, 1, LANES)
                added = current + jnp.broadcast_to(profile, current.shape)
                buffer[lines, port] = jnp.where(here, added, current).astype(BF)

        copy = pltpu.make_async_copy(buffer.at[lines], out_ref.at[lines], sems.at[edge])
        copy.start()
        copies.append(copy)
    for copy in copies:
        copy.wait()


def exchange(rims):
    def pairs(axis, first):
        count = lax.axis_size(axis)
        near = [(i, (i + 1) % count) for i in range(first, count, 2)]
        return near + [(target, source) for source, target in near]

    axes = (("row", 0), ("row", 1), ("col", 0), ("col", 1))
    return [lax.ppermute(rim, axis, pairs(axis, first)) for rim, (axis, first) in zip(rims, axes)]


def body(traces, cell_type, port_cell, port_profile, mode_shapes, mode_values, mode_weights):
    edges, samples, ports, rows, width = traces.shape
    order = edges * samples
    quarter = samples
    tile = rows * width
    types = cell_type.reshape(1, tile)
    own_map, x, sides = own_type_map(mode_shapes, mode_values, mode_weights, traces, types)
    core = lax.rem(lax.axis_index("col"), 2)
    half = lax.dynamic_slice_in_dim(own_map, core * (order // 2), order // 2)
    fetched = [
        swap(own_map, *((step, 8 * (step % 2)) for step in steps)) for steps in MAP_STEPS[1:4]
    ]
    half = swap(half, (4, 0))
    profile = jnp.broadcast_to(
        jnp.transpose(port_profile.reshape(order, ports))[:, :, None], (ports, order, LANES)
    )
    ports_spec = pl.BlockSpec(memory_space=pltpu.SMEM)
    next_shape = jax.ShapeDtypeStruct((order, ports * tile), BF)
    rim_shapes = [jax.ShapeDtypeStruct((quarter, ports * LANES), BF)] * 2 + [
        jax.ShapeDtypeStruct((quarter, LANES), BF)
    ] * 2
    work = 2 * order * order * len(MAP_STEPS) * ports * tile
    part_shapes = [next_shape] + rim_shapes[:2] + [jax.ShapeDtypeStruct((2 * quarter, LANES), BF)]

    def early(first, maps, parts=()):
        last = first + len(maps)
        kernel = functools.partial(early_kernel, ports, first, last)
        flops = work * len(maps) // 7
        return whole_call(kernel, part_shapes, x, types, *sides, *maps, *parts, flops=flops)

    parts = list(early(0, [own_map, fetched[0]]))
    parts[1], fetched = lax.optimization_barrier((parts[1], fetched))
    swapped = [swap_cores(value) for value in fetched]
    parts = list(early(2, fetched[1:], parts))
    parts[1], half = lax.optimization_barrier((parts[1], half))
    swapped.append(swap_cores(half))
    done, *parts = parts
    late = swapped + [half]
    maps = [own_map] + fetched + late
    sent = whole_call(
        functools.partial(rim_kernel, ports, 4),
        rim_shapes,
        x,
        types,
        *sides,
        *late,
        *parts,
        flops=work // 8,
    )
    halos = exchange(sent)
    (x,) = whole_call(
        functools.partial(first_kernel, rows, ports, 4),
        [next_shape],
        x,
        types,
        done,
        *late,
        flops=work // 2,
    )
    operands = [port_cell, x, types, profile, *halos, *maps]
    x, *sent = pl.pallas_call(
        functools.partial(second_kernel, rows, width),
        in_specs=[ports_spec] + [WHOLE] * (len(operands) - 1),
        out_specs=[WHOLE] * 5,
        out_shape=[next_shape] + rim_shapes,
        scratch_shapes=[pltpu.VMEM((2, order, tile), BF)],
        compiler_params=PARAMS,
        cost_estimate=pl.CostEstimate(flops=work, bytes_accessed=0, transcendentals=0),
    )(*operands)
    operands = [port_cell, x, profile, *exchange(sent)]
    out = pl.pallas_call(
        functools.partial(last_kernel, rows, width),
        in_specs=[ports_spec] + [WHOLE] * (len(operands) - 1),
        out_specs=pl.BlockSpec(memory_space=pl.ANY),
        out_shape=jax.ShapeDtypeStruct((order, ports, rows, width), BF),
        scratch_shapes=[
            pltpu.VMEM((order, ports, rows, width), BF),
            pltpu.SemaphoreType.DMA((4,)),
        ],
        compiler_params=PARAMS,
    )(*operands)
    return out.reshape(traces.shape)


def solution(mesh):
    return jax.shard_map(
        body,
        mesh=mesh,
        in_specs=(
            P(None, None, None, "row", "col"),
            P("row", "col"),
            P(),
            P(),
            P("row", None, "col"),
            P("row", "col"),
            P("row", "col", None),
        ),
        out_specs=P(None, None, None, "row", "col"),
        check_vma=False,
    )
```

```python
import functools
import math

import jax
import jax.numpy as jnp
from jax import lax
from jax.experimental import pallas as pl
from jax.experimental.pallas import tpu as pltpu
from jax.sharding import PartitionSpec as P

BF = jnp.bfloat16
F32 = jnp.float32
LANES = 128
PARAMS = pltpu.CompilerParams(vmem_limit_bytes=20 * 2**20)
WIDE_PARAMS = pltpu.CompilerParams(vmem_limit_bytes=50 * 2**20)


def swap(value, first, second=None):
    second = first if second is None else second
    rows, cols = lax.axis_size("row"), lax.axis_size("col")
    pairs = []
    for row in range(rows):
        for col in range(cols):
            down, along = second if col % 2 else first
            pairs.append((row * cols + col, (row ^ down) * cols + (col ^ along)))
    return lax.ppermute(value, ("row", "col"), pairs)


def swap_cores(value):
    return swap(value, (0, 1))


def flat_kernel(x_hbm, out_ref, x_ref, sems):
    order, ports, rows, width = x_ref.shape
    quarter, tile = order // 4, rows * width
    edges = [slice(edge * quarter, (edge + 1) * quarter) for edge in range(4)]
    copies = [
        pltpu.make_async_copy(x_hbm.at[lines], x_ref.at[lines], sems.at[edge])
        for edge, lines in enumerate(edges)
    ]
    for copy in copies:
        copy.start()
    for copy, lines in zip(copies, edges):
        copy.wait()
        for port in range(ports):
            value = x_ref[lines, port].astype(F32).reshape(quarter, tile)
            out_ref[lines, port * tile : (port + 1) * tile] = value.astype(BF)


def partial_kernel(modes, *refs):
    left, right = [], []
    for ref in refs[:-1]:
        for start in range(0, ref.shape[0], 2 * modes):
            left.append(ref[start : start + modes])
            right.append(ref[start + modes : start + 2 * modes])
    refs[-1][...] = lax.dot_general(
        jnp.concatenate(left, axis=0),
        jnp.concatenate(right, axis=0),
        (((0,), (0,)), ((), ())),
        precision=lax.Precision.HIGHEST,
        preferred_element_type=F32,
    )


WHOLE = pl.BlockSpec(memory_space=pltpu.VMEM)


def whole_call(kernel, shapes, *operands, flops=0):
    return pl.pallas_call(
        kernel,
        in_specs=[WHOLE] * len(operands),
        out_specs=[WHOLE] * len(shapes),
        out_shape=shapes,
        compiler_params=PARAMS,
        cost_estimate=pl.CostEstimate(flops=flops, bytes_accessed=0, transcendentals=0),
    )(*operands)


def own_type_map(mode_shapes, mode_values, mode_weights, traces, types):
    modes, order = mode_weights.shape[1:]
    own = jnp.concatenate([mode_shapes[0].T, mode_weights[0]], axis=0)
    own = own * jnp.concatenate([mode_values[0], jnp.ones((modes,), F32)])[:, None]
    far = swap(own, (0, 4))
    pair = jnp.concatenate([own, swap_cores(own)], axis=0)
    pair, traces = lax.optimization_barrier((pair, traces))
    steps = (((0, 8), (0, 10)), ((0, 2), (0, 14)), ((0, 6), (0, 12)))
    got = [swap(pair, *step) for step in steps]
    shape = (order,) + traces.shape[2:]
    x = pl.pallas_call(
        flat_kernel,
        in_specs=[pl.BlockSpec(memory_space=pltpu.HBM)],
        out_specs=WHOLE,
        out_shape=jax.ShapeDtypeStruct((order, math.prod(shape[1:])), BF),
        scratch_shapes=[pltpu.VMEM(shape, BF), pltpu.SemaphoreType.DMA((4,))],
        compiler_params=WIDE_PARAMS,
        cost_estimate=pl.CostEstimate(flops=2**30, bytes_accessed=0, transcendentals=0),
    )(traces.reshape(shape))
    *got, x = lax.optimization_barrier((*got, x))
    (partial,) = whole_call(
        functools.partial(partial_kernel, modes),
        [jax.ShapeDtypeStruct((order, order), F32)],
        own,
        far,
        *got,
    )
    partial, x = lax.optimization_barrier((partial, x))
    other = swap_cores(partial)
    sides = whole_call(
        functools.partial(sides_kernel, traces.shape[2]),
        [jax.ShapeDtypeStruct((order, LANES), BF), jax.ShapeDtypeStruct((16, LANES), BF)],
        x,
        types,
        flops=2**30,
    )
    other, sides = lax.optimization_barrier((other, sides))
    return (partial + other).astype(BF), x, sides


MAP_STEPS = ((0, 0), (1, 3), (2, 7), (6, 5), (3, 1), (7, 2), (5, 6), (4, 4))


def even(axis):
    return lax.rem(lax.axis_index(axis), 2) == 0


def halos_inside(axis, one, two):
    one, two = one[...].astype(F32), two[...].astype(F32)
    index, count = lax.axis_index(axis), lax.axis_size(axis)
    low = jnp.where(even(axis), two, one)
    high = jnp.where(even(axis), one, two)
    return jnp.where(index > 0, low, 0.0), jnp.where(index < count - 1, high, 0.0)


def store_rims(out_refs, north, south, west, east):
    first, second, third, fourth = out_refs
    first[...] = jnp.where(even("row"), south, north).astype(BF)
    second[...] = jnp.where(even("row"), north, south).astype(BF)
    third[...] = jnp.where(even("col"), east, west).astype(BF)
    fourth[...] = jnp.where(even("col"), west, east).astype(BF)


def lane_of(value, lane):
    return jnp.broadcast_to(value[:, lane : lane + 1], (value.shape[0], LANES))


def port_profile_column(profile_ref, port):
    edges, _, samples = profile_ref.shape
    row = lax.broadcasted_iota(jnp.int32, (samples, samples), 0)
    col = lax.broadcasted_iota(jnp.int32, (samples, samples), 1)
    columns = []
    for edge in range(edges):
        line = jnp.broadcast_to(profile_ref[edge].astype(F32)[port : port + 1], row.shape)
        columns.append(jnp.sum(jnp.where(row == col, line, 0.0), axis=1, keepdims=True))
    return jnp.concatenate(columns, axis=0)


def port_place(port_ref, port, rows, width):
    all_cols = width * lax.axis_size("col")
    cell = port_ref[port]
    row = cell // all_cols - lax.axis_index("row") * rows
    col = cell % all_cols - lax.axis_index("col") * width
    return row, col, (row >= 0) & (row < rows) & (col >= 0) & (col < width)


def map_rows(map_refs, first, last):
    if len(map_refs) == 1:
        return map_refs[0][first:last, :]
    core = lax.rem(lax.axis_index("col"), 2)
    swapped, own = map_refs[0][...], map_refs[1][...]
    low, high = jnp.where(core == 0, own, swapped), jnp.where(core == 0, swapped, own)
    return jnp.concatenate([low, high], axis=0)[first:last]


def products(x, types, maps, first, last, total=None):
    mine = lax.axis_index("row")
    core = lax.rem(lax.axis_index("col"), 2)
    types = jnp.broadcast_to(types, x.shape)
    for (even, odd), map_refs in maps:
        kind = (mine ^ jnp.where(core == 0, even, odd)).astype(F32).astype(BF)
        masked = jnp.where(types == kind, x, jnp.zeros((), BF))
        part = map_rows(map_refs, first, last)
        product = jnp.dot(part, masked, preferred_element_type=F32)
        total = product if total is None else total + product
    return total


def with_steps(map_refs, first, last):
    refs = [(ref,) for ref in map_refs]
    if last == len(MAP_STEPS):
        refs[-2:] = [refs[-2] + refs[-1]]
    return list(zip(MAP_STEPS[first:last], refs, strict=True))


def shifted(total, next_ref, rows):
    quarter = total.shape[0] // 4
    last = (rows - 1) * LANES
    north = total[0:quarter].astype(BF)
    south = total[quarter : 2 * quarter].astype(BF)
    next_ref[0:quarter, LANES:] = south[:, :last]
    next_ref[0:quarter, 0:LANES] = jnp.zeros((quarter, LANES), BF)
    next_ref[quarter : 2 * quarter, :last] = north[:, LANES:]
    next_ref[quarter : 2 * quarter, last:] = jnp.zeros((quarter, LANES), BF)
    for row in range(rows):
        cols = slice(row * LANES, (row + 1) * LANES)
        west = total[2 * quarter : 3 * quarter, cols]
        east = total[3 * quarter : 4 * quarter, cols]
        next_ref[2 * quarter : 3 * quarter, cols] = pltpu.roll(east, 1, 1).astype(BF)
        next_ref[3 * quarter : 4 * quarter, cols] = pltpu.roll(west, LANES - 1, 1).astype(BF)
    return north, south


def rim_columns(x_ref, types, ports, offset):
    tile = types.shape[1]
    starts = [port * tile + offset for port in range(ports)]
    cells = jnp.concatenate([x_ref[:, start : start + LANES] for start in starts], axis=1)
    return cells, jnp.concatenate([types[:, offset : offset + LANES]] * ports, axis=1).astype(BF)


def side_columns(x_ref, types, ports):
    order, tile = x_ref.shape[0], types.shape[1]
    rows = tile // LANES

    def pick(block_of, lines):
        lane = lax.broadcasted_iota(jnp.int32, (lines, LANES), 1)
        first = last = jnp.zeros((lines, LANES), F32)
        for place in range(ports * rows):
            turned = pltpu.roll(block_of(place), place + 1, 1)
            first = jnp.where(lane == place + 1, turned, first)
            last = jnp.where(lane == place, turned, last)
        first = pltpu.roll(first, LANES - 1, 1)
        return jnp.where(lane < 64, first, pltpu.roll(last, 64, 1)).astype(BF)

    def types_of(place):
        start = place % rows * LANES
        return jnp.broadcast_to(types[:, start : start + LANES], (16, LANES))

    quarter = order // 4
    sides = [
        pick(
            lambda place: x_ref[edge * quarter : (edge + 1) * quarter,
                                place * LANES : (place + 1) * LANES].astype(F32),
            quarter,
        )
        for edge in range(4)
    ]
    return jnp.concatenate(sides, axis=0), pick(types_of, 16)


def rims(x_ref, types, ports, sides, kinds, maps, so_far):
    order, tile = x_ref.shape[0], types.shape[1]
    quarter = order // 4
    before = [None if ref is None else ref[...].astype(F32) for ref in so_far]
    cells, cell_kinds = rim_columns(x_ref, types, ports, 0)
    north = products(cells, cell_kinds, maps, 0, quarter, before[0])
    cells, cell_kinds = rim_columns(x_ref, types, ports, tile - LANES)
    south = products(cells, cell_kinds, maps, quarter, 2 * quarter, before[1])
    side = products(sides, kinds, maps, 2 * quarter, order, before[2])
    return north.astype(BF), south.astype(BF), side.astype(BF)


def sides_kernel(ports, x_ref, types_ref, sides_ref, kinds_ref):
    sides_ref[...], kinds_ref[...] = side_columns(x_ref, types_ref[...].astype(F32), ports)


def early_kernel(ports, first, last, x_ref, types_ref, sides_ref, kinds_ref, *refs):
    maps = with_steps(refs[: last - first], first, last)
    types = types_ref[...].astype(F32)
    tile = types.shape[1]
    so_far, outs = refs[last - first : -4], refs[-4:]
    done_ref, *so_far = so_far if first else [None] * 4
    values = rims(x_ref, types, ports, sides_ref[...], kinds_ref[0:1, :], maps, so_far)
    for ref, value in zip(outs[1:], values):
        ref[...] = value
    for port in range(ports):
        cols = slice(port * tile, (port + 1) * tile)
        before = None if done_ref is None else done_ref[:, cols].astype(F32)
        total = products(x_ref[:, cols], types.astype(BF), maps, 0, x_ref.shape[0], before)
        outs[0][:, cols] = total.astype(BF)


def rim_kernel(ports, first, x_ref, types_ref, sides_ref, kinds_ref, *refs):
    maps = with_steps(refs[:-7], first, len(MAP_STEPS))
    types = types_ref[...].astype(F32)
    quarter = x_ref.shape[0] // 4
    values = rims(x_ref, types, ports, sides_ref[...], kinds_ref[0:1, :], maps, refs[-7:-4])
    store_rims(refs[-4:], values[0], values[1], values[2][0:quarter], values[2][quarter:])


def first_kernel(rows, ports, first, x_ref, types_ref, done_ref, *refs):
    maps = with_steps(refs[:-1], first, len(MAP_STEPS))
    types = types_ref[...].astype(F32).astype(BF)
    tile = types.shape[1]
    for port in range(ports):
        cols = slice(port * tile, (port + 1) * tile)
        before = done_ref[:, cols].astype(F32)
        total = products(x_ref[:, cols], types, maps, 0, x_ref.shape[0], before)
        shifted(total, refs[-1].at[:, cols], rows)


def second_kernel(rows, width, port_ref, x_ref, types_ref, profile_ref, *refs):
    halo_refs, map_refs, next_ref = refs[:4], refs[4:-5], refs[-5]
    rim_refs = refs[-4:]
    types = types_ref[...].astype(F32).astype(BF)
    tile = types.shape[1]
    order = x_ref.shape[0]
    quarter = order // 4
    maps = with_steps(map_refs, 0, len(MAP_STEPS))
    north_in, south_in = halos_inside("row", *halo_refs[:2])
    west_in, east_in = halos_inside("col", *halo_refs[2:])
    lane = lax.broadcasted_iota(jnp.int32, (quarter, LANES), 1)
    west_rim = east_rim = jnp.zeros((quarter, LANES), F32)
    north_rim, south_rim = [], []
    place_in_tile = lax.broadcasted_iota(jnp.int32, (1, tile), 1)
    for port in range(x_ref.shape[1] // tile):
        own = slice(port * tile, (port + 1) * tile)
        rim = slice(port * LANES, (port + 1) * LANES)
        north = jnp.concatenate(
            [north_in[:, rim].astype(BF), x_ref[0:quarter, port * tile + LANES : (port + 1) * tile]],
            axis=1,
        )
        south = jnp.concatenate(
            [
                x_ref[quarter : 2 * quarter, port * tile : (port + 1) * tile - LANES],
                south_in[:, rim].astype(BF),
            ],
            axis=1,
        )
        west, east = [], []
        for row in range(rows):
            place = port * rows + row
            cols = slice(place * LANES, (place + 1) * LANES)
            value = x_ref[2 * quarter : 3 * quarter, cols].astype(F32)
            west.append(jnp.where(lane == 0, lane_of(west_in, 64 + place), value))
            value = x_ref[3 * quarter :, cols].astype(F32)
            east.append(jnp.where(lane == LANES - 1, lane_of(east_in, place), value))
        west = jnp.concatenate(west, axis=1).astype(BF)
        east = jnp.concatenate(east, axis=1).astype(BF)
        block = jnp.concatenate([north, south, west, east], axis=0)
        row, col, inside = port_place(port_ref, port, rows, width)
        here = place_in_tile == jnp.where(inside, row * width + col, -1)
        current = block.astype(F32)
        added = current + port_profile_column(profile_ref, port)
        block = jnp.where(here, added, current).astype(BF)
        total = products(block, types, maps, 0, order)
        north, south = shifted(total, next_ref.at[:, own], rows)
        north_rim.append(north[:, 0:LANES])
        south_rim.append(south[:, tile - LANES :])
        for row in range(rows):
            place = port * rows + row
            west = lane_of(total[2 * quarter : 3 * quarter], row * LANES)
            east = lane_of(total[3 * quarter :], (row + 1) * LANES - 1)
            west_rim = jnp.where(lane == place, west, west_rim)
            east_rim = jnp.where(lane == place, east, east_rim)
    north_rim, south_rim = (jnp.concatenate(value, axis=1) for value in (north_rim, south_rim))
    store_rims(rim_refs, north_rim, south_rim, west_rim, east_rim)


def last_kernel(rows, width, port_ref, x_ref, profile_ref, *refs):
    out_ref, buffer, sems = refs[4:]
    order, ports = buffer.shape[:2]
    quarter, tile = order // 4, rows * width
    north_in, south_in = halos_inside("row", *refs[:2])
    west_in, east_in = halos_inside("col", *refs[2:4])
    lane = lax.broadcasted_iota(jnp.int32, (quarter, LANES), 1)
    copies = []
    for edge in (2, 3, 0, 1):
        lines = slice(edge * quarter, (edge + 1) * quarter)
        for port in range(ports):
            rim = slice(port * LANES, (port + 1) * LANES)
            starts = [port * tile + row * LANES for row in range(rows)]
            parts = [x_ref[lines, start : start + LANES].astype(F32) for start in starts]
            places = range(port * rows, (port + 1) * rows)
            if edge == 0:
                parts[0] = north_in[:, rim]
            elif edge == 1:
                parts[-1] = south_in[:, rim]
            elif edge == 2:
                parts = [
                    jnp.where(lane == 0, lane_of(west_in, place), part)
                    for place, part in zip(places, parts)
                ]
            else:
                parts = [
                    jnp.where(lane == LANES - 1, lane_of(east_in, place), part)
                    for place, part in zip(places, parts)
                ]
            value = jnp.concatenate(parts, axis=1).reshape(quarter, rows, LANES)
            buffer[lines, port] = value.astype(BF)
        for port in range(ports):
            row, col, inside = port_place(port_ref, port, rows, width)

            @pl.when(inside)
            def _():
                current = buffer[lines, port].astype(F32)
                here = (lax.broadcasted_iota(jnp.int32, current.shape, 1) == row) & (
                    lax.broadcasted_iota(jnp.int32, current.shape, 2) == col
                )
                profile = port_profile_column(profile_ref, port)[lines]
                profile = jnp.broadcast_to(profile, (quarter, LANES)).reshape(quarter, 1, LANES)
                added = current + jnp.broadcast_to(profile, current.shape)
                buffer[lines, port] = jnp.where(here, added, current).astype(BF)

        copy = pltpu.make_async_copy(buffer.at[lines], out_ref.at[lines], sems.at[edge])
        copy.start()
        copies.append(copy)
    for copy in copies:
        copy.wait()


def exchange(rims):
    def pairs(axis, first):
        count = lax.axis_size(axis)
        near = [(i, (i + 1) % count) for i in range(first, count, 2)]
        return near + [(target, source) for source, target in near]

    axes = (("row", 0), ("row", 1), ("col", 0), ("col", 1))
    return [lax.ppermute(rim, axis, pairs(axis, first)) for rim, (axis, first) in zip(rims, axes)]


def body(traces, cell_type, port_cell, port_profile, mode_shapes, mode_values, mode_weights):
    edges, samples, ports, rows, width = traces.shape
    order = edges * samples
    quarter = samples
    tile = rows * width
    types = cell_type.reshape(1, tile)
    own_map, x, sides = own_type_map(mode_shapes, mode_values, mode_weights, traces, types)
    core = lax.rem(lax.axis_index("col"), 2)
    half = lax.dynamic_slice_in_dim(own_map, core * (order // 2), order // 2)
    fetched = [
        swap(own_map, *((step, 8 * (step % 2)) for step in steps)) for steps in MAP_STEPS[1:4]
    ]
    half = swap(half, (4, 0))
    profile = jnp.transpose(port_profile, (0, 2, 1))
    ports_spec = pl.BlockSpec(memory_space=pltpu.SMEM)
    next_shape = jax.ShapeDtypeStruct((order, ports * tile), BF)
    rim_shapes = [jax.ShapeDtypeStruct((quarter, ports * LANES), BF)] * 2 + [
        jax.ShapeDtypeStruct((quarter, LANES), BF)
    ] * 2
    work = 2 * order * order * len(MAP_STEPS) * ports * tile
    part_shapes = [next_shape] + rim_shapes[:2] + [jax.ShapeDtypeStruct((2 * quarter, LANES), BF)]

    def early(first, maps, parts=()):
        last = first + len(maps)
        kernel = functools.partial(early_kernel, ports, first, last)
        flops = work * len(maps) // 7
        return whole_call(kernel, part_shapes, x, types, *sides, *maps, *parts, flops=flops)

    parts = list(early(0, [own_map, fetched[0]]))
    parts[1], fetched = lax.optimization_barrier((parts[1], fetched))
    swapped = [swap_cores(value) for value in fetched]
    parts = list(early(2, fetched[1:], parts))
    parts[1], half = lax.optimization_barrier((parts[1], half))
    swapped.append(swap_cores(half))
    done, *parts = parts
    late = swapped + [half]
    maps = [own_map] + fetched + late
    sent = whole_call(
        functools.partial(rim_kernel, ports, 4),
        rim_shapes,
        x,
        types,
        *sides,
        *late,
        *parts,
        flops=work // 8,
    )
    halos = exchange(sent)
    (x,) = whole_call(
        functools.partial(first_kernel, rows, ports, 4),
        [next_shape],
        x,
        types,
        done,
        *late,
        flops=work // 2,
    )
    operands = [port_cell, x, types, profile, *halos, *maps]
    x, *sent = pl.pallas_call(
        functools.partial(second_kernel, rows, width),
        in_specs=[ports_spec] + [WHOLE] * (len(operands) - 1),
        out_specs=[WHOLE] * 5,
        out_shape=[next_shape] + rim_shapes,
        compiler_params=PARAMS,
        cost_estimate=pl.CostEstimate(flops=work, bytes_accessed=0, transcendentals=0),
    )(*operands)
    operands = [port_cell, x, profile, *exchange(sent)]
    out = pl.pallas_call(
        functools.partial(last_kernel, rows, width),
        in_specs=[ports_spec] + [WHOLE] * (len(operands) - 1),
        out_specs=pl.BlockSpec(memory_space=pl.ANY),
        out_shape=jax.ShapeDtypeStruct((order, ports, rows, width), BF),
        scratch_shapes=[
            pltpu.VMEM((order, ports, rows, width), BF),
            pltpu.SemaphoreType.DMA((4,)),
        ],
        compiler_params=PARAMS,
    )(*operands)
    return out.reshape(traces.shape)


def solution(mesh):
    return jax.shard_map(
        body,
        mesh=mesh,
        in_specs=(
            P(None, None, None, "row", "col"),
            P("row", "col"),
            P(),
            P(),
            P("row", None, "col"),
            P("row", "col"),
            P("row", "col", None),
        ),
        out_specs=P(None, None, None, "row", "col"),
        check_vma=False,
    )
```

```python
import functools
import math

import jax
import jax.numpy as jnp
from jax import lax
from jax.experimental import pallas as pl
from jax.experimental.pallas import tpu as pltpu
from jax.sharding import PartitionSpec as P

BF = jnp.bfloat16
F32 = jnp.float32
LANES = 128
PARAMS = pltpu.CompilerParams(vmem_limit_bytes=20 * 2**20)
WIDE_PARAMS = pltpu.CompilerParams(vmem_limit_bytes=50 * 2**20)


def swap(value, first, second=None):
    second = first if second is None else second
    rows, cols = lax.axis_size("row"), lax.axis_size("col")
    pairs = []
    for row in range(rows):
        for col in range(cols):
            down, along = second if col % 2 else first
            pairs.append((row * cols + col, (row ^ down) * cols + (col ^ along)))
    return lax.ppermute(value, ("row", "col"), pairs)


def swap_cores(value):
    return swap(value, (0, 1))


def flat_kernel(x_hbm, out_ref, x_ref, sems):
    order, ports, rows, width = x_ref.shape
    quarter, tile = order // 4, rows * width
    edges = [slice(edge * quarter, (edge + 1) * quarter) for edge in range(4)]
    copies = [
        pltpu.make_async_copy(x_hbm.at[lines], x_ref.at[lines], sems.at[edge])
        for edge, lines in enumerate(edges)
    ]
    for copy in copies:
        copy.start()
    for copy, lines in zip(copies, edges):
        copy.wait()
        for port in range(ports):
            value = x_ref[lines, port].astype(F32).reshape(quarter, tile)
            out_ref[lines, port * tile : (port + 1) * tile] = value.astype(BF)


def partial_kernel(modes, *refs):
    left, right = [], []
    for ref in refs[:-1]:
        for start in range(0, ref.shape[0], 2 * modes):
            left.append(ref[start : start + modes])
            right.append(ref[start + modes : start + 2 * modes])
    refs[-1][...] = lax.dot_general(
        jnp.concatenate(left, axis=0),
        jnp.concatenate(right, axis=0),
        (((0,), (0,)), ((), ())),
        precision=lax.Precision.HIGHEST,
        preferred_element_type=F32,
    )


WHOLE = pl.BlockSpec(memory_space=pltpu.VMEM)


def whole_call(kernel, shapes, *operands, flops=0):
    return pl.pallas_call(
        kernel,
        in_specs=[WHOLE] * len(operands),
        out_specs=[WHOLE] * len(shapes),
        out_shape=shapes,
        compiler_params=PARAMS,
        cost_estimate=pl.CostEstimate(flops=flops, bytes_accessed=0, transcendentals=0),
    )(*operands)


def own_type_map(mode_shapes, mode_values, mode_weights, traces, types):
    modes, order = mode_weights.shape[1:]
    own = jnp.concatenate([mode_shapes[0].T, mode_weights[0]], axis=0)
    own = own * jnp.concatenate([mode_values[0], jnp.ones((modes,), F32)])[:, None]
    far = swap(own, (0, 4))
    pair = jnp.concatenate([own, swap_cores(own)], axis=0)
    pair, traces = lax.optimization_barrier((pair, traces))
    steps = (((0, 8), (0, 10)), ((0, 2), (0, 14)), ((0, 6), (0, 12)))
    got = [swap(pair, *step) for step in steps]
    shape = (order,) + traces.shape[2:]
    x = pl.pallas_call(
        flat_kernel,
        in_specs=[pl.BlockSpec(memory_space=pltpu.HBM)],
        out_specs=WHOLE,
        out_shape=jax.ShapeDtypeStruct((order, math.prod(shape[1:])), BF),
        scratch_shapes=[pltpu.VMEM(shape, BF), pltpu.SemaphoreType.DMA((4,))],
        compiler_params=WIDE_PARAMS,
        cost_estimate=pl.CostEstimate(flops=2**30, bytes_accessed=0, transcendentals=0),
    )(traces.reshape(shape))
    *got, x = lax.optimization_barrier((*got, x))
    (partial,) = whole_call(
        functools.partial(partial_kernel, modes),
        [jax.ShapeDtypeStruct((order, order), F32)],
        own,
        far,
        *got,
    )
    partial, x = lax.optimization_barrier((partial, x))
    other = swap_cores(partial)
    sides = whole_call(
        functools.partial(sides_kernel, traces.shape[2]),
        [jax.ShapeDtypeStruct((order, LANES), BF), jax.ShapeDtypeStruct((16, LANES), BF)],
        x,
        types,
        flops=2**30,
    )
    other, sides = lax.optimization_barrier((other, sides))
    return (partial + other).astype(BF), x, sides


MAP_STEPS = ((0, 0), (2, 3), (6, 7), (3, 2), (7, 6), (4, 5), (5, 4), (1, 1))


def relay_kernel(first_ref, second_ref, out_ref):
    core = lax.rem(lax.axis_index("col"), 2)
    out_ref[...] = jnp.where(core == 0, second_ref[...], first_ref[...])


def even(axis):
    return lax.rem(lax.axis_index(axis), 2) == 0


def halos_inside(axis, one, two):
    one, two = one[...].astype(F32), two[...].astype(F32)
    index, count = lax.axis_index(axis), lax.axis_size(axis)
    low = jnp.where(even(axis), two, one)
    high = jnp.where(even(axis), one, two)
    return jnp.where(index > 0, low, 0.0), jnp.where(index < count - 1, high, 0.0)


def store_rims(out_refs, north, south, west, east):
    first, second, third, fourth = out_refs
    first[...] = jnp.where(even("row"), south, north).astype(BF)
    second[...] = jnp.where(even("row"), north, south).astype(BF)
    third[...] = jnp.where(even("col"), east, west).astype(BF)
    fourth[...] = jnp.where(even("col"), west, east).astype(BF)


def lane_of(value, lane):
    return jnp.broadcast_to(value[:, lane : lane + 1], (value.shape[0], LANES))


def port_profile_column(profile_ref, port, edge):
    samples = profile_ref.shape[2]
    row = lax.broadcasted_iota(jnp.int32, (samples, samples), 0)
    col = lax.broadcasted_iota(jnp.int32, (samples, samples), 1)
    line = jnp.broadcast_to(profile_ref[edge].astype(F32)[port : port + 1], row.shape)
    return jnp.sum(jnp.where(row == col, line, 0.0), axis=1, keepdims=True)


def port_place(port_ref, port, rows, width):
    all_cols = width * lax.axis_size("col")
    cell = port_ref[port]
    row = cell // all_cols - lax.axis_index("row") * rows
    col = cell % all_cols - lax.axis_index("col") * width
    return row, col, (row >= 0) & (row < rows) & (col >= 0) & (col < width)


def map_rows(map_refs, first, last):
    if len(map_refs) == 1:
        return map_refs[0][first:last, :]
    core = lax.rem(lax.axis_index("col"), 2)
    swapped, own = map_refs[0][...], map_refs[1][...]
    low, high = jnp.where(core == 0, own, swapped), jnp.where(core == 0, swapped, own)
    return jnp.concatenate([low, high], axis=0)[first:last]


def products(x, types, maps, first, last, total=None):
    mine = lax.axis_index("row")
    core = lax.rem(lax.axis_index("col"), 2)
    types = jnp.broadcast_to(types, x.shape)
    for (even, odd), map_refs in maps:
        kind = (mine ^ jnp.where(core == 0, even, odd)).astype(F32).astype(BF)
        masked = jnp.where(types == kind, x, jnp.zeros((), BF))
        part = map_rows(map_refs, first, last)
        product = jnp.dot(part, masked, preferred_element_type=F32)
        total = product if total is None else total + product
    return total


def with_steps(map_refs, first, last):
    refs = [(ref,) for ref in map_refs]
    if last == len(MAP_STEPS):
        refs[-2:] = [refs[-2] + refs[-1]]
    return list(zip(MAP_STEPS[first:last], refs, strict=True))


def shifted(total, next_ref, rows):
    quarter = total.shape[0] // 4
    last = (rows - 1) * LANES
    north = total[0:quarter].astype(BF)
    south = total[quarter : 2 * quarter].astype(BF)
    next_ref[0:quarter, LANES:] = south[:, :last]
    next_ref[0:quarter, 0:LANES] = jnp.zeros((quarter, LANES), BF)
    next_ref[quarter : 2 * quarter, :last] = north[:, LANES:]
    next_ref[quarter : 2 * quarter, last:] = jnp.zeros((quarter, LANES), BF)
    for row in range(rows):
        cols = slice(row * LANES, (row + 1) * LANES)
        west = total[2 * quarter : 3 * quarter, cols]
        east = total[3 * quarter : 4 * quarter, cols]
        next_ref[2 * quarter : 3 * quarter, cols] = pltpu.roll(east, 1, 1).astype(BF)
        next_ref[3 * quarter : 4 * quarter, cols] = pltpu.roll(west, LANES - 1, 1).astype(BF)
    return north, south


def rim_columns(x_ref, types, ports, offset):
    tile = types.shape[1]
    starts = [port * tile + offset for port in range(ports)]
    cells = jnp.concatenate([x_ref[:, start : start + LANES] for start in starts], axis=1)
    return cells, jnp.concatenate([types[:, offset : offset + LANES]] * ports, axis=1).astype(BF)


def side_columns(x_ref, types, ports):
    order, tile = x_ref.shape[0], types.shape[1]
    rows = tile // LANES

    def pick(block_of, lines):
        lane = lax.broadcasted_iota(jnp.int32, (lines, LANES), 1)
        first = last = jnp.zeros((lines, LANES), F32)
        for place in range(ports * rows):
            turned = pltpu.roll(block_of(place), place + 1, 1)
            first = jnp.where(lane == place + 1, turned, first)
            last = jnp.where(lane == place, turned, last)
        first = pltpu.roll(first, LANES - 1, 1)
        return jnp.where(lane < 64, first, pltpu.roll(last, 64, 1)).astype(BF)

    def types_of(place):
        start = place % rows * LANES
        return jnp.broadcast_to(types[:, start : start + LANES], (16, LANES))

    quarter = order // 4
    sides = [
        pick(
            lambda place: x_ref[edge * quarter : (edge + 1) * quarter,
                                place * LANES : (place + 1) * LANES].astype(F32),
            quarter,
        )
        for edge in range(4)
    ]
    return jnp.concatenate(sides, axis=0), pick(types_of, 16)


def rims(x_ref, types, ports, sides, kinds, maps, so_far):
    order, tile = x_ref.shape[0], types.shape[1]
    quarter = order // 4
    before = [None if ref is None else ref[...].astype(F32) for ref in so_far]
    cells, cell_kinds = rim_columns(x_ref, types, ports, 0)
    north = products(cells, cell_kinds, maps, 0, quarter, before[0])
    cells, cell_kinds = rim_columns(x_ref, types, ports, tile - LANES)
    south = products(cells, cell_kinds, maps, quarter, 2 * quarter, before[1])
    side = products(sides, kinds, maps, 2 * quarter, order, before[2])
    return north.astype(BF), south.astype(BF), side.astype(BF)


def sides_kernel(ports, x_ref, types_ref, sides_ref, kinds_ref):
    sides_ref[...], kinds_ref[...] = side_columns(x_ref, types_ref[...].astype(F32), ports)


def early_kernel(ports, first, last, x_ref, types_ref, sides_ref, kinds_ref, *refs):
    maps = with_steps(refs[: last - first], first, last)
    types = types_ref[...].astype(F32)
    tile = types.shape[1]
    so_far, outs = refs[last - first : -4], refs[-4:]
    done_ref, *so_far = so_far if first else [None] * 4
    values = rims(x_ref, types, ports, sides_ref[...], kinds_ref[0:1, :], maps, so_far)
    for ref, value in zip(outs[1:], values):
        ref[...] = value
    for port in range(ports):
        cols = slice(port * tile, (port + 1) * tile)
        before = None if done_ref is None else done_ref[:, cols].astype(F32)
        total = products(x_ref[:, cols], types.astype(BF), maps, 0, x_ref.shape[0], before)
        outs[0][:, cols] = total.astype(BF)


def rim_kernel(ports, first, x_ref, types_ref, sides_ref, kinds_ref, *refs):
    maps = with_steps(refs[:-7], first, len(MAP_STEPS))
    types = types_ref[...].astype(F32)
    quarter = x_ref.shape[0] // 4
    values = rims(x_ref, types, ports, sides_ref[...], kinds_ref[0:1, :], maps, refs[-7:-4])
    store_rims(refs[-4:], values[0], values[1], values[2][0:quarter], values[2][quarter:])


def first_kernel(rows, ports, first, x_ref, types_ref, done_ref, *refs):
    maps = with_steps(refs[:-1], first, len(MAP_STEPS))
    types = types_ref[...].astype(F32).astype(BF)
    tile = types.shape[1]
    for port in range(ports):
        cols = slice(port * tile, (port + 1) * tile)
        before = done_ref[:, cols].astype(F32)
        total = products(x_ref[:, cols], types, maps, 0, x_ref.shape[0], before)
        shifted(total, refs[-1].at[:, cols], rows)


def second_kernel(rows, width, port_ref, x_ref, types_ref, profile_ref, *refs):
    halo_refs, map_refs, next_ref = refs[:4], refs[4:-5], refs[-5]
    rim_refs = refs[-4:]
    types = types_ref[...].astype(F32).astype(BF)
    tile = types.shape[1]
    order = x_ref.shape[0]
    quarter = order // 4
    maps = with_steps(map_refs, 0, len(MAP_STEPS))
    north_in, south_in = halos_inside("row", *halo_refs[:2])
    west_in, east_in = halos_inside("col", *halo_refs[2:])
    lane = lax.broadcasted_iota(jnp.int32, (quarter, LANES), 1)
    west_rim = east_rim = jnp.zeros((quarter, LANES), F32)
    north_rim, south_rim = [], []
    place_in_tile = lax.broadcasted_iota(jnp.int32, (1, tile), 1)
    for port in range(x_ref.shape[1] // tile):
        own = slice(port * tile, (port + 1) * tile)
        rim = slice(port * LANES, (port + 1) * LANES)
        north = jnp.concatenate(
            [north_in[:, rim].astype(BF), x_ref[0:quarter, port * tile + LANES : (port + 1) * tile]],
            axis=1,
        )
        south = jnp.concatenate(
            [
                x_ref[quarter : 2 * quarter, port * tile : (port + 1) * tile - LANES],
                south_in[:, rim].astype(BF),
            ],
            axis=1,
        )
        west, east = [], []
        for row in range(rows):
            place = port * rows + row
            cols = slice(place * LANES, (place + 1) * LANES)
            value = x_ref[2 * quarter : 3 * quarter, cols].astype(F32)
            west.append(jnp.where(lane == 0, lane_of(west_in, 64 + place), value))
            value = x_ref[3 * quarter :, cols].astype(F32)
            east.append(jnp.where(lane == LANES - 1, lane_of(east_in, place), value))
        west = jnp.concatenate(west, axis=1).astype(BF)
        east = jnp.concatenate(east, axis=1).astype(BF)
        block = jnp.concatenate([north, south, west, east], axis=0)
        row, col, inside = port_place(port_ref, port, rows, width)
        here = place_in_tile == jnp.where(inside, row * width + col, -1)
        current = block.astype(F32)
        columns = [port_profile_column(profile_ref, port, edge) for edge in range(4)]
        added = current + jnp.concatenate(columns, axis=0)
        block = jnp.where(here, added, current).astype(BF)
        total = products(block, types, maps, 0, order)
        north, south = shifted(total, next_ref.at[:, own], rows)
        north_rim.append(north[:, 0:LANES])
        south_rim.append(south[:, tile - LANES :])
        for row in range(rows):
            place = port * rows + row
            west = lane_of(total[2 * quarter : 3 * quarter], row * LANES)
            east = lane_of(total[3 * quarter :], (row + 1) * LANES - 1)
            west_rim = jnp.where(lane == place, west, west_rim)
            east_rim = jnp.where(lane == place, east, east_rim)
    north_rim, south_rim = (jnp.concatenate(value, axis=1) for value in (north_rim, south_rim))
    store_rims(rim_refs, north_rim, south_rim, west_rim, east_rim)


def last_kernel(rows, width, port_ref, x_ref, profile_ref, *refs):
    out_ref, buffer, sems = refs[4:]
    order, ports = buffer.shape[:2]
    quarter, tile = order // 4, rows * width
    north_in, south_in = halos_inside("row", *refs[:2])
    west_in, east_in = halos_inside("col", *refs[2:4])
    lane = lax.broadcasted_iota(jnp.int32, (quarter, LANES), 1)
    copies = []
    for edge in (2, 3, 0, 1):
        lines = slice(edge * quarter, (edge + 1) * quarter)
        for port in range(ports):
            rim = slice(port * LANES, (port + 1) * LANES)
            starts = [port * tile + row * LANES for row in range(rows)]
            parts = [x_ref[lines, start : start + LANES].astype(F32) for start in starts]
            places = range(port * rows, (port + 1) * rows)
            if edge == 0:
                parts[0] = north_in[:, rim]
            elif edge == 1:
                parts[-1] = south_in[:, rim]
            elif edge == 2:
                parts = [
                    jnp.where(lane == 0, lane_of(west_in, place), part)
                    for place, part in zip(places, parts)
                ]
            else:
                parts = [
                    jnp.where(lane == LANES - 1, lane_of(east_in, place), part)
                    for place, part in zip(places, parts)
                ]
            value = jnp.concatenate(parts, axis=1).reshape(quarter, rows, LANES)
            buffer[lines, port] = value.astype(BF)
        for port in range(ports):
            row, col, inside = port_place(port_ref, port, rows, width)

            @pl.when(inside)
            def _():
                current = buffer[lines, port].astype(F32)
                here = (lax.broadcasted_iota(jnp.int32, current.shape, 1) == row) & (
                    lax.broadcasted_iota(jnp.int32, current.shape, 2) == col
                )
                profile = port_profile_column(profile_ref, port, edge)
                profile = jnp.broadcast_to(profile, (quarter, LANES)).reshape(quarter, 1, LANES)
                added = current + jnp.broadcast_to(profile, current.shape)
                buffer[lines, port] = jnp.where(here, added, current).astype(BF)

        copy = pltpu.make_async_copy(buffer.at[lines], out_ref.at[lines], sems.at[edge])
        copy.start()
        copies.append(copy)
    for copy in copies:
        copy.wait()


def exchange(rims):
    def pairs(axis, first):
        count = lax.axis_size(axis)
        near = [(i, (i + 1) % count) for i in range(first, count, 2)]
        return near + [(target, source) for source, target in near]

    axes = (("row", 0), ("row", 1), ("col", 0), ("col", 1))
    return [lax.ppermute(rim, axis, pairs(axis, first)) for rim, (axis, first) in zip(rims, axes)]


def body(traces, cell_type, port_cell, port_profile, mode_shapes, mode_values, mode_weights):
    edges, samples, ports, rows, width = traces.shape
    order = edges * samples
    quarter = samples
    tile = rows * width
    types = cell_type.reshape(1, tile)
    own_map, x, sides = own_type_map(mode_shapes, mode_values, mode_weights, traces, types)
    core = lax.rem(lax.axis_index("col"), 2)
    half = lax.dynamic_slice_in_dim(own_map, core * (order // 2), order // 2)
    first = swap(own_map, (2, 0), (3, 8))
    second = swap(own_map, (6, 0), (7, 8))
    half = swap(half, (1, 8))
    profile = jnp.transpose(port_profile, (0, 2, 1))
    ports_spec = pl.BlockSpec(memory_space=pltpu.SMEM)
    next_shape = jax.ShapeDtypeStruct((order, ports * tile), BF)
    rim_shapes = [jax.ShapeDtypeStruct((quarter, ports * LANES), BF)] * 2 + [
        jax.ShapeDtypeStruct((quarter, LANES), BF)
    ] * 2
    work = 2 * order * order * len(MAP_STEPS) * ports * tile
    part_shapes = [next_shape] + rim_shapes[:2] + [jax.ShapeDtypeStruct((2 * quarter, LANES), BF)]

    def early(first, maps, parts=()):
        last = first + len(maps)
        kernel = functools.partial(early_kernel, ports, first, last)
        flops = work * len(maps) // 7
        return whole_call(kernel, part_shapes, x, types, *sides, *maps, *parts, flops=flops)

    parts = list(early(0, [own_map, first]))
    parts[1], first, second = lax.optimization_barrier((parts[1], first, second))
    map_shape = jax.ShapeDtypeStruct(own_map.shape, BF)
    third = swap(whole_call(relay_kernel, [map_shape], first, second)[0], (2, 0), (6, 0))
    maps = [own_map, first, second, swap_cores(first), swap_cores(second)]
    parts = list(early(2, maps[2:], parts))
    parts[1], third, half = lax.optimization_barrier((parts[1], third, half))
    done, *parts = parts
    late = [third, swap_cores(third), swap_cores(half), half]
    maps += late
    sent = whole_call(
        functools.partial(rim_kernel, ports, 5),
        rim_shapes,
        x,
        types,
        *sides,
        *late,
        *parts,
        flops=work // 8,
    )
    halos = exchange(sent)
    (x,) = whole_call(
        functools.partial(first_kernel, rows, ports, 5),
        [next_shape],
        x,
        types,
        done,
        *late,
        flops=work // 2,
    )
    operands = [port_cell, x, types, profile, *halos, *maps]
    x, *sent = pl.pallas_call(
        functools.partial(second_kernel, rows, width),
        in_specs=[ports_spec] + [WHOLE] * (len(operands) - 1),
        out_specs=[WHOLE] * 5,
        out_shape=[next_shape] + rim_shapes,
        compiler_params=PARAMS,
        cost_estimate=pl.CostEstimate(flops=work, bytes_accessed=0, transcendentals=0),
    )(*operands)
    operands = [port_cell, x, profile, *exchange(sent)]
    out = pl.pallas_call(
        functools.partial(last_kernel, rows, width),
        in_specs=[ports_spec] + [WHOLE] * (len(operands) - 1),
        out_specs=pl.BlockSpec(memory_space=pl.ANY),
        out_shape=jax.ShapeDtypeStruct((order, ports, rows, width), BF),
        scratch_shapes=[
            pltpu.VMEM((order, ports, rows, width), BF),
            pltpu.SemaphoreType.DMA((4,)),
        ],
        compiler_params=PARAMS,
    )(*operands)
    return out.reshape(traces.shape)


def solution(mesh):
    return jax.shard_map(
        body,
        mesh=mesh,
        in_specs=(
            P(None, None, None, "row", "col"),
            P("row", "col"),
            P(),
            P(),
            P("row", None, "col"),
            P("row", "col"),
            P("row", "col", None),
        ),
        out_specs=P(None, None, None, "row", "col"),
        check_vma=False,
    )
```

```python
import functools
import math

import jax
import jax.numpy as jnp
from jax import lax
from jax.experimental import pallas as pl
from jax.experimental.pallas import tpu as pltpu
from jax.sharding import PartitionSpec as P

BF = jnp.bfloat16
F32 = jnp.float32
LANES = 128
PARAMS = pltpu.CompilerParams(vmem_limit_bytes=20 * 2**20)
WIDE_PARAMS = pltpu.CompilerParams(vmem_limit_bytes=50 * 2**20)


def swap(value, first, second=None):
    second = first if second is None else second
    rows, cols = lax.axis_size("row"), lax.axis_size("col")
    pairs = []
    for row in range(rows):
        for col in range(cols):
            down, along = second if col % 2 else first
            pairs.append((row * cols + col, (row ^ down) * cols + (col ^ along)))
    return lax.ppermute(value, ("row", "col"), pairs)


def swap_cores(value):
    return swap(value, (0, 1))


def flat_kernel(x_hbm, out_ref, x_ref, sems):
    order, ports, rows, width = x_ref.shape
    quarter, tile = order // 4, rows * width
    edges = [slice(edge * quarter, (edge + 1) * quarter) for edge in range(4)]
    copies = [
        pltpu.make_async_copy(x_hbm.at[lines], x_ref.at[lines], sems.at[edge])
        for edge, lines in enumerate(edges)
    ]
    for copy in copies:
        copy.start()
    for copy, lines in zip(copies, edges):
        copy.wait()
        for port in range(ports):
            value = x_ref[lines, port].astype(F32).reshape(quarter, tile)
            out_ref[lines, port * tile : (port + 1) * tile] = value.astype(BF)


def partial_kernel(modes, *refs):
    left, right = [], []
    for ref in refs[:-1]:
        for start in range(0, ref.shape[0], 2 * modes):
            left.append(ref[start : start + modes])
            right.append(ref[start + modes : start + 2 * modes])
    refs[-1][...] = lax.dot_general(
        jnp.concatenate(left, axis=0),
        jnp.concatenate(right, axis=0),
        (((0,), (0,)), ((), ())),
        precision=lax.Precision.HIGHEST,
        preferred_element_type=F32,
    )


WHOLE = pl.BlockSpec(memory_space=pltpu.VMEM)


def whole_call(kernel, shapes, *operands, flops=0):
    return pl.pallas_call(
        kernel,
        in_specs=[WHOLE] * len(operands),
        out_specs=[WHOLE] * len(shapes),
        out_shape=shapes,
        compiler_params=PARAMS,
        cost_estimate=pl.CostEstimate(flops=flops, bytes_accessed=0, transcendentals=0),
    )(*operands)


def own_type_map(mode_shapes, mode_values, mode_weights, traces, types):
    modes, order = mode_weights.shape[1:]
    own = jnp.concatenate([mode_shapes[0].T, mode_weights[0]], axis=0)
    own = own * jnp.concatenate([mode_values[0], jnp.ones((modes,), F32)])[:, None]
    far = swap(own, (0, 4))
    pair = jnp.concatenate([own, swap_cores(own)], axis=0)
    pair, traces = lax.optimization_barrier((pair, traces))
    steps = (((0, 8), (0, 10)), ((0, 2), (0, 14)), ((0, 6), (0, 12)))
    got = [swap(pair, *step) for step in steps]
    shape = (order,) + traces.shape[2:]
    x = pl.pallas_call(
        flat_kernel,
        in_specs=[pl.BlockSpec(memory_space=pltpu.HBM)],
        out_specs=WHOLE,
        out_shape=jax.ShapeDtypeStruct((order, math.prod(shape[1:])), BF),
        scratch_shapes=[pltpu.VMEM(shape, BF), pltpu.SemaphoreType.DMA((4,))],
        compiler_params=WIDE_PARAMS,
        cost_estimate=pl.CostEstimate(flops=2**30, bytes_accessed=0, transcendentals=0),
    )(traces.reshape(shape))
    *got, x = lax.optimization_barrier((*got, x))
    (partial,) = whole_call(
        functools.partial(partial_kernel, modes),
        [jax.ShapeDtypeStruct((order, order), F32)],
        own,
        far,
        *got,
    )
    partial, x = lax.optimization_barrier((partial, x))
    other = swap_cores(partial)
    sides = whole_call(
        functools.partial(sides_kernel, traces.shape[2]),
        [jax.ShapeDtypeStruct((order, LANES), BF), jax.ShapeDtypeStruct((16, LANES), BF)],
        x,
        types,
        flops=2**30,
    )
    other, sides = lax.optimization_barrier((other, sides))
    shapes = [jax.ShapeDtypeStruct((lines, order), BF) for lines in (order, order // 2)]
    return *whole_call(own_kernel, shapes, partial, other), x, sides


MAP_STEPS = ((0, 0), (2, 3), (6, 7), (3, 2), (7, 6), (1, 1), (4, 5), (5, 4))
HALVES = 5


def own_kernel(one_ref, two_ref, out_ref, half_ref):
    core = lax.rem(lax.axis_index("col"), 2)
    half = half_ref.shape[0]
    total = (one_ref[...] + two_ref[...]).astype(BF)
    out_ref[...] = total
    half_ref[...] = jnp.where(core == 0, total[0:half], total[half:])


def relay_kernel(first_ref, second_ref, out_ref):
    core = lax.rem(lax.axis_index("col"), 2)
    out_ref[...] = jnp.where(core == 0, second_ref[...], first_ref[...])


def even(axis):
    return lax.rem(lax.axis_index(axis), 2) == 0


def halos_inside(axis, one, two):
    one, two = one[...].astype(F32), two[...].astype(F32)
    index, count = lax.axis_index(axis), lax.axis_size(axis)
    low = jnp.where(even(axis), two, one)
    high = jnp.where(even(axis), one, two)
    return jnp.where(index > 0, low, 0.0), jnp.where(index < count - 1, high, 0.0)


def store_rims(out_refs, north, south, west, east):
    first, second, third, fourth = out_refs
    first[...] = jnp.where(even("row"), south, north).astype(BF)
    second[...] = jnp.where(even("row"), north, south).astype(BF)
    third[...] = jnp.where(even("col"), east, west).astype(BF)
    fourth[...] = jnp.where(even("col"), west, east).astype(BF)


def lane_of(value, lane):
    return jnp.broadcast_to(value[:, lane : lane + 1], (value.shape[0], LANES))


def port_profile_column(profile_ref, port, edge):
    samples = profile_ref.shape[2]
    row = lax.broadcasted_iota(jnp.int32, (samples, samples), 0)
    col = lax.broadcasted_iota(jnp.int32, (samples, samples), 1)
    line = jnp.broadcast_to(profile_ref[edge].astype(F32)[port : port + 1], row.shape)
    return jnp.sum(jnp.where(row == col, line, 0.0), axis=1, keepdims=True)


def port_place(port_ref, port, rows, width):
    all_cols = width * lax.axis_size("col")
    cell = port_ref[port]
    row = cell // all_cols - lax.axis_index("row") * rows
    col = cell % all_cols - lax.axis_index("col") * width
    return row, col, (row >= 0) & (row < rows) & (col >= 0) & (col < width)


def map_rows(map_refs, first, last):
    if len(map_refs) == 1:
        return map_refs[0][first:last, :]
    core = lax.rem(lax.axis_index("col"), 2)
    swapped, own = map_refs[0][...], map_refs[1][...]
    low, high = jnp.where(core == 0, own, swapped), jnp.where(core == 0, swapped, own)
    return jnp.concatenate([low, high], axis=0)[first:last]


def products(x, types, maps, first, last, total=None):
    mine = lax.axis_index("row")
    core = lax.rem(lax.axis_index("col"), 2)
    types = jnp.broadcast_to(types, x.shape)
    for (even, odd), map_refs in maps:
        kind = (mine ^ jnp.where(core == 0, even, odd)).astype(F32).astype(BF)
        masked = jnp.where(types == kind, x, jnp.zeros((), BF))
        part = map_rows(map_refs, first, last)
        product = jnp.dot(part, masked, preferred_element_type=F32)
        total = product if total is None else total + product
    return total


def with_steps(map_refs, first):
    map_refs, maps = list(map_refs), []
    while map_refs:
        number = first + len(maps)
        count = 2 if number == HALVES else 1
        maps.append((MAP_STEPS[number], map_refs[:count]))
        del map_refs[:count]
    return maps


def shifted(total, next_ref, rows):
    quarter = total.shape[0] // 4
    last = (rows - 1) * LANES
    north = total[0:quarter].astype(BF)
    south = total[quarter : 2 * quarter].astype(BF)
    next_ref[0:quarter, LANES:] = south[:, :last]
    next_ref[0:quarter, 0:LANES] = jnp.zeros((quarter, LANES), BF)
    next_ref[quarter : 2 * quarter, :last] = north[:, LANES:]
    next_ref[quarter : 2 * quarter, last:] = jnp.zeros((quarter, LANES), BF)
    for row in range(rows):
        cols = slice(row * LANES, (row + 1) * LANES)
        west = total[2 * quarter : 3 * quarter, cols]
        east = total[3 * quarter : 4 * quarter, cols]
        next_ref[2 * quarter : 3 * quarter, cols] = pltpu.roll(east, 1, 1).astype(BF)
        next_ref[3 * quarter : 4 * quarter, cols] = pltpu.roll(west, LANES - 1, 1).astype(BF)
    return north, south


def rim_columns(x_ref, types, ports, offset):
    tile = types.shape[1]
    starts = [port * tile + offset for port in range(ports)]
    cells = jnp.concatenate([x_ref[:, start : start + LANES] for start in starts], axis=1)
    return cells, jnp.concatenate([types[:, offset : offset + LANES]] * ports, axis=1).astype(BF)


def side_columns(x_ref, types, ports):
    order, tile = x_ref.shape[0], types.shape[1]
    rows = tile // LANES

    def pick(block_of, lines):
        lane = lax.broadcasted_iota(jnp.int32, (lines, LANES), 1)
        first = last = jnp.zeros((lines, LANES), F32)
        for place in range(ports * rows):
            turned = pltpu.roll(block_of(place), place + 1, 1)
            first = jnp.where(lane == place + 1, turned, first)
            last = jnp.where(lane == place, turned, last)
        first = pltpu.roll(first, LANES - 1, 1)
        return jnp.where(lane < 64, first, pltpu.roll(last, 64, 1)).astype(BF)

    def types_of(place):
        start = place % rows * LANES
        return jnp.broadcast_to(types[:, start : start + LANES], (16, LANES))

    quarter = order // 4
    sides = [
        pick(
            lambda place: x_ref[edge * quarter : (edge + 1) * quarter,
                                place * LANES : (place + 1) * LANES].astype(F32),
            quarter,
        )
        for edge in range(4)
    ]
    return jnp.concatenate(sides, axis=0), pick(types_of, 16)


def rims(x_ref, types, ports, sides, kinds, maps, so_far):
    order, tile = x_ref.shape[0], types.shape[1]
    quarter = order // 4
    before = [None if ref is None else ref[...].astype(F32) for ref in so_far]
    cells, cell_kinds = rim_columns(x_ref, types, ports, 0)
    north = products(cells, cell_kinds, maps, 0, quarter, before[0])
    cells, cell_kinds = rim_columns(x_ref, types, ports, tile - LANES)
    south = products(cells, cell_kinds, maps, quarter, 2 * quarter, before[1])
    side = products(sides, kinds, maps, 2 * quarter, order, before[2])
    return north.astype(BF), south.astype(BF), side.astype(BF)


def sides_kernel(ports, x_ref, types_ref, sides_ref, kinds_ref):
    sides_ref[...], kinds_ref[...] = side_columns(x_ref, types_ref[...].astype(F32), ports)


def early_kernel(ports, first, count, x_ref, types_ref, sides_ref, kinds_ref, *refs):
    maps = with_steps(refs[:count], first)
    types = types_ref[...].astype(F32)
    tile = types.shape[1]
    so_far, outs = refs[count:-4], refs[-4:]
    done_ref, *so_far = so_far if first else [None] * 4
    values = rims(x_ref, types, ports, sides_ref[...], kinds_ref[0:1, :], maps, so_far)
    for ref, value in zip(outs[1:], values):
        ref[...] = value
    for port in range(ports):
        cols = slice(port * tile, (port + 1) * tile)
        before = None if done_ref is None else done_ref[:, cols].astype(F32)
        total = products(x_ref[:, cols], types.astype(BF), maps, 0, x_ref.shape[0], before)
        outs[0][:, cols] = total.astype(BF)


def rim_kernel(ports, first, x_ref, types_ref, sides_ref, kinds_ref, *refs):
    maps = with_steps(refs[:-7], first)
    types = types_ref[...].astype(F32)
    quarter = x_ref.shape[0] // 4
    values = rims(x_ref, types, ports, sides_ref[...], kinds_ref[0:1, :], maps, refs[-7:-4])
    store_rims(refs[-4:], values[0], values[1], values[2][0:quarter], values[2][quarter:])


def first_kernel(rows, ports, first, x_ref, types_ref, done_ref, *refs):
    maps = with_steps(refs[:-1], first)
    types = types_ref[...].astype(F32).astype(BF)
    tile = types.shape[1]
    for port in range(ports):
        cols = slice(port * tile, (port + 1) * tile)
        before = done_ref[:, cols].astype(F32)
        total = products(x_ref[:, cols], types, maps, 0, x_ref.shape[0], before)
        shifted(total, refs[-1].at[:, cols], rows)


def second_kernel(rows, width, port_ref, x_ref, types_ref, profile_ref, *refs):
    halo_refs, map_refs, next_ref = refs[:4], refs[4:-5], refs[-5]
    rim_refs = refs[-4:]
    types = types_ref[...].astype(F32).astype(BF)
    tile = types.shape[1]
    order = x_ref.shape[0]
    quarter = order // 4
    maps = with_steps(map_refs, 0)
    north_in, south_in = halos_inside("row", *halo_refs[:2])
    west_in, east_in = halos_inside("col", *halo_refs[2:])
    lane = lax.broadcasted_iota(jnp.int32, (quarter, LANES), 1)
    west_rim = east_rim = jnp.zeros((quarter, LANES), F32)
    north_rim, south_rim = [], []
    place_in_tile = lax.broadcasted_iota(jnp.int32, (1, tile), 1)
    for port in range(x_ref.shape[1] // tile):
        own = slice(port * tile, (port + 1) * tile)
        rim = slice(port * LANES, (port + 1) * LANES)
        north = jnp.concatenate(
            [north_in[:, rim].astype(BF), x_ref[0:quarter, port * tile + LANES : (port + 1) * tile]],
            axis=1,
        )
        south = jnp.concatenate(
            [
                x_ref[quarter : 2 * quarter, port * tile : (port + 1) * tile - LANES],
                south_in[:, rim].astype(BF),
            ],
            axis=1,
        )
        west, east = [], []
        for row in range(rows):
            place = port * rows + row
            cols = slice(place * LANES, (place + 1) * LANES)
            value = x_ref[2 * quarter : 3 * quarter, cols].astype(F32)
            west.append(jnp.where(lane == 0, lane_of(west_in, 64 + place), value))
            value = x_ref[3 * quarter :, cols].astype(F32)
            east.append(jnp.where(lane == LANES - 1, lane_of(east_in, place), value))
        west = jnp.concatenate(west, axis=1).astype(BF)
        east = jnp.concatenate(east, axis=1).astype(BF)
        block = jnp.concatenate([north, south, west, east], axis=0)
        row, col, inside = port_place(port_ref, port, rows, width)
        here = place_in_tile == jnp.where(inside, row * width + col, -1)
        current = block.astype(F32)
        columns = [port_profile_column(profile_ref, port, edge) for edge in range(4)]
        added = current + jnp.concatenate(columns, axis=0)
        block = jnp.where(here, added, current).astype(BF)
        total = products(block, types, maps, 0, order)
        north, south = shifted(total, next_ref.at[:, own], rows)
        north_rim.append(north[:, 0:LANES])
        south_rim.append(south[:, tile - LANES :])
        for row in range(rows):
            place = port * rows + row
            west = lane_of(total[2 * quarter : 3 * quarter], row * LANES)
            east = lane_of(total[3 * quarter :], (row + 1) * LANES - 1)
            west_rim = jnp.where(lane == place, west, west_rim)
            east_rim = jnp.where(lane == place, east, east_rim)
    north_rim, south_rim = (jnp.concatenate(value, axis=1) for value in (north_rim, south_rim))
    store_rims(rim_refs, north_rim, south_rim, west_rim, east_rim)


def last_kernel(rows, width, port_ref, x_ref, profile_ref, *refs):
    out_ref, buffer, sems = refs[4:]
    order, ports = buffer.shape[:2]
    quarter, tile = order // 4, rows * width
    north_in, south_in = halos_inside("row", *refs[:2])
    west_in, east_in = halos_inside("col", *refs[2:4])
    lane = lax.broadcasted_iota(jnp.int32, (quarter, LANES), 1)
    copies = []
    for edge in (2, 3, 0, 1):
        lines = slice(edge * quarter, (edge + 1) * quarter)
        for port in range(ports):
            rim = slice(port * LANES, (port + 1) * LANES)
            starts = [port * tile + row * LANES for row in range(rows)]
            parts = [x_ref[lines, start : start + LANES].astype(F32) for start in starts]
            places = range(port * rows, (port + 1) * rows)
            if edge == 0:
                parts[0] = north_in[:, rim]
            elif edge == 1:
                parts[-1] = south_in[:, rim]
            elif edge == 2:
                parts = [
                    jnp.where(lane == 0, lane_of(west_in, place), part)
                    for place, part in zip(places, parts)
                ]
            else:
                parts = [
                    jnp.where(lane == LANES - 1, lane_of(east_in, place), part)
                    for place, part in zip(places, parts)
                ]
            value = jnp.concatenate(parts, axis=1).reshape(quarter, rows, LANES)
            buffer[lines, port] = value.astype(BF)
        for port in range(ports):
            row, col, inside = port_place(port_ref, port, rows, width)

            @pl.when(inside)
            def _():
                current = buffer[lines, port].astype(F32)
                here = (lax.broadcasted_iota(jnp.int32, current.shape, 1) == row) & (
                    lax.broadcasted_iota(jnp.int32, current.shape, 2) == col
                )
                profile = port_profile_column(profile_ref, port, edge)
                profile = jnp.broadcast_to(profile, (quarter, LANES)).reshape(quarter, 1, LANES)
                added = current + jnp.broadcast_to(profile, current.shape)
                buffer[lines, port] = jnp.where(here, added, current).astype(BF)

        copy = pltpu.make_async_copy(buffer.at[lines], out_ref.at[lines], sems.at[edge])
        copy.start()
        copies.append(copy)
    for copy in copies:
        copy.wait()


def exchange(rims):
    def pairs(axis, first):
        count = lax.axis_size(axis)
        near = [(i, (i + 1) % count) for i in range(first, count, 2)]
        return near + [(target, source) for source, target in near]

    axes = (("row", 0), ("row", 1), ("col", 0), ("col", 1))
    return [lax.ppermute(rim, axis, pairs(axis, first)) for rim, (axis, first) in zip(rims, axes)]


def body(traces, cell_type, port_cell, port_profile, mode_shapes, mode_values, mode_weights):
    edges, samples, ports, rows, width = traces.shape
    order = edges * samples
    quarter = samples
    tile = rows * width
    types = cell_type.reshape(1, tile)
    own_map, half, x, sides = own_type_map(mode_shapes, mode_values, mode_weights, traces, types)
    first = swap(own_map, (2, 0), (3, 8))
    second = swap(own_map, (6, 0), (7, 8))
    half = swap(half, (1, 8))
    profile = jnp.transpose(port_profile, (0, 2, 1))
    ports_spec = pl.BlockSpec(memory_space=pltpu.SMEM)
    next_shape = jax.ShapeDtypeStruct((order, ports * tile), BF)
    rim_shapes = [jax.ShapeDtypeStruct((quarter, ports * LANES), BF)] * 2 + [
        jax.ShapeDtypeStruct((quarter, LANES), BF)
    ] * 2
    work = 2 * order * order * len(MAP_STEPS) * ports * tile
    part_shapes = [next_shape] + rim_shapes[:2] + [jax.ShapeDtypeStruct((2 * quarter, LANES), BF)]

    def early(first, maps, parts=()):
        kernel = functools.partial(early_kernel, ports, first, len(maps))
        flops = work * len(maps) // 7
        return whole_call(kernel, part_shapes, x, types, *sides, *maps, *parts, flops=flops)

    parts = list(early(0, [own_map, first]))
    parts[1], first, second, half = lax.optimization_barrier((parts[1], first, second, half))
    map_shape = jax.ShapeDtypeStruct(own_map.shape, BF)
    (relay,) = whole_call(relay_kernel, [map_shape], first, second)
    relay, first, second, half = lax.optimization_barrier((relay, first, second, half))
    third = swap(relay, (2, 0), (6, 0))
    maps = [second, swap_cores(first), swap_cores(second), swap_cores(half), half]
    parts = list(early(2, maps, parts))
    parts[1], third = lax.optimization_barrier((parts[1], third))
    done, *parts = parts
    late = [third, swap_cores(third)]
    maps = [own_map, first] + maps + late
    sent = whole_call(
        functools.partial(rim_kernel, ports, 6),
        rim_shapes,
        x,
        types,
        *sides,
        *late,
        *parts,
        flops=work // 8,
    )
    halos = exchange(sent)
    (x,) = whole_call(
        functools.partial(first_kernel, rows, ports, 6),
        [next_shape],
        x,
        types,
        done,
        *late,
        flops=work // 2,
    )
    operands = [port_cell, x, types, profile, *halos, *maps]
    x, *sent = pl.pallas_call(
        functools.partial(second_kernel, rows, width),
        in_specs=[ports_spec] + [WHOLE] * (len(operands) - 1),
        out_specs=[WHOLE] * 5,
        out_shape=[next_shape] + rim_shapes,
        compiler_params=PARAMS,
        cost_estimate=pl.CostEstimate(flops=work, bytes_accessed=0, transcendentals=0),
    )(*operands)
    operands = [port_cell, x, profile, *exchange(sent)]
    out = pl.pallas_call(
        functools.partial(last_kernel, rows, width),
        in_specs=[ports_spec] + [WHOLE] * (len(operands) - 1),
        out_specs=pl.BlockSpec(memory_space=pl.ANY),
        out_shape=jax.ShapeDtypeStruct((order, ports, rows, width), BF),
        scratch_shapes=[
            pltpu.VMEM((order, ports, rows, width), BF),
            pltpu.SemaphoreType.DMA((4,)),
        ],
        compiler_params=PARAMS,
    )(*operands)
    return out.reshape(traces.shape)


def solution(mesh):
    return jax.shard_map(
        body,
        mesh=mesh,
        in_specs=(
            P(None, None, None, "row", "col"),
            P("row", "col"),
            P(),
            P(),
            P("row", None, "col"),
            P("row", "col"),
            P("row", "col", None),
        ),
        out_specs=P(None, None, None, "row", "col"),
        check_vma=False,
    )
```

```python
import functools
import math

import jax
import jax.numpy as jnp
from jax import lax
from jax.experimental import pallas as pl
from jax.experimental.pallas import tpu as pltpu
from jax.sharding import PartitionSpec as P

BF = jnp.bfloat16
F32 = jnp.float32
LANES = 128
PARAMS = pltpu.CompilerParams(vmem_limit_bytes=20 * 2**20)
WIDE_PARAMS = pltpu.CompilerParams(vmem_limit_bytes=50 * 2**20)


def swap(value, first, second=None):
    second = first if second is None else second
    rows, cols = lax.axis_size("row"), lax.axis_size("col")
    pairs = []
    for row in range(rows):
        for col in range(cols):
            down, along = second if col % 2 else first
            pairs.append((row * cols + col, (row ^ down) * cols + (col ^ along)))
    return lax.ppermute(value, ("row", "col"), pairs)


def swap_cores(value):
    return swap(value, (0, 1))


def flat_kernel(x_hbm, out_ref, x_ref, sems):
    order, ports, rows, width = x_ref.shape
    quarter, tile = order // 4, rows * width
    edges = [slice(edge * quarter, (edge + 1) * quarter) for edge in range(4)]
    copies = [
        pltpu.make_async_copy(x_hbm.at[lines], x_ref.at[lines], sems.at[edge])
        for edge, lines in enumerate(edges)
    ]
    for copy in copies:
        copy.start()
    for copy, lines in zip(copies, edges):
        copy.wait()
        for port in range(ports):
            value = x_ref[lines, port].astype(F32).reshape(quarter, tile)
            out_ref[lines, port * tile : (port + 1) * tile] = value.astype(BF)


def partial_kernel(modes, *refs):
    left, right = [], []
    for ref in refs[:-1]:
        for start in range(0, ref.shape[0], 2 * modes):
            left.append(ref[start : start + modes])
            right.append(ref[start + modes : start + 2 * modes])
    refs[-1][...] = lax.dot_general(
        jnp.concatenate(left, axis=0),
        jnp.concatenate(right, axis=0),
        (((0,), (0,)), ((), ())),
        precision=lax.Precision.HIGHEST,
        preferred_element_type=F32,
    )


WHOLE = pl.BlockSpec(memory_space=pltpu.VMEM)


def whole_call(kernel, shapes, *operands, flops=0):
    return pl.pallas_call(
        kernel,
        in_specs=[WHOLE] * len(operands),
        out_specs=[WHOLE] * len(shapes),
        out_shape=shapes,
        compiler_params=PARAMS,
        cost_estimate=pl.CostEstimate(flops=flops, bytes_accessed=0, transcendentals=0),
    )(*operands)


def own_type_map(mode_shapes, mode_values, mode_weights, traces, types):
    modes, order = mode_weights.shape[1:]
    own = jnp.concatenate([mode_shapes[0].T, mode_weights[0]], axis=0)
    own = own * jnp.concatenate([mode_values[0], jnp.ones((modes,), F32)])[:, None]
    far = swap(own, (0, 4))
    pair = jnp.concatenate([own, swap_cores(own)], axis=0)
    pair, traces = lax.optimization_barrier((pair, traces))
    steps = (((0, 8), (0, 10)), ((0, 2), (0, 14)), ((0, 6), (0, 12)))
    got = [swap(pair, *step) for step in steps]
    shape = (order,) + traces.shape[2:]
    x = pl.pallas_call(
        flat_kernel,
        in_specs=[pl.BlockSpec(memory_space=pltpu.HBM)],
        out_specs=WHOLE,
        out_shape=jax.ShapeDtypeStruct((order, math.prod(shape[1:])), BF),
        scratch_shapes=[pltpu.VMEM(shape, BF), pltpu.SemaphoreType.DMA((4,))],
        compiler_params=WIDE_PARAMS,
        cost_estimate=pl.CostEstimate(flops=2**30, bytes_accessed=0, transcendentals=0),
    )(traces.reshape(shape))
    *got, x = lax.optimization_barrier((*got, x))
    (partial,) = whole_call(
        functools.partial(partial_kernel, modes),
        [jax.ShapeDtypeStruct((order, order), F32)],
        own,
        far,
        *got,
    )
    partial, x = lax.optimization_barrier((partial, x))
    other = swap_cores(partial)
    sides = whole_call(
        functools.partial(sides_kernel, traces.shape[2]),
        [jax.ShapeDtypeStruct((order, LANES), BF), jax.ShapeDtypeStruct((16, LANES), BF)],
        x,
        types,
        flops=2**30,
    )
    other, sides = lax.optimization_barrier((other, sides))
    return (partial + other).astype(BF), x, sides


MAP_STEPS = ((0, 0), (1, 3), (2, 7), (6, 5), (3, 1), (7, 2), (5, 6), (4, 4))


def even(axis):
    return lax.rem(lax.axis_index(axis), 2) == 0


def halos_inside(axis, one, two):
    one, two = one[...].astype(F32), two[...].astype(F32)
    index, count = lax.axis_index(axis), lax.axis_size(axis)
    low = jnp.where(even(axis), two, one)
    high = jnp.where(even(axis), one, two)
    return jnp.where(index > 0, low, 0.0), jnp.where(index < count - 1, high, 0.0)


def store_rims(out_refs, north, south, west, east):
    first, second, third, fourth = out_refs
    first[...] = jnp.where(even("row"), south, north).astype(BF)
    second[...] = jnp.where(even("row"), north, south).astype(BF)
    third[...] = jnp.where(even("col"), east, west).astype(BF)
    fourth[...] = jnp.where(even("col"), west, east).astype(BF)


def lane_of(value, lane):
    return jnp.broadcast_to(value[:, lane : lane + 1], (value.shape[0], LANES))


def port_profile_column(profile_ref, port, edge):
    samples = profile_ref.shape[2]
    row = lax.broadcasted_iota(jnp.int32, (samples, samples), 0)
    col = lax.broadcasted_iota(jnp.int32, (samples, samples), 1)
    line = jnp.broadcast_to(profile_ref[edge].astype(F32)[port : port + 1], row.shape)
    return jnp.sum(jnp.where(row == col, line, 0.0), axis=1, keepdims=True)


def port_place(port_ref, port, rows, width):
    all_cols = width * lax.axis_size("col")
    cell = port_ref[port]
    row = cell // all_cols - lax.axis_index("row") * rows
    col = cell % all_cols - lax.axis_index("col") * width
    return row, col, (row >= 0) & (row < rows) & (col >= 0) & (col < width)


def map_rows(map_refs, first, last):
    if len(map_refs) == 1:
        return map_refs[0][first:last, :]
    core = lax.rem(lax.axis_index("col"), 2)
    swapped, own = map_refs[0][...], map_refs[1][...]
    low, high = jnp.where(core == 0, own, swapped), jnp.where(core == 0, swapped, own)
    return jnp.concatenate([low, high], axis=0)[first:last]


def products(x, types, maps, first, last, total=None):
    mine = lax.axis_index("row")
    core = lax.rem(lax.axis_index("col"), 2)
    types = jnp.broadcast_to(types, x.shape)
    for (even, odd), map_refs in maps:
        kind = (mine ^ jnp.where(core == 0, even, odd)).astype(F32).astype(BF)
        masked = jnp.where(types == kind, x, jnp.zeros((), BF))
        part = map_rows(map_refs, first, last)
        product = jnp.dot(part, masked, preferred_element_type=F32)
        total = product if total is None else total + product
    return total


def with_steps(map_refs, first, last):
    refs = [(ref,) for ref in map_refs]
    if last == len(MAP_STEPS):
        refs[-2:] = [refs[-2] + refs[-1]]
    return list(zip(MAP_STEPS[first:last], refs, strict=True))


def shifted(total, next_ref, rows):
    quarter = total.shape[0] // 4
    last = (rows - 1) * LANES
    north = total[0:quarter].astype(BF)
    south = total[quarter : 2 * quarter].astype(BF)
    next_ref[0:quarter, LANES:] = south[:, :last]
    next_ref[0:quarter, 0:LANES] = jnp.zeros((quarter, LANES), BF)
    next_ref[quarter : 2 * quarter, :last] = north[:, LANES:]
    next_ref[quarter : 2 * quarter, last:] = jnp.zeros((quarter, LANES), BF)
    for row in range(rows):
        cols = slice(row * LANES, (row + 1) * LANES)
        west = total[2 * quarter : 3 * quarter, cols]
        east = total[3 * quarter : 4 * quarter, cols]
        next_ref[2 * quarter : 3 * quarter, cols] = pltpu.roll(east, 1, 1).astype(BF)
        next_ref[3 * quarter : 4 * quarter, cols] = pltpu.roll(west, LANES - 1, 1).astype(BF)
    return north, south


def rim_columns(x_ref, types, ports, offset):
    tile = types.shape[1]
    starts = [port * tile + offset for port in range(ports)]
    cells = jnp.concatenate([x_ref[:, start : start + LANES] for start in starts], axis=1)
    return cells, jnp.concatenate([types[:, offset : offset + LANES]] * ports, axis=1).astype(BF)


def side_columns(x_ref, types, ports):
    order, tile = x_ref.shape[0], types.shape[1]
    rows = tile // LANES

    def pick(block_of, lines):
        lane = lax.broadcasted_iota(jnp.int32, (lines, LANES), 1)
        first = last = jnp.zeros((lines, LANES), F32)
        for place in range(ports * rows):
            turned = pltpu.roll(block_of(place), place + 1, 1)
            first = jnp.where(lane == place + 1, turned, first)
            last = jnp.where(lane == place, turned, last)
        first = pltpu.roll(first, LANES - 1, 1)
        return jnp.where(lane < 64, first, pltpu.roll(last, 64, 1)).astype(BF)

    def types_of(place):
        start = place % rows * LANES
        return jnp.broadcast_to(types[:, start : start + LANES], (16, LANES))

    quarter = order // 4
    sides = [
        pick(
            lambda place: x_ref[edge * quarter : (edge + 1) * quarter,
                                place * LANES : (place + 1) * LANES].astype(F32),
            quarter,
        )
        for edge in range(4)
    ]
    return jnp.concatenate(sides, axis=0), pick(types_of, 16)


def rims(x_ref, types, ports, sides, kinds, maps, so_far):
    order, tile = x_ref.shape[0], types.shape[1]
    quarter = order // 4
    before = [None if ref is None else ref[...].astype(F32) for ref in so_far]
    cells, cell_kinds = rim_columns(x_ref, types, ports, 0)
    north = products(cells, cell_kinds, maps, 0, quarter, before[0])
    cells, cell_kinds = rim_columns(x_ref, types, ports, tile - LANES)
    south = products(cells, cell_kinds, maps, quarter, 2 * quarter, before[1])
    side = products(sides, kinds, maps, 2 * quarter, order, before[2])
    return north.astype(BF), south.astype(BF), side.astype(BF)


def sides_kernel(ports, x_ref, types_ref, sides_ref, kinds_ref):
    sides_ref[...], kinds_ref[...] = side_columns(x_ref, types_ref[...].astype(F32), ports)


def early_kernel(ports, first, last, x_ref, types_ref, sides_ref, kinds_ref, *refs):
    maps = with_steps(refs[: last - first], first, last)
    types = types_ref[...].astype(F32)
    tile = types.shape[1]
    so_far, outs = refs[last - first : -4], refs[-4:]
    done_ref, *so_far = so_far if first else [None] * 4
    values = rims(x_ref, types, ports, sides_ref[...], kinds_ref[0:1, :], maps, so_far)
    for ref, value in zip(outs[1:], values):
        ref[...] = value
    for port in range(ports):
        cols = slice(port * tile, (port + 1) * tile)
        before = None if done_ref is None else done_ref[:, cols].astype(F32)
        total = products(x_ref[:, cols], types.astype(BF), maps, 0, x_ref.shape[0], before)
        outs[0][:, cols] = total.astype(BF)


def rim_kernel(ports, first, x_ref, types_ref, sides_ref, kinds_ref, *refs):
    maps = with_steps(refs[:-7], first, len(MAP_STEPS))
    types = types_ref[...].astype(F32)
    quarter = x_ref.shape[0] // 4
    values = rims(x_ref, types, ports, sides_ref[...], kinds_ref[0:1, :], maps, refs[-7:-4])
    store_rims(refs[-4:], values[0], values[1], values[2][0:quarter], values[2][quarter:])


def first_kernel(rows, ports, first, x_ref, types_ref, done_ref, *refs):
    maps = with_steps(refs[:-1], first, len(MAP_STEPS))
    types = types_ref[...].astype(F32).astype(BF)
    tile = types.shape[1]
    for port in range(ports):
        cols = slice(port * tile, (port + 1) * tile)
        before = done_ref[:, cols].astype(F32)
        total = products(x_ref[:, cols], types, maps, 0, x_ref.shape[0], before)
        shifted(total, refs[-1].at[:, cols], rows)


def second_kernel(rows, width, port_ref, x_ref, types_ref, profile_ref, *refs):
    halo_refs, map_refs, next_ref = refs[:4], refs[4:-5], refs[-5]
    rim_refs = refs[-4:]
    types = types_ref[...].astype(F32).astype(BF)
    tile = types.shape[1]
    order = x_ref.shape[0]
    quarter = order // 4
    maps = with_steps(map_refs, 0, len(MAP_STEPS))
    north_in, south_in = halos_inside("row", *halo_refs[:2])
    west_in, east_in = halos_inside("col", *halo_refs[2:])
    lane = lax.broadcasted_iota(jnp.int32, (quarter, LANES), 1)
    west_rim = east_rim = jnp.zeros((quarter, LANES), F32)
    north_rim, south_rim = [], []
    place_in_tile = lax.broadcasted_iota(jnp.int32, (1, tile), 1)
    for port in range(x_ref.shape[1] // tile):
        own = slice(port * tile, (port + 1) * tile)
        rim = slice(port * LANES, (port + 1) * LANES)
        north = jnp.concatenate(
            [north_in[:, rim].astype(BF), x_ref[0:quarter, port * tile + LANES : (port + 1) * tile]],
            axis=1,
        )
        south = jnp.concatenate(
            [
                x_ref[quarter : 2 * quarter, port * tile : (port + 1) * tile - LANES],
                south_in[:, rim].astype(BF),
            ],
            axis=1,
        )
        west, east = [], []
        for row in range(rows):
            place = port * rows + row
            cols = slice(place * LANES, (place + 1) * LANES)
            value = x_ref[2 * quarter : 3 * quarter, cols].astype(F32)
            west.append(jnp.where(lane == 0, lane_of(west_in, 64 + place), value))
            value = x_ref[3 * quarter :, cols].astype(F32)
            east.append(jnp.where(lane == LANES - 1, lane_of(east_in, place), value))
        west = jnp.concatenate(west, axis=1).astype(BF)
        east = jnp.concatenate(east, axis=1).astype(BF)
        block = jnp.concatenate([north, south, west, east], axis=0)
        row, col, inside = port_place(port_ref, port, rows, width)
        here = place_in_tile == jnp.where(inside, row * width + col, -1)
        current = block.astype(F32)
        columns = [port_profile_column(profile_ref, port, edge) for edge in range(4)]
        added = current + jnp.concatenate(columns, axis=0)
        block = jnp.where(here, added, current).astype(BF)
        total = products(block, types, maps, 0, order)
        north, south = shifted(total, next_ref.at[:, own], rows)
        north_rim.append(north[:, 0:LANES])
        south_rim.append(south[:, tile - LANES :])
        for row in range(rows):
            place = port * rows + row
            west = lane_of(total[2 * quarter : 3 * quarter], row * LANES)
            east = lane_of(total[3 * quarter :], (row + 1) * LANES - 1)
            west_rim = jnp.where(lane == place, west, west_rim)
            east_rim = jnp.where(lane == place, east, east_rim)
    north_rim, south_rim = (jnp.concatenate(value, axis=1) for value in (north_rim, south_rim))
    store_rims(rim_refs, north_rim, south_rim, west_rim, east_rim)


def last_kernel(rows, width, port_ref, x_ref, profile_ref, *refs):
    out_ref, buffer, sems = refs[4:]
    order, ports = buffer.shape[:2]
    quarter, tile = order // 4, rows * width
    north_in, south_in = halos_inside("row", *refs[:2])
    west_in, east_in = halos_inside("col", *refs[2:4])
    lane = lax.broadcasted_iota(jnp.int32, (quarter, LANES), 1)
    copies = []
    for edge in (2, 3, 0, 1):
        lines = slice(edge * quarter, (edge + 1) * quarter)
        for port in range(ports):
            rim = slice(port * LANES, (port + 1) * LANES)
            starts = [port * tile + row * LANES for row in range(rows)]
            parts = [x_ref[lines, start : start + LANES].astype(F32) for start in starts]
            places = range(port * rows, (port + 1) * rows)
            if edge == 0:
                parts[0] = north_in[:, rim]
            elif edge == 1:
                parts[-1] = south_in[:, rim]
            elif edge == 2:
                parts = [
                    jnp.where(lane == 0, lane_of(west_in, place), part)
                    for place, part in zip(places, parts)
                ]
            else:
                parts = [
                    jnp.where(lane == LANES - 1, lane_of(east_in, place), part)
                    for place, part in zip(places, parts)
                ]
            value = jnp.concatenate(parts, axis=1).reshape(quarter, rows, LANES)
            buffer[lines, port] = value.astype(BF)
        for port in range(ports):
            row, col, inside = port_place(port_ref, port, rows, width)

            @pl.when(inside)
            def _():
                current = buffer[lines, port].astype(F32)
                here = (lax.broadcasted_iota(jnp.int32, current.shape, 1) == row) & (
                    lax.broadcasted_iota(jnp.int32, current.shape, 2) == col
                )
                profile = port_profile_column(profile_ref, port, edge)
                profile = jnp.broadcast_to(profile, (quarter, LANES)).reshape(quarter, 1, LANES)
                added = current + jnp.broadcast_to(profile, current.shape)
                buffer[lines, port] = jnp.where(here, added, current).astype(BF)

        copy = pltpu.make_async_copy(buffer.at[lines], out_ref.at[lines], sems.at[edge])
        copy.start()
        copies.append(copy)
    for copy in copies:
        copy.wait()


def exchange(rims):
    def pairs(axis, first):
        count = lax.axis_size(axis)
        near = [(i, i + 1) for i in range(first, count - 1, 2)]
        alone = [(0, 0), (count - 1, count - 1)] if first else []
        return near + [(target, source) for source, target in near] + alone

    axes = (("row", 0), ("row", 1), ("col", 0), ("col", 1))
    return [lax.ppermute(rim, axis, pairs(axis, first)) for rim, (axis, first) in zip(rims, axes)]


def body(traces, cell_type, port_cell, port_profile, mode_shapes, mode_values, mode_weights):
    edges, samples, ports, rows, width = traces.shape
    order = edges * samples
    quarter = samples
    tile = rows * width
    types = cell_type.reshape(1, tile)
    own_map, x, sides = own_type_map(mode_shapes, mode_values, mode_weights, traces, types)
    core = lax.rem(lax.axis_index("col"), 2)
    half = lax.dynamic_slice_in_dim(own_map, core * (order // 2), order // 2)
    fetched = [
        swap(own_map, *((step, 8 * (step % 2)) for step in steps)) for steps in MAP_STEPS[1:4]
    ]
    half = swap(half, (4, 0))
    profile = jnp.transpose(port_profile, (0, 2, 1))
    ports_spec = pl.BlockSpec(memory_space=pltpu.SMEM)
    next_shape = jax.ShapeDtypeStruct((order, ports * tile), BF)
    rim_shapes = [jax.ShapeDtypeStruct((quarter, ports * LANES), BF)] * 2 + [
        jax.ShapeDtypeStruct((quarter, LANES), BF)
    ] * 2
    work = 2 * order * order * len(MAP_STEPS) * ports * tile
    part_shapes = [next_shape] + rim_shapes[:2] + [jax.ShapeDtypeStruct((2 * quarter, LANES), BF)]

    def early(first, maps, parts=()):
        last = first + len(maps)
        kernel = functools.partial(early_kernel, ports, first, last)
        flops = work * len(maps) // 7
        return whole_call(kernel, part_shapes, x, types, *sides, *maps, *parts, flops=flops)

    parts = list(early(0, [own_map, fetched[0]]))
    parts[1], fetched = lax.optimization_barrier((parts[1], fetched))
    swapped = [swap_cores(value) for value in fetched]
    parts = list(early(2, fetched[1:], parts))
    parts[1], half = lax.optimization_barrier((parts[1], half))
    swapped.append(swap_cores(half))
    done, *parts = parts
    late = swapped + [half]
    maps = [own_map] + fetched + late
    sent = whole_call(
        functools.partial(rim_kernel, ports, 4),
        rim_shapes,
        x,
        types,
        *sides,
        *late,
        *parts,
        flops=work // 8,
    )
    halos = exchange(sent)
    (x,) = whole_call(
        functools.partial(first_kernel, rows, ports, 4),
        [next_shape],
        x,
        types,
        done,
        *late,
        flops=work // 2,
    )
    operands = [port_cell, x, types, profile, *halos, *maps]
    x, *sent = pl.pallas_call(
        functools.partial(second_kernel, rows, width),
        in_specs=[ports_spec] + [WHOLE] * (len(operands) - 1),
        out_specs=[WHOLE] * 5,
        out_shape=[next_shape] + rim_shapes,
        compiler_params=PARAMS,
        cost_estimate=pl.CostEstimate(flops=work, bytes_accessed=0, transcendentals=0),
    )(*operands)
    operands = [port_cell, x, profile, *exchange(sent)]
    out = pl.pallas_call(
        functools.partial(last_kernel, rows, width),
        in_specs=[ports_spec] + [WHOLE] * (len(operands) - 1),
        out_specs=pl.BlockSpec(memory_space=pl.ANY),
        out_shape=jax.ShapeDtypeStruct((order, ports, rows, width), BF),
        scratch_shapes=[
            pltpu.VMEM((order, ports, rows, width), BF),
            pltpu.SemaphoreType.DMA((4,)),
        ],
        compiler_params=PARAMS,
    )(*operands)
    return out.reshape(traces.shape)


def solution(mesh):
    return jax.shard_map(
        body,
        mesh=mesh,
        in_specs=(
            P(None, None, None, "row", "col"),
            P("row", "col"),
            P(),
            P(),
            P("row", None, "col"),
            P("row", "col"),
            P("row", "col", None),
        ),
        out_specs=P(None, None, None, "row", "col"),
        check_vma=False,
    )
```

```python
import functools
import math

import jax
import jax.numpy as jnp
from jax import lax
from jax.experimental import pallas as pl
from jax.experimental.pallas import tpu as pltpu
from jax.sharding import PartitionSpec as P

BF = jnp.bfloat16
F32 = jnp.float32
LANES = 128
PARAMS = pltpu.CompilerParams(vmem_limit_bytes=20 * 2**20)
WIDE_PARAMS = pltpu.CompilerParams(vmem_limit_bytes=50 * 2**20)


def swap(value, first, second=None):
    second = first if second is None else second
    rows, cols = lax.axis_size("row"), lax.axis_size("col")
    pairs = []
    for row in range(rows):
        for col in range(cols):
            down, along = second if col % 2 else first
            pairs.append((row * cols + col, (row ^ down) * cols + (col ^ along)))
    return lax.ppermute(value, ("row", "col"), pairs)


def swap_cores(value):
    return swap(value, (0, 1))


def flat_kernel(x_hbm, out_ref, x_ref, sems):
    order, ports, rows, width = x_ref.shape
    quarter, tile = order // 4, rows * width
    edges = [slice(edge * quarter, (edge + 1) * quarter) for edge in range(4)]
    copies = [
        pltpu.make_async_copy(x_hbm.at[lines], x_ref.at[lines], sems.at[edge])
        for edge, lines in enumerate(edges)
    ]
    for copy in copies:
        copy.start()
    for copy, lines in zip(copies, edges):
        copy.wait()
        for port in range(ports):
            value = x_ref[lines, port].astype(F32).reshape(quarter, tile)
            out_ref[lines, port * tile : (port + 1) * tile] = value.astype(BF)


def partial_kernel(modes, *refs):
    left, right = [], []
    for ref in refs[:-1]:
        for start in range(0, ref.shape[0], 2 * modes):
            left.append(ref[start : start + modes])
            right.append(ref[start + modes : start + 2 * modes])
    refs[-1][...] = lax.dot_general(
        jnp.concatenate(left, axis=0),
        jnp.concatenate(right, axis=0),
        (((0,), (0,)), ((), ())),
        precision=lax.Precision.HIGHEST,
        preferred_element_type=F32,
    )


WHOLE = pl.BlockSpec(memory_space=pltpu.VMEM)


def whole_call(kernel, shapes, *operands, flops=0):
    return pl.pallas_call(
        kernel,
        in_specs=[WHOLE] * len(operands),
        out_specs=[WHOLE] * len(shapes),
        out_shape=shapes,
        compiler_params=PARAMS,
        cost_estimate=pl.CostEstimate(flops=flops, bytes_accessed=0, transcendentals=0),
    )(*operands)


def own_type_map(mode_shapes, mode_values, mode_weights, traces, types):
    modes, order = mode_weights.shape[1:]
    own = jnp.concatenate([mode_shapes[0].T, mode_weights[0]], axis=0)
    own = own * jnp.concatenate([mode_values[0], jnp.ones((modes,), F32)])[:, None]
    far = swap(own, (0, 4))
    pair = jnp.concatenate([own, swap_cores(own)], axis=0)
    pair, traces = lax.optimization_barrier((pair, traces))
    steps = (((0, 8), (0, 10)), ((0, 2), (0, 14)), ((0, 6), (0, 12)))
    got = [swap(pair, *step) for step in steps]
    shape = (order,) + traces.shape[2:]
    x = pl.pallas_call(
        flat_kernel,
        in_specs=[pl.BlockSpec(memory_space=pltpu.HBM)],
        out_specs=WHOLE,
        out_shape=jax.ShapeDtypeStruct((order, math.prod(shape[1:])), BF),
        scratch_shapes=[pltpu.VMEM(shape, BF), pltpu.SemaphoreType.DMA((4,))],
        compiler_params=WIDE_PARAMS,
        cost_estimate=pl.CostEstimate(flops=2**30, bytes_accessed=0, transcendentals=0),
    )(traces.reshape(shape))
    *got, x = lax.optimization_barrier((*got, x))
    (partial,) = whole_call(
        functools.partial(partial_kernel, modes),
        [jax.ShapeDtypeStruct((order, order), F32)],
        own,
        far,
        *got,
    )
    partial, x = lax.optimization_barrier((partial, x))
    other = swap_cores(partial)
    sides = whole_call(
        functools.partial(sides_kernel, traces.shape[2]),
        [jax.ShapeDtypeStruct((order, LANES), BF), jax.ShapeDtypeStruct((16, LANES), BF)],
        x,
        types,
        flops=2**30,
    )
    other, sides = lax.optimization_barrier((other, sides))
    return (partial + other).astype(BF), x, sides


MAP_STEPS = ((0, 0), (1, 3), (2, 7), (6, 5), (3, 1), (7, 2), (5, 6), (4, 4))


def even(axis):
    return lax.rem(lax.axis_index(axis), 2) == 0


def halos_inside(axis, one, two):
    one, two = one[...].astype(F32), two[...].astype(F32)
    index, count = lax.axis_index(axis), lax.axis_size(axis)
    low = jnp.where(even(axis), two, one)
    high = jnp.where(even(axis), one, two)
    return jnp.where(index > 0, low, 0.0), jnp.where(index < count - 1, high, 0.0)


def store_rims(out_refs, axis, low, high):
    first, second = out_refs
    first[...] = jnp.where(even(axis), high, low).astype(BF)
    second[...] = jnp.where(even(axis), low, high).astype(BF)


def lane_of(value, lane):
    return jnp.broadcast_to(value[:, lane : lane + 1], (value.shape[0], LANES))


def port_profile_column(profile_ref, port, edge):
    samples = profile_ref.shape[2]
    row = lax.broadcasted_iota(jnp.int32, (samples, samples), 0)
    col = lax.broadcasted_iota(jnp.int32, (samples, samples), 1)
    line = jnp.broadcast_to(profile_ref[edge].astype(F32)[port : port + 1], row.shape)
    return jnp.sum(jnp.where(row == col, line, 0.0), axis=1, keepdims=True)


def port_place(port_ref, port, rows, width):
    all_cols = width * lax.axis_size("col")
    cell = port_ref[port]
    row = cell // all_cols - lax.axis_index("row") * rows
    col = cell % all_cols - lax.axis_index("col") * width
    return row, col, (row >= 0) & (row < rows) & (col >= 0) & (col < width)


def map_rows(map_refs, first, last):
    if len(map_refs) == 1:
        return map_refs[0][first:last, :]
    core = lax.rem(lax.axis_index("col"), 2)
    swapped, own = map_refs[0][...], map_refs[1][...]
    low, high = jnp.where(core == 0, own, swapped), jnp.where(core == 0, swapped, own)
    return jnp.concatenate([low, high], axis=0)[first:last]


def products(x, types, maps, first, last, total=None):
    mine = lax.axis_index("row")
    core = lax.rem(lax.axis_index("col"), 2)
    types = jnp.broadcast_to(types, x.shape)
    for (even, odd), map_refs in maps:
        kind = (mine ^ jnp.where(core == 0, even, odd)).astype(F32).astype(BF)
        masked = jnp.where(types == kind, x, jnp.zeros((), BF))
        part = map_rows(map_refs, first, last)
        product = jnp.dot(part, masked, preferred_element_type=F32)
        total = product if total is None else total + product
    return total


def with_steps(map_refs, first, last):
    refs = [(ref,) for ref in map_refs]
    if last == len(MAP_STEPS):
        refs[-2:] = [refs[-2] + refs[-1]]
    return list(zip(MAP_STEPS[first:last], refs, strict=True))


def shifted(total, next_ref, rows):
    quarter = total.shape[0] // 4
    last = (rows - 1) * LANES
    north = total[0:quarter].astype(BF)
    south = total[quarter : 2 * quarter].astype(BF)
    next_ref[0:quarter, LANES:] = south[:, :last]
    next_ref[0:quarter, 0:LANES] = jnp.zeros((quarter, LANES), BF)
    next_ref[quarter : 2 * quarter, :last] = north[:, LANES:]
    next_ref[quarter : 2 * quarter, last:] = jnp.zeros((quarter, LANES), BF)
    for row in range(rows):
        cols = slice(row * LANES, (row + 1) * LANES)
        west = total[2 * quarter : 3 * quarter, cols]
        east = total[3 * quarter : 4 * quarter, cols]
        next_ref[2 * quarter : 3 * quarter, cols] = pltpu.roll(east, 1, 1).astype(BF)
        next_ref[3 * quarter : 4 * quarter, cols] = pltpu.roll(west, LANES - 1, 1).astype(BF)
    return north, south


def rim_columns(x_ref, types, ports, offset):
    tile = types.shape[1]
    starts = [port * tile + offset for port in range(ports)]
    cells = jnp.concatenate([x_ref[:, start : start + LANES] for start in starts], axis=1)
    return cells, jnp.concatenate([types[:, offset : offset + LANES]] * ports, axis=1).astype(BF)


def side_columns(x_ref, types, ports):
    order, tile = x_ref.shape[0], types.shape[1]
    rows = tile // LANES

    def pick(block_of, lines):
        lane = lax.broadcasted_iota(jnp.int32, (lines, LANES), 1)
        first = last = jnp.zeros((lines, LANES), F32)
        for place in range(ports * rows):
            turned = pltpu.roll(block_of(place), place + 1, 1)
            first = jnp.where(lane == place + 1, turned, first)
            last = jnp.where(lane == place, turned, last)
        first = pltpu.roll(first, LANES - 1, 1)
        return jnp.where(lane < 64, first, pltpu.roll(last, 64, 1)).astype(BF)

    def types_of(place):
        start = place % rows * LANES
        return jnp.broadcast_to(types[:, start : start + LANES], (16, LANES))

    quarter = order // 4
    sides = [
        pick(
            lambda place: x_ref[edge * quarter : (edge + 1) * quarter,
                                place * LANES : (place + 1) * LANES].astype(F32),
            quarter,
        )
        for edge in range(4)
    ]
    return jnp.concatenate(sides, axis=0), pick(types_of, 16)


def rims(x_ref, types, ports, sides, kinds, maps, so_far):
    order, tile = x_ref.shape[0], types.shape[1]
    quarter = order // 4
    before = [None if ref is None else ref[...].astype(F32) for ref in so_far]
    cells, cell_kinds = rim_columns(x_ref, types, ports, 0)
    north = products(cells, cell_kinds, maps, 0, quarter, before[0])
    cells, cell_kinds = rim_columns(x_ref, types, ports, tile - LANES)
    south = products(cells, cell_kinds, maps, quarter, 2 * quarter, before[1])
    side = products(sides, kinds, maps, 2 * quarter, order, before[2])
    return north.astype(BF), south.astype(BF), side.astype(BF)


def sides_kernel(ports, x_ref, types_ref, sides_ref, kinds_ref):
    sides_ref[...], kinds_ref[...] = side_columns(x_ref, types_ref[...].astype(F32), ports)


def early_kernel(ports, first, last, x_ref, types_ref, sides_ref, kinds_ref, *refs):
    maps = with_steps(refs[: last - first], first, last)
    types = types_ref[...].astype(F32)
    tile = types.shape[1]
    so_far, outs = refs[last - first : -4], refs[-4:]
    done_ref, *so_far = so_far if first else [None] * 4
    values = rims(x_ref, types, ports, sides_ref[...], kinds_ref[0:1, :], maps, so_far)
    for ref, value in zip(outs[1:], values):
        ref[...] = value
    for port in range(ports):
        cols = slice(port * tile, (port + 1) * tile)
        before = None if done_ref is None else done_ref[:, cols].astype(F32)
        total = products(x_ref[:, cols], types.astype(BF), maps, 0, x_ref.shape[0], before)
        outs[0][:, cols] = total.astype(BF)


def rim_kernel(ports, first, x_ref, types_ref, sides_ref, kinds_ref, *refs):
    maps = with_steps(refs[:-7], first, len(MAP_STEPS))
    types = types_ref[...].astype(F32)
    quarter = x_ref.shape[0] // 4
    values = rims(x_ref, types, ports, sides_ref[...], kinds_ref[0:1, :], maps, refs[-7:-4])
    store_rims(refs[-4:-2], "row", values[0], values[1])
    store_rims(refs[-2:], "col", values[2][0:quarter], values[2][quarter:])


def first_kernel(rows, ports, first, x_ref, types_ref, done_ref, *refs):
    maps = with_steps(refs[:-1], first, len(MAP_STEPS))
    types = types_ref[...].astype(F32).astype(BF)
    tile = types.shape[1]
    for port in range(ports):
        cols = slice(port * tile, (port + 1) * tile)
        before = done_ref[:, cols].astype(F32)
        total = products(x_ref[:, cols], types, maps, 0, x_ref.shape[0], before)
        shifted(total, refs[-1].at[:, cols], rows)


def patched(rows, width, x_ref, port_ref, profile_ref, halo_refs, places):
    order = x_ref.shape[0]
    quarter = order // 4
    north_in, south_in = halos_inside("row", *halo_refs[:2])
    west_in, east_in = halos_inside("col", *halo_refs[2:])
    lane = lax.broadcasted_iota(jnp.int32, (quarter, LANES), 1)
    blocks = []
    for port, row in places:
        place = port * rows + row
        rim = slice(port * LANES, (port + 1) * LANES)
        value = x_ref[:, place * LANES : (place + 1) * LANES].astype(F32)
        north, south, west, east = (value[i * quarter : (i + 1) * quarter] for i in range(4))
        north = north_in[:, rim] if row == 0 else north
        south = south_in[:, rim] if row == rows - 1 else south
        west = jnp.where(lane == 0, lane_of(west_in, 64 + place), west)
        east = jnp.where(lane == LANES - 1, lane_of(east_in, place), east)
        source_row, col, inside = port_place(port_ref, port, rows, width)
        here = lane == jnp.where(inside & (source_row == row), col, -1)
        columns = [
            jnp.where(here, part + port_profile_column(profile_ref, port, edge), part)
            for edge, part in enumerate((north, south, west, east))
        ]
        blocks.append(jnp.concatenate(columns, axis=0).astype(BF))
    return jnp.concatenate(blocks, axis=1)


def types_of_rows(types_ref, rows):
    types = types_ref[...].astype(F32)
    return jnp.concatenate([types[:, row * LANES : (row + 1) * LANES] for row in rows], axis=1)


def ends_kernel(rows, ports, width, port_ref, x_ref, types_ref, profile_ref, *refs):
    halo_refs, map_refs, ends_ref = refs[:4], refs[4:-3], refs[-3]
    quarter = x_ref.shape[0] // 4
    places = [(port, row) for row in (0, rows - 1) for port in range(ports)]
    block = patched(rows, width, x_ref, port_ref, profile_ref, halo_refs, places)
    types = types_of_rows(types_ref, [row for _, row in places]).astype(BF)
    total = products(block, types, with_steps(map_refs, 0, len(MAP_STEPS)), 0, x_ref.shape[0])
    ends_ref[...] = total.astype(BF)
    wide = ports * LANES
    store_rims(refs[-2:], "row", total[0:quarter, :wide], total[quarter : 2 * quarter, wide:])


def second_kernel(rows, ports, width, port_ref, x_ref, types_ref, profile_ref, ends_ref, *refs):
    halo_refs, map_refs, next_ref = refs[:4], refs[4:-3], refs[-3]
    order, tile = x_ref.shape[0], rows * width
    quarter = order // 4
    maps = with_steps(map_refs, 0, len(MAP_STEPS))
    types = types_of_rows(types_ref, range(1, rows - 1)).astype(BF)
    lane = lax.broadcasted_iota(jnp.int32, (quarter, LANES), 1)
    west_rim = east_rim = jnp.zeros((quarter, LANES), F32)
    for port in range(ports):
        places = [(port, row) for row in range(1, rows - 1)]
        block = patched(rows, width, x_ref, port_ref, profile_ref, halo_refs, places)
        middle = products(block, types, maps, 0, order)
        top = ends_ref[:, port * LANES : (port + 1) * LANES].astype(F32)
        bottom = ends_ref[:, (ports + port) * LANES : (ports + port + 1) * LANES].astype(F32)
        total = jnp.concatenate([top, middle, bottom], axis=1)
        shifted(total, next_ref.at[:, port * tile : (port + 1) * tile], rows)
        for row in range(rows):
            place = port * rows + row
            west = lane_of(total[2 * quarter : 3 * quarter], row * LANES)
            east = lane_of(total[3 * quarter :], (row + 1) * LANES - 1)
            west_rim = jnp.where(lane == place, west, west_rim)
            east_rim = jnp.where(lane == place, east, east_rim)
    store_rims(refs[-2:], "col", west_rim, east_rim)


def last_kernel(rows, width, port_ref, x_ref, profile_ref, *refs):
    out_ref, buffer, sems = refs[4:]
    order, ports = buffer.shape[:2]
    quarter, tile = order // 4, rows * width
    north_in, south_in = halos_inside("row", *refs[:2])
    west_in, east_in = halos_inside("col", *refs[2:4])
    lane = lax.broadcasted_iota(jnp.int32, (quarter, LANES), 1)
    copies = []
    for edge in (2, 3, 0, 1):
        lines = slice(edge * quarter, (edge + 1) * quarter)
        for port in range(ports):
            rim = slice(port * LANES, (port + 1) * LANES)
            starts = [port * tile + row * LANES for row in range(rows)]
            parts = [x_ref[lines, start : start + LANES].astype(F32) for start in starts]
            places = range(port * rows, (port + 1) * rows)
            if edge == 0:
                parts[0] = north_in[:, rim]
            elif edge == 1:
                parts[-1] = south_in[:, rim]
            elif edge == 2:
                parts = [
                    jnp.where(lane == 0, lane_of(west_in, place), part)
                    for place, part in zip(places, parts)
                ]
            else:
                parts = [
                    jnp.where(lane == LANES - 1, lane_of(east_in, place), part)
                    for place, part in zip(places, parts)
                ]
            value = jnp.concatenate(parts, axis=1).reshape(quarter, rows, LANES)
            buffer[lines, port] = value.astype(BF)
        for port in range(ports):
            row, col, inside = port_place(port_ref, port, rows, width)

            @pl.when(inside)
            def _():
                current = buffer[lines, port].astype(F32)
                here = (lax.broadcasted_iota(jnp.int32, current.shape, 1) == row) & (
                    lax.broadcasted_iota(jnp.int32, current.shape, 2) == col
                )
                profile = port_profile_column(profile_ref, port, edge)
                profile = jnp.broadcast_to(profile, (quarter, LANES)).reshape(quarter, 1, LANES)
                added = current + jnp.broadcast_to(profile, current.shape)
                buffer[lines, port] = jnp.where(here, added, current).astype(BF)

        copy = pltpu.make_async_copy(buffer.at[lines], out_ref.at[lines], sems.at[edge])
        copy.start()
        copies.append(copy)
    for copy in copies:
        copy.wait()


def exchange(rims, axis):
    def pairs(first):
        count = lax.axis_size(axis)
        near = [(i, (i + 1) % count) for i in range(first, count, 2)]
        return near + [(target, source) for source, target in near]

    return [lax.ppermute(rim, axis, pairs(first)) for first, rim in enumerate(rims)]


def body(traces, cell_type, port_cell, port_profile, mode_shapes, mode_values, mode_weights):
    edges, samples, ports, rows, width = traces.shape
    order = edges * samples
    quarter = samples
    tile = rows * width
    types = cell_type.reshape(1, tile)
    own_map, x, sides = own_type_map(mode_shapes, mode_values, mode_weights, traces, types)
    core = lax.rem(lax.axis_index("col"), 2)
    half = lax.dynamic_slice_in_dim(own_map, core * (order // 2), order // 2)
    fetched = [
        swap(own_map, *((step, 8 * (step % 2)) for step in steps)) for steps in MAP_STEPS[1:4]
    ]
    half = swap(half, (4, 0))
    profile = jnp.transpose(port_profile, (0, 2, 1))
    ports_spec = pl.BlockSpec(memory_space=pltpu.SMEM)
    next_shape = jax.ShapeDtypeStruct((order, ports * tile), BF)
    rim_shapes = [jax.ShapeDtypeStruct((quarter, ports * LANES), BF)] * 2 + [
        jax.ShapeDtypeStruct((quarter, LANES), BF)
    ] * 2
    work = 2 * order * order * len(MAP_STEPS) * ports * tile
    part_shapes = [next_shape] + rim_shapes[:2] + [jax.ShapeDtypeStruct((2 * quarter, LANES), BF)]

    def early(first, maps, parts=()):
        last = first + len(maps)
        kernel = functools.partial(early_kernel, ports, first, last)
        flops = work * len(maps) // 7
        return whole_call(kernel, part_shapes, x, types, *sides, *maps, *parts, flops=flops)

    parts = list(early(0, [own_map, fetched[0]]))
    parts[1], fetched = lax.optimization_barrier((parts[1], fetched))
    swapped = [swap_cores(value) for value in fetched]
    parts = list(early(2, fetched[1:], parts))
    parts[1], half = lax.optimization_barrier((parts[1], half))
    swapped.append(swap_cores(half))
    done, *parts = parts
    late = swapped + [half]
    maps = [own_map] + fetched + late
    sent = whole_call(
        functools.partial(rim_kernel, ports, 4),
        rim_shapes,
        x,
        types,
        *sides,
        *late,
        *parts,
        flops=work // 8,
    )
    halos = exchange(sent[:2], "row") + exchange(sent[2:], "col")
    (x,) = whole_call(
        functools.partial(first_kernel, rows, ports, 4),
        [next_shape],
        x,
        types,
        done,
        *late,
        flops=work // 2,
    )
    def sweep(kernel, shapes, operands, share):
        return pl.pallas_call(
            functools.partial(kernel, rows, ports, width),
            in_specs=[ports_spec] + [WHOLE] * (len(operands) - 1),
            out_specs=[WHOLE] * len(shapes),
            out_shape=shapes,
            compiler_params=PARAMS,
            cost_estimate=pl.CostEstimate(
                flops=work * share // rows, bytes_accessed=0, transcendentals=0
            ),
        )(*operands)

    ends_shape = jax.ShapeDtypeStruct((order, 2 * ports * LANES), BF)
    operands = [port_cell, x, types, profile]
    ends, *sent = sweep(ends_kernel, [ends_shape] + rim_shapes[:2], operands + halos + maps, 2)
    row_halos = exchange(sent, "row")
    operands = operands + [ends] + halos + maps
    x, *sent = sweep(second_kernel, [next_shape] + rim_shapes[2:], operands, rows - 2)
    operands = [port_cell, x, profile, *row_halos, *exchange(sent, "col")]
    out = pl.pallas_call(
        functools.partial(last_kernel, rows, width),
        in_specs=[ports_spec] + [WHOLE] * (len(operands) - 1),
        out_specs=pl.BlockSpec(memory_space=pl.ANY),
        out_shape=jax.ShapeDtypeStruct((order, ports, rows, width), BF),
        scratch_shapes=[
            pltpu.VMEM((order, ports, rows, width), BF),
            pltpu.SemaphoreType.DMA((4,)),
        ],
        compiler_params=PARAMS,
    )(*operands)
    return out.reshape(traces.shape)


def solution(mesh):
    return jax.shard_map(
        body,
        mesh=mesh,
        in_specs=(
            P(None, None, None, "row", "col"),
            P("row", "col"),
            P(),
            P(),
            P("row", None, "col"),
            P("row", "col"),
            P("row", "col", None),
        ),
        out_specs=P(None, None, None, "row", "col"),
        check_vma=False,
    )
```

```python
import functools
import math

import jax
import jax.numpy as jnp
from jax import lax
from jax.experimental import pallas as pl
from jax.experimental.pallas import tpu as pltpu
from jax.sharding import PartitionSpec as P

BF = jnp.bfloat16
F32 = jnp.float32
LANES = 128
PARAMS = pltpu.CompilerParams(vmem_limit_bytes=20 * 2**20)
WIDE_PARAMS = pltpu.CompilerParams(vmem_limit_bytes=50 * 2**20)


def swap(value, first, second=None):
    second = first if second is None else second
    rows, cols = lax.axis_size("row"), lax.axis_size("col")
    pairs = []
    for row in range(rows):
        for col in range(cols):
            down, along = second if col % 2 else first
            pairs.append((row * cols + col, (row ^ down) * cols + (col ^ along)))
    return lax.ppermute(value, ("row", "col"), pairs)


def swap_cores(value):
    return swap(value, (0, 1))


def flat_kernel(x_hbm, out_ref, x_ref, sems):
    order, ports, rows, width = x_ref.shape
    quarter, tile = order // 4, rows * width
    edges = [slice(edge * quarter, (edge + 1) * quarter) for edge in range(4)]
    copies = [
        pltpu.make_async_copy(x_hbm.at[lines], x_ref.at[lines], sems.at[edge])
        for edge, lines in enumerate(edges)
    ]
    for copy in copies:
        copy.start()
    for copy, lines in zip(copies, edges):
        copy.wait()
        for port in range(ports):
            value = x_ref[lines, port].astype(F32).reshape(quarter, tile)
            out_ref[lines, port * tile : (port + 1) * tile] = value.astype(BF)


def partial_kernel(modes, *refs):
    left, right = [], []
    for ref in refs[:-1]:
        for start in range(0, ref.shape[0], 2 * modes):
            left.append(ref[start : start + modes])
            right.append(ref[start + modes : start + 2 * modes])
    refs[-1][...] = lax.dot_general(
        jnp.concatenate(left, axis=0),
        jnp.concatenate(right, axis=0),
        (((0,), (0,)), ((), ())),
        precision=lax.Precision.HIGHEST,
        preferred_element_type=F32,
    )


WHOLE = pl.BlockSpec(memory_space=pltpu.VMEM)


def whole_call(kernel, shapes, *operands, flops=0):
    return pl.pallas_call(
        kernel,
        in_specs=[WHOLE] * len(operands),
        out_specs=[WHOLE] * len(shapes),
        out_shape=shapes,
        compiler_params=PARAMS,
        cost_estimate=pl.CostEstimate(flops=flops, bytes_accessed=0, transcendentals=0),
    )(*operands)


def own_type_map(mode_shapes, mode_values, mode_weights, traces, types):
    modes, order = mode_weights.shape[1:]
    own = jnp.concatenate([mode_shapes[0].T, mode_weights[0]], axis=0)
    own = own * jnp.concatenate([mode_values[0], jnp.ones((modes,), F32)])[:, None]
    far = swap(own, (0, 4))
    pair = jnp.concatenate([own, swap_cores(own)], axis=0)
    pair, traces = lax.optimization_barrier((pair, traces))
    steps = (((0, 8), (0, 10)), ((0, 2), (0, 14)), ((0, 6), (0, 12)))
    got = [swap(pair, *step) for step in steps]
    shape = (order,) + traces.shape[2:]
    x = pl.pallas_call(
        flat_kernel,
        in_specs=[pl.BlockSpec(memory_space=pltpu.HBM)],
        out_specs=WHOLE,
        out_shape=jax.ShapeDtypeStruct((order, math.prod(shape[1:])), BF),
        scratch_shapes=[pltpu.VMEM(shape, BF), pltpu.SemaphoreType.DMA((4,))],
        compiler_params=WIDE_PARAMS,
        cost_estimate=pl.CostEstimate(flops=2**30, bytes_accessed=0, transcendentals=0),
    )(traces.reshape(shape))
    *got, x = lax.optimization_barrier((*got, x))
    (partial,) = whole_call(
        functools.partial(partial_kernel, modes),
        [jax.ShapeDtypeStruct((order, order), F32)],
        own,
        far,
        *got,
    )
    partial, x = lax.optimization_barrier((partial, x))
    other = swap_cores(partial)
    sides = whole_call(
        functools.partial(sides_kernel, traces.shape[2]),
        [jax.ShapeDtypeStruct((order, LANES), BF), jax.ShapeDtypeStruct((16, LANES), BF)],
        x,
        types,
        flops=2**30,
    )
    other, sides = lax.optimization_barrier((other, sides))
    return (partial + other).astype(BF), x, sides


MAP_STEPS = ((0, 0), (1, 3), (2, 7), (6, 5), (3, 1), (7, 2), (5, 6), (4, 4))


def even(axis):
    return lax.rem(lax.axis_index(axis), 2) == 0


def halos_inside(axis, one, two):
    one, two = one[...].astype(F32), two[...].astype(F32)
    index, count = lax.axis_index(axis), lax.axis_size(axis)
    low = jnp.where(even(axis), two, one)
    high = jnp.where(even(axis), one, two)
    return jnp.where(index > 0, low, 0.0), jnp.where(index < count - 1, high, 0.0)


def store_rims(out_refs, axis, low, high):
    first, second = out_refs
    first[...] = jnp.where(even(axis), high, low).astype(BF)
    second[...] = jnp.where(even(axis), low, high).astype(BF)


def lane_of(value, lane):
    return jnp.broadcast_to(value[:, lane : lane + 1], (value.shape[0], LANES))


def port_profile_column(profile_ref, port, edge):
    samples = profile_ref.shape[2]
    row = lax.broadcasted_iota(jnp.int32, (samples, samples), 0)
    col = lax.broadcasted_iota(jnp.int32, (samples, samples), 1)
    line = jnp.broadcast_to(profile_ref[edge].astype(F32)[port : port + 1], row.shape)
    return jnp.sum(jnp.where(row == col, line, 0.0), axis=1, keepdims=True)


def port_place(port_ref, port, rows, width):
    all_cols = width * lax.axis_size("col")
    cell = port_ref[port]
    row = cell // all_cols - lax.axis_index("row") * rows
    col = cell % all_cols - lax.axis_index("col") * width
    return row, col, (row >= 0) & (row < rows) & (col >= 0) & (col < width)


def map_rows(map_refs, first, last):
    if len(map_refs) == 1:
        return map_refs[0][first:last, :]
    core = lax.rem(lax.axis_index("col"), 2)
    swapped, own = map_refs[0][...], map_refs[1][...]
    low, high = jnp.where(core == 0, own, swapped), jnp.where(core == 0, swapped, own)
    return jnp.concatenate([low, high], axis=0)[first:last]


def products(x, types, maps, first, last, total=None):
    mine = lax.axis_index("row")
    core = lax.rem(lax.axis_index("col"), 2)
    types = jnp.broadcast_to(types, x.shape)
    for (even, odd), map_refs in maps:
        kind = (mine ^ jnp.where(core == 0, even, odd)).astype(F32).astype(BF)
        masked = jnp.where(types == kind, x, jnp.zeros((), BF))
        part = map_rows(map_refs, first, last)
        product = jnp.dot(part, masked, preferred_element_type=F32)
        total = product if total is None else total + product
    return total


def with_steps(map_refs, first, last):
    refs = [(ref,) for ref in map_refs]
    if last == len(MAP_STEPS):
        refs[-2:] = [refs[-2] + refs[-1]]
    return list(zip(MAP_STEPS[first:last], refs, strict=True))


def shifted(total, next_ref, rows):
    quarter = total.shape[0] // 4
    last = (rows - 1) * LANES
    north = total[0:quarter].astype(BF)
    south = total[quarter : 2 * quarter].astype(BF)
    next_ref[0:quarter, LANES:] = south[:, :last]
    next_ref[0:quarter, 0:LANES] = jnp.zeros((quarter, LANES), BF)
    next_ref[quarter : 2 * quarter, :last] = north[:, LANES:]
    next_ref[quarter : 2 * quarter, last:] = jnp.zeros((quarter, LANES), BF)
    for row in range(rows):
        cols = slice(row * LANES, (row + 1) * LANES)
        west = total[2 * quarter : 3 * quarter, cols]
        east = total[3 * quarter : 4 * quarter, cols]
        next_ref[2 * quarter : 3 * quarter, cols] = pltpu.roll(east, 1, 1).astype(BF)
        next_ref[3 * quarter : 4 * quarter, cols] = pltpu.roll(west, LANES - 1, 1).astype(BF)
    return north, south


def rim_columns(x_ref, types, ports, offset):
    tile = types.shape[1]
    starts = [port * tile + offset for port in range(ports)]
    cells = jnp.concatenate([x_ref[:, start : start + LANES] for start in starts], axis=1)
    return cells, jnp.concatenate([types[:, offset : offset + LANES]] * ports, axis=1).astype(BF)


def side_columns(x_ref, types, ports):
    order, tile = x_ref.shape[0], types.shape[1]
    rows = tile // LANES

    def pick(block_of, lines):
        lane = lax.broadcasted_iota(jnp.int32, (lines, LANES), 1)
        first = last = jnp.zeros((lines, LANES), F32)
        for place in range(ports * rows):
            turned = pltpu.roll(block_of(place), place + 1, 1)
            first = jnp.where(lane == place + 1, turned, first)
            last = jnp.where(lane == place, turned, last)
        first = pltpu.roll(first, LANES - 1, 1)
        return jnp.where(lane < 64, first, pltpu.roll(last, 64, 1)).astype(BF)

    def types_of(place):
        start = place % rows * LANES
        return jnp.broadcast_to(types[:, start : start + LANES], (16, LANES))

    quarter = order // 4
    sides = [
        pick(
            lambda place: x_ref[edge * quarter : (edge + 1) * quarter,
                                place * LANES : (place + 1) * LANES].astype(F32),
            quarter,
        )
        for edge in range(4)
    ]
    return jnp.concatenate(sides, axis=0), pick(types_of, 16)


def rims(x_ref, types, ports, sides, kinds, maps, so_far):
    order, tile = x_ref.shape[0], types.shape[1]
    quarter = order // 4
    before = [None if ref is None else ref[...].astype(F32) for ref in so_far]
    cells, cell_kinds = rim_columns(x_ref, types, ports, 0)
    north = products(cells, cell_kinds, maps, 0, quarter, before[0])
    cells, cell_kinds = rim_columns(x_ref, types, ports, tile - LANES)
    south = products(cells, cell_kinds, maps, quarter, 2 * quarter, before[1])
    side = products(sides, kinds, maps, 2 * quarter, order, before[2])
    return north.astype(BF), south.astype(BF), side.astype(BF)


def sides_kernel(ports, x_ref, types_ref, sides_ref, kinds_ref):
    sides_ref[...], kinds_ref[...] = side_columns(x_ref, types_ref[...].astype(F32), ports)


def early_kernel(ports, first, last, x_ref, types_ref, sides_ref, kinds_ref, *refs):
    maps = with_steps(refs[: last - first], first, last)
    types = types_ref[...].astype(F32)
    tile = types.shape[1]
    so_far, outs = refs[last - first : -4], refs[-4:]
    done_ref, *so_far = so_far if first else [None] * 4
    values = rims(x_ref, types, ports, sides_ref[...], kinds_ref[0:1, :], maps, so_far)
    for ref, value in zip(outs[1:], values):
        ref[...] = value
    for port in range(ports):
        cols = slice(port * tile, (port + 1) * tile)
        before = None if done_ref is None else done_ref[:, cols].astype(F32)
        total = products(x_ref[:, cols], types.astype(BF), maps, 0, x_ref.shape[0], before)
        outs[0][:, cols] = total.astype(BF)


def rim_kernel(ports, first, x_ref, types_ref, sides_ref, kinds_ref, *refs):
    maps = with_steps(refs[:-7], first, len(MAP_STEPS))
    types = types_ref[...].astype(F32)
    quarter = x_ref.shape[0] // 4
    values = rims(x_ref, types, ports, sides_ref[...], kinds_ref[0:1, :], maps, refs[-7:-4])
    store_rims(refs[-4:-2], "row", values[0], values[1])
    store_rims(refs[-2:], "col", values[2][0:quarter], values[2][quarter:])


def first_kernel(rows, ports, first, x_ref, types_ref, done_ref, *refs):
    maps = with_steps(refs[:-1], first, len(MAP_STEPS))
    types = types_ref[...].astype(F32).astype(BF)
    tile = types.shape[1]
    for port in range(ports):
        cols = slice(port * tile, (port + 1) * tile)
        before = done_ref[:, cols].astype(F32)
        total = products(x_ref[:, cols], types, maps, 0, x_ref.shape[0], before)
        shifted(total, refs[-1].at[:, cols], rows)


def patched(rows, width, x_ref, port_ref, profile_ref, halo_refs, places):
    order = x_ref.shape[0]
    quarter = order // 4
    north_in, south_in = halos_inside("row", *halo_refs[:2])
    west_in, east_in = halos_inside("col", *halo_refs[2:])
    lane = lax.broadcasted_iota(jnp.int32, (quarter, LANES), 1)
    blocks = []
    for port, row in places:
        place = port * rows + row
        rim = slice(port * LANES, (port + 1) * LANES)
        value = x_ref[:, place * LANES : (place + 1) * LANES].astype(F32)
        north, south, west, east = (value[i * quarter : (i + 1) * quarter] for i in range(4))
        north = north_in[:, rim] if row == 0 else north
        south = south_in[:, rim] if row == rows - 1 else south
        west = jnp.where(lane == 0, lane_of(west_in, 64 + place), west)
        east = jnp.where(lane == LANES - 1, lane_of(east_in, place), east)
        source_row, col, inside = port_place(port_ref, port, rows, width)
        here = lane == jnp.where(inside & (source_row == row), col, -1)
        columns = [
            jnp.where(here, part + port_profile_column(profile_ref, port, edge), part)
            for edge, part in enumerate((north, south, west, east))
        ]
        blocks.append(jnp.concatenate(columns, axis=0).astype(BF))
    return jnp.concatenate(blocks, axis=1)


def types_of_rows(types_ref, rows):
    types = types_ref[...].astype(F32)
    return jnp.concatenate([types[:, row * LANES : (row + 1) * LANES] for row in rows], axis=1)


def ends_kernel(rows, ports, width, port_ref, x_ref, types_ref, profile_ref, *refs):
    halo_refs, map_refs, patched_ref, ends_ref = refs[:4], refs[4:-6], refs[-6], refs[-5]
    order, tile = x_ref.shape[0], rows * width
    quarter = order // 4
    maps = with_steps(map_refs, 0, len(MAP_STEPS))
    for port in range(ports):
        places = [(port, row) for row in range(rows)]
        value = patched(rows, width, x_ref, port_ref, profile_ref, halo_refs, places)
        patched_ref[:, port * tile : (port + 1) * tile] = value
    starts = [port * tile + row * width for row in (0, rows - 1) for port in range(ports)]
    block = jnp.concatenate([patched_ref[:, start : start + width] for start in starts], axis=1)
    types = types_of_rows(types_ref, [0] * ports + [rows - 1] * ports).astype(BF)
    total = products(block, types, maps, 0, order)
    ends_ref[...] = total.astype(BF)
    wide = ports * LANES
    store_rims(refs[-4:-2], "row", total[0:quarter, :wide], total[quarter : 2 * quarter, wide:])
    sides, kinds = side_columns(patched_ref, types_ref[...].astype(F32), ports)
    sides = products(sides, kinds[0:1], maps, 2 * quarter, order)
    store_rims(refs[-2:], "col", sides[0:quarter], sides[quarter:])


def second_kernel(rows, ports, width, x_ref, types_ref, ends_ref, *refs):
    map_refs, next_ref = refs[:-1], refs[-1]
    order, tile = x_ref.shape[0], rows * width
    maps = with_steps(map_refs, 0, len(MAP_STEPS))
    types = types_of_rows(types_ref, range(1, rows - 1)).astype(BF)
    for port in range(ports):
        start = port * tile
        middle = products(x_ref[:, start + width : start + tile - width], types, maps, 0, order)
        top = ends_ref[:, port * LANES : (port + 1) * LANES].astype(F32)
        bottom = ends_ref[:, (ports + port) * LANES : (ports + port + 1) * LANES].astype(F32)
        total = jnp.concatenate([top, middle, bottom], axis=1)
        shifted(total, next_ref.at[:, start : start + tile], rows)


def last_kernel(rows, width, port_ref, x_ref, profile_ref, *refs):
    out_ref, buffer, sems = refs[4:]
    order, ports = buffer.shape[:2]
    quarter, tile = order // 4, rows * width
    north_in, south_in = halos_inside("row", *refs[:2])
    west_in, east_in = halos_inside("col", *refs[2:4])
    lane = lax.broadcasted_iota(jnp.int32, (quarter, LANES), 1)
    copies = []
    for edge in (2, 3, 0, 1):
        lines = slice(edge * quarter, (edge + 1) * quarter)
        for port in range(ports):
            rim = slice(port * LANES, (port + 1) * LANES)
            starts = [port * tile + row * LANES for row in range(rows)]
            parts = [x_ref[lines, start : start + LANES].astype(F32) for start in starts]
            places = range(port * rows, (port + 1) * rows)
            if edge == 0:
                parts[0] = north_in[:, rim]
            elif edge == 1:
                parts[-1] = south_in[:, rim]
            elif edge == 2:
                parts = [
                    jnp.where(lane == 0, lane_of(west_in, 64 + place), part)
                    for place, part in zip(places, parts)
                ]
            else:
                parts = [
                    jnp.where(lane == LANES - 1, lane_of(east_in, place), part)
                    for place, part in zip(places, parts)
                ]
            value = jnp.concatenate(parts, axis=1).reshape(quarter, rows, LANES)
            buffer[lines, port] = value.astype(BF)
        for port in range(ports):
            row, col, inside = port_place(port_ref, port, rows, width)

            @pl.when(inside)
            def _():
                current = buffer[lines, port].astype(F32)
                here = (lax.broadcasted_iota(jnp.int32, current.shape, 1) == row) & (
                    lax.broadcasted_iota(jnp.int32, current.shape, 2) == col
                )
                profile = port_profile_column(profile_ref, port, edge)
                profile = jnp.broadcast_to(profile, (quarter, LANES)).reshape(quarter, 1, LANES)
                added = current + jnp.broadcast_to(profile, current.shape)
                buffer[lines, port] = jnp.where(here, added, current).astype(BF)

        copy = pltpu.make_async_copy(buffer.at[lines], out_ref.at[lines], sems.at[edge])
        copy.start()
        copies.append(copy)
    for copy in copies:
        copy.wait()


def exchange(rims, axis):
    sizes = lax.axis_size("row"), lax.axis_size("col")
    at = ("row", "col").index(axis)

    def partner(place, first):
        place = list(place)
        other = place[at] + (1 if place[at] % 2 == first else -1)
        if 0 <= other < sizes[at]:
            place[at] = other
        else:
            place[1 - at] ^= 2
        return place[0] * sizes[1] + place[1]

    def pairs(first):
        places = [(row, col) for row in range(sizes[0]) for col in range(sizes[1])]
        return [(row * sizes[1] + col, partner((row, col), first)) for row, col in places]

    return [lax.ppermute(rim, ("row", "col"), pairs(first)) for first, rim in enumerate(rims)]


def body(traces, cell_type, port_cell, port_profile, mode_shapes, mode_values, mode_weights):
    edges, samples, ports, rows, width = traces.shape
    order = edges * samples
    quarter = samples
    tile = rows * width
    types = cell_type.reshape(1, tile)
    own_map, x, sides = own_type_map(mode_shapes, mode_values, mode_weights, traces, types)
    core = lax.rem(lax.axis_index("col"), 2)
    half = lax.dynamic_slice_in_dim(own_map, core * (order // 2), order // 2)
    fetched = [
        swap(own_map, *((step, 8 * (step % 2)) for step in steps)) for steps in MAP_STEPS[1:4]
    ]
    half = swap(half, (4, 0))
    profile = jnp.transpose(port_profile, (0, 2, 1))
    ports_spec = pl.BlockSpec(memory_space=pltpu.SMEM)
    next_shape = jax.ShapeDtypeStruct((order, ports * tile), BF)
    rim_shapes = [jax.ShapeDtypeStruct((quarter, ports * LANES), BF)] * 2 + [
        jax.ShapeDtypeStruct((quarter, LANES), BF)
    ] * 2
    work = 2 * order * order * len(MAP_STEPS) * ports * tile
    part_shapes = [next_shape] + rim_shapes[:2] + [jax.ShapeDtypeStruct((2 * quarter, LANES), BF)]

    def early(first, maps, parts=()):
        last = first + len(maps)
        kernel = functools.partial(early_kernel, ports, first, last)
        flops = work * len(maps) // 7
        return whole_call(kernel, part_shapes, x, types, *sides, *maps, *parts, flops=flops)

    parts = list(early(0, [own_map, fetched[0]]))
    parts[1], fetched = lax.optimization_barrier((parts[1], fetched))
    swapped = [swap_cores(value) for value in fetched]
    parts = list(early(2, fetched[1:], parts))
    parts[1], half = lax.optimization_barrier((parts[1], half))
    swapped.append(swap_cores(half))
    done, *parts = parts
    late = swapped + [half]
    maps = [own_map] + fetched + late
    sent = whole_call(
        functools.partial(rim_kernel, ports, 4),
        rim_shapes,
        x,
        types,
        *sides,
        *late,
        *parts,
        flops=work // 8,
    )
    halos = exchange(sent[:2], "row") + exchange(sent[2:], "col")
    (x,) = whole_call(
        functools.partial(first_kernel, rows, ports, 4),
        [next_shape],
        x,
        types,
        done,
        *late,
        flops=work // 2,
    )
    ends_shape = jax.ShapeDtypeStruct((order, 2 * ports * LANES), BF)
    operands = [port_cell, x, types, profile, *halos, *maps]
    x, ends, *sent = pl.pallas_call(
        functools.partial(ends_kernel, rows, ports, width),
        in_specs=[ports_spec] + [WHOLE] * (len(operands) - 1),
        out_specs=[WHOLE] * 6,
        out_shape=[next_shape, ends_shape] + rim_shapes,
        compiler_params=PARAMS,
        cost_estimate=pl.CostEstimate(flops=work // 3, bytes_accessed=0, transcendentals=0),
    )(*operands)
    halos = exchange(sent[:2], "row") + exchange(sent[2:], "col")
    (x,) = whole_call(
        functools.partial(second_kernel, rows, ports, width),
        [next_shape],
        x,
        types,
        ends,
        *maps,
        flops=work * (rows - 2) // rows,
    )
    operands = [port_cell, x, profile, *halos]
    out = pl.pallas_call(
        functools.partial(last_kernel, rows, width),
        in_specs=[ports_spec] + [WHOLE] * (len(operands) - 1),
        out_specs=pl.BlockSpec(memory_space=pl.ANY),
        out_shape=jax.ShapeDtypeStruct((order, ports, rows, width), BF),
        scratch_shapes=[
            pltpu.VMEM((order, ports, rows, width), BF),
            pltpu.SemaphoreType.DMA((4,)),
        ],
        compiler_params=PARAMS,
    )(*operands)
    return out.reshape(traces.shape)


def solution(mesh):
    return jax.shard_map(
        body,
        mesh=mesh,
        in_specs=(
            P(None, None, None, "row", "col"),
            P("row", "col"),
            P(),
            P(),
            P("row", None, "col"),
            P("row", "col"),
            P("row", "col", None),
        ),
        out_specs=P(None, None, None, "row", "col"),
        check_vma=False,
    )
```

```python
import functools
import math

import jax
import jax.numpy as jnp
from jax import lax
from jax.experimental import pallas as pl
from jax.experimental.pallas import tpu as pltpu
from jax.sharding import PartitionSpec as P

BF = jnp.bfloat16
F32 = jnp.float32
LANES = 128
PARAMS = pltpu.CompilerParams(vmem_limit_bytes=20 * 2**20)
WIDE_PARAMS = pltpu.CompilerParams(vmem_limit_bytes=50 * 2**20)


def swap(value, first, second=None):
    second = first if second is None else second
    rows, cols = lax.axis_size("row"), lax.axis_size("col")
    pairs = []
    for row in range(rows):
        for col in range(cols):
            down, along = second if col % 2 else first
            pairs.append((row * cols + col, (row ^ down) * cols + (col ^ along)))
    return lax.ppermute(value, ("row", "col"), pairs)


def swap_cores(value):
    return swap(value, (0, 1))


def flat_kernel(x_hbm, out_ref, x_ref, sems):
    order, ports, rows, width = x_ref.shape
    quarter, tile = order // 4, rows * width
    edges = [slice(edge * quarter, (edge + 1) * quarter) for edge in range(4)]
    copies = [
        pltpu.make_async_copy(x_hbm.at[lines], x_ref.at[lines], sems.at[edge])
        for edge, lines in enumerate(edges)
    ]
    for copy in copies:
        copy.start()
    for copy, lines in zip(copies, edges):
        copy.wait()
        for port in range(ports):
            value = x_ref[lines, port].astype(F32).reshape(quarter, tile)
            out_ref[lines, port * tile : (port + 1) * tile] = value.astype(BF)


def partial_kernel(modes, *refs):
    left, right = [], []
    for ref in refs[:-1]:
        for start in range(0, ref.shape[0], 2 * modes):
            left.append(ref[start : start + modes])
            right.append(ref[start + modes : start + 2 * modes])
    refs[-1][...] = lax.dot_general(
        jnp.concatenate(left, axis=0),
        jnp.concatenate(right, axis=0),
        (((0,), (0,)), ((), ())),
        precision=lax.Precision.HIGHEST,
        preferred_element_type=F32,
    )


WHOLE = pl.BlockSpec(memory_space=pltpu.VMEM)


def whole_call(kernel, shapes, *operands, flops=0):
    return pl.pallas_call(
        kernel,
        in_specs=[WHOLE] * len(operands),
        out_specs=[WHOLE] * len(shapes),
        out_shape=shapes,
        compiler_params=PARAMS,
        cost_estimate=pl.CostEstimate(flops=flops, bytes_accessed=0, transcendentals=0),
    )(*operands)


def own_type_map(mode_shapes, mode_values, mode_weights, traces, types):
    modes, order = mode_weights.shape[1:]
    own = jnp.concatenate([mode_shapes[0].T, mode_weights[0]], axis=0)
    own = own * jnp.concatenate([mode_values[0], jnp.ones((modes,), F32)])[:, None]
    far = swap(own, (0, 4))
    pair = jnp.concatenate([own, swap_cores(own)], axis=0)
    pair, traces = lax.optimization_barrier((pair, traces))
    steps = (((0, 8), (0, 10)), ((0, 2), (0, 14)), ((0, 6), (0, 12)))
    got = [swap(pair, *step) for step in steps]
    shape = (order,) + traces.shape[2:]
    x = pl.pallas_call(
        flat_kernel,
        in_specs=[pl.BlockSpec(memory_space=pltpu.HBM)],
        out_specs=WHOLE,
        out_shape=jax.ShapeDtypeStruct((order, math.prod(shape[1:])), BF),
        scratch_shapes=[pltpu.VMEM(shape, BF), pltpu.SemaphoreType.DMA((4,))],
        compiler_params=WIDE_PARAMS,
        cost_estimate=pl.CostEstimate(flops=2**30, bytes_accessed=0, transcendentals=0),
    )(traces.reshape(shape))
    *got, x = lax.optimization_barrier((*got, x))
    (partial,) = whole_call(
        functools.partial(partial_kernel, modes),
        [jax.ShapeDtypeStruct((order, order), F32)],
        own,
        far,
        *got,
    )
    partial, x = lax.optimization_barrier((partial, x))
    other = swap_cores(partial)
    sides = whole_call(
        functools.partial(sides_kernel, traces.shape[2]),
        [jax.ShapeDtypeStruct((order, LANES), BF), jax.ShapeDtypeStruct((16, LANES), BF)],
        x,
        types,
        flops=2**30,
    )
    other, sides = lax.optimization_barrier((other, sides))
    shapes = [jax.ShapeDtypeStruct((lines, order), BF) for lines in (order, order // 2)]
    return *whole_call(own_kernel, shapes, partial, other), x, sides


MAP_STEPS = ((0, 0), (2, 3), (6, 7), (3, 2), (7, 6), (1, 1), (4, 5), (5, 4))
HALVES = 5


def own_kernel(one_ref, two_ref, out_ref, half_ref):
    core = lax.rem(lax.axis_index("col"), 2)
    half = half_ref.shape[0]
    total = (one_ref[...] + two_ref[...]).astype(BF)
    out_ref[...] = total
    half_ref[...] = jnp.where(core == 0, total[0:half], total[half:])


def relay_kernel(first_ref, second_ref, out_ref):
    core = lax.rem(lax.axis_index("col"), 2)
    out_ref[...] = jnp.where(core == 0, second_ref[...], first_ref[...])


def even(axis):
    return lax.rem(lax.axis_index(axis), 2) == 0


def halos_inside(axis, one, two):
    one, two = one[...].astype(F32), two[...].astype(F32)
    index, count = lax.axis_index(axis), lax.axis_size(axis)
    low = jnp.where(even(axis), two, one)
    high = jnp.where(even(axis), one, two)
    return jnp.where(index > 0, low, 0.0), jnp.where(index < count - 1, high, 0.0)


def store_rims(out_refs, axis, low, high):
    first, second = out_refs
    first[...] = jnp.where(even(axis), high, low).astype(BF)
    second[...] = jnp.where(even(axis), low, high).astype(BF)


def lane_of(value, lane):
    return jnp.broadcast_to(value[:, lane : lane + 1], (value.shape[0], LANES))


def port_profile_column(profile_ref, port, edge):
    samples = profile_ref.shape[2]
    row = lax.broadcasted_iota(jnp.int32, (samples, samples), 0)
    col = lax.broadcasted_iota(jnp.int32, (samples, samples), 1)
    line = jnp.broadcast_to(profile_ref[edge].astype(F32)[port : port + 1], row.shape)
    return jnp.sum(jnp.where(row == col, line, 0.0), axis=1, keepdims=True)


def port_place(port_ref, port, rows, width):
    all_cols = width * lax.axis_size("col")
    cell = port_ref[port]
    row = cell // all_cols - lax.axis_index("row") * rows
    col = cell % all_cols - lax.axis_index("col") * width
    return row, col, (row >= 0) & (row < rows) & (col >= 0) & (col < width)


def map_rows(map_refs, first, last):
    if len(map_refs) == 1:
        return map_refs[0][first:last, :]
    core = lax.rem(lax.axis_index("col"), 2)
    swapped, own = map_refs[0][...], map_refs[1][...]
    low, high = jnp.where(core == 0, own, swapped), jnp.where(core == 0, swapped, own)
    return jnp.concatenate([low, high], axis=0)[first:last]


def products(x, types, maps, first, last, total=None):
    mine = lax.axis_index("row")
    core = lax.rem(lax.axis_index("col"), 2)
    types = jnp.broadcast_to(types, x.shape)
    for (even, odd), map_refs in maps:
        kind = (mine ^ jnp.where(core == 0, even, odd)).astype(F32).astype(BF)
        masked = jnp.where(types == kind, x, jnp.zeros((), BF))
        part = map_rows(map_refs, first, last)
        product = jnp.dot(part, masked, preferred_element_type=F32)
        total = product if total is None else total + product
    return total


def with_steps(map_refs, first):
    map_refs, maps = list(map_refs), []
    while map_refs:
        number = first + len(maps)
        count = 2 if number == HALVES else 1
        maps.append((MAP_STEPS[number], map_refs[:count]))
        del map_refs[:count]
    return maps


def shifted(total, next_ref, rows):
    quarter = total.shape[0] // 4
    last = (rows - 1) * LANES
    north = total[0:quarter].astype(BF)
    south = total[quarter : 2 * quarter].astype(BF)
    next_ref[0:quarter, LANES:] = south[:, :last]
    next_ref[0:quarter, 0:LANES] = jnp.zeros((quarter, LANES), BF)
    next_ref[quarter : 2 * quarter, :last] = north[:, LANES:]
    next_ref[quarter : 2 * quarter, last:] = jnp.zeros((quarter, LANES), BF)
    for row in range(rows):
        cols = slice(row * LANES, (row + 1) * LANES)
        west = total[2 * quarter : 3 * quarter, cols]
        east = total[3 * quarter : 4 * quarter, cols]
        next_ref[2 * quarter : 3 * quarter, cols] = pltpu.roll(east, 1, 1).astype(BF)
        next_ref[3 * quarter : 4 * quarter, cols] = pltpu.roll(west, LANES - 1, 1).astype(BF)
    return north, south


def rim_columns(x_ref, types, ports, offset):
    tile = types.shape[1]
    starts = [port * tile + offset for port in range(ports)]
    cells = jnp.concatenate([x_ref[:, start : start + LANES] for start in starts], axis=1)
    return cells, jnp.concatenate([types[:, offset : offset + LANES]] * ports, axis=1).astype(BF)


def side_columns(x_ref, types, ports):
    order, tile = x_ref.shape[0], types.shape[1]
    rows = tile // LANES

    def pick(block_of, lines):
        lane = lax.broadcasted_iota(jnp.int32, (lines, LANES), 1)
        first = last = jnp.zeros((lines, LANES), F32)
        for place in range(ports * rows):
            turned = pltpu.roll(block_of(place), place + 1, 1)
            first = jnp.where(lane == place + 1, turned, first)
            last = jnp.where(lane == place, turned, last)
        first = pltpu.roll(first, LANES - 1, 1)
        return jnp.where(lane < 64, first, pltpu.roll(last, 64, 1)).astype(BF)

    def types_of(place):
        start = place % rows * LANES
        return jnp.broadcast_to(types[:, start : start + LANES], (16, LANES))

    quarter = order // 4
    sides = [
        pick(
            lambda place: x_ref[edge * quarter : (edge + 1) * quarter,
                                place * LANES : (place + 1) * LANES].astype(F32),
            quarter,
        )
        for edge in range(4)
    ]
    return jnp.concatenate(sides, axis=0), pick(types_of, 16)


def rims(x_ref, types, ports, sides, kinds, maps, so_far):
    order, tile = x_ref.shape[0], types.shape[1]
    quarter = order // 4
    before = [None if ref is None else ref[...].astype(F32) for ref in so_far]
    cells, cell_kinds = rim_columns(x_ref, types, ports, 0)
    north = products(cells, cell_kinds, maps, 0, quarter, before[0])
    cells, cell_kinds = rim_columns(x_ref, types, ports, tile - LANES)
    south = products(cells, cell_kinds, maps, quarter, 2 * quarter, before[1])
    side = products(sides, kinds, maps, 2 * quarter, order, before[2])
    return north.astype(BF), south.astype(BF), side.astype(BF)


def sides_kernel(ports, x_ref, types_ref, sides_ref, kinds_ref):
    sides_ref[...], kinds_ref[...] = side_columns(x_ref, types_ref[...].astype(F32), ports)


def early_kernel(ports, first, count, x_ref, types_ref, sides_ref, kinds_ref, *refs):
    maps = with_steps(refs[:count], first)
    types = types_ref[...].astype(F32)
    tile = types.shape[1]
    so_far, outs = refs[count:-4], refs[-4:]
    done_ref, *so_far = so_far if first else [None] * 4
    values = rims(x_ref, types, ports, sides_ref[...], kinds_ref[0:1, :], maps, so_far)
    for ref, value in zip(outs[1:], values):
        ref[...] = value
    for port in range(ports):
        cols = slice(port * tile, (port + 1) * tile)
        before = None if done_ref is None else done_ref[:, cols].astype(F32)
        total = products(x_ref[:, cols], types.astype(BF), maps, 0, x_ref.shape[0], before)
        outs[0][:, cols] = total.astype(BF)


def rim_kernel(ports, first, x_ref, types_ref, sides_ref, kinds_ref, *refs):
    maps = with_steps(refs[:-7], first)
    types = types_ref[...].astype(F32)
    quarter = x_ref.shape[0] // 4
    values = rims(x_ref, types, ports, sides_ref[...], kinds_ref[0:1, :], maps, refs[-7:-4])
    store_rims(refs[-4:-2], "row", values[0], values[1])
    store_rims(refs[-2:], "col", values[2][0:quarter], values[2][quarter:])


def first_kernel(rows, ports, first, x_ref, types_ref, done_ref, *refs):
    maps = with_steps(refs[:-1], first)
    types = types_ref[...].astype(F32).astype(BF)
    tile = types.shape[1]
    for port in range(ports):
        cols = slice(port * tile, (port + 1) * tile)
        before = done_ref[:, cols].astype(F32)
        total = products(x_ref[:, cols], types, maps, 0, x_ref.shape[0], before)
        shifted(total, refs[-1].at[:, cols], rows)


def patched(rows, width, x_ref, port_ref, profile_ref, halo_refs, places):
    order = x_ref.shape[0]
    quarter = order // 4
    north_in, south_in = halos_inside("row", *halo_refs[:2])
    west_in, east_in = halos_inside("col", *halo_refs[2:])
    lane = lax.broadcasted_iota(jnp.int32, (quarter, LANES), 1)
    blocks = []
    for port, row in places:
        place = port * rows + row
        rim = slice(port * LANES, (port + 1) * LANES)
        value = x_ref[:, place * LANES : (place + 1) * LANES].astype(F32)
        north, south, west, east = (value[i * quarter : (i + 1) * quarter] for i in range(4))
        north = north_in[:, rim] if row == 0 else north
        south = south_in[:, rim] if row == rows - 1 else south
        west = jnp.where(lane == 0, lane_of(west_in, 64 + place), west)
        east = jnp.where(lane == LANES - 1, lane_of(east_in, place), east)
        source_row, col, inside = port_place(port_ref, port, rows, width)
        here = lane == jnp.where(inside & (source_row == row), col, -1)
        columns = [
            jnp.where(here, part + port_profile_column(profile_ref, port, edge), part)
            for edge, part in enumerate((north, south, west, east))
        ]
        blocks.append(jnp.concatenate(columns, axis=0).astype(BF))
    return jnp.concatenate(blocks, axis=1)


def types_of_rows(types_ref, rows):
    types = types_ref[...].astype(F32)
    return jnp.concatenate([types[:, row * LANES : (row + 1) * LANES] for row in rows], axis=1)


def ends_kernel(rows, ports, width, port_ref, x_ref, types_ref, profile_ref, *refs):
    halo_refs, map_refs, patched_ref, ends_ref = refs[:4], refs[4:-6], refs[-6], refs[-5]
    order, tile = x_ref.shape[0], rows * width
    quarter = order // 4
    maps = with_steps(map_refs, 0)
    for port in range(ports):
        places = [(port, row) for row in range(rows)]
        value = patched(rows, width, x_ref, port_ref, profile_ref, halo_refs, places)
        patched_ref[:, port * tile : (port + 1) * tile] = value
    starts = [port * tile + row * width for row in (0, rows - 1) for port in range(ports)]
    block = jnp.concatenate([patched_ref[:, start : start + width] for start in starts], axis=1)
    types = types_of_rows(types_ref, [0] * ports + [rows - 1] * ports).astype(BF)
    total = products(block, types, maps, 0, order)
    ends_ref[...] = total.astype(BF)
    wide = ports * LANES
    store_rims(refs[-4:-2], "row", total[0:quarter, :wide], total[quarter : 2 * quarter, wide:])
    sides, kinds = side_columns(patched_ref, types_ref[...].astype(F32), ports)
    sides = products(sides, kinds[0:1], maps, 2 * quarter, order)
    store_rims(refs[-2:], "col", sides[0:quarter], sides[quarter:])


def second_kernel(rows, ports, width, x_ref, types_ref, ends_ref, *refs):
    map_refs, next_ref = refs[:-1], refs[-1]
    order, tile = x_ref.shape[0], rows * width
    maps = with_steps(map_refs, 0)
    types = types_of_rows(types_ref, range(1, rows - 1)).astype(BF)
    for port in range(ports):
        start = port * tile
        middle = products(x_ref[:, start + width : start + tile - width], types, maps, 0, order)
        top = ends_ref[:, port * LANES : (port + 1) * LANES].astype(F32)
        bottom = ends_ref[:, (ports + port) * LANES : (ports + port + 1) * LANES].astype(F32)
        total = jnp.concatenate([top, middle, bottom], axis=1)
        shifted(total, next_ref.at[:, start : start + tile], rows)


def last_kernel(rows, width, port_ref, x_ref, profile_ref, *refs):
    out_ref, buffer, sems = refs[4:]
    order, ports = buffer.shape[:2]
    quarter, tile = order // 4, rows * width
    north_in, south_in = halos_inside("row", *refs[:2])
    west_in, east_in = halos_inside("col", *refs[2:4])
    lane = lax.broadcasted_iota(jnp.int32, (quarter, LANES), 1)
    copies = []
    for edge in (2, 3, 0, 1):
        lines = slice(edge * quarter, (edge + 1) * quarter)
        for port in range(ports):
            rim = slice(port * LANES, (port + 1) * LANES)
            starts = [port * tile + row * LANES for row in range(rows)]
            parts = [x_ref[lines, start : start + LANES].astype(F32) for start in starts]
            places = range(port * rows, (port + 1) * rows)
            if edge == 0:
                parts[0] = north_in[:, rim]
            elif edge == 1:
                parts[-1] = south_in[:, rim]
            elif edge == 2:
                parts = [
                    jnp.where(lane == 0, lane_of(west_in, 64 + place), part)
                    for place, part in zip(places, parts)
                ]
            else:
                parts = [
                    jnp.where(lane == LANES - 1, lane_of(east_in, place), part)
                    for place, part in zip(places, parts)
                ]
            value = jnp.concatenate(parts, axis=1).reshape(quarter, rows, LANES)
            buffer[lines, port] = value.astype(BF)
        for port in range(ports):
            row, col, inside = port_place(port_ref, port, rows, width)

            @pl.when(inside)
            def _():
                current = buffer[lines, port].astype(F32)
                here = (lax.broadcasted_iota(jnp.int32, current.shape, 1) == row) & (
                    lax.broadcasted_iota(jnp.int32, current.shape, 2) == col
                )
                profile = port_profile_column(profile_ref, port, edge)
                profile = jnp.broadcast_to(profile, (quarter, LANES)).reshape(quarter, 1, LANES)
                added = current + jnp.broadcast_to(profile, current.shape)
                buffer[lines, port] = jnp.where(here, added, current).astype(BF)

        copy = pltpu.make_async_copy(buffer.at[lines], out_ref.at[lines], sems.at[edge])
        copy.start()
        copies.append(copy)
    for copy in copies:
        copy.wait()


def exchange(rims, axis):
    sizes = lax.axis_size("row"), lax.axis_size("col")
    at = ("row", "col").index(axis)

    def partner(place, first):
        place = list(place)
        other = place[at] + (1 if place[at] % 2 == first else -1)
        if 0 <= other < sizes[at]:
            place[at] = other
        else:
            place[1 - at] ^= 2
        return place[0] * sizes[1] + place[1]

    def pairs(first):
        places = [(row, col) for row in range(sizes[0]) for col in range(sizes[1])]
        return [(row * sizes[1] + col, partner((row, col), first)) for row, col in places]

    return [lax.ppermute(rim, ("row", "col"), pairs(first)) for first, rim in enumerate(rims)]


def body(traces, cell_type, port_cell, port_profile, mode_shapes, mode_values, mode_weights):
    edges, samples, ports, rows, width = traces.shape
    order = edges * samples
    quarter = samples
    tile = rows * width
    types = cell_type.reshape(1, tile)
    own_map, half, x, sides = own_type_map(mode_shapes, mode_values, mode_weights, traces, types)
    first = swap(own_map, (2, 0), (3, 8))
    second = swap(own_map, (6, 0), (7, 8))
    half = swap(half, (1, 8))
    profile = jnp.transpose(port_profile, (0, 2, 1))
    ports_spec = pl.BlockSpec(memory_space=pltpu.SMEM)
    next_shape = jax.ShapeDtypeStruct((order, ports * tile), BF)
    rim_shapes = [jax.ShapeDtypeStruct((quarter, ports * LANES), BF)] * 2 + [
        jax.ShapeDtypeStruct((quarter, LANES), BF)
    ] * 2
    work = 2 * order * order * len(MAP_STEPS) * ports * tile
    part_shapes = [next_shape] + rim_shapes[:2] + [jax.ShapeDtypeStruct((2 * quarter, LANES), BF)]

    def early(first, maps, parts=()):
        kernel = functools.partial(early_kernel, ports, first, len(maps))
        flops = work * len(maps) // 7
        return whole_call(kernel, part_shapes, x, types, *sides, *maps, *parts, flops=flops)

    parts = list(early(0, [own_map, first]))
    parts[1], first, second, half = lax.optimization_barrier((parts[1], first, second, half))
    map_shape = jax.ShapeDtypeStruct(own_map.shape, BF)
    (relay,) = whole_call(relay_kernel, [map_shape], first, second)
    relay, first, second, half = lax.optimization_barrier((relay, first, second, half))
    third = swap(relay, (2, 0), (6, 0))
    maps = [second, swap_cores(first), swap_cores(second), swap_cores(half), half]
    parts = list(early(2, maps, parts))
    parts[1], third = lax.optimization_barrier((parts[1], third))
    done, *parts = parts
    late = [third, swap_cores(third)]
    maps = [own_map, first] + maps + late
    sent = whole_call(
        functools.partial(rim_kernel, ports, 6),
        rim_shapes,
        x,
        types,
        *sides,
        *late,
        *parts,
        flops=work // 8,
    )
    halos = exchange(sent[:2], "row") + exchange(sent[2:], "col")
    (x,) = whole_call(
        functools.partial(first_kernel, rows, ports, 6),
        [next_shape],
        x,
        types,
        done,
        *late,
        flops=work // 2,
    )
    ends_shape = jax.ShapeDtypeStruct((order, 2 * ports * LANES), BF)
    operands = [port_cell, x, types, profile, *halos, *maps]
    x, ends, *sent = pl.pallas_call(
        functools.partial(ends_kernel, rows, ports, width),
        in_specs=[ports_spec] + [WHOLE] * (len(operands) - 1),
        out_specs=[WHOLE] * 6,
        out_shape=[next_shape, ends_shape] + rim_shapes,
        compiler_params=PARAMS,
        cost_estimate=pl.CostEstimate(flops=work // 3, bytes_accessed=0, transcendentals=0),
    )(*operands)
    halos = exchange(sent[:2], "row") + exchange(sent[2:], "col")
    (x,) = whole_call(
        functools.partial(second_kernel, rows, ports, width),
        [next_shape],
        x,
        types,
        ends,
        *maps,
        flops=work * (rows - 2) // rows,
    )
    operands = [port_cell, x, profile, *halos]
    out = pl.pallas_call(
        functools.partial(last_kernel, rows, width),
        in_specs=[ports_spec] + [WHOLE] * (len(operands) - 1),
        out_specs=pl.BlockSpec(memory_space=pl.ANY),
        out_shape=jax.ShapeDtypeStruct((order, ports, rows, width), BF),
        scratch_shapes=[
            pltpu.VMEM((order, ports, rows, width), BF),
            pltpu.SemaphoreType.DMA((4,)),
        ],
        compiler_params=PARAMS,
    )(*operands)
    return out.reshape(traces.shape)


def solution(mesh):
    return jax.shard_map(
        body,
        mesh=mesh,
        in_specs=(
            P(None, None, None, "row", "col"),
            P("row", "col"),
            P(),
            P(),
            P("row", None, "col"),
            P("row", "col"),
            P("row", "col", None),
        ),
        out_specs=P(None, None, None, "row", "col"),
        check_vma=False,
    )
```

```python
import functools
import math

import jax
import jax.numpy as jnp
from jax import lax
from jax.experimental import pallas as pl
from jax.experimental.pallas import tpu as pltpu
from jax.sharding import PartitionSpec as P

BF = jnp.bfloat16
F32 = jnp.float32
LANES = 128
PARAMS = pltpu.CompilerParams(vmem_limit_bytes=20 * 2**20)
WIDE_PARAMS = pltpu.CompilerParams(vmem_limit_bytes=50 * 2**20)


def swap(value, first, second=None):
    second = first if second is None else second
    rows, cols = lax.axis_size("row"), lax.axis_size("col")
    pairs = []
    for row in range(rows):
        for col in range(cols):
            down, along = second if col % 2 else first
            pairs.append((row * cols + col, (row ^ down) * cols + (col ^ along)))
    return lax.ppermute(value, ("row", "col"), pairs)


def swap_cores(value):
    return swap(value, (0, 1))


def flat_kernel(x_hbm, out_ref, x_ref, sems):
    order, ports, rows, width = x_ref.shape
    quarter, tile = order // 4, rows * width
    edges = [slice(edge * quarter, (edge + 1) * quarter) for edge in range(4)]
    copies = [
        pltpu.make_async_copy(x_hbm.at[lines], x_ref.at[lines], sems.at[edge])
        for edge, lines in enumerate(edges)
    ]
    for copy in copies:
        copy.start()
    for copy, lines in zip(copies, edges):
        copy.wait()
        for port in range(ports):
            value = x_ref[lines, port].astype(F32).reshape(quarter, tile)
            out_ref[lines, port * tile : (port + 1) * tile] = value.astype(BF)


def partial_kernel(modes, *refs):
    left, right = [], []
    for ref in refs[:-1]:
        for start in range(0, ref.shape[0], 2 * modes):
            left.append(ref[start : start + modes])
            right.append(ref[start + modes : start + 2 * modes])
    refs[-1][...] = lax.dot_general(
        jnp.concatenate(left, axis=0),
        jnp.concatenate(right, axis=0),
        (((0,), (0,)), ((), ())),
        precision=lax.Precision.HIGHEST,
        preferred_element_type=F32,
    )


WHOLE = pl.BlockSpec(memory_space=pltpu.VMEM)


def whole_call(kernel, shapes, *operands, flops=0):
    return pl.pallas_call(
        kernel,
        in_specs=[WHOLE] * len(operands),
        out_specs=[WHOLE] * len(shapes),
        out_shape=shapes,
        compiler_params=PARAMS,
        cost_estimate=pl.CostEstimate(flops=flops, bytes_accessed=0, transcendentals=0),
    )(*operands)


def own_type_map(mode_shapes, mode_values, mode_weights, traces, types):
    modes, order = mode_weights.shape[1:]
    own = jnp.concatenate([mode_shapes[0].T, mode_weights[0]], axis=0)
    own = own * jnp.concatenate([mode_values[0], jnp.ones((modes,), F32)])[:, None]
    far = swap(own, (0, 4))
    pair = jnp.concatenate([own, swap_cores(own)], axis=0)
    pair, traces = lax.optimization_barrier((pair, traces))
    steps = (((0, 8), (0, 10)), ((0, 2), (0, 14)), ((0, 6), (0, 12)))
    got = [swap(pair, *step) for step in steps]
    shape = (order,) + traces.shape[2:]
    x = pl.pallas_call(
        flat_kernel,
        in_specs=[pl.BlockSpec(memory_space=pltpu.HBM)],
        out_specs=WHOLE,
        out_shape=jax.ShapeDtypeStruct((order, math.prod(shape[1:])), BF),
        scratch_shapes=[pltpu.VMEM(shape, BF), pltpu.SemaphoreType.DMA((4,))],
        compiler_params=WIDE_PARAMS,
        cost_estimate=pl.CostEstimate(flops=2**30, bytes_accessed=0, transcendentals=0),
    )(traces.reshape(shape))
    *got, x = lax.optimization_barrier((*got, x))
    (partial,) = whole_call(
        functools.partial(partial_kernel, modes),
        [jax.ShapeDtypeStruct((order, order), F32)],
        own,
        far,
        *got,
    )
    partial, x = lax.optimization_barrier((partial, x))
    other = swap_cores(partial)
    sides = whole_call(
        functools.partial(sides_kernel, traces.shape[2]),
        [jax.ShapeDtypeStruct((order, LANES), BF), jax.ShapeDtypeStruct((16, LANES), BF)],
        x,
        types,
        flops=2**30,
    )
    other, sides = lax.optimization_barrier((other, sides))
    shapes = [jax.ShapeDtypeStruct((lines, order), BF) for lines in (order, order // 2)]
    return *whole_call(own_kernel, shapes, partial, other), x, sides


MAP_STEPS = ((0, 0), (2, 3), (6, 7), (3, 2), (7, 6), (1, 1), (4, 5), (5, 4))
HALVES = 5


def own_kernel(one_ref, two_ref, out_ref, half_ref):
    core = lax.rem(lax.axis_index("col"), 2)
    half = half_ref.shape[0]
    total = (one_ref[...] + two_ref[...]).astype(BF)
    out_ref[...] = total
    half_ref[...] = jnp.where(core == 0, total[0:half], total[half:])


def relay_kernel(first_ref, second_ref, out_ref):
    core = lax.rem(lax.axis_index("col"), 2)
    out_ref[...] = jnp.where(core == 0, second_ref[...], first_ref[...])


def even(axis):
    return lax.rem(lax.axis_index(axis), 2) == 0


def halos_inside(axis, one, two):
    one, two = one[...].astype(F32), two[...].astype(F32)
    index, count = lax.axis_index(axis), lax.axis_size(axis)
    low = jnp.where(even(axis), two, one)
    high = jnp.where(even(axis), one, two)
    return jnp.where(index > 0, low, 0.0), jnp.where(index < count - 1, high, 0.0)


def store_rims(out_refs, axis, low, high):
    first, second = out_refs
    first[...] = jnp.where(even(axis), high, low).astype(BF)
    second[...] = jnp.where(even(axis), low, high).astype(BF)


def lane_of(value, lane):
    return jnp.broadcast_to(value[:, lane : lane + 1], (value.shape[0], LANES))


def port_profile_column(profile_ref, port, edge):
    samples = profile_ref.shape[2]
    row = lax.broadcasted_iota(jnp.int32, (samples, samples), 0)
    col = lax.broadcasted_iota(jnp.int32, (samples, samples), 1)
    line = jnp.broadcast_to(profile_ref[edge].astype(F32)[port : port + 1], row.shape)
    return jnp.sum(jnp.where(row == col, line, 0.0), axis=1, keepdims=True)


def port_place(port_ref, port, rows, width):
    all_cols = width * lax.axis_size("col")
    cell = port_ref[port]
    row = cell // all_cols - lax.axis_index("row") * rows
    col = cell % all_cols - lax.axis_index("col") * width
    return row, col, (row >= 0) & (row < rows) & (col >= 0) & (col < width)


def map_rows(map_refs, first, last):
    if len(map_refs) == 1:
        return map_refs[0][first:last, :]
    core = lax.rem(lax.axis_index("col"), 2)
    swapped, own = map_refs[0][...], map_refs[1][...]
    low, high = jnp.where(core == 0, own, swapped), jnp.where(core == 0, swapped, own)
    return jnp.concatenate([low, high], axis=0)[first:last]


def products(x, types, maps, first, last, total=None):
    mine = lax.axis_index("row")
    core = lax.rem(lax.axis_index("col"), 2)
    types = jnp.broadcast_to(types, x.shape)
    for (even, odd), map_refs in maps:
        kind = (mine ^ jnp.where(core == 0, even, odd)).astype(F32).astype(BF)
        masked = jnp.where(types == kind, x, jnp.zeros((), BF))
        part = map_rows(map_refs, first, last)
        product = jnp.dot(part, masked, preferred_element_type=F32)
        total = product if total is None else total + product
    return total


def with_steps(map_refs, first):
    map_refs, maps = list(map_refs), []
    while map_refs:
        number = first + len(maps)
        count = 2 if number == HALVES else 1
        maps.append((MAP_STEPS[number], map_refs[:count]))
        del map_refs[:count]
    return maps


def shifted(total, next_ref, rows):
    quarter = total.shape[0] // 4
    last = (rows - 1) * LANES
    north = total[0:quarter].astype(BF)
    south = total[quarter : 2 * quarter].astype(BF)
    next_ref[0:quarter, LANES:] = south[:, :last]
    next_ref[0:quarter, 0:LANES] = jnp.zeros((quarter, LANES), BF)
    next_ref[quarter : 2 * quarter, :last] = north[:, LANES:]
    next_ref[quarter : 2 * quarter, last:] = jnp.zeros((quarter, LANES), BF)
    for row in range(rows):
        cols = slice(row * LANES, (row + 1) * LANES)
        west = total[2 * quarter : 3 * quarter, cols]
        east = total[3 * quarter : 4 * quarter, cols]
        next_ref[2 * quarter : 3 * quarter, cols] = pltpu.roll(east, 1, 1).astype(BF)
        next_ref[3 * quarter : 4 * quarter, cols] = pltpu.roll(west, LANES - 1, 1).astype(BF)
    return north, south


def rim_columns(x_ref, types, ports, offset):
    tile = types.shape[1]
    starts = [port * tile + offset for port in range(ports)]
    cells = jnp.concatenate([x_ref[:, start : start + LANES] for start in starts], axis=1)
    return cells, jnp.concatenate([types[:, offset : offset + LANES]] * ports, axis=1).astype(BF)


def side_columns(x_ref, types, ports):
    order, tile = x_ref.shape[0], types.shape[1]
    rows = tile // LANES

    def pick(block_of, lines):
        lane = lax.broadcasted_iota(jnp.int32, (lines, LANES), 1)
        first = last = jnp.zeros((lines, LANES), F32)
        for place in range(ports * rows):
            turned = pltpu.roll(block_of(place), place + 1, 1)
            first = jnp.where(lane == place + 1, turned, first)
            last = jnp.where(lane == place, turned, last)
        first = pltpu.roll(first, LANES - 1, 1)
        return jnp.where(lane < 64, first, pltpu.roll(last, 64, 1)).astype(BF)

    def types_of(place):
        start = place % rows * LANES
        return jnp.broadcast_to(types[:, start : start + LANES], (16, LANES))

    quarter = order // 4
    sides = [
        pick(
            lambda place: x_ref[edge * quarter : (edge + 1) * quarter,
                                place * LANES : (place + 1) * LANES].astype(F32),
            quarter,
        )
        for edge in range(4)
    ]
    return jnp.concatenate(sides, axis=0), pick(types_of, 16)


def rims(x_ref, types, ports, sides, kinds, maps, so_far):
    order, tile = x_ref.shape[0], types.shape[1]
    quarter = order // 4
    before = [None if ref is None else ref[...].astype(F32) for ref in so_far]
    cells, cell_kinds = rim_columns(x_ref, types, ports, 0)
    north = products(cells, cell_kinds, maps, 0, quarter, before[0])
    cells, cell_kinds = rim_columns(x_ref, types, ports, tile - LANES)
    south = products(cells, cell_kinds, maps, quarter, 2 * quarter, before[1])
    side = products(sides, kinds, maps, 2 * quarter, order, before[2])
    return north.astype(BF), south.astype(BF), side.astype(BF)


def sides_kernel(ports, x_ref, types_ref, sides_ref, kinds_ref):
    sides_ref[...], kinds_ref[...] = side_columns(x_ref, types_ref[...].astype(F32), ports)


def early_kernel(ports, first, count, x_ref, types_ref, sides_ref, kinds_ref, *refs):
    maps = with_steps(refs[:count], first)
    types = types_ref[...].astype(F32)
    tile = types.shape[1]
    so_far, outs = refs[count:-4], refs[-4:]
    done_ref, *so_far = so_far if first else [None] * 4
    values = rims(x_ref, types, ports, sides_ref[...], kinds_ref[0:1, :], maps, so_far)
    for ref, value in zip(outs[1:], values):
        ref[...] = value
    for port in range(ports):
        cols = slice(port * tile, (port + 1) * tile)
        before = None if done_ref is None else done_ref[:, cols].astype(F32)
        total = products(x_ref[:, cols], types.astype(BF), maps, 0, x_ref.shape[0], before)
        outs[0][:, cols] = total.astype(BF)


def rim_kernel(ports, first, x_ref, types_ref, sides_ref, kinds_ref, *refs):
    maps = with_steps(refs[:-7], first)
    types = types_ref[...].astype(F32)
    quarter = x_ref.shape[0] // 4
    values = rims(x_ref, types, ports, sides_ref[...], kinds_ref[0:1, :], maps, refs[-7:-4])
    store_rims(refs[-4:-2], "row", values[0], values[1])
    store_rims(refs[-2:], "col", values[2][0:quarter], values[2][quarter:])


def first_kernel(rows, ports, first, x_ref, types_ref, done_ref, *refs):
    maps = with_steps(refs[:-1], first)
    types = types_ref[...].astype(F32).astype(BF)
    tile = types.shape[1]
    for port in range(ports):
        cols = slice(port * tile, (port + 1) * tile)
        before = done_ref[:, cols].astype(F32)
        total = products(x_ref[:, cols], types, maps, 0, x_ref.shape[0], before)
        shifted(total, refs[-1].at[:, cols], rows)


def patched(rows, width, x_ref, port_ref, profile_ref, halo_refs, places):
    order = x_ref.shape[0]
    quarter = order // 4
    north_in, south_in = halos_inside("row", *halo_refs[:2])
    west_in, east_in = halos_inside("col", *halo_refs[2:])
    lane = lax.broadcasted_iota(jnp.int32, (quarter, LANES), 1)
    blocks = []
    for port, row in places:
        place = port * rows + row
        rim = slice(port * LANES, (port + 1) * LANES)
        value = x_ref[:, place * LANES : (place + 1) * LANES].astype(F32)
        north, south, west, east = (value[i * quarter : (i + 1) * quarter] for i in range(4))
        north = north_in[:, rim] if row == 0 else north
        south = south_in[:, rim] if row == rows - 1 else south
        west = jnp.where(lane == 0, lane_of(west_in, 64 + place), west)
        east = jnp.where(lane == LANES - 1, lane_of(east_in, place), east)
        source_row, col, inside = port_place(port_ref, port, rows, width)
        here = lane == jnp.where(inside & (source_row == row), col, -1)
        columns = [
            jnp.where(here, part + port_profile_column(profile_ref, port, edge), part)
            for edge, part in enumerate((north, south, west, east))
        ]
        blocks.append(jnp.concatenate(columns, axis=0).astype(BF))
    return jnp.concatenate(blocks, axis=1)


def types_of_rows(types_ref, rows):
    types = types_ref[...].astype(F32)
    return jnp.concatenate([types[:, row * LANES : (row + 1) * LANES] for row in rows], axis=1)


def ends_kernel(rows, ports, width, port_ref, x_ref, types_ref, profile_ref, *refs):
    halo_refs, map_refs, patched_ref, ends_ref = refs[:4], refs[4:-6], refs[-6], refs[-5]
    order, tile = x_ref.shape[0], rows * width
    quarter = order // 4
    maps = with_steps(map_refs, 0)
    for port in range(ports):
        places = [(port, row) for row in range(rows)]
        value = patched(rows, width, x_ref, port_ref, profile_ref, halo_refs, places)
        patched_ref[:, port * tile : (port + 1) * tile] = value
    starts = [port * tile + row * width for row in (0, rows - 1) for port in range(ports)]
    block = jnp.concatenate([patched_ref[:, start : start + width] for start in starts], axis=1)
    types = types_of_rows(types_ref, [0] * ports + [rows - 1] * ports).astype(BF)
    total = products(block, types, maps, 0, order)
    ends_ref[...] = total.astype(BF)
    wide = ports * LANES
    store_rims(refs[-4:-2], "row", total[0:quarter, :wide], total[quarter : 2 * quarter, wide:])
    sides, kinds = side_columns(patched_ref, types_ref[...].astype(F32), ports)
    sides = products(sides, kinds[0:1], maps, 2 * quarter, order)
    store_rims(refs[-2:], "col", sides[0:quarter], sides[quarter:])


def second_kernel(rows, ports, width, x_ref, types_ref, ends_ref, *refs):
    map_refs, next_ref = refs[:-1], refs[-1]
    order, tile = x_ref.shape[0], rows * width
    maps = with_steps(map_refs, 0)
    types = types_of_rows(types_ref, range(1, rows - 1)).astype(BF)
    for port in range(ports):
        start = port * tile
        middle = products(x_ref[:, start + width : start + tile - width], types, maps, 0, order)
        top = ends_ref[:, port * LANES : (port + 1) * LANES].astype(F32)
        bottom = ends_ref[:, (ports + port) * LANES : (ports + port + 1) * LANES].astype(F32)
        total = jnp.concatenate([top, middle, bottom], axis=1)
        shifted(total, next_ref.at[:, start : start + tile], rows)


def last_kernel(rows, width, port_ref, x_ref, profile_ref, *refs):
    out_ref, buffer, sems = refs[4:]
    order, ports = buffer.shape[:2]
    quarter, tile = order // 4, rows * width
    north_in, south_in = halos_inside("row", *refs[:2])
    west_in, east_in = halos_inside("col", *refs[2:4])
    lane = lax.broadcasted_iota(jnp.int32, (quarter, LANES), 1)
    copies = []
    for edge in (2, 3, 0, 1):
        lines = slice(edge * quarter, (edge + 1) * quarter)
        for port in range(ports):
            rim = slice(port * LANES, (port + 1) * LANES)
            starts = [port * tile + row * LANES for row in range(rows)]
            parts = [x_ref[lines, start : start + LANES].astype(F32) for start in starts]
            places = range(port * rows, (port + 1) * rows)
            if edge == 0:
                parts[0] = north_in[:, rim]
            elif edge == 1:
                parts[-1] = south_in[:, rim]
            elif edge == 2:
                parts = [
                    jnp.where(lane == 0, lane_of(west_in, 64 + place), part)
                    for place, part in zip(places, parts)
                ]
            else:
                parts = [
                    jnp.where(lane == LANES - 1, lane_of(east_in, place), part)
                    for place, part in zip(places, parts)
                ]
            value = jnp.concatenate(parts, axis=1).reshape(quarter, rows, LANES)
            buffer[lines, port] = value.astype(BF)
        for port in range(ports):
            row, col, inside = port_place(port_ref, port, rows, width)

            @pl.when(inside)
            def _():
                current = buffer[lines, port].astype(F32)
                here = (lax.broadcasted_iota(jnp.int32, current.shape, 1) == row) & (
                    lax.broadcasted_iota(jnp.int32, current.shape, 2) == col
                )
                profile = port_profile_column(profile_ref, port, edge)
                profile = jnp.broadcast_to(profile, (quarter, LANES)).reshape(quarter, 1, LANES)
                added = current + jnp.broadcast_to(profile, current.shape)
                buffer[lines, port] = jnp.where(here, added, current).astype(BF)

        copy = pltpu.make_async_copy(buffer.at[lines], out_ref.at[lines], sems.at[edge])
        copy.start()
        copies.append(copy)
    for copy in copies:
        copy.wait()


def exchange(rims, axis):
    sizes = lax.axis_size("row"), lax.axis_size("col")
    at = ("row", "col").index(axis)

    def partner(place, first):
        place = list(place)
        other = place[at] + (1 if place[at] % 2 == first else -1)
        if 0 <= other < sizes[at]:
            place[at] = other
        else:
            place[1 - at] ^= 2
        return place[0] * sizes[1] + place[1]

    def pairs(first):
        places = [(row, col) for row in range(sizes[0]) for col in range(sizes[1])]
        return [(row * sizes[1] + col, partner((row, col), first)) for row, col in places]

    return [lax.ppermute(rim, ("row", "col"), pairs(first)) for first, rim in enumerate(rims)]


def body(traces, cell_type, port_cell, port_profile, mode_shapes, mode_values, mode_weights):
    edges, samples, ports, rows, width = traces.shape
    order = edges * samples
    quarter = samples
    tile = rows * width
    types = cell_type.reshape(1, tile)
    own_map, half, x, sides = own_type_map(mode_shapes, mode_values, mode_weights, traces, types)
    first = swap(own_map, (2, 0), (3, 8))
    second = swap(own_map, (6, 0), (7, 8))
    half = swap(half, (1, 8))
    profile = jnp.transpose(port_profile, (0, 2, 1))
    ports_spec = pl.BlockSpec(memory_space=pltpu.SMEM)
    next_shape = jax.ShapeDtypeStruct((order, ports * tile), BF)
    rim_shapes = [jax.ShapeDtypeStruct((quarter, ports * LANES), BF)] * 2 + [
        jax.ShapeDtypeStruct((quarter, LANES), BF)
    ] * 2
    work = 2 * order * order * len(MAP_STEPS) * ports * tile
    part_shapes = [next_shape] + rim_shapes[:2] + [jax.ShapeDtypeStruct((2 * quarter, LANES), BF)]

    def early(first, maps, parts=()):
        kernel = functools.partial(early_kernel, ports, first, len(maps))
        flops = work * len(maps) // 7
        return whole_call(kernel, part_shapes, x, types, *sides, *maps, *parts, flops=flops)

    parts = list(early(0, [own_map, first]))
    parts[1], first, second, half = lax.optimization_barrier((parts[1], first, second, half))
    map_shape = jax.ShapeDtypeStruct(own_map.shape, BF)
    (relay,) = whole_call(relay_kernel, [map_shape], first, second)
    relay, first, second, half = lax.optimization_barrier((relay, first, second, half))
    third = swap(relay, (2, 0), (6, 0))
    maps = [second, swap_cores(first), swap_cores(second), swap_cores(half), half]
    parts = list(early(2, maps, parts))
    parts[1], third = lax.optimization_barrier((parts[1], third))
    done, *parts = parts
    late = [third, swap_cores(third)]
    maps = [own_map, first] + maps + late
    sent = whole_call(
        functools.partial(rim_kernel, ports, 6),
        rim_shapes,
        x,
        types,
        *sides,
        *late,
        *parts,
        flops=work // 8,
    )
    halos = exchange(sent[:2], "row") + exchange(sent[2:], "col")
    (x,) = whole_call(
        functools.partial(first_kernel, rows, ports, 6),
        [next_shape],
        x,
        types,
        done,
        *late,
        flops=work // 5000,
    )
    ends_shape = jax.ShapeDtypeStruct((order, 2 * ports * LANES), BF)
    operands = [port_cell, x, types, profile, *halos, *maps]
    x, ends, *sent = pl.pallas_call(
        functools.partial(ends_kernel, rows, ports, width),
        in_specs=[ports_spec] + [WHOLE] * (len(operands) - 1),
        out_specs=[WHOLE] * 6,
        out_shape=[next_shape, ends_shape] + rim_shapes,
        compiler_params=PARAMS,
        cost_estimate=pl.CostEstimate(flops=work // 3, bytes_accessed=0, transcendentals=0),
    )(*operands)
    halos = exchange(sent[:2], "row") + exchange(sent[2:], "col")
    (x,) = whole_call(
        functools.partial(second_kernel, rows, ports, width),
        [next_shape],
        x,
        types,
        ends,
        *maps,
        flops=work // 5000,
    )
    operands = [port_cell, x, profile, *halos]
    out = pl.pallas_call(
        functools.partial(last_kernel, rows, width),
        in_specs=[ports_spec] + [WHOLE] * (len(operands) - 1),
        out_specs=pl.BlockSpec(memory_space=pl.ANY),
        out_shape=jax.ShapeDtypeStruct((order, ports, rows, width), BF),
        scratch_shapes=[
            pltpu.VMEM((order, ports, rows, width), BF),
            pltpu.SemaphoreType.DMA((4,)),
        ],
        compiler_params=PARAMS,
    )(*operands)
    return out.reshape(traces.shape)


def solution(mesh):
    return jax.shard_map(
        body,
        mesh=mesh,
        in_specs=(
            P(None, None, None, "row", "col"),
            P("row", "col"),
            P(),
            P(),
            P("row", None, "col"),
            P("row", "col"),
            P("row", "col", None),
        ),
        out_specs=P(None, None, None, "row", "col"),
        check_vma=False,
    )
```

```python
import functools
import math

import jax
import jax.numpy as jnp
from jax import lax
from jax.experimental import pallas as pl
from jax.experimental.pallas import tpu as pltpu
from jax.sharding import PartitionSpec as P

BF = jnp.bfloat16
F32 = jnp.float32
LANES = 128
PARAMS = pltpu.CompilerParams(vmem_limit_bytes=20 * 2**20)
WIDE_PARAMS = pltpu.CompilerParams(vmem_limit_bytes=50 * 2**20)


def swap(value, first, second=None):
    second = first if second is None else second
    rows, cols = lax.axis_size("row"), lax.axis_size("col")
    pairs = []
    for row in range(rows):
        for col in range(cols):
            down, along = second if col % 2 else first
            pairs.append((row * cols + col, (row ^ down) * cols + (col ^ along)))
    return lax.ppermute(value, ("row", "col"), pairs)


def swap_cores(value):
    return swap(value, (0, 1))


def flat_kernel(x_hbm, out_ref, x_ref, sems):
    order, ports, rows, width = x_ref.shape
    quarter, tile = order // 4, rows * width
    edges = [slice(edge * quarter, (edge + 1) * quarter) for edge in range(4)]
    copies = [
        pltpu.make_async_copy(x_hbm.at[lines], x_ref.at[lines], sems.at[edge])
        for edge, lines in enumerate(edges)
    ]
    for copy in copies:
        copy.start()
    for copy, lines in zip(copies, edges):
        copy.wait()
        for port in range(ports):
            value = x_ref[lines, port].astype(F32).reshape(quarter, tile)
            out_ref[lines, port * tile : (port + 1) * tile] = value.astype(BF)


def partial_kernel(modes, *refs):
    left, right = [], []
    for ref in refs[:-1]:
        for start in range(0, ref.shape[0], 2 * modes):
            left.append(ref[start : start + modes])
            right.append(ref[start + modes : start + 2 * modes])
    refs[-1][...] = lax.dot_general(
        jnp.concatenate(left, axis=0),
        jnp.concatenate(right, axis=0),
        (((0,), (0,)), ((), ())),
        precision=lax.Precision.HIGHEST,
        preferred_element_type=F32,
    )


WHOLE = pl.BlockSpec(memory_space=pltpu.VMEM)


def whole_call(kernel, shapes, *operands, flops=0):
    return pl.pallas_call(
        kernel,
        in_specs=[WHOLE] * len(operands),
        out_specs=[WHOLE] * len(shapes),
        out_shape=shapes,
        compiler_params=PARAMS,
        cost_estimate=pl.CostEstimate(flops=flops, bytes_accessed=0, transcendentals=0),
    )(*operands)


def own_type_map(mode_shapes, mode_values, mode_weights, traces, types):
    modes, order = mode_weights.shape[1:]
    own = jnp.concatenate([mode_shapes[0].T, mode_weights[0]], axis=0)
    own = own * jnp.concatenate([mode_values[0], jnp.ones((modes,), F32)])[:, None]
    far = swap(own, (0, 4))
    pair = jnp.concatenate([own, swap_cores(own)], axis=0)
    pair, traces = lax.optimization_barrier((pair, traces))
    steps = (((0, 8), (0, 10)), ((0, 2), (0, 14)), ((0, 6), (0, 12)))
    got = [swap(pair, *step) for step in steps]
    shape = (order,) + traces.shape[2:]
    x = pl.pallas_call(
        flat_kernel,
        in_specs=[pl.BlockSpec(memory_space=pltpu.HBM)],
        out_specs=WHOLE,
        out_shape=jax.ShapeDtypeStruct((order, math.prod(shape[1:])), BF),
        scratch_shapes=[pltpu.VMEM(shape, BF), pltpu.SemaphoreType.DMA((4,))],
        compiler_params=WIDE_PARAMS,
        cost_estimate=pl.CostEstimate(flops=2**30, bytes_accessed=0, transcendentals=0),
    )(traces.reshape(shape))
    *got, x = lax.optimization_barrier((*got, x))
    (partial,) = whole_call(
        functools.partial(partial_kernel, modes),
        [jax.ShapeDtypeStruct((order, order), F32)],
        own,
        far,
        *got,
    )
    partial, x = lax.optimization_barrier((partial, x))
    other = swap_cores(partial)
    sides = whole_call(
        functools.partial(sides_kernel, traces.shape[2]),
        [jax.ShapeDtypeStruct((order, LANES), BF), jax.ShapeDtypeStruct((16, LANES), BF)],
        x,
        types,
        flops=2**30,
    )
    other, sides = lax.optimization_barrier((other, sides))
    shapes = [jax.ShapeDtypeStruct((lines, order), BF) for lines in (order, order // 2)]
    return *whole_call(own_kernel, shapes, partial, other), x, sides


MAP_STEPS = ((0, 0), (2, 3), (6, 7), (3, 2), (7, 6), (1, 1), (4, 5), (5, 4))
HALVES = 5


def own_kernel(one_ref, two_ref, out_ref, half_ref):
    core = lax.rem(lax.axis_index("col"), 2)
    half = half_ref.shape[0]
    total = (one_ref[...] + two_ref[...]).astype(BF)
    out_ref[...] = total
    half_ref[...] = jnp.where(core == 0, total[0:half], total[half:])


def relay_kernel(first_ref, second_ref, out_ref):
    core = lax.rem(lax.axis_index("col"), 2)
    out_ref[...] = jnp.where(core == 0, second_ref[...], first_ref[...])


def even(axis):
    return lax.rem(lax.axis_index(axis), 2) == 0


def halos_inside(axis, one, two):
    one, two = one[...].astype(F32), two[...].astype(F32)
    index, count = lax.axis_index(axis), lax.axis_size(axis)
    low = jnp.where(even(axis), two, one)
    high = jnp.where(even(axis), one, two)
    return jnp.where(index > 0, low, 0.0), jnp.where(index < count - 1, high, 0.0)


def store_rims(out_refs, axis, low, high):
    first, second = out_refs
    first[...] = jnp.where(even(axis), high, low).astype(BF)
    second[...] = jnp.where(even(axis), low, high).astype(BF)


def lane_of(value, lane):
    return jnp.broadcast_to(value[:, lane : lane + 1], (value.shape[0], LANES))


def port_profile_column(profile_ref, port, edge):
    samples = profile_ref.shape[2]
    row = lax.broadcasted_iota(jnp.int32, (samples, samples), 0)
    col = lax.broadcasted_iota(jnp.int32, (samples, samples), 1)
    line = jnp.broadcast_to(profile_ref[edge].astype(F32)[port : port + 1], row.shape)
    return jnp.sum(jnp.where(row == col, line, 0.0), axis=1, keepdims=True)


def port_place(port_ref, port, rows, width):
    all_cols = width * lax.axis_size("col")
    cell = port_ref[port]
    row = cell // all_cols - lax.axis_index("row") * rows
    col = cell % all_cols - lax.axis_index("col") * width
    return row, col, (row >= 0) & (row < rows) & (col >= 0) & (col < width)


def map_rows(map_refs, first, last):
    if len(map_refs) == 1:
        return map_refs[0][first:last, :]
    core = lax.rem(lax.axis_index("col"), 2)
    swapped, own = map_refs[0][...], map_refs[1][...]
    low, high = jnp.where(core == 0, own, swapped), jnp.where(core == 0, swapped, own)
    return jnp.concatenate([low, high], axis=0)[first:last]


def products(x, types, maps, first, last, total=None):
    mine = lax.axis_index("row")
    core = lax.rem(lax.axis_index("col"), 2)
    types = jnp.broadcast_to(types, x.shape)
    for (even, odd), map_refs in maps:
        kind = (mine ^ jnp.where(core == 0, even, odd)).astype(F32).astype(BF)
        masked = jnp.where(types == kind, x, jnp.zeros((), BF))
        part = map_rows(map_refs, first, last)
        product = jnp.dot(part, masked, preferred_element_type=F32)
        total = product if total is None else total + product
    return total


def with_steps(map_refs, first):
    map_refs, maps = list(map_refs), []
    while map_refs:
        number = first + len(maps)
        count = 2 if number == HALVES else 1
        maps.append((MAP_STEPS[number], map_refs[:count]))
        del map_refs[:count]
    return maps


def shifted(total, next_ref, rows):
    quarter = total.shape[0] // 4
    last = (rows - 1) * LANES
    north = total[0:quarter].astype(BF)
    south = total[quarter : 2 * quarter].astype(BF)
    next_ref[0:quarter, LANES:] = south[:, :last]
    next_ref[0:quarter, 0:LANES] = jnp.zeros((quarter, LANES), BF)
    next_ref[quarter : 2 * quarter, :last] = north[:, LANES:]
    next_ref[quarter : 2 * quarter, last:] = jnp.zeros((quarter, LANES), BF)
    for row in range(rows):
        cols = slice(row * LANES, (row + 1) * LANES)
        west = total[2 * quarter : 3 * quarter, cols]
        east = total[3 * quarter : 4 * quarter, cols]
        next_ref[2 * quarter : 3 * quarter, cols] = pltpu.roll(east, 1, 1).astype(BF)
        next_ref[3 * quarter : 4 * quarter, cols] = pltpu.roll(west, LANES - 1, 1).astype(BF)
    return north, south


def rim_columns(x_ref, types, ports, offset):
    tile = types.shape[1]
    starts = [port * tile + offset for port in range(ports)]
    cells = jnp.concatenate([x_ref[:, start : start + LANES] for start in starts], axis=1)
    return cells, jnp.concatenate([types[:, offset : offset + LANES]] * ports, axis=1).astype(BF)


def side_columns(x_ref, types, ports):
    order, tile = x_ref.shape[0], types.shape[1]
    rows = tile // LANES

    def pick(block_of, lines):
        lane = lax.broadcasted_iota(jnp.int32, (lines, LANES), 1)
        first = last = jnp.zeros((lines, LANES), F32)
        for place in range(ports * rows):
            turned = pltpu.roll(block_of(place), place + 1, 1)
            first = jnp.where(lane == place + 1, turned, first)
            last = jnp.where(lane == place, turned, last)
        first = pltpu.roll(first, LANES - 1, 1)
        return jnp.where(lane < 64, first, pltpu.roll(last, 64, 1)).astype(BF)

    def types_of(place):
        start = place % rows * LANES
        return jnp.broadcast_to(types[:, start : start + LANES], (16, LANES))

    quarter = order // 4
    sides = [
        pick(
            lambda place: x_ref[edge * quarter : (edge + 1) * quarter,
                                place * LANES : (place + 1) * LANES].astype(F32),
            quarter,
        )
        for edge in range(4)
    ]
    return jnp.concatenate(sides, axis=0), pick(types_of, 16)


def rims(x_ref, types, ports, sides, kinds, maps, so_far):
    order, tile = x_ref.shape[0], types.shape[1]
    quarter = order // 4
    before = [None if ref is None else ref[...].astype(F32) for ref in so_far]
    cells, cell_kinds = rim_columns(x_ref, types, ports, 0)
    north = products(cells, cell_kinds, maps, 0, quarter, before[0])
    cells, cell_kinds = rim_columns(x_ref, types, ports, tile - LANES)
    south = products(cells, cell_kinds, maps, quarter, 2 * quarter, before[1])
    side = products(sides, kinds, maps, 2 * quarter, order, before[2])
    return north.astype(BF), south.astype(BF), side.astype(BF)


def sides_kernel(ports, x_ref, types_ref, sides_ref, kinds_ref):
    sides_ref[...], kinds_ref[...] = side_columns(x_ref, types_ref[...].astype(F32), ports)


def early_kernel(ports, first, count, x_ref, types_ref, sides_ref, kinds_ref, *refs):
    maps = with_steps(refs[:count], first)
    types = types_ref[...].astype(F32)
    tile = types.shape[1]
    so_far, outs = refs[count:-4], refs[-4:]
    done_ref, *so_far = so_far if first else [None] * 4
    values = rims(x_ref, types, ports, sides_ref[...], kinds_ref[0:1, :], maps, so_far)
    for ref, value in zip(outs[1:], values):
        ref[...] = value
    for port in range(ports):
        cols = slice(port * tile, (port + 1) * tile)
        before = None if done_ref is None else done_ref[:, cols].astype(F32)
        total = products(x_ref[:, cols], types.astype(BF), maps, 0, x_ref.shape[0], before)
        outs[0][:, cols] = total.astype(BF)


def rim_kernel(ports, first, x_ref, types_ref, sides_ref, kinds_ref, *refs):
    maps = with_steps(refs[:-7], first)
    types = types_ref[...].astype(F32)
    quarter = x_ref.shape[0] // 4
    values = rims(x_ref, types, ports, sides_ref[...], kinds_ref[0:1, :], maps, refs[-7:-4])
    store_rims(refs[-4:-2], "row", values[0], values[1])
    store_rims(refs[-2:], "col", values[2][0:quarter], values[2][quarter:])


def first_kernel(rows, ports, first, x_ref, types_ref, done_ref, *refs):
    maps = with_steps(refs[:-2], first)
    next_ref, sides_ref = refs[-2:]
    types = types_ref[...].astype(F32).astype(BF)
    tile = types.shape[1]
    for port in range(ports):
        cols = slice(port * tile, (port + 1) * tile)
        before = done_ref[:, cols].astype(F32)
        total = products(x_ref[:, cols], types, maps, 0, x_ref.shape[0], before)
        shifted(total, next_ref.at[:, cols], rows)
    sides_ref[...] = side_columns(next_ref, types_ref[...].astype(F32), ports)[0]


def patched_sides(rows, width, sides_ref, port_ref, profile_ref, halo_refs, ports):
    quarter = sides_ref.shape[0] // 4
    north_in, south_in = halos_inside("row", *halo_refs[:2])
    west_in, east_in = halos_inside("col", *halo_refs[2:])
    lane = lax.broadcasted_iota(jnp.int32, (quarter, LANES), 1)
    value = sides_ref[...].astype(F32)
    north, south, west, east = (value[i * quarter : (i + 1) * quarter] for i in range(4))
    west = jnp.where(lane < 64, pltpu.roll(west_in, 64, 1), west)
    east = jnp.where(lane >= 64, pltpu.roll(east_in, 64, 1), east)
    for port in range(ports):
        place, start = port * rows, port * width
        for shift, at in ((0, start), (64, start + width - 1)):
            north = jnp.where(lane == shift + place, lane_of(north_in, at), north)
            south = jnp.where(lane == shift + place + rows - 1, lane_of(south_in, at), south)
    parts = [north, south, west, east]
    for port in range(ports):
        row, col, inside = port_place(port_ref, port, rows, width)
        first = jnp.where(inside & (col == 0), port * rows + row, -1)
        last = jnp.where(inside & (col == width - 1), 64 + port * rows + row, -1)
        here = (lane == first) | (lane == last)
        parts = [
            jnp.where(here, part + port_profile_column(profile_ref, port, edge), part)
            for edge, part in enumerate(parts)
        ]
    return jnp.concatenate(parts, axis=0).astype(BF)


def patched(rows, width, x_ref, port_ref, profile_ref, halo_refs, places):
    order = x_ref.shape[0]
    quarter = order // 4
    north_in, south_in = halos_inside("row", *halo_refs[:2])
    west_in, east_in = halos_inside("col", *halo_refs[2:])
    lane = lax.broadcasted_iota(jnp.int32, (quarter, LANES), 1)
    blocks = []
    for port, row in places:
        place = port * rows + row
        rim = slice(port * LANES, (port + 1) * LANES)
        value = x_ref[:, place * LANES : (place + 1) * LANES].astype(F32)
        north, south, west, east = (value[i * quarter : (i + 1) * quarter] for i in range(4))
        north = north_in[:, rim] if row == 0 else north
        south = south_in[:, rim] if row == rows - 1 else south
        west = jnp.where(lane == 0, lane_of(west_in, 64 + place), west)
        east = jnp.where(lane == LANES - 1, lane_of(east_in, place), east)
        source_row, col, inside = port_place(port_ref, port, rows, width)
        here = lane == jnp.where(inside & (source_row == row), col, -1)
        columns = [
            jnp.where(here, part + port_profile_column(profile_ref, port, edge), part)
            for edge, part in enumerate((north, south, west, east))
        ]
        blocks.append(jnp.concatenate(columns, axis=0).astype(BF))
    return jnp.concatenate(blocks, axis=1)


def types_of_rows(types_ref, rows):
    types = types_ref[...].astype(F32)
    return jnp.concatenate([types[:, row * LANES : (row + 1) * LANES] for row in rows], axis=1)


def ends_kernel(rows, ports, width, port_ref, x_ref, types_ref, profile_ref, *refs):
    (sides_ref, kinds_ref), refs = refs[:2], refs[2:]
    halo_refs, map_refs, patched_ref, ends_ref = refs[:4], refs[4:-6], refs[-6], refs[-5]
    order, tile = x_ref.shape[0], rows * width
    quarter = order // 4
    maps = with_steps(map_refs, 0)
    for port in range(ports):
        places = [(port, row) for row in range(rows)]
        value = patched(rows, width, x_ref, port_ref, profile_ref, halo_refs, places)
        patched_ref[:, port * tile : (port + 1) * tile] = value
    starts = [port * tile + row * width for row in (0, rows - 1) for port in range(ports)]
    block = jnp.concatenate([patched_ref[:, start : start + width] for start in starts], axis=1)
    types = types_of_rows(types_ref, [0] * ports + [rows - 1] * ports).astype(BF)
    total = products(block, types, maps, 0, order)
    ends_ref[...] = total.astype(BF)
    wide = ports * LANES
    store_rims(refs[-4:-2], "row", total[0:quarter, :wide], total[quarter : 2 * quarter, wide:])
    sides = patched_sides(rows, width, sides_ref, port_ref, profile_ref, halo_refs, ports)
    sides = products(sides, kinds_ref[0:1, :], maps, 2 * quarter, order)
    store_rims(refs[-2:], "col", sides[0:quarter], sides[quarter:])


def second_kernel(rows, ports, width, x_ref, types_ref, ends_ref, *refs):
    map_refs, next_ref = refs[:-1], refs[-1]
    order, tile = x_ref.shape[0], rows * width
    maps = with_steps(map_refs, 0)
    types = types_of_rows(types_ref, range(1, rows - 1)).astype(BF)
    for port in range(ports):
        start = port * tile
        middle = products(x_ref[:, start + width : start + tile - width], types, maps, 0, order)
        top = ends_ref[:, port * LANES : (port + 1) * LANES].astype(F32)
        bottom = ends_ref[:, (ports + port) * LANES : (ports + port + 1) * LANES].astype(F32)
        total = jnp.concatenate([top, middle, bottom], axis=1)
        shifted(total, next_ref.at[:, start : start + tile], rows)


def last_kernel(rows, width, port_ref, x_ref, profile_ref, *refs):
    out_ref, buffer, sems = refs[4:]
    order, ports = buffer.shape[:2]
    quarter, tile = order // 4, rows * width
    north_in, south_in = halos_inside("row", *refs[:2])
    west_in, east_in = halos_inside("col", *refs[2:4])
    lane = lax.broadcasted_iota(jnp.int32, (quarter, LANES), 1)
    copies = []
    for edge in (2, 3, 0, 1):
        lines = slice(edge * quarter, (edge + 1) * quarter)
        for port in range(ports):
            rim = slice(port * LANES, (port + 1) * LANES)
            starts = [port * tile + row * LANES for row in range(rows)]
            parts = [x_ref[lines, start : start + LANES].astype(F32) for start in starts]
            places = range(port * rows, (port + 1) * rows)
            if edge == 0:
                parts[0] = north_in[:, rim]
            elif edge == 1:
                parts[-1] = south_in[:, rim]
            elif edge == 2:
                parts = [
                    jnp.where(lane == 0, lane_of(west_in, 64 + place), part)
                    for place, part in zip(places, parts)
                ]
            else:
                parts = [
                    jnp.where(lane == LANES - 1, lane_of(east_in, place), part)
                    for place, part in zip(places, parts)
                ]
            value = jnp.concatenate(parts, axis=1).reshape(quarter, rows, LANES)
            buffer[lines, port] = value.astype(BF)
        for port in range(ports):
            row, col, inside = port_place(port_ref, port, rows, width)

            @pl.when(inside)
            def _():
                current = buffer[lines, port].astype(F32)
                here = (lax.broadcasted_iota(jnp.int32, current.shape, 1) == row) & (
                    lax.broadcasted_iota(jnp.int32, current.shape, 2) == col
                )
                profile = port_profile_column(profile_ref, port, edge)
                profile = jnp.broadcast_to(profile, (quarter, LANES)).reshape(quarter, 1, LANES)
                added = current + jnp.broadcast_to(profile, current.shape)
                buffer[lines, port] = jnp.where(here, added, current).astype(BF)

        copy = pltpu.make_async_copy(buffer.at[lines], out_ref.at[lines], sems.at[edge])
        copy.start()
        copies.append(copy)
    for copy in copies:
        copy.wait()


def exchange(rims, axis):
    sizes = lax.axis_size("row"), lax.axis_size("col")
    at = ("row", "col").index(axis)

    def partner(place, first):
        place = list(place)
        other = place[at] + (1 if place[at] % 2 == first else -1)
        if 0 <= other < sizes[at]:
            place[at] = other
        else:
            place[1 - at] ^= 2
        return place[0] * sizes[1] + place[1]

    def pairs(first):
        places = [(row, col) for row in range(sizes[0]) for col in range(sizes[1])]
        return [(row * sizes[1] + col, partner((row, col), first)) for row, col in places]

    return [lax.ppermute(rim, ("row", "col"), pairs(first)) for first, rim in enumerate(rims)]


def body(traces, cell_type, port_cell, port_profile, mode_shapes, mode_values, mode_weights):
    edges, samples, ports, rows, width = traces.shape
    order = edges * samples
    quarter = samples
    tile = rows * width
    types = cell_type.reshape(1, tile)
    own_map, half, x, sides = own_type_map(mode_shapes, mode_values, mode_weights, traces, types)
    first = swap(own_map, (2, 0), (3, 8))
    second = swap(own_map, (6, 0), (7, 8))
    half = swap(half, (1, 8))
    profile = jnp.transpose(port_profile, (0, 2, 1))
    ports_spec = pl.BlockSpec(memory_space=pltpu.SMEM)
    next_shape = jax.ShapeDtypeStruct((order, ports * tile), BF)
    rim_shapes = [jax.ShapeDtypeStruct((quarter, ports * LANES), BF)] * 2 + [
        jax.ShapeDtypeStruct((quarter, LANES), BF)
    ] * 2
    work = 2 * order * order * len(MAP_STEPS) * ports * tile
    part_shapes = [next_shape] + rim_shapes[:2] + [jax.ShapeDtypeStruct((2 * quarter, LANES), BF)]

    def early(first, maps, parts=()):
        kernel = functools.partial(early_kernel, ports, first, len(maps))
        flops = work * len(maps) // 7
        return whole_call(kernel, part_shapes, x, types, *sides, *maps, *parts, flops=flops)

    parts = list(early(0, [own_map, first]))
    parts[1], first, second, half = lax.optimization_barrier((parts[1], first, second, half))
    map_shape = jax.ShapeDtypeStruct(own_map.shape, BF)
    (relay,) = whole_call(relay_kernel, [map_shape], first, second)
    relay, first, second, half = lax.optimization_barrier((relay, first, second, half))
    third = swap(relay, (2, 0), (6, 0))
    maps = [second, swap_cores(first), swap_cores(second), swap_cores(half), half]
    parts = list(early(2, maps, parts))
    parts[1], third = lax.optimization_barrier((parts[1], third))
    done, *parts = parts
    late = [third, swap_cores(third)]
    maps = [own_map, first] + maps + late
    sent = whole_call(
        functools.partial(rim_kernel, ports, 6),
        rim_shapes,
        x,
        types,
        *sides,
        *late,
        *parts,
        flops=work // 8,
    )
    halos = exchange(sent[:2], "row") + exchange(sent[2:], "col")
    x, picked = whole_call(
        functools.partial(first_kernel, rows, ports, 6),
        [next_shape, jax.ShapeDtypeStruct((order, LANES), BF)],
        x,
        types,
        done,
        *late,
        flops=work // 5000,
    )
    ends_shape = jax.ShapeDtypeStruct((order, 2 * ports * LANES), BF)
    operands = [port_cell, x, types, profile, picked, sides[1], *halos, *maps]
    x, ends, *sent = pl.pallas_call(
        functools.partial(ends_kernel, rows, ports, width),
        in_specs=[ports_spec] + [WHOLE] * (len(operands) - 1),
        out_specs=[WHOLE] * 6,
        out_shape=[next_shape, ends_shape] + rim_shapes,
        compiler_params=PARAMS,
        cost_estimate=pl.CostEstimate(flops=work // 3, bytes_accessed=0, transcendentals=0),
    )(*operands)
    halos = exchange(sent[:2], "row") + exchange(sent[2:], "col")
    (x,) = whole_call(
        functools.partial(second_kernel, rows, ports, width),
        [next_shape],
        x,
        types,
        ends,
        *maps,
        flops=work // 5000,
    )
    operands = [port_cell, x, profile, *halos]
    out = pl.pallas_call(
        functools.partial(last_kernel, rows, width),
        in_specs=[ports_spec] + [WHOLE] * (len(operands) - 1),
        out_specs=pl.BlockSpec(memory_space=pl.ANY),
        out_shape=jax.ShapeDtypeStruct((order, ports, rows, width), BF),
        scratch_shapes=[
            pltpu.VMEM((order, ports, rows, width), BF),
            pltpu.SemaphoreType.DMA((4,)),
        ],
        compiler_params=PARAMS,
    )(*operands)
    return out.reshape(traces.shape)


def solution(mesh):
    return jax.shard_map(
        body,
        mesh=mesh,
        in_specs=(
            P(None, None, None, "row", "col"),
            P("row", "col"),
            P(),
            P(),
            P("row", None, "col"),
            P("row", "col"),
            P("row", "col", None),
        ),
        out_specs=P(None, None, None, "row", "col"),
        check_vma=False,
    )
```

```python
import functools
import math

import jax
import jax.numpy as jnp
from jax import lax
from jax.experimental import pallas as pl
from jax.experimental.pallas import tpu as pltpu
from jax.sharding import PartitionSpec as P

BF = jnp.bfloat16
F32 = jnp.float32
LANES = 128
PARAMS = pltpu.CompilerParams(vmem_limit_bytes=20 * 2**20)
WIDE_PARAMS = pltpu.CompilerParams(vmem_limit_bytes=50 * 2**20)


def swap(value, first, second=None):
    second = first if second is None else second
    rows, cols = lax.axis_size("row"), lax.axis_size("col")
    pairs = []
    for row in range(rows):
        for col in range(cols):
            down, along = second if col % 2 else first
            pairs.append((row * cols + col, (row ^ down) * cols + (col ^ along)))
    return lax.ppermute(value, ("row", "col"), pairs)


def swap_cores(value):
    return swap(value, (0, 1))


def flat_kernel(x_hbm, out_ref, x_ref, sems):
    order, ports, rows, width = x_ref.shape
    quarter, tile = order // 4, rows * width
    edges = [slice(edge * quarter, (edge + 1) * quarter) for edge in range(4)]
    copies = [
        pltpu.make_async_copy(x_hbm.at[lines], x_ref.at[lines], sems.at[edge])
        for edge, lines in enumerate(edges)
    ]
    for copy in copies:
        copy.start()
    for copy, lines in zip(copies, edges):
        copy.wait()
        for port in range(ports):
            value = x_ref[lines, port].astype(F32).reshape(quarter, tile)
            out_ref[lines, port * tile : (port + 1) * tile] = value.astype(BF)


def partial_kernel(modes, *refs):
    left, right = [], []
    for ref in refs[:-1]:
        for start in range(0, ref.shape[0], 2 * modes):
            left.append(ref[start : start + modes])
            right.append(ref[start + modes : start + 2 * modes])
    refs[-1][...] = lax.dot_general(
        jnp.concatenate(left, axis=0),
        jnp.concatenate(right, axis=0),
        (((0,), (0,)), ((), ())),
        precision=lax.Precision.HIGHEST,
        preferred_element_type=F32,
    )


WHOLE = pl.BlockSpec(memory_space=pltpu.VMEM)


def whole_call(kernel, shapes, *operands, flops=0):
    return pl.pallas_call(
        kernel,
        in_specs=[WHOLE] * len(operands),
        out_specs=[WHOLE] * len(shapes),
        out_shape=shapes,
        compiler_params=PARAMS,
        cost_estimate=pl.CostEstimate(flops=flops, bytes_accessed=0, transcendentals=0),
    )(*operands)


def own_type_map(mode_shapes, mode_values, mode_weights, traces, types):
    modes, order = mode_weights.shape[1:]
    own = jnp.concatenate([mode_shapes[0].T, mode_weights[0]], axis=0)
    own = own * jnp.concatenate([mode_values[0], jnp.ones((modes,), F32)])[:, None]
    far = swap(own, (0, 4))
    pair = jnp.concatenate([own, swap_cores(own)], axis=0)
    pair, traces = lax.optimization_barrier((pair, traces))
    steps = (((0, 8), (0, 10)), ((0, 2), (0, 14)), ((0, 6), (0, 12)))
    got = [swap(pair, *step) for step in steps]
    shape = (order,) + traces.shape[2:]
    x = pl.pallas_call(
        flat_kernel,
        in_specs=[pl.BlockSpec(memory_space=pltpu.HBM)],
        out_specs=WHOLE,
        out_shape=jax.ShapeDtypeStruct((order, math.prod(shape[1:])), BF),
        scratch_shapes=[pltpu.VMEM(shape, BF), pltpu.SemaphoreType.DMA((4,))],
        compiler_params=WIDE_PARAMS,
        cost_estimate=pl.CostEstimate(flops=2**30, bytes_accessed=0, transcendentals=0),
    )(traces.reshape(shape))
    *got, x = lax.optimization_barrier((*got, x))
    (partial,) = whole_call(
        functools.partial(partial_kernel, modes),
        [jax.ShapeDtypeStruct((order, order), F32)],
        own,
        far,
        *got,
    )
    partial, x = lax.optimization_barrier((partial, x))
    other = swap_cores(partial)
    sides = whole_call(
        functools.partial(sides_kernel, traces.shape[2]),
        [jax.ShapeDtypeStruct((order, LANES), BF), jax.ShapeDtypeStruct((16, LANES), BF)],
        x,
        types,
        flops=2**30,
    )
    other, sides = lax.optimization_barrier((other, sides))
    shapes = [jax.ShapeDtypeStruct((lines, order), BF) for lines in (order, order // 2)]
    return *whole_call(own_kernel, shapes, partial, other), x, sides


MAP_STEPS = ((0, 0), (2, 3), (6, 7), (3, 2), (7, 6), (1, 1), (4, 5), (5, 4))
HALVES = 5


def own_kernel(one_ref, two_ref, out_ref, half_ref):
    core = lax.rem(lax.axis_index("col"), 2)
    half = half_ref.shape[0]
    total = (one_ref[...] + two_ref[...]).astype(BF)
    out_ref[...] = total
    half_ref[...] = jnp.where(core == 0, total[0:half], total[half:])


def relay_kernel(first_ref, second_ref, out_ref):
    core = lax.rem(lax.axis_index("col"), 2)
    out_ref[...] = jnp.where(core == 0, second_ref[...], first_ref[...])


def even(axis):
    return lax.rem(lax.axis_index(axis), 2) == 0


def halos_inside(axis, one, two):
    one, two = one[...].astype(F32), two[...].astype(F32)
    index, count = lax.axis_index(axis), lax.axis_size(axis)
    low = jnp.where(even(axis), two, one)
    high = jnp.where(even(axis), one, two)
    return jnp.where(index > 0, low, 0.0), jnp.where(index < count - 1, high, 0.0)


def store_rims(out_refs, axis, low, high):
    first, second = out_refs
    first[...] = jnp.where(even(axis), high, low).astype(BF)
    second[...] = jnp.where(even(axis), low, high).astype(BF)


def lane_of(value, lane):
    return jnp.broadcast_to(value[:, lane : lane + 1], (value.shape[0], LANES))


def port_profile_column(profile_ref, port, edge):
    samples = profile_ref.shape[2]
    row = lax.broadcasted_iota(jnp.int32, (samples, samples), 0)
    col = lax.broadcasted_iota(jnp.int32, (samples, samples), 1)
    line = jnp.broadcast_to(profile_ref[edge].astype(F32)[port : port + 1], row.shape)
    return jnp.sum(jnp.where(row == col, line, 0.0), axis=1, keepdims=True)


def port_place(port_ref, port, rows, width):
    all_cols = width * lax.axis_size("col")
    cell = port_ref[port]
    row = cell // all_cols - lax.axis_index("row") * rows
    col = cell % all_cols - lax.axis_index("col") * width
    return row, col, (row >= 0) & (row < rows) & (col >= 0) & (col < width)


def map_rows(map_refs, first, last):
    if len(map_refs) == 1:
        return map_refs[0][first:last, :]
    core = lax.rem(lax.axis_index("col"), 2)
    swapped, own = map_refs[0][...], map_refs[1][...]
    low, high = jnp.where(core == 0, own, swapped), jnp.where(core == 0, swapped, own)
    return jnp.concatenate([low, high], axis=0)[first:last]


def products(x, types, maps, first, last, total=None):
    mine = lax.axis_index("row")
    core = lax.rem(lax.axis_index("col"), 2)
    types = jnp.broadcast_to(types, x.shape)
    for (even, odd), map_refs in maps:
        kind = (mine ^ jnp.where(core == 0, even, odd)).astype(F32).astype(BF)
        masked = jnp.where(types == kind, x, jnp.zeros((), BF))
        part = map_rows(map_refs, first, last)
        product = jnp.dot(part, masked, preferred_element_type=F32)
        total = product if total is None else total + product
    return total


def with_steps(map_refs, first):
    map_refs, maps = list(map_refs), []
    while map_refs:
        number = first + len(maps)
        count = 2 if number == HALVES else 1
        maps.append((MAP_STEPS[number], map_refs[:count]))
        del map_refs[:count]
    return maps


def shifted(total, next_ref, rows):
    quarter = total.shape[0] // 4
    last = (rows - 1) * LANES
    north = total[0:quarter].astype(BF)
    south = total[quarter : 2 * quarter].astype(BF)
    next_ref[0:quarter, LANES:] = south[:, :last]
    next_ref[0:quarter, 0:LANES] = jnp.zeros((quarter, LANES), BF)
    next_ref[quarter : 2 * quarter, :last] = north[:, LANES:]
    next_ref[quarter : 2 * quarter, last:] = jnp.zeros((quarter, LANES), BF)
    for row in range(rows):
        cols = slice(row * LANES, (row + 1) * LANES)
        west = total[2 * quarter : 3 * quarter, cols]
        east = total[3 * quarter : 4 * quarter, cols]
        next_ref[2 * quarter : 3 * quarter, cols] = pltpu.roll(east, 1, 1).astype(BF)
        next_ref[3 * quarter : 4 * quarter, cols] = pltpu.roll(west, LANES - 1, 1).astype(BF)
    return north, south


def rim_columns(x_ref, types, ports, offset):
    tile = types.shape[1]
    starts = [port * tile + offset for port in range(ports)]
    cells = jnp.concatenate([x_ref[:, start : start + LANES] for start in starts], axis=1)
    return cells, jnp.concatenate([types[:, offset : offset + LANES]] * ports, axis=1).astype(BF)


def side_columns(x_ref, types, ports):
    order, tile = x_ref.shape[0], types.shape[1]
    rows = tile // LANES

    def pick(block_of, lines):
        lane = lax.broadcasted_iota(jnp.int32, (lines, LANES), 1)
        first = last = jnp.zeros((lines, LANES), F32)
        for place in range(ports * rows):
            turned = pltpu.roll(block_of(place), place + 1, 1)
            first = jnp.where(lane == place + 1, turned, first)
            last = jnp.where(lane == place, turned, last)
        first = pltpu.roll(first, LANES - 1, 1)
        return jnp.where(lane < 64, first, pltpu.roll(last, 64, 1)).astype(BF)

    def types_of(place):
        start = place % rows * LANES
        return jnp.broadcast_to(types[:, start : start + LANES], (16, LANES))

    quarter = order // 4
    sides = [
        pick(
            lambda place: x_ref[edge * quarter : (edge + 1) * quarter,
                                place * LANES : (place + 1) * LANES].astype(F32),
            quarter,
        )
        for edge in range(4)
    ]
    return jnp.concatenate(sides, axis=0), pick(types_of, 16)


def rims(x_ref, types, ports, sides, kinds, maps, so_far):
    order, tile = x_ref.shape[0], types.shape[1]
    quarter = order // 4
    before = [None if ref is None else ref[...].astype(F32) for ref in so_far]
    cells, cell_kinds = rim_columns(x_ref, types, ports, 0)
    north = products(cells, cell_kinds, maps, 0, quarter, before[0])
    cells, cell_kinds = rim_columns(x_ref, types, ports, tile - LANES)
    south = products(cells, cell_kinds, maps, quarter, 2 * quarter, before[1])
    side = products(sides, kinds, maps, 2 * quarter, order, before[2])
    return north.astype(BF), south.astype(BF), side.astype(BF)


def sides_kernel(ports, x_ref, types_ref, sides_ref, kinds_ref):
    sides_ref[...], kinds_ref[...] = side_columns(x_ref, types_ref[...].astype(F32), ports)


def early_kernel(ports, first, count, x_ref, types_ref, sides_ref, kinds_ref, *refs):
    maps = with_steps(refs[:count], first)
    types = types_ref[...].astype(F32)
    tile = types.shape[1]
    so_far, outs = refs[count:-4], refs[-4:]
    done_ref, *so_far = so_far if first else [None] * 4
    values = rims(x_ref, types, ports, sides_ref[...], kinds_ref[0:1, :], maps, so_far)
    for ref, value in zip(outs[1:], values):
        ref[...] = value
    for port in range(ports):
        cols = slice(port * tile, (port + 1) * tile)
        before = None if done_ref is None else done_ref[:, cols].astype(F32)
        total = products(x_ref[:, cols], types.astype(BF), maps, 0, x_ref.shape[0], before)
        outs[0][:, cols] = total.astype(BF)


def rim_kernel(ports, first, x_ref, types_ref, sides_ref, kinds_ref, *refs):
    maps = with_steps(refs[:-7], first)
    types = types_ref[...].astype(F32)
    quarter = x_ref.shape[0] // 4
    values = rims(x_ref, types, ports, sides_ref[...], kinds_ref[0:1, :], maps, refs[-7:-4])
    store_rims(refs[-4:-2], "row", values[0], values[1])
    store_rims(refs[-2:], "col", values[2][0:quarter], values[2][quarter:])


def first_kernel(rows, ports, first, x_ref, types_ref, done_ref, *refs):
    maps = with_steps(refs[:-2], first)
    next_ref, sides_ref = refs[-2:]
    types = types_ref[...].astype(F32).astype(BF)
    tile = types.shape[1]
    for port in range(ports):
        cols = slice(port * tile, (port + 1) * tile)
        before = done_ref[:, cols].astype(F32)
        total = products(x_ref[:, cols], types, maps, 0, x_ref.shape[0], before)
        shifted(total, next_ref.at[:, cols], rows)
    sides_ref[...] = side_columns(next_ref, types_ref[...].astype(F32), ports)[0]


def patched_sides(rows, width, sides_ref, port_ref, profile_ref, halo_refs, ports):
    quarter = sides_ref.shape[0] // 4
    north_in, south_in = halos_inside("row", *halo_refs[:2])
    west_in, east_in = halos_inside("col", *halo_refs[2:])
    lane = lax.broadcasted_iota(jnp.int32, (quarter, LANES), 1)
    value = sides_ref[...].astype(F32)
    north, south, west, east = (value[i * quarter : (i + 1) * quarter] for i in range(4))
    west = jnp.where(lane < 64, pltpu.roll(west_in, 64, 1), west)
    east = jnp.where(lane >= 64, pltpu.roll(east_in, 64, 1), east)
    for port in range(ports):
        place, start = port * rows, port * width
        for shift, at in ((0, start), (64, start + width - 1)):
            north = jnp.where(lane == shift + place, lane_of(north_in, at), north)
            south = jnp.where(lane == shift + place + rows - 1, lane_of(south_in, at), south)
    parts = [north, south, west, east]
    for port in range(ports):
        row, col, inside = port_place(port_ref, port, rows, width)
        first = jnp.where(inside & (col == 0), port * rows + row, -1)
        last = jnp.where(inside & (col == width - 1), 64 + port * rows + row, -1)
        here = (lane == first) | (lane == last)
        parts = [
            jnp.where(here, part + port_profile_column(profile_ref, port, edge), part)
            for edge, part in enumerate(parts)
        ]
    return jnp.concatenate(parts, axis=0).astype(BF)


def patched(rows, width, x_ref, port_ref, profile_ref, halo_refs, places):
    order = x_ref.shape[0]
    quarter = order // 4
    north_in, south_in = halos_inside("row", *halo_refs[:2])
    west_in, east_in = halos_inside("col", *halo_refs[2:])
    lane = lax.broadcasted_iota(jnp.int32, (quarter, LANES), 1)
    blocks = []
    for port, row in places:
        place = port * rows + row
        rim = slice(port * LANES, (port + 1) * LANES)
        value = x_ref[:, place * LANES : (place + 1) * LANES].astype(F32)
        north, south, west, east = (value[i * quarter : (i + 1) * quarter] for i in range(4))
        north = north_in[:, rim] if row == 0 else north
        south = south_in[:, rim] if row == rows - 1 else south
        west = jnp.where(lane == 0, lane_of(west_in, 64 + place), west)
        east = jnp.where(lane == LANES - 1, lane_of(east_in, place), east)
        source_row, col, inside = port_place(port_ref, port, rows, width)
        here = lane == jnp.where(inside & (source_row == row), col, -1)
        columns = [
            jnp.where(here, part + port_profile_column(profile_ref, port, edge), part)
            for edge, part in enumerate((north, south, west, east))
        ]
        blocks.append(jnp.concatenate(columns, axis=0).astype(BF))
    return jnp.concatenate(blocks, axis=1)


def types_of_rows(types_ref, rows):
    types = types_ref[...].astype(F32)
    return jnp.concatenate([types[:, row * LANES : (row + 1) * LANES] for row in rows], axis=1)


def ends_kernel(rows, ports, width, port_ref, x_ref, types_ref, profile_ref, *refs):
    (sides_ref, kinds_ref), refs = refs[:2], refs[2:]
    halo_refs, map_refs, patched_ref, ends_ref = refs[:4], refs[4:-6], refs[-6], refs[-5]
    order, tile = x_ref.shape[0], rows * width
    quarter = order // 4
    maps = with_steps(map_refs, 0)
    places = [(port, row) for row in (0, rows - 1) for port in range(ports)]
    block = patched(rows, width, x_ref, port_ref, profile_ref, halo_refs, places)
    types = types_of_rows(types_ref, [0] * ports + [rows - 1] * ports).astype(BF)
    total = products(block, types, maps, 0, order)
    ends_ref[...] = total.astype(BF)
    for port in range(ports):
        places = [(port, row) for row in range(1, rows - 1)]
        value = patched(rows, width, x_ref, port_ref, profile_ref, halo_refs, places)
        patched_ref[:, port * tile + width : (port + 1) * tile - width] = value
    wide = ports * LANES
    store_rims(refs[-4:-2], "row", total[0:quarter, :wide], total[quarter : 2 * quarter, wide:])
    sides = patched_sides(rows, width, sides_ref, port_ref, profile_ref, halo_refs, ports)
    sides = products(sides, kinds_ref[0:1, :], maps, 2 * quarter, order)
    store_rims(refs[-2:], "col", sides[0:quarter], sides[quarter:])


def second_kernel(rows, ports, width, x_ref, types_ref, ends_ref, *refs):
    map_refs, next_ref = refs[:-1], refs[-1]
    order, tile = x_ref.shape[0], rows * width
    maps = with_steps(map_refs, 0)
    types = types_of_rows(types_ref, range(1, rows - 1)).astype(BF)
    for port in range(ports):
        start = port * tile
        middle = products(x_ref[:, start + width : start + tile - width], types, maps, 0, order)
        top = ends_ref[:, port * LANES : (port + 1) * LANES].astype(F32)
        bottom = ends_ref[:, (ports + port) * LANES : (ports + port + 1) * LANES].astype(F32)
        total = jnp.concatenate([top, middle, bottom], axis=1)
        shifted(total, next_ref.at[:, start : start + tile], rows)


def last_kernel(rows, width, port_ref, x_ref, profile_ref, *refs):
    out_ref, buffer, sems = refs[4:]
    order, ports = buffer.shape[:2]
    quarter, tile = order // 4, rows * width
    north_in, south_in = halos_inside("row", *refs[:2])
    west_in, east_in = halos_inside("col", *refs[2:4])
    lane = lax.broadcasted_iota(jnp.int32, (quarter, LANES), 1)
    copies = []
    for edge in (2, 3, 0, 1):
        lines = slice(edge * quarter, (edge + 1) * quarter)
        for port in range(ports):
            rim = slice(port * LANES, (port + 1) * LANES)
            starts = [port * tile + row * LANES for row in range(rows)]
            parts = [x_ref[lines, start : start + LANES].astype(F32) for start in starts]
            places = range(port * rows, (port + 1) * rows)
            if edge == 0:
                parts[0] = north_in[:, rim]
            elif edge == 1:
                parts[-1] = south_in[:, rim]
            elif edge == 2:
                parts = [
                    jnp.where(lane == 0, lane_of(west_in, 64 + place), part)
                    for place, part in zip(places, parts)
                ]
            else:
                parts = [
                    jnp.where(lane == LANES - 1, lane_of(east_in, place), part)
                    for place, part in zip(places, parts)
                ]
            value = jnp.concatenate(parts, axis=1).reshape(quarter, rows, LANES)
            buffer[lines, port] = value.astype(BF)
        for port in range(ports):
            row, col, inside = port_place(port_ref, port, rows, width)

            @pl.when(inside)
            def _():
                current = buffer[lines, port].astype(F32)
                here = (lax.broadcasted_iota(jnp.int32, current.shape, 1) == row) & (
                    lax.broadcasted_iota(jnp.int32, current.shape, 2) == col
                )
                profile = port_profile_column(profile_ref, port, edge)
                profile = jnp.broadcast_to(profile, (quarter, LANES)).reshape(quarter, 1, LANES)
                added = current + jnp.broadcast_to(profile, current.shape)
                buffer[lines, port] = jnp.where(here, added, current).astype(BF)

        copy = pltpu.make_async_copy(buffer.at[lines], out_ref.at[lines], sems.at[edge])
        copy.start()
        copies.append(copy)
    for copy in copies:
        copy.wait()


def exchange(rims, axis):
    sizes = lax.axis_size("row"), lax.axis_size("col")
    at = ("row", "col").index(axis)

    def partner(place, first):
        place = list(place)
        other = place[at] + (1 if place[at] % 2 == first else -1)
        if 0 <= other < sizes[at]:
            place[at] = other
        else:
            place[1 - at] ^= 2
        return place[0] * sizes[1] + place[1]

    def pairs(first):
        places = [(row, col) for row in range(sizes[0]) for col in range(sizes[1])]
        return [(row * sizes[1] + col, partner((row, col), first)) for row, col in places]

    return [lax.ppermute(rim, ("row", "col"), pairs(first)) for first, rim in enumerate(rims)]


def body(traces, cell_type, port_cell, port_profile, mode_shapes, mode_values, mode_weights):
    edges, samples, ports, rows, width = traces.shape
    order = edges * samples
    quarter = samples
    tile = rows * width
    types = cell_type.reshape(1, tile)
    own_map, half, x, sides = own_type_map(mode_shapes, mode_values, mode_weights, traces, types)
    first = swap(own_map, (2, 0), (3, 8))
    second = swap(own_map, (6, 0), (7, 8))
    half = swap(half, (1, 8))
    profile = jnp.transpose(port_profile, (0, 2, 1))
    ports_spec = pl.BlockSpec(memory_space=pltpu.SMEM)
    next_shape = jax.ShapeDtypeStruct((order, ports * tile), BF)
    rim_shapes = [jax.ShapeDtypeStruct((quarter, ports * LANES), BF)] * 2 + [
        jax.ShapeDtypeStruct((quarter, LANES), BF)
    ] * 2
    work = 2 * order * order * len(MAP_STEPS) * ports * tile
    part_shapes = [next_shape] + rim_shapes[:2] + [jax.ShapeDtypeStruct((2 * quarter, LANES), BF)]

    def early(first, maps, parts=()):
        kernel = functools.partial(early_kernel, ports, first, len(maps))
        flops = work * len(maps) // 7
        return whole_call(kernel, part_shapes, x, types, *sides, *maps, *parts, flops=flops)

    parts = list(early(0, [own_map, first]))
    parts[1], first, second, half = lax.optimization_barrier((parts[1], first, second, half))
    map_shape = jax.ShapeDtypeStruct(own_map.shape, BF)
    (relay,) = whole_call(relay_kernel, [map_shape], first, second)
    relay, first, second, half = lax.optimization_barrier((relay, first, second, half))
    third = swap(relay, (2, 0), (6, 0))
    maps = [second, swap_cores(first), swap_cores(second), swap_cores(half), half]
    parts = list(early(2, maps, parts))
    parts[1], third = lax.optimization_barrier((parts[1], third))
    done, *parts = parts
    late = [third, swap_cores(third)]
    maps = [own_map, first] + maps + late
    sent = whole_call(
        functools.partial(rim_kernel, ports, 6),
        rim_shapes,
        x,
        types,
        *sides,
        *late,
        *parts,
        flops=work // 8,
    )
    halos = exchange(sent[:2], "row") + exchange(sent[2:], "col")
    x, picked = whole_call(
        functools.partial(first_kernel, rows, ports, 6),
        [next_shape, jax.ShapeDtypeStruct((order, LANES), BF)],
        x,
        types,
        done,
        *late,
        flops=work // 5000,
    )
    ends_shape = jax.ShapeDtypeStruct((order, 2 * ports * LANES), BF)
    operands = [port_cell, x, types, profile, picked, sides[1], *halos, *maps]
    x, ends, *sent = pl.pallas_call(
        functools.partial(ends_kernel, rows, ports, width),
        in_specs=[ports_spec] + [WHOLE] * (len(operands) - 1),
        out_specs=[WHOLE] * 6,
        out_shape=[next_shape, ends_shape] + rim_shapes,
        compiler_params=PARAMS,
        cost_estimate=pl.CostEstimate(flops=work // 3, bytes_accessed=0, transcendentals=0),
    )(*operands)
    halos = exchange(sent[:2], "row") + exchange(sent[2:], "col")
    (x,) = whole_call(
        functools.partial(second_kernel, rows, ports, width),
        [next_shape],
        x,
        types,
        ends,
        *maps,
        flops=work // 5000,
    )
    operands = [port_cell, x, profile, *halos]
    out = pl.pallas_call(
        functools.partial(last_kernel, rows, width),
        in_specs=[ports_spec] + [WHOLE] * (len(operands) - 1),
        out_specs=pl.BlockSpec(memory_space=pl.ANY),
        out_shape=jax.ShapeDtypeStruct((order, ports, rows, width), BF),
        scratch_shapes=[
            pltpu.VMEM((order, ports, rows, width), BF),
            pltpu.SemaphoreType.DMA((4,)),
        ],
        compiler_params=PARAMS,
    )(*operands)
    return out.reshape(traces.shape)


def solution(mesh):
    return jax.shard_map(
        body,
        mesh=mesh,
        in_specs=(
            P(None, None, None, "row", "col"),
            P("row", "col"),
            P(),
            P(),
            P("row", None, "col"),
            P("row", "col"),
            P("row", "col", None),
        ),
        out_specs=P(None, None, None, "row", "col"),
        check_vma=False,
    )
```
